32 devices in a mesh: dp: 4 (over x, core), ctx: 8 (over z, y).
Axes of the slice: x: 2, y: 2, z: 4, core: 2. Of those that a mesh axis runs over, the one named last changes fastest.
Arguments:
- hidden_in: bfloat16 [4, 1024, 2048], P('dp', 'ctx')
- grad_out: bfloat16 [4, 1024, 2048], P('dp', 'ctx'), may hold values from -6 to 6
- seg_len: int32 [4, 9], P('dp'), may hold values from 32 to 512, as said below
- seg_parent: int32 [4, 9], P('dp'), may hold values from 0 to 7, as said below
- gain_attn: bfloat16 [2048], replicated, may hold values from 0.5 to 1.5
- shift_attn: bfloat16 [2048], replicated, may hold values from -1 to 1
- w_qkv: bfloat16 [6144, 2048], P('ctx'), may hold values from -0.125 to 0.125
- bias_qkv: bfloat16 [6144], replicated, may hold values from -1 to 1
- w_out: bfloat16 [2048, 2048], P('ctx'), may hold values from -1 to 1
- bias_out: bfloat16 [2048], replicated, may hold values from -1 to 1
- gain_mlp: bfloat16 [2048], replicated, may hold values from 0.5 to 1.5
- shift_mlp: bfloat16 [2048], replicated, may hold values from -1 to 1
- w_up: bfloat16 [8192, 2048], P('ctx'), may hold values from -0.125 to 0.125
- bias_up: bfloat16 [8192], replicated, may hold values from -1 to 1
- w_down: bfloat16 [8192, 2048], P('ctx'), may hold values from -0.0625 to 0.0625
- bias_down: bfloat16 [2048], replicated, may hold values from -1 to 1
Outputs:
- hidden_out: bfloat16 [4, 1024, 2048], P('dp', 'ctx')
- grad_in: float32 [4, 1024, 2048], P('dp', 'ctx')
- grad_gain_attn: float32 [2048], replicated
- grad_shift_attn: float32 [2048], replicated
- grad_w_qkv: float32 [6144, 2048], P('ctx')
- grad_bias_qkv: float32 [6144], replicated
- grad_w_out: float32 [2048, 2048], P('ctx')
- grad_bias_out: float32 [2048], replicated
- grad_gain_mlp: float32 [2048], replicated
- grad_shift_mlp: float32 [2048], replicated
- grad_w_up: float32 [8192, 2048], P('ctx')
- grad_bias_up: float32 [8192], replicated
- grad_w_down: float32 [8192, 2048], P('ctx')
- grad_bias_down: float32 [2048], replicated
The draws below stay inside these ranges and needn't reach their ends.
Inputs may be any that keep to these rules, and one draw needn't show every extreme that they name: `seg_len`: lengths of a tree's 9 segments in stored order; they sum to 1024; segment 0, the trunk, holds 256 to 512 tokens, and in every draw some tree's trunk holds exactly 512; every other segment holds 32 or more. `seg_parent`: segment 0 is its own parent; four segments are branches with parent 0; each of the four others is a leaf whose parent is a branch stored before it, one leaf to a branch.
All inputs are finite; a program needn't handle non-finite values.
Results may differ from the reference program's by a relative error of at most 0.015.
Values may be sent and summed in bfloat16 or wider, within the bound.
A program may use at most 960 MiB of HBM per device.

```python
import math
import jax
import jax.numpy as jnp
from jax import lax

D = 2048
HEADS = 16
HEAD_DIM = 128
ROT_DIM = 32
FF = 8192
SEGS = 9
TREE = 1024
TREES = 4


def draw_hidden_in(key, part):
    base_key, row_key, column_key = jax.random.split(jax.random.fold_in(key, 3), 3)
    array_shape = (TREES, TREE, D)
    row_scale = jnp.exp(jax.random.uniform(row_key, (TREES, TREE, 1), minval=math.log(0.4), maxval=math.log(4.0)))
    column_scale = jnp.exp(jax.random.uniform(column_key, (1, 1, D), minval=math.log(0.4), maxval=math.log(4.0)))
    return (jax.random.normal(base_key, array_shape) * row_scale * column_scale).astype(jnp.bfloat16)


def draw_seg_len(key, part):
    seg_key = jax.random.fold_in(key, 5)
    pick_key, trees_key = jax.random.split(seg_key)
    longest_tree = jax.random.randint(pick_key, (), 0, TREES)

    def one_tree(tree_key, tree_label):
        trunk_key, share_key = jax.random.split(tree_key)
        drawn_trunk = TREE // 4 + jax.random.randint(trunk_key, (), 0, TREE // 4 + 1)
        trunk = jnp.where(tree_label == longest_tree, TREE // 2, drawn_trunk)
        base_len = TREE // 32
        spare = TREE - trunk - (SEGS - 1) * base_len
        shares_raw = jax.random.randint(share_key, (SEGS - 1,), 1, 9)
        shares = shares_raw * spare // jnp.sum(shares_raw)
        labels = jnp.arange(SEGS - 1)
        shares = shares + jnp.where(labels == SEGS - 2, spare - jnp.sum(shares), 0)
        return jnp.concatenate([jnp.reshape(trunk, (1,)), base_len + shares]).astype(jnp.int32)
    tree_keys = jax.random.split(trees_key, TREES)
    return jax.vmap(one_tree)(tree_keys, jnp.arange(TREES))


def draw_seg_parent(key, part):

    def one_tree(tree_key):
        order_key, mode_key = jax.random.split(tree_key)
        order = jax.random.permutation(order_key, 4).astype(jnp.int32)
        layout_mode = jax.random.randint(mode_key, (), 0, 2)
        depth_first = jnp.array([0, 0, 1, 0, 3, 0, 5, 0, 7], dtype=jnp.int32)
        breadth_first = jnp.concatenate([jnp.zeros((5,), jnp.int32), 1 + order])
        return jnp.where(layout_mode == 0, depth_first, breadth_first).astype(jnp.int32)
    tree_keys = jax.random.split(jax.random.fold_in(key, 7), TREES)
    return jax.vmap(one_tree)(tree_keys)


def levels(stream_key, dims, pieces, smallest, top_value):
    gain = 1.0
    for position, blocks in pieces:
        heights = jax.random.uniform(jax.random.fold_in(jax.random.fold_in(stream_key, 6), position), (blocks,), jnp.float32, smallest / len(pieces), top_value / len(pieces))
        gain = gain * jnp.repeat(jnp.exp(heights), dims[position] // blocks).reshape((-1,) + (1,) * (len(dims) - 1 - position))
    return gain


def normal_values(stream_key, extent, deviation, limit, cuts=(), kind=jnp.bfloat16):
    entries = jax.random.normal(stream_key, extent, jnp.float32) * deviation
    if len(cuts) > 0:
        entries = levels(stream_key, extent, cuts, -0.22, 0.18) * entries
    return jnp.clip(entries, min=-limit, max=limit).astype(kind)


def setup_inputs(seed: int = 0) -> dict:
    arg_keys = jax.random.split(jax.random.key(seed), 17)
    return {
        "hidden_in": draw_hidden_in(jax.random.fold_in(arg_keys[16], 71), 0),
        "grad_out": normal_values(arg_keys[1], (TREES, TREE, D), 1.0, 6.0, ((0, 4), (1, 8))),
        "seg_len": draw_seg_len(jax.random.fold_in(arg_keys[16], 71), 0),
        "seg_parent": draw_seg_parent(jax.random.fold_in(arg_keys[16], 71), 0),
        "gain_attn": jnp.clip(1.0 + 0.1 * jax.random.normal(arg_keys[4], (D,), jnp.float32), 0.5, 1.5).astype(jnp.bfloat16),
        "shift_attn": normal_values(arg_keys[5], (D,), 0.2, 1.0),
        "w_qkv": normal_values(arg_keys[6], (3 * D, D), D ** -0.5, 0.125, ((0, 8),)),
        "bias_qkv": normal_values(arg_keys[7], (3 * D,), 0.2, 1.0),
        "w_out": normal_values(arg_keys[8], (D, D), (max(1, D * 16 // TREE)) ** -0.5, 1.0, ((0, 8),)),
        "bias_out": normal_values(arg_keys[9], (D,), 0.2, 1.0),
        "gain_mlp": jnp.clip(1.0 + 0.1 * jax.random.normal(arg_keys[10], (D,), jnp.float32), 0.5, 1.5).astype(jnp.bfloat16),
        "shift_mlp": normal_values(arg_keys[11], (D,), 0.2, 1.0),
        "w_up": normal_values(arg_keys[12], (FF, D), D ** -0.5, 0.125, ((0, 8),)),
        "bias_up": normal_values(arg_keys[13], (FF,), 0.2, 1.0),
        "w_down": normal_values(arg_keys[14], (FF, D), FF ** -0.5, 0.0625, ((0, 8),)),
        "bias_down": normal_values(arg_keys[15], (D,), 0.2, 1.0),
    }


@jax.custom_vjp
def low(v):
    return lax.optimization_barrier(v.astype(jnp.bfloat16)).astype(jnp.float32)

@jax.custom_vjp
def low_back(v):
    return v

def low_keep(v):
    return (low(v), None)

def low_pass(kept, grad):
    return (grad,)

def back_keep(v):
    return (v, None)

def back_low(kept, grad):
    return (low(grad),)
low.defvjp(low_keep, low_pass)
low_back.defvjp(back_keep, back_low)
norm_eps = 1e-05
masked_score = -1e+30
highest = lax.Precision.HIGHEST

def layer_norm(values, gain_vec, shift_vec):
    average = lax.optimization_barrier(jnp.mean(values, axis=-1, keepdims=True))
    centred = values - average
    spread = lax.optimization_barrier(jnp.mean(centred * centred, axis=-1, keepdims=True))
    return centred * lax.rsqrt(spread + norm_eps) * gain_vec + shift_vec

def tree_tables(seg_len, seg_parent):
    seg_count = seg_len.shape[0]
    seg_ends = jnp.cumsum(seg_len).astype(jnp.int32)
    seg_starts = (seg_ends - seg_len).astype(jnp.int32)
    labels = jnp.arange(seg_count, dtype=jnp.int32)
    parent_hit = seg_parent[:, None] == labels[None, :]
    grand_parent = lax.optimization_barrier(jnp.sum(jnp.where(parent_hit, seg_parent[None, :], 0), axis=1)).astype(jnp.int32)
    itself = labels[:, None] == labels[None, :]
    ancestor = itself | parent_hit | (grand_parent[:, None] == labels[None, :])
    path_start = lax.optimization_barrier(jnp.sum(jnp.where(ancestor & jnp.logical_not(itself), seg_len[None, :], 0), axis=1)).astype(jnp.int32)
    return (seg_ends, seg_starts, ancestor, path_start)

def rotary_tables(path_pos):
    half_dim = ROT_DIM // 2
    inverse = jnp.power(10000.0, -2.0 * jnp.arange(half_dim, dtype=jnp.float32) / ROT_DIM)
    angles = path_pos.astype(jnp.float32)[:, None] * inverse[None, :]
    angles = jnp.concatenate([angles, angles], axis=1)
    return (jnp.cos(angles), jnp.sin(angles))

def rotate(head_values, cosine, sine):
    half_dim = ROT_DIM // 2
    turned = head_values[..., :ROT_DIM]
    swapped = jnp.concatenate([-turned[..., half_dim:], turned[..., :half_dim]], axis=-1)
    mixed = turned * cosine[:, None, :] + swapped * sine[:, None, :]
    return jnp.concatenate([mixed, head_values[..., ROT_DIM:]], axis=-1)

def attention(queries, keys, values, seg_index, query_reach):
    total_rows = queries.shape[0]
    block_rows = 512 if total_rows % 512 == 0 else total_rows
    block_count = total_rows // block_rows
    scale_factor = 1.0 / math.sqrt(HEAD_DIM)
    token_rows = jnp.arange(total_rows, dtype=jnp.int32)

    def one_block(block_items):
        query_block, reach_block, row_block = block_items
        scores = jnp.einsum('qhd,khd->qhk', query_block, keys, precision=highest) * scale_factor
        scores = low_back(scores)
        reach_keys = jnp.take(reach_block, seg_index, axis=1)
        allowed = reach_keys & (token_rows[None, :] <= row_block[:, None])
        scores = jnp.where(allowed[:, None, :], scores, masked_score)
        row_top = lax.optimization_barrier(jnp.max(scores, axis=-1, keepdims=True))
        expo = jnp.exp(scores - row_top)
        prob_mass = expo / lax.optimization_barrier(jnp.sum(expo, axis=-1, keepdims=True))
        prob_mass = low(prob_mass)
        return jnp.einsum('qhk,khd->qhd', prob_mass, values, precision=highest)
    block_items = (queries.reshape(block_count, block_rows, HEADS, HEAD_DIM), query_reach.reshape(block_count, block_rows, query_reach.shape[1]), token_rows.reshape(block_count, block_rows))
    outputs = lax.map(jax.checkpoint(one_block), block_items)
    return outputs.reshape(total_rows, HEADS * HEAD_DIM)

def one_tree(inputs, params, tables):
    gain_attn, shift_attn, w_qkv, bias_qkv, w_out, bias_out, gain_mlp, shift_mlp, w_up, bias_up, w_down, bias_down = params
    cosine, sine, seg_index, query_reach = tables
    total_rows = inputs.shape[0]
    x_attn = low(layer_norm(inputs, gain_attn, shift_attn))
    x_mlp = low(layer_norm(inputs, gain_mlp, shift_mlp))
    qkv = low_back(jnp.dot(x_attn, w_qkv.T, precision=highest) + bias_qkv)
    head_shape = (total_rows, HEADS, HEAD_DIM)
    queries = low(rotate(qkv[:, :D].reshape(head_shape), cosine, sine))
    keys = low(rotate(qkv[:, D:2 * D].reshape(head_shape), cosine, sine))
    values = low(qkv[:, 2 * D:].reshape(head_shape))
    attended = low(low_back(attention(queries, keys, values, seg_index, query_reach)))
    attn_proj = jnp.dot(attended, w_out.T, precision=highest) + bias_out
    pre_act = low_back(jnp.dot(x_mlp, w_up.T, precision=highest) + bias_up)
    activated = low(jax.nn.gelu(pre_act, approximate=False))
    mlp_out = jnp.dot(activated, w_down, precision=highest) + bias_down
    return inputs + attn_proj + mlp_out

def reference(hidden_in, grad_out, seg_len, seg_parent, gain_attn, shift_attn, w_qkv, bias_qkv, w_out, bias_out, gain_mlp, shift_mlp, w_up, bias_up, w_down, bias_down):
    params = tuple((member.astype(jnp.float32) for member in (gain_attn, shift_attn, w_qkv, bias_qkv, w_out, bias_out, gain_mlp, shift_mlp, w_up, bias_up, w_down, bias_down)))
    inputs = hidden_in.astype(jnp.float32)
    tree_count = hidden_in.shape[0]
    total_rows = hidden_in.shape[1]
    tables = []
    for tree_index in range(tree_count):
        seg_ends, seg_starts, ancestor, path_start = tree_tables(seg_len[tree_index], seg_parent[tree_index])
        token_rows = jnp.arange(total_rows, dtype=jnp.int32)
        seg_index = lax.optimization_barrier(jnp.sum((token_rows[:, None] >= seg_ends[None, :]).astype(jnp.int32), axis=1)).astype(jnp.int32)
        path_pos = (token_rows + jnp.take(path_start - seg_starts, seg_index)).astype(jnp.int32)
        cosine, sine = rotary_tables(path_pos)
        query_reach = jnp.take(ancestor, seg_index, axis=0)
        tables.append((cosine, sine, seg_index, query_reach))

    def forward(layer_inputs, layer_params):
        return jnp.stack([one_tree(layer_inputs[tree_index], layer_params, tables[tree_index]) for tree_index in range(tree_count)])
    result, pull = jax.vjp(forward, inputs, params)
    input_grad, param_grads = pull(grad_out.astype(jnp.float32))
    return (result.astype(jnp.bfloat16), input_grad, param_grads[0], param_grads[1], param_grads[2], param_grads[3], param_grads[4], param_grads[5], param_grads[6], param_grads[7], param_grads[8], param_grads[9], param_grads[10], param_grads[11])
```

```python
import math

import jax
import jax.numpy as jnp
from jax import lax
from jax.sharding import PartitionSpec as P

D = 2048
HEADS = 16
HEAD_DIM = 128
ROT_DIM = 32
FF = 8192

norm_eps = 1e-05
masked_score = -1e30
f32 = jnp.float32
bf16 = jnp.bfloat16


def tree_tables(seg_len, seg_parent):
    seg_count = seg_len.shape[0]
    labels = jnp.arange(seg_count, dtype=jnp.int32)
    earlier = labels[:, None] > labels[None, :]
    seg_starts = jnp.sum(jnp.where(earlier, seg_len[None, :], 0), axis=1)
    seg_ends = seg_starts + seg_len
    parent_hit = seg_parent[:, None] == labels[None, :]
    grand_parent = jnp.sum(jnp.where(parent_hit, seg_parent[None, :], 0), axis=1)
    itself = labels[:, None] == labels[None, :]
    ancestor = itself | parent_hit | (grand_parent[:, None] == labels[None, :])
    path_start = jnp.sum(jnp.where(ancestor & jnp.logical_not(itself), seg_len[None, :], 0), axis=1)
    return (seg_ends, seg_starts, ancestor, path_start)


def rotary_tables(path_pos):
    half_dim = ROT_DIM // 2
    inverse = jnp.power(10000.0, -2.0 * jnp.arange(half_dim, dtype=f32) / ROT_DIM)
    angles = path_pos.astype(f32)[:, None] * inverse[None, :]
    angles = jnp.concatenate([angles, angles], axis=1)
    return (jnp.cos(angles), jnp.sin(angles))


def rotate(head_values, cosine, sine):
    half_dim = ROT_DIM // 2
    turned = head_values[..., :ROT_DIM]
    swapped = jnp.concatenate([-turned[..., half_dim:], turned[..., :half_dim]], axis=-1)
    mixed = turned * cosine[:, None, :] + swapped * sine[:, None, :]
    return jnp.concatenate([mixed, head_values[..., ROT_DIM:]], axis=-1)


def gelu_slope(pre_act):
    normal_cdf = 0.5 * (1.0 + lax.erf(pre_act / math.sqrt(2.0)))
    return normal_cdf + pre_act * jnp.exp(-0.5 * pre_act * pre_act) / math.sqrt(2.0 * math.pi)


def dot_nt(a, b):
    return lax.dot_general(a, b, (((1,), (1,)), ((), ())), preferred_element_type=f32)


def dot_nn(a, b):
    return lax.dot_general(a, b, (((1,), (0,)), ((), ())), preferred_element_type=f32)


def dot_tn(a, b):
    return lax.dot_general(a, b, (((0,), (0,)), ((), ())), preferred_element_type=f32)


def body(
    hidden_in,
    grad_out,
    seg_len,
    seg_parent,
    gain_attn,
    shift_attn,
    w_qkv,
    bias_qkv,
    w_out,
    bias_out,
    gain_mlp,
    shift_mlp,
    w_up,
    bias_up,
    w_down,
    bias_down,
):
    group = lax.axis_size("ctx")
    me = lax.axis_index("ctx")
    local_rows = hidden_in.shape[1]
    tokens = local_rows * group
    head_count = HEADS // group
    head_cols = head_count * HEAD_DIM
    head_shape = (tokens, head_count, HEAD_DIM)
    scale = 1.0 / math.sqrt(HEAD_DIM)

    hidden_all = lax.all_gather(hidden_in[0], "ctx", axis=0, tiled=True)
    grad_all = lax.all_gather(grad_out[0], "ctx", axis=0, tiled=True)

    blocks = w_qkv.reshape(3, head_cols, D)
    arrived = jnp.stack(
        [
            lax.ppermute(blocks[j], "ctx", [(c, (3 * c + j) % group) for c in range(group)])
            for j in range(3)
        ]
    )
    slots = [(kind * group + me) % 3 for kind in range(3)]
    w_heads = [lax.dynamic_index_in_dim(arrived, slot, 0, keepdims=False) for slot in slots]
    w_out_cols = lax.all_to_all(
        w_out, "ctx", split_axis=1, concat_axis=0, tiled=True
    )

    seg_ends, seg_starts, ancestor, path_start = tree_tables(seg_len[0], seg_parent[0])
    ids = jnp.arange(tokens, dtype=jnp.int32)
    seg_index = jnp.sum((ids[:, None] >= seg_ends[None, :]).astype(jnp.int32), axis=1)
    labels = jnp.arange(seg_ends.shape[0], dtype=jnp.int32)
    hot = (seg_index[:, None] == labels[None, :]).astype(f32)
    reach = jnp.dot(hot, ancestor.astype(f32))
    path_pos = ids + jnp.sum(hot.astype(jnp.int32) * (path_start - seg_starts)[None, :], axis=1)
    cosine, sine = rotary_tables(path_pos)
    allowed = (jnp.dot(reach, hot.T) > 0.5) & (ids[None, :] <= ids[:, None])

    gain_a = gain_attn.astype(f32)
    gain_m = gain_mlp.astype(f32)
    hid = hidden_all.astype(f32)
    mean = jnp.mean(hid, axis=-1, keepdims=True)
    centred = hid - mean
    rstd = lax.rsqrt(jnp.mean(centred * centred, axis=-1, keepdims=True) + norm_eps)
    normed = centred * rstd
    x_attn = (normed * gain_a + shift_attn.astype(f32)).astype(bf16)
    x_mlp = (normed * gain_m + shift_mlp.astype(f32)).astype(bf16)

    my_bias = [
        lax.dynamic_slice_in_dim(bias_qkv, kind * D + me * head_cols, head_cols).astype(f32)
        for kind in range(3)
    ]
    q_raw, k_raw, v_raw = [
        (dot_nt(x_attn, w_heads[kind]) + my_bias[kind]).reshape(head_shape) for kind in range(3)
    ]
    q = rotate(q_raw, cosine, sine).astype(bf16)
    k = rotate(k_raw, cosine, sine).astype(bf16)
    v = v_raw.astype(bf16)
    scores = jnp.einsum("qhd,khd->hqk", q, k, preferred_element_type=f32) * scale
    scores = jnp.where(allowed[None], scores, masked_score)
    top = jnp.max(scores, axis=-1, keepdims=True)
    expo = jnp.exp(scores - top)
    probs = expo / jnp.sum(expo, axis=-1, keepdims=True)
    weights = probs.astype(bf16)
    attended = jnp.einsum("hqk,khd->qhd", weights, v, preferred_element_type=f32).astype(bf16)
    attended = attended.reshape(tokens, head_cols)

    up_bias = lax.dynamic_slice_in_dim(bias_up, me * w_up.shape[0], w_up.shape[0]).astype(f32)
    pre_act = dot_nt(x_mlp, w_up) + up_bias
    act = jax.nn.gelu(pre_act, approximate=False).astype(bf16)
    partial = dot_nt(attended, w_out_cols) + dot_nn(act, w_down)
    summed = lax.psum_scatter(partial.astype(bf16), "ctx", scatter_dimension=0, tiled=True)
    hidden_out = (
        hidden_in[0].astype(f32) + summed.astype(f32) + bias_out.astype(f32) + bias_down.astype(f32)
    ).astype(bf16)

    grad_w_down = dot_tn(act, grad_all).astype(bf16)
    pre_grad = (dot_nt(grad_all, w_down) * gelu_slope(pre_act)).astype(bf16)
    grad_w_up = dot_tn(pre_grad, x_mlp).astype(bf16)
    mlp_in_grad = dot_nn(pre_grad, w_up)

    grad_w_out_cols = dot_tn(grad_all, attended).astype(bf16)
    att_grad = dot_nn(grad_all, w_out_cols).astype(bf16).reshape(head_shape)
    prob_grad = jnp.einsum("qhd,khd->hqk", att_grad, v, preferred_element_type=f32)
    delta = jnp.sum(probs * prob_grad, axis=-1, keepdims=True)
    score_grad = (probs * (prob_grad - delta)).astype(bf16)
    q_grad = jnp.einsum("hqk,khd->qhd", score_grad, k, preferred_element_type=f32) * scale
    k_grad = jnp.einsum("hqk,qhd->khd", score_grad, q, preferred_element_type=f32) * scale
    v_grad = jnp.einsum("hqk,qhd->khd", weights, att_grad, preferred_element_type=f32)
    qkv_grad = [
        rotate(q_grad, cosine, -sine).astype(bf16).reshape(tokens, head_cols),
        rotate(k_grad, cosine, -sine).astype(bf16).reshape(tokens, head_cols),
        v_grad.astype(bf16).reshape(tokens, head_cols),
    ]
    attn_in_grad = sum(dot_nn(qkv_grad[kind], w_heads[kind]) for kind in range(3))
    grad_heads = jnp.stack([dot_tn(qkv_grad[kind], x_attn).astype(bf16) for kind in range(3)])

    back = attn_in_grad * gain_a + mlp_in_grad * gain_m
    w_sum = lax.psum_scatter(back.astype(bf16), "ctx", scatter_dimension=0, tiled=True).astype(f32)
    start = me * local_rows
    my_rstd = lax.dynamic_slice_in_dim(rstd, start, local_rows)
    my_normed = (
        hidden_in[0].astype(f32) - lax.dynamic_slice_in_dim(mean, start, local_rows)
    ) * my_rstd
    grad_f = grad_out[0].astype(f32)
    grad_in = (
        grad_f
        + (
            w_sum
            - jnp.mean(w_sum, axis=-1, keepdims=True)
            - my_normed * jnp.mean(w_sum * my_normed, axis=-1, keepdims=True)
        )
        * my_rstd
    )

    def widen(part, length, at):
        return lax.dynamic_update_slice(jnp.zeros((length,), f32), part, (at,))

    bias_qkv_grad = jnp.concatenate(
        [
            widen(jnp.sum(qkv_grad[kind], axis=0, dtype=f32), D, me * head_cols)
            for kind in range(3)
        ]
    )
    vectors = jnp.concatenate(
        [
            jnp.sum(attn_in_grad * normed, axis=0),
            jnp.sum(attn_in_grad, axis=0),
            jnp.sum(mlp_in_grad * normed, axis=0),
            jnp.sum(mlp_in_grad, axis=0),
            bias_qkv_grad,
            jnp.sum(grad_f, axis=0),
            widen(jnp.sum(pre_grad, axis=0, dtype=f32), FF, me * w_up.shape[0]),
        ]
    )
    vectors = lax.psum(vectors, ("dp", "ctx"))
    cuts = [D, D, D, D, 3 * D, D, FF]
    ends = [sum(cuts[: i + 1]) for i in range(len(cuts))]
    gain_grad_a, shift_grad_a, gain_grad_m, shift_grad_m, qkv_bias_grad, out_bias_grad, up_bias_grad = [
        vectors[end - cut : end] for cut, end in zip(cuts, ends)
    ]

    returned = []
    for j in range(3):
        kind_of_slot = sum(
            kind * ((kind * group + me) % 3 == j).astype(jnp.int32) for kind in range(3)
        )
        block = lax.dynamic_index_in_dim(grad_heads, kind_of_slot, 0, keepdims=False)
        returned.append(
            lax.ppermute(block, "ctx", [((3 * c + j) % group, c) for c in range(group)])
        )
    grad_w_qkv = jnp.concatenate(returned, axis=0)
    grad_w_out = lax.all_to_all(
        grad_w_out_cols, "ctx", split_axis=0, concat_axis=1, tiled=True
    )
    return (
        hidden_out[None],
        grad_in[None],
        gain_grad_a,
        shift_grad_a,
        lax.psum(grad_w_qkv, "dp").astype(f32),
        qkv_bias_grad,
        lax.psum(grad_w_out, "dp").astype(f32),
        out_bias_grad,
        gain_grad_m,
        shift_grad_m,
        lax.psum(grad_w_up, "dp").astype(f32),
        up_bias_grad,
        lax.psum(grad_w_down, "dp").astype(f32),
        out_bias_grad,
    )


block_limit = 512


def layer_norm(values, gain_vec, shift_vec):
    average = jnp.mean(values, axis=-1, keepdims=True)
    centred = values - average
    spread = jnp.mean(centred * centred, axis=-1, keepdims=True)
    return centred * lax.rsqrt(spread + norm_eps) * gain_vec + shift_vec


def segment_hot(row_ids, seg_ends):
    seg_index = jnp.sum((row_ids[:, None] >= seg_ends[None, :]).astype(jnp.int32), axis=1)
    labels = jnp.arange(seg_ends.shape[0], dtype=jnp.int32)
    return (seg_index[:, None] == labels[None, :]).astype(jnp.float32)


def row_lookup(row_ids, seg_ends, ancestor_f):
    row_hot = segment_hot(row_ids, seg_ends)
    return (row_hot, jnp.dot(row_hot, ancestor_f))


def permitted(query_ids, query_reach, key_ids, key_hot):
    linked = jnp.dot(query_reach, key_hot.T) > 0.5
    return linked & (key_ids[None, :] <= query_ids[:, None])


def inner_block(row_count):
    block_rows = row_count
    while block_rows > block_limit and block_rows % 2 == 0:
        block_rows = block_rows // 2
    return block_rows


def gather_body(
    hidden_in,
    grad_out,
    seg_len,
    seg_parent,
    gain_attn,
    shift_attn,
    w_qkv,
    bias_qkv,
    w_out,
    bias_out,
    gain_mlp,
    shift_mlp,
    w_up,
    bias_up,
    w_down,
    bias_down,
):
    local_rows = hidden_in.shape[1]
    scale_factor = 1.0 / math.sqrt(HEAD_DIM)
    head_shape = (local_rows, HEADS, HEAD_DIM)
    seg_ends, seg_starts, ancestor, path_start = tree_tables(seg_len[0], seg_parent[0])
    ancestor_f = ancestor.astype(jnp.float32)
    my_ids = lax.axis_index("ctx") * local_rows + jnp.arange(local_rows, dtype=jnp.int32)
    my_hot, my_reach = row_lookup(my_ids, seg_ends, ancestor_f)
    shift_table = path_start - seg_starts
    path_pos = my_ids + jnp.sum(my_hot.astype(jnp.int32) * shift_table[None, :], axis=1)
    cosine, sine = rotary_tables(path_pos)
    inputs_f = hidden_in[0].astype(jnp.float32)
    gain_a = gain_attn.astype(jnp.float32)
    shift_a = shift_attn.astype(jnp.float32)
    gain_m = gain_mlp.astype(jnp.float32)
    shift_m = shift_mlp.astype(jnp.float32)
    bias_up_f = bias_up.astype(jnp.float32)
    x_attn = layer_norm(inputs_f, gain_a, shift_a).astype(jnp.bfloat16)
    x_mlp = layer_norm(inputs_f, gain_m, shift_m).astype(jnp.bfloat16)
    qkv = jnp.einsum(
        "td,nd->tn",
        x_attn,
        lax.all_gather(w_qkv, "ctx", axis=0, tiled=True),
        preferred_element_type=jnp.float32,
    ) + bias_qkv.astype(jnp.float32)
    queries = rotate(qkv[:, :D].reshape(head_shape), cosine, sine).astype(jnp.bfloat16)
    keys_heads = rotate(qkv[:, D : 2 * D].reshape(head_shape), cosine, sine).astype(jnp.bfloat16)
    values_flat = qkv[:, 2 * D :].astype(jnp.bfloat16)
    values_heads = values_flat.reshape(head_shape)
    keys_flat = keys_heads.reshape(local_rows, D)
    queries_flat = queries.reshape(local_rows, D)

    def split_blocks(shard_pieces):
        row_count = shard_pieces[0].shape[0]
        block_rows = inner_block(row_count)
        block_count = row_count // block_rows
        shaped = tuple(
            (member.reshape(block_count, block_rows, HEADS, HEAD_DIM) for member in shard_pieces)
        )
        starts = block_rows * jnp.arange(block_count, dtype=jnp.int32)
        return shaped + (starts,)

    def attend_block(fold_state, block_items):
        key_block, value_block, block_start = block_items
        block_rows = key_block.shape[0]
        key_ids = block_start + jnp.arange(block_rows, dtype=jnp.int32)
        allowed = permitted(my_ids, my_reach, key_ids, segment_hot(key_ids, seg_ends))
        row_top, row_total, partial_value = fold_state
        scores = (
            jnp.einsum("qhd,khd->qhk", queries, key_block, preferred_element_type=jnp.float32)
            * scale_factor
        )
        scores = jnp.where(allowed[:, None, :], scores, masked_score)
        new_top = jnp.maximum(row_top, jnp.max(scores, axis=-1))
        factor = jnp.exp(row_top - new_top)
        weights = jnp.exp(scores - new_top[:, :, None])
        row_total = row_total * factor + jnp.sum(weights, axis=-1)
        partial_value = partial_value * factor[:, :, None] + jnp.einsum(
            "qhk,khd->qhd",
            weights.astype(jnp.bfloat16),
            value_block,
            preferred_element_type=jnp.float32,
        )
        fold_state = (new_top, row_total, partial_value)
        return (fold_state, None)

    start_state = (
        jnp.full((local_rows, HEADS), masked_score, jnp.float32),
        jnp.zeros((local_rows, HEADS), jnp.float32),
        jnp.zeros(head_shape, jnp.float32),
    )
    row_top, row_total, partial_value = lax.scan(
        attend_block,
        start_state,
        split_blocks(
            (
                lax.all_gather(keys_flat, "ctx", axis=0, tiled=True),
                lax.all_gather(values_flat, "ctx", axis=0, tiled=True),
            )
        ),
    )[0]
    log_total = row_top + jnp.log(row_total)
    attended_f = partial_value / row_total[:, :, None]
    attended = attended_f.reshape(local_rows, D).astype(jnp.bfloat16)
    attn_proj = jnp.einsum(
        "td,nd->tn",
        attended,
        lax.all_gather(w_out, "ctx", axis=0, tiled=True),
        preferred_element_type=jnp.float32,
    )

    def mlp_pre(up_rows):
        return (
            jnp.einsum("td,nd->tn", x_mlp, up_rows, preferred_element_type=jnp.float32) + bias_up_f
        )

    up_rows = lax.all_gather(w_up, "ctx", axis=0, tiled=True)
    down_rows = lax.all_gather(w_down, "ctx", axis=0, tiled=True)
    activated = jax.nn.gelu(mlp_pre(up_rows), approximate=False).astype(jnp.bfloat16)
    mlp_sum = jnp.dot(activated, down_rows, preferred_element_type=jnp.float32)
    bias_out_f = bias_out.astype(jnp.float32)
    bias_down_f = bias_down.astype(jnp.float32)
    hidden_out = (inputs_f + attn_proj + bias_out_f + mlp_sum + bias_down_f).astype(jnp.bfloat16)
    grad_b = grad_out[0]
    grad_f = grad_b.astype(jnp.float32)
    up_rows = lax.all_gather(w_up, "ctx", axis=0, tiled=True)
    down_rows = lax.all_gather(w_down, "ctx", axis=0, tiled=True)
    pre_act = mlp_pre(up_rows)
    activated = jax.nn.gelu(pre_act, approximate=False).astype(jnp.bfloat16)
    act_grad = jnp.einsum("td,nd->tn", grad_b, down_rows, preferred_element_type=jnp.float32)
    pre_grad = (act_grad * gelu_slope(pre_act)).astype(jnp.bfloat16)
    input_grad = jnp.dot(pre_grad, up_rows, preferred_element_type=jnp.float32)
    act_all = activated
    pre_grad_all = pre_grad
    act_all, pre_grad_all, mlp_in_grad = (act_all, pre_grad_all, input_grad)
    attended_grad = jnp.dot(
        grad_b, lax.all_gather(w_out, "ctx", axis=0, tiled=True), preferred_element_type=jnp.float32
    ).astype(jnp.bfloat16)
    attended_grad_heads = attended_grad.reshape(head_shape)
    row_delta = jnp.sum(attended_grad_heads.astype(jnp.float32) * attended_f, axis=-1)
    all_log_total, all_delta = (
        lax.all_gather(log_total, "ctx", axis=0, tiled=True),
        lax.all_gather(row_delta, "ctx", axis=0, tiled=True),
    )

    def back_block(fold_state, block_items):
        key_block, value_block, query_block, grad_block, block_start = block_items
        block_rows = key_block.shape[0]
        other_ids = block_start + jnp.arange(block_rows, dtype=jnp.int32)
        other_hot, other_reach = row_lookup(other_ids, seg_ends, ancestor_f)
        allowed_in = permitted(my_ids, my_reach, other_ids, other_hot)
        allowed_out = permitted(other_ids, other_reach, my_ids, my_hot)
        other_log = lax.dynamic_slice_in_dim(all_log_total, block_start, block_rows, 0)
        other_delta = lax.dynamic_slice_in_dim(all_delta, block_start, block_rows, 0)
        query_grad, key_grad, value_grad = fold_state
        scores = (
            jnp.einsum("qhd,khd->qhk", queries, key_block, preferred_element_type=jnp.float32)
            * scale_factor
        )
        scores = jnp.where(allowed_in[:, None, :], scores, masked_score)
        prob_mass = jnp.exp(scores - log_total[:, :, None])
        prob_grad = jnp.einsum(
            "qhd,khd->qhk", attended_grad_heads, value_block, preferred_element_type=jnp.float32
        )
        score_grad = (prob_mass * (prob_grad - row_delta[:, :, None])).astype(jnp.bfloat16)
        query_grad = (
            query_grad
            + jnp.einsum("qhk,khd->qhd", score_grad, key_block, preferred_element_type=jnp.float32)
            * scale_factor
        )
        outgoing_key_grad = key_grad
        outgoing_value_grad = value_grad
        scores = (
            jnp.einsum("qhd,khd->qhk", query_block, keys_heads, preferred_element_type=jnp.float32)
            * scale_factor
        )
        scores = jnp.where(allowed_out[:, None, :], scores, masked_score)
        prob_mass = jnp.exp(scores - other_log[:, :, None])
        outgoing_value_grad = outgoing_value_grad + jnp.einsum(
            "qhk,qhd->khd",
            prob_mass.astype(jnp.bfloat16),
            grad_block,
            preferred_element_type=jnp.float32,
        )
        prob_grad = jnp.einsum(
            "qhd,khd->qhk", grad_block, values_heads, preferred_element_type=jnp.float32
        )
        score_grad = (prob_mass * (prob_grad - other_delta[:, :, None])).astype(jnp.bfloat16)
        outgoing_key_grad = (
            outgoing_key_grad
            + jnp.einsum(
                "qhk,qhd->khd", score_grad, query_block, preferred_element_type=jnp.float32
            )
            * scale_factor
        )
        fold_state = (query_grad, outgoing_key_grad, outgoing_value_grad)
        return (fold_state, None)

    zero_heads = jnp.zeros(head_shape, jnp.float32)
    query_grad, key_grad, value_grad = lax.scan(
        back_block,
        (zero_heads, zero_heads, zero_heads),
        split_blocks(
            (
                lax.all_gather(keys_flat, "ctx", axis=0, tiled=True),
                lax.all_gather(values_flat, "ctx", axis=0, tiled=True),
                lax.all_gather(queries_flat, "ctx", axis=0, tiled=True),
                lax.all_gather(attended_grad, "ctx", axis=0, tiled=True),
            )
        ),
    )[0]

    def turn(head_values):
        return rotate(head_values, cosine, sine)

    unturn = jax.vjp(turn, zero_heads)[1]
    qkv_grad = jnp.concatenate(
        [
            unturn(query_grad)[0].reshape(local_rows, D),
            unturn(key_grad)[0].reshape(local_rows, D),
            value_grad.reshape(local_rows, D),
        ],
        axis=1,
    ).astype(jnp.bfloat16)
    attn_in_grad = jnp.dot(
        qkv_grad,
        lax.all_gather(w_qkv, "ctx", axis=0, tiled=True),
        preferred_element_type=jnp.float32,
    )
    pull_attn = jax.vjp(layer_norm, inputs_f, gain_a, shift_a)[1]
    input_part_a, gain_grad_a, shift_grad_a = pull_attn(attn_in_grad)
    pull_mlp = jax.vjp(layer_norm, inputs_f, gain_m, shift_m)[1]
    input_part_m, gain_grad_m, shift_grad_m = pull_mlp(mlp_in_grad)
    grad_in = (grad_f + input_part_a + input_part_m)[None]
    vector_sums = lax.psum(
        (
            gain_grad_a,
            shift_grad_a,
            gain_grad_m,
            shift_grad_m,
            jnp.sum(qkv_grad, axis=0, dtype=jnp.float32),
            jnp.sum(grad_f, axis=0),
            jnp.sum(pre_grad_all, axis=0, dtype=jnp.float32),
        ),
        ("dp", "ctx"),
    )
    group_count = lax.axis_size("ctx")
    section_rows = (3 * D // group_count, D // group_count, FF // group_count, FF // group_count)
    term_sources = (
        (qkv_grad, x_attn),
        (grad_b, attended),
        (pre_grad_all, x_mlp),
        (act_all, grad_b),
    )
    owner_rows = sum(section_rows)
    blocks = jnp.arange(owner_rows * lax.axis_size("ctx") // owner_rows, dtype=jnp.int32)
    parts_list = []
    for (column_source, other_side), full_rows in zip(term_sources, section_rows):
        sub_rows = full_rows // 1
        column_ids = (
            blocks[:, None] * sub_rows + jnp.arange(sub_rows, dtype=jnp.int32)[None, :]
        ).reshape(-1)
        columns = jnp.take(column_source, column_ids, axis=1)
        block_term = jnp.einsum(
            "tr,td->rd", columns, other_side, preferred_element_type=jnp.float32
        )
        parts_list.append(block_term.reshape(blocks.shape[0], sub_rows, D))
    owned_term = lax.psum_scatter(
        jnp.concatenate(parts_list, axis=1).reshape(-1, D).astype(jnp.bfloat16),
        "ctx",
        scatter_dimension=0,
        tiled=True,
    ).astype(jnp.float32)
    cut_a = section_rows[0]
    cut_b = cut_a + section_rows[1]
    cut_c = cut_b + section_rows[2]
    weight_grads = (
        lax.psum(owned_term[:cut_a].astype(jnp.bfloat16), "dp").astype(jnp.float32),
        lax.psum(owned_term[cut_a:cut_b].astype(jnp.bfloat16), "dp").astype(jnp.float32),
        lax.psum(owned_term[cut_b:cut_c].astype(jnp.bfloat16), "dp").astype(jnp.float32),
        lax.psum(owned_term[cut_c:].astype(jnp.bfloat16), "dp").astype(jnp.float32),
    )
    return (
        hidden_out[None],
        grad_in,
        vector_sums[0],
        vector_sums[1],
        weight_grads[0],
        vector_sums[4],
        weight_grads[1],
        vector_sums[5],
        vector_sums[2],
        vector_sums[3],
        weight_grads[2],
        vector_sums[6],
        weight_grads[3],
        vector_sums[5],
    )


def solution(mesh):
    token = P("dp", "ctx", None)
    rows = P("ctx", None)
    return jax.shard_map(
        body if HEADS % mesh.shape["ctx"] == 0 else gather_body,
        mesh=mesh,
        in_specs=(
            token,
            token,
            P("dp", None),
            P("dp", None),
            P(),
            P(),
            rows,
            P(),
            rows,
            P(),
            P(),
            P(),
            rows,
            P(),
            rows,
            P(),
        ),
        out_specs=(
            token,
            token,
            P(),
            P(),
            rows,
            P(),
            rows,
            P(),
            P(),
            P(),
            rows,
            P(),
            rows,
            P(),
        ),
        check_vma=False,
    )
```

```python
import functools
import math

import jax
import jax.numpy as jnp
from jax import lax
from jax.experimental import pallas as pl
from jax.experimental.pallas import tpu as pltpu
from jax.sharding import PartitionSpec as P

D = 2048
HEADS = 16
HEAD_DIM = 128
ROT_DIM = 32
FF = 8192

norm_eps = 1e-05
masked_score = -1e30
f32 = jnp.float32
bf16 = jnp.bfloat16


def tree_tables(seg_len, seg_parent):
    seg_count = seg_len.shape[0]
    labels = jnp.arange(seg_count, dtype=jnp.int32)
    earlier = labels[:, None] > labels[None, :]
    seg_starts = jnp.sum(jnp.where(earlier, seg_len[None, :], 0), axis=1)
    seg_ends = seg_starts + seg_len
    parent_hit = seg_parent[:, None] == labels[None, :]
    grand_parent = jnp.sum(jnp.where(parent_hit, seg_parent[None, :], 0), axis=1)
    itself = labels[:, None] == labels[None, :]
    ancestor = itself | parent_hit | (grand_parent[:, None] == labels[None, :])
    path_start = jnp.sum(jnp.where(ancestor & jnp.logical_not(itself), seg_len[None, :], 0), axis=1)
    return (seg_ends, seg_starts, ancestor, path_start)


def rotary_tables(path_pos):
    half_dim = ROT_DIM // 2
    inverse = jnp.power(10000.0, -2.0 * jnp.arange(half_dim, dtype=f32) / ROT_DIM)
    angles = path_pos.astype(f32)[:, None] * inverse[None, :]
    angles = jnp.concatenate([angles, angles], axis=1)
    return (jnp.cos(angles), jnp.sin(angles))


def rotate(head_values, cosine, sine):
    half_dim = ROT_DIM // 2
    turned = head_values[..., :ROT_DIM]
    swapped = jnp.concatenate([-turned[..., half_dim:], turned[..., :half_dim]], axis=-1)
    mixed = turned * cosine[:, None, :] + swapped * sine[:, None, :]
    return jnp.concatenate([mixed, head_values[..., ROT_DIM:]], axis=-1)


def gelu_slope(pre_act):
    normal_cdf = 0.5 * (1.0 + lax.erf(pre_act / math.sqrt(2.0)))
    return normal_cdf + pre_act * jnp.exp(-0.5 * pre_act * pre_act) / math.sqrt(2.0 * math.pi)


def dot_nt(a, b):
    return lax.dot_general(a, b, (((1,), (1,)), ((), ())), preferred_element_type=f32)


def dot_nn(a, b):
    return lax.dot_general(a, b, (((1,), (0,)), ((), ())), preferred_element_type=f32)


def dot_tn(a, b):
    return lax.dot_general(a, b, (((0,), (0,)), ((), ())), preferred_element_type=f32)


MESH = pl.DeviceIdType.MESH
RAILS = 2


def place(group):
    dp = lax.axis_index("dp")
    ctx = lax.axis_index("ctx")
    return dp, ctx, ctx // RAILS, ctx % RAILS, group // RAILS


def copy_to(src, dst, send, recv, device):
    return pltpu.make_async_remote_copy(
        src_ref=src,
        dst_ref=dst,
        send_sem=send,
        recv_sem=recv,
        device_id=device,
        device_id_type=MESH,
    )


def signal(device):
    barrier = pltpu.get_barrier_semaphore()
    pl.semaphore_signal(barrier, inc=1, device_id=device, device_id_type=MESH)


def arrive(count):
    pl.semaphore_wait(pltpu.get_barrier_semaphore(), count)


def gather_kernel(group, *refs):
    count = 2
    sources, outs = refs[:count], refs[count : 2 * count]
    own_sem, y_send, y_recv, up_send, up_recv, down_send, down_recv = refs[2 * count :]
    dp, ctx, z, y, depth = place(group)
    rows = sources[0].shape[0]
    other = (dp, z * RAILS + 1 - y)
    above = (dp, jnp.minimum(z + 1, depth - 1) * RAILS + y)
    below = (dp, jnp.maximum(z - 1, 0) * RAILS + y)
    has_above, has_below = z < depth - 1, z > 0

    signal(other)
    pl.when(has_above)(lambda: signal(above))
    pl.when(has_below)(lambda: signal(below))
    arrive(1 + has_above.astype(jnp.int32) + has_below.astype(jnp.int32))

    def chunk(i, at_z, at_y):
        start = pl.multiple_of((at_z * RAILS + at_y) * rows, rows)
        return outs[i].at[pl.ds(start, rows)]

    def to_other(i, at_z, source=None):
        here = chunk(i, at_z, y)
        return copy_to(
            here if source is None else source, here, y_send.at[i, at_z], y_recv.at[i, at_z], other
        )

    def upward(i, k, source=None):
        here = chunk(i, jnp.maximum(z - k, 0), y)
        return copy_to(
            here if source is None else source, here, up_send.at[i, k], up_recv.at[i, k + 1], above
        )

    def downward(i, k, source=None):
        here = chunk(i, jnp.minimum(z + k, depth - 1), y)
        return copy_to(
            here if source is None else source,
            here,
            down_send.at[i, k],
            down_recv.at[i, k + 1],
            below,
        )

    own = [
        pltpu.make_async_copy(sources[i], chunk(i, z, y), own_sem.at[i]) for i in range(count)
    ]
    for i in range(count):
        to_other(i, z, sources[i]).start()
        pl.when(has_above)(lambda i=i: upward(i, 0, sources[i]).start())
        pl.when(has_below)(lambda i=i: downward(i, 0, sources[i]).start())
        own[i].start()
    for i in range(count):
        for k in range(1, depth):

            @pl.when(z >= k)
            def _():
                at_z = jnp.maximum(z - k, 0)
                here = chunk(i, at_z, y)
                copy_to(here, here, up_send.at[i, 0], up_recv.at[i, k], above).wait_recv()
                pl.when(has_above)(lambda: upward(i, k).start())
                to_other(i, at_z).start()

            @pl.when(z + k < depth)
            def _():
                at_z = jnp.minimum(z + k, depth - 1)
                here = chunk(i, at_z, y)
                copy_to(here, here, down_send.at[i, 0], down_recv.at[i, k], below).wait_recv()
                pl.when(has_below)(lambda: downward(i, k).start())
                to_other(i, at_z).start()

    for i in range(count):
        own[i].wait()
        for k in range(depth - 1):
            pl.when(has_above & (z >= k))(lambda: upward(i, k).wait_send())
            pl.when(has_below & (z + k < depth))(lambda: downward(i, k).wait_send())
        for at_z in range(depth):
            to_other(i, at_z).wait_send()
            here = chunk(i, at_z, 1 - y)
            copy_to(here, here, y_send.at[i, at_z], y_recv.at[i, at_z], other).wait_recv()


def gather_tokens(group, first, second):
    rows, columns = first.shape
    depth = group // RAILS
    sems = pltpu.SemaphoreType.DMA
    out = jax.ShapeDtypeStruct((group * rows, columns), first.dtype)
    return pl.pallas_call(
        functools.partial(gather_kernel, group),
        out_shape=(out, out),
        in_specs=[pl.BlockSpec(memory_space=pl.ANY)] * 2,
        out_specs=[pl.BlockSpec(memory_space=pl.ANY)] * 2,
        scratch_shapes=[sems((2,))] + [sems((2, depth))] * 6,
        compiler_params=pltpu.CompilerParams(collective_id=0, has_side_effects=True),
        name="gather_tokens",
    )(first, second)


def reduce_kernel(group, tiles, *refs):
    count = len(tiles)
    parts, grads, vectors = refs[:2], refs[2 : 2 + count], refs[2 + count]
    refs = refs[3 + count :]
    outs, grads_out, vectors_out = refs[:2], refs[2 : 2 + count], refs[2 + count]
    refs = refs[3 + count :]
    own, y_buf, up_buf, down_buf, mine, from_core, from_x, vec_buf = refs[:8]
    (
        own_sem,
        y_send,
        y_recv,
        up_send,
        up_recv,
        down_send,
        down_recv,
        out_sem,
        mine_sem,
        core_send,
        core_recv,
        x_send,
        x_recv,
        keep_sem,
        done_send,
        done_recv,
        vec_send,
        vec_recv,
    ) = refs[8:]
    dp, ctx, z, y, depth = place(group)
    rows = outs[0].shape[0]
    x, core = dp // 2, dp % 2
    other = (dp, z * RAILS + 1 - y)
    above = (dp, jnp.minimum(z + 1, depth - 1) * RAILS + y)
    below = (dp, jnp.maximum(z - 1, 0) * RAILS + y)
    sibling = (x * 2 + 1 - core, ctx)
    across = ((1 - x) * 2 + core, ctx)
    pair = (dp, (z + 1 - 2 * (z % 2)) * RAILS + y)
    pair_far = (dp, lax.rem(z + 2, depth) * RAILS + y)
    has_above, has_below = z < depth - 1, z > 0

    for device in (other, sibling, across, pair, pair_far):
        signal(device)
    inner = (z > 0) & (z < depth - 1)
    pl.when(inner)(lambda: signal((dp, jnp.clip(z - 1 + 2 * (z % 2), 0, depth - 1) * RAILS + y)))
    arrive(5 + inner.astype(jnp.int32))

    def part_chunk(i, at_z, at_y):
        start = pl.multiple_of((at_z * RAILS + at_y) * rows, rows)
        return parts[i].at[pl.ds(start, rows)]

    half = mine.shape[1]

    spots = [(n, m) for n, amount in enumerate(tiles) for m in range(amount)]
    tiles = len(spots)

    def tile_half(arrays, t, which):
        n, m = spots[t]
        start = pl.multiple_of((2 * m + which) * half, half)
        return arrays[n].at[pl.ds(start, half)]

    def fetch(t):
        return pltpu.make_async_copy(tile_half(grads, t, core), mine.at[t], mine_sem.at[t])

    def to_core(t):
        return copy_to(
            tile_half(grads, t, 1 - core),
            from_core.at[t],
            core_send.at[t],
            core_recv.at[t],
            sibling,
        )

    def to_x(t):
        return copy_to(mine.at[t], from_x.at[t], x_send.at[t], x_recv.at[t], across)

    def keep(t):
        return pltpu.make_async_copy(
            from_core.at[t], tile_half(grads_out, t, core), keep_sem.at[t]
        )

    def finish(t):
        return copy_to(
            from_core.at[t],
            tile_half(grads_out, t, core),
            done_send.at[t],
            done_recv.at[t],
            sibling,
        )

    def add(target, left, right):
        step = 32

        @pl.loop(0, target.shape[0] // step)
        def _(n):
            at = pl.ds(pl.multiple_of(n * step, step), step)
            target[at, :] = (left[at, :].astype(f32) + right[at, :].astype(f32)).astype(
                target.dtype
            )

    def core_sum(t):
        fetch(t).wait()
        to_core(t).wait_recv()
        add(mine.at[t], mine.at[t], from_core.at[t])
        to_x(t).start()

    def x_sum(t):
        to_x(t).wait_recv()
        add(from_core.at[t], mine.at[t], from_x.at[t])
        keep(t).start()
        finish(t).start()

    low = z < depth // 2
    order = [
        jnp.where(low, depth - 1, 0),
        jnp.where(low, depth - 2, 1),
        jnp.where(low, 1 - z, 2 * depth - 3 - z),
        z,
    ]

    def hold(i, s):
        return pltpu.make_async_copy(
            part_chunk(i, order[s], y), own.at[i, order[s]], own_sem.at[i, s]
        )

    def swap(i, s):
        return copy_to(
            part_chunk(i, order[s], 1 - y),
            y_buf.at[i, order[s]],
            y_send.at[i, s],
            y_recv.at[i, s],
            other,
        )

    def upward(i, at):
        return copy_to(own.at[i, at], up_buf.at[i, at], up_send.at[i, at], up_recv.at[i, at], above)

    def downward(i, at):
        return copy_to(
            own.at[i, at], down_buf.at[i, at], down_send.at[i, at], down_recv.at[i, at], below
        )

    def scatter_step(i, s):
        at = order[s]
        hold(i, s).wait()
        swap(i, s).wait_recv()
        add(own.at[i, at], own.at[i, at], y_buf.at[i, at])

        @pl.when((at >= z) & has_below)
        def _():
            upward(i, at).wait_recv()
            add(own.at[i, at], own.at[i, at], up_buf.at[i, at])

        @pl.when((at <= z) & has_above)
        def _():
            downward(i, at).wait_recv()
            add(own.at[i, at], own.at[i, at], down_buf.at[i, at])

        pl.when(at > z)(lambda: upward(i, at).start())
        pl.when(at < z)(lambda: downward(i, at).start())

    def scatter_out(i):
        return pltpu.make_async_copy(own.at[i, z], outs[i], out_sem.at[i])

    stages = (sibling, across, other, pair, pair_far)

    def exchange(n):
        return copy_to(
            vec_buf.at[2 * n], vec_buf.at[2 * n + 1], vec_send.at[n], vec_recv.at[n], stages[n]
        )

    for t in range(tiles):
        fetch(t).start()
        to_core(t).start()
    vec_buf[0] = vectors[...]
    exchange(0).start()
    for i in range(2):
        for s in range(depth):
            hold(i, s).start()
            swap(i, s).start()
    core_sum(0)
    core_sum(1)
    steps = [(i, s) for i in range(2) for s in range(depth)]
    for t in range(tiles):
        if t + 2 < tiles:
            core_sum(t + 2)
        if t < len(stages):
            exchange(t).wait_recv()
            total = vec_buf[2 * t] + vec_buf[2 * t + 1]
            if t + 1 < len(stages):
                vec_buf[2 * t + 2] = total
                exchange(t + 1).start()
            else:
                vectors_out[...] = total
        if t < len(steps):
            scatter_step(*steps[t])
            if steps[t][1] == depth - 1:
                scatter_out(steps[t][0]).start()
        x_sum(t)
    for t in range(tiles):
        to_core(t).wait_send()
        to_x(t).wait_send()
        keep(t).wait()
        finish(t).wait_send()
        copy_to(
            from_core.at[t],
            tile_half(grads_out, t, 1 - core),
            done_send.at[t],
            done_recv.at[t],
            sibling,
        ).wait_recv()
    for n in range(len(stages)):
        exchange(n).wait_send()
    for i in range(2):
        scatter_out(i).wait()
        for s in range(depth):
            swap(i, s).wait_send()
            at = order[s]
            pl.when(at > z)(lambda: upward(i, at).wait_send())
            pl.when(at < z)(lambda: downward(i, at).wait_send())


def reduce_all(group, first, second, grads, vectors):
    tokens, columns = first.shape
    depth = group // RAILS
    rows = tokens // group
    half = 128
    tiles = [grad.shape[0] // (2 * half) for grad in grads]
    sems = pltpu.SemaphoreType.DMA
    part = jax.ShapeDtypeStruct((rows, columns), first.dtype)
    anywhere = pl.BlockSpec(memory_space=pl.ANY)
    vmem = pl.BlockSpec(memory_space=pltpu.VMEM)
    chunks = pltpu.VMEM((2, depth, rows, columns), first.dtype)
    halves = pltpu.VMEM((sum(tiles), half, columns), first.dtype)
    results = pl.pallas_call(
        functools.partial(reduce_kernel, group, tiles),
        out_shape=(
            part,
            part,
            *[jax.ShapeDtypeStruct(grad.shape, grad.dtype) for grad in grads],
            jax.ShapeDtypeStruct(vectors.shape, vectors.dtype),
        ),
        in_specs=[anywhere] * (2 + len(grads)) + [vmem],
        out_specs=[anywhere] * (2 + len(grads)) + [vmem],
        scratch_shapes=[chunks] * 4
        + [halves] * 3
        + [pltpu.VMEM((10,) + vectors.shape, vectors.dtype)]
        + [sems((2, depth))] * 7
        + [sems((2,))]
        + [sems((sum(tiles),))] * 8
        + [sems((5,))] * 2,
        compiler_params=pltpu.CompilerParams(
            collective_id=1, has_side_effects=True, vmem_limit_bytes=56 * 2**20
        ),
        name="reduce_all",
    )(first, second, *grads, vectors)
    return results[0], results[1], results[2:-1], results[-1]


def body(
    hidden_in,
    grad_out,
    seg_len,
    seg_parent,
    gain_attn,
    shift_attn,
    w_qkv,
    bias_qkv,
    w_out,
    bias_out,
    gain_mlp,
    shift_mlp,
    w_up,
    bias_up,
    w_down,
    bias_down,
):
    group = lax.axis_size("ctx")
    me = lax.axis_index("ctx")
    local_rows = hidden_in.shape[1]
    tokens = local_rows * group
    head_count = HEADS // group
    head_cols = head_count * HEAD_DIM
    head_shape = (tokens, head_count, HEAD_DIM)
    scale = 1.0 / math.sqrt(HEAD_DIM)

    hidden_all, grad_all = gather_tokens(group, hidden_in[0], grad_out[0])

    w_out_cols = lax.all_to_all(
        w_out, "ctx", split_axis=1, concat_axis=0, tiled=True
    )

    seg_ends, seg_starts, ancestor, path_start = tree_tables(seg_len[0], seg_parent[0])
    ids = jnp.arange(tokens, dtype=jnp.int32)
    seg_index = jnp.sum((ids[:, None] >= seg_ends[None, :]).astype(jnp.int32), axis=1)
    labels = jnp.arange(seg_ends.shape[0], dtype=jnp.int32)
    hot = (seg_index[:, None] == labels[None, :]).astype(f32)
    reach = jnp.dot(hot, ancestor.astype(f32))
    path_pos = ids + jnp.sum(hot.astype(jnp.int32) * (path_start - seg_starts)[None, :], axis=1)
    cosine, sine = rotary_tables(path_pos)
    allowed = (jnp.dot(reach, hot.T) > 0.5) & (ids[None, :] <= ids[:, None])

    gain_a = gain_attn.astype(f32)
    gain_m = gain_mlp.astype(f32)
    hid = hidden_all.astype(f32)
    mean = jnp.mean(hid, axis=-1, keepdims=True)
    centred = hid - mean
    rstd = lax.rsqrt(jnp.mean(centred * centred, axis=-1, keepdims=True) + norm_eps)
    normed = centred * rstd
    x_attn = (normed * gain_a + shift_attn.astype(f32)).astype(bf16)
    x_mlp = (normed * gain_m + shift_mlp.astype(f32)).astype(bf16)

    my_bias = lax.dynamic_slice_in_dim(bias_qkv, me * 3 * head_cols, 3 * head_cols)
    raw = dot_nt(x_attn, w_qkv) + my_bias.astype(f32)
    arrived = []
    for j in range(3):
        turns = (3 * me + j) // group < 2
        block = raw[:, j * head_cols : (j + 1) * head_cols].reshape(head_shape)
        block = rotate(block, jnp.where(turns, cosine, 1.0), jnp.where(turns, sine, 0.0))
        arrived.append(
            lax.ppermute(
                block.astype(bf16), "ctx", [(c, (3 * c + j) % group) for c in range(group)]
            )
        )
    arrived = jnp.stack(arrived)
    q, k, v = [
        lax.dynamic_index_in_dim(arrived, (kind * group + me) % 3, 0, keepdims=False)
        for kind in range(3)
    ]
    scores = jnp.einsum("qhd,khd->hqk", q, k, preferred_element_type=f32) * scale
    scores = jnp.where(allowed[None], scores, masked_score)
    top = jnp.max(scores, axis=-1, keepdims=True)
    expo = jnp.exp(scores - top)
    probs = expo / jnp.sum(expo, axis=-1, keepdims=True)
    weights = probs.astype(bf16)
    attended = jnp.einsum("hqk,khd->qhd", weights, v, preferred_element_type=f32).astype(bf16)
    attended = attended.reshape(tokens, head_cols)

    up_bias = lax.dynamic_slice_in_dim(bias_up, me * w_up.shape[0], w_up.shape[0]).astype(f32)
    pre_act = dot_nt(x_mlp, w_up) + up_bias
    act = jax.nn.gelu(pre_act, approximate=False).astype(bf16)
    partial = (dot_nt(attended, w_out_cols) + dot_nn(act, w_down)).astype(bf16)

    grad_w_down = dot_tn(act, grad_all).astype(bf16)
    pre_grad = (dot_nt(grad_all, w_down) * gelu_slope(pre_act)).astype(bf16)
    grad_w_up = dot_tn(pre_grad, x_mlp).astype(bf16)
    mlp_in_grad = dot_nn(pre_grad, w_up)

    grad_w_out_cols = dot_tn(grad_all, attended).astype(bf16)
    att_grad = dot_nn(grad_all, w_out_cols).astype(bf16).reshape(head_shape)
    prob_grad = jnp.einsum("qhd,khd->hqk", att_grad, v, preferred_element_type=f32)
    delta = jnp.sum(probs * prob_grad, axis=-1, keepdims=True)
    score_grad = (probs * (prob_grad - delta)).astype(bf16)
    q_grad = jnp.einsum("hqk,khd->qhd", score_grad, k, preferred_element_type=f32) * scale
    k_grad = jnp.einsum("hqk,qhd->khd", score_grad, q, preferred_element_type=f32) * scale
    v_grad = jnp.einsum("hqk,qhd->khd", weights, att_grad, preferred_element_type=f32)
    qkv_grad = [
        rotate(q_grad, cosine, -sine).astype(bf16).reshape(tokens, head_cols),
        rotate(k_grad, cosine, -sine).astype(bf16).reshape(tokens, head_cols),
        v_grad.astype(bf16).reshape(tokens, head_cols),
    ]
    qkv_grad = jnp.stack(qkv_grad)
    returned = []
    for j in range(3):
        kind_of_slot = sum(
            kind * ((kind * group + me) % 3 == j).astype(jnp.int32) for kind in range(3)
        )
        block = lax.dynamic_index_in_dim(qkv_grad, kind_of_slot, 0, keepdims=False)
        returned.append(
            lax.ppermute(block, "ctx", [((3 * c + j) % group, c) for c in range(group)])
        )
    qkv_grad = jnp.concatenate(returned, axis=1)
    attn_in_grad = dot_nn(qkv_grad, w_qkv)
    grad_w_qkv = dot_tn(qkv_grad, x_attn).astype(bf16)
    grad_w_out = lax.all_to_all(
        grad_w_out_cols, "ctx", split_axis=0, concat_axis=1, tiled=True
    )
    back = (attn_in_grad * gain_a + mlp_in_grad * gain_m).astype(bf16)

    def widen(part, length):
        at = me * part.shape[0]
        return lax.dynamic_update_slice(jnp.zeros((length,), f32), part, (at,))

    grad_f = grad_out[0].astype(f32)
    vectors = jnp.concatenate(
        [
            jnp.sum(attn_in_grad * normed, axis=0),
            jnp.sum(attn_in_grad, axis=0),
            jnp.sum(mlp_in_grad * normed, axis=0),
            jnp.sum(mlp_in_grad, axis=0),
            widen(jnp.sum(qkv_grad, axis=0, dtype=f32), 3 * D),
            jnp.sum(grad_f, axis=0),
            widen(jnp.sum(pre_grad, axis=0, dtype=f32), FF),
        ]
    )
    summed, w_sum, sums, vectors = reduce_all(
        group,
        partial,
        back,
        (grad_w_down, grad_w_up, grad_w_out, grad_w_qkv),
        vectors.reshape(-1, 1024),
    )
    vectors = vectors.reshape(-1)
    w_sum = w_sum.astype(f32)
    hidden_out = (
        hidden_in[0].astype(f32) + summed.astype(f32) + bias_out.astype(f32) + bias_down.astype(f32)
    ).astype(bf16)
    start = me * local_rows
    my_rstd = lax.dynamic_slice_in_dim(rstd, start, local_rows)
    my_normed = (
        hidden_in[0].astype(f32) - lax.dynamic_slice_in_dim(mean, start, local_rows)
    ) * my_rstd
    grad_in = (
        grad_f
        + (
            w_sum
            - jnp.mean(w_sum, axis=-1, keepdims=True)
            - my_normed * jnp.mean(w_sum * my_normed, axis=-1, keepdims=True)
        )
        * my_rstd
    )

    cuts = [D, D, D, D, 3 * D, D, FF]
    ends = [sum(cuts[: i + 1]) for i in range(len(cuts))]
    gain_grad_a, shift_grad_a, gain_grad_m, shift_grad_m, qkv_bias_grad, out_bias_grad, up_bias_grad = [
        vectors[end - cut : end] for cut, end in zip(cuts, ends)
    ]

    return (
        hidden_out[None],
        grad_in[None],
        gain_grad_a,
        shift_grad_a,
        sums[3].astype(f32),
        qkv_bias_grad,
        sums[2].astype(f32),
        out_bias_grad,
        gain_grad_m,
        shift_grad_m,
        sums[1].astype(f32),
        up_bias_grad,
        sums[0].astype(f32),
        out_bias_grad,
    )


block_limit = 512


def layer_norm(values, gain_vec, shift_vec):
    average = jnp.mean(values, axis=-1, keepdims=True)
    centred = values - average
    spread = jnp.mean(centred * centred, axis=-1, keepdims=True)
    return centred * lax.rsqrt(spread + norm_eps) * gain_vec + shift_vec


def segment_hot(row_ids, seg_ends):
    seg_index = jnp.sum((row_ids[:, None] >= seg_ends[None, :]).astype(jnp.int32), axis=1)
    labels = jnp.arange(seg_ends.shape[0], dtype=jnp.int32)
    return (seg_index[:, None] == labels[None, :]).astype(jnp.float32)


def row_lookup(row_ids, seg_ends, ancestor_f):
    row_hot = segment_hot(row_ids, seg_ends)
    return (row_hot, jnp.dot(row_hot, ancestor_f))


def permitted(query_ids, query_reach, key_ids, key_hot):
    linked = jnp.dot(query_reach, key_hot.T) > 0.5
    return linked & (key_ids[None, :] <= query_ids[:, None])


def inner_block(row_count):
    block_rows = row_count
    while block_rows > block_limit and block_rows % 2 == 0:
        block_rows = block_rows // 2
    return block_rows


def gather_body(
    hidden_in,
    grad_out,
    seg_len,
    seg_parent,
    gain_attn,
    shift_attn,
    w_qkv,
    bias_qkv,
    w_out,
    bias_out,
    gain_mlp,
    shift_mlp,
    w_up,
    bias_up,
    w_down,
    bias_down,
):
    local_rows = hidden_in.shape[1]
    scale_factor = 1.0 / math.sqrt(HEAD_DIM)
    head_shape = (local_rows, HEADS, HEAD_DIM)
    seg_ends, seg_starts, ancestor, path_start = tree_tables(seg_len[0], seg_parent[0])
    ancestor_f = ancestor.astype(jnp.float32)
    my_ids = lax.axis_index("ctx") * local_rows + jnp.arange(local_rows, dtype=jnp.int32)
    my_hot, my_reach = row_lookup(my_ids, seg_ends, ancestor_f)
    shift_table = path_start - seg_starts
    path_pos = my_ids + jnp.sum(my_hot.astype(jnp.int32) * shift_table[None, :], axis=1)
    cosine, sine = rotary_tables(path_pos)
    inputs_f = hidden_in[0].astype(jnp.float32)
    gain_a = gain_attn.astype(jnp.float32)
    shift_a = shift_attn.astype(jnp.float32)
    gain_m = gain_mlp.astype(jnp.float32)
    shift_m = shift_mlp.astype(jnp.float32)
    bias_up_f = bias_up.astype(jnp.float32)
    x_attn = layer_norm(inputs_f, gain_a, shift_a).astype(jnp.bfloat16)
    x_mlp = layer_norm(inputs_f, gain_m, shift_m).astype(jnp.bfloat16)
    qkv = jnp.einsum(
        "td,nd->tn",
        x_attn,
        lax.all_gather(w_qkv, "ctx", axis=0, tiled=True),
        preferred_element_type=jnp.float32,
    ) + bias_qkv.astype(jnp.float32)
    queries = rotate(qkv[:, :D].reshape(head_shape), cosine, sine).astype(jnp.bfloat16)
    keys_heads = rotate(qkv[:, D : 2 * D].reshape(head_shape), cosine, sine).astype(jnp.bfloat16)
    values_flat = qkv[:, 2 * D :].astype(jnp.bfloat16)
    values_heads = values_flat.reshape(head_shape)
    keys_flat = keys_heads.reshape(local_rows, D)
    queries_flat = queries.reshape(local_rows, D)

    def split_blocks(shard_pieces):
        row_count = shard_pieces[0].shape[0]
        block_rows = inner_block(row_count)
        block_count = row_count // block_rows
        shaped = tuple(
            (member.reshape(block_count, block_rows, HEADS, HEAD_DIM) for member in shard_pieces)
        )
        starts = block_rows * jnp.arange(block_count, dtype=jnp.int32)
        return shaped + (starts,)

    def attend_block(fold_state, block_items):
        key_block, value_block, block_start = block_items
        block_rows = key_block.shape[0]
        key_ids = block_start + jnp.arange(block_rows, dtype=jnp.int32)
        allowed = permitted(my_ids, my_reach, key_ids, segment_hot(key_ids, seg_ends))
        row_top, row_total, partial_value = fold_state
        scores = (
            jnp.einsum("qhd,khd->qhk", queries, key_block, preferred_element_type=jnp.float32)
            * scale_factor
        )
        scores = jnp.where(allowed[:, None, :], scores, masked_score)
        new_top = jnp.maximum(row_top, jnp.max(scores, axis=-1))
        factor = jnp.exp(row_top - new_top)
        weights = jnp.exp(scores - new_top[:, :, None])
        row_total = row_total * factor + jnp.sum(weights, axis=-1)
        partial_value = partial_value * factor[:, :, None] + jnp.einsum(
            "qhk,khd->qhd",
            weights.astype(jnp.bfloat16),
            value_block,
            preferred_element_type=jnp.float32,
        )
        fold_state = (new_top, row_total, partial_value)
        return (fold_state, None)

    start_state = (
        jnp.full((local_rows, HEADS), masked_score, jnp.float32),
        jnp.zeros((local_rows, HEADS), jnp.float32),
        jnp.zeros(head_shape, jnp.float32),
    )
    row_top, row_total, partial_value = lax.scan(
        attend_block,
        start_state,
        split_blocks(
            (
                lax.all_gather(keys_flat, "ctx", axis=0, tiled=True),
                lax.all_gather(values_flat, "ctx", axis=0, tiled=True),
            )
        ),
    )[0]
    log_total = row_top + jnp.log(row_total)
    attended_f = partial_value / row_total[:, :, None]
    attended = attended_f.reshape(local_rows, D).astype(jnp.bfloat16)
    attn_proj = jnp.einsum(
        "td,nd->tn",
        attended,
        lax.all_gather(w_out, "ctx", axis=0, tiled=True),
        preferred_element_type=jnp.float32,
    )

    def mlp_pre(up_rows):
        return (
            jnp.einsum("td,nd->tn", x_mlp, up_rows, preferred_element_type=jnp.float32) + bias_up_f
        )

    up_rows = lax.all_gather(w_up, "ctx", axis=0, tiled=True)
    down_rows = lax.all_gather(w_down, "ctx", axis=0, tiled=True)
    activated = jax.nn.gelu(mlp_pre(up_rows), approximate=False).astype(jnp.bfloat16)
    mlp_sum = jnp.dot(activated, down_rows, preferred_element_type=jnp.float32)
    bias_out_f = bias_out.astype(jnp.float32)
    bias_down_f = bias_down.astype(jnp.float32)
    hidden_out = (inputs_f + attn_proj + bias_out_f + mlp_sum + bias_down_f).astype(jnp.bfloat16)
    grad_b = grad_out[0]
    grad_f = grad_b.astype(jnp.float32)
    up_rows = lax.all_gather(w_up, "ctx", axis=0, tiled=True)
    down_rows = lax.all_gather(w_down, "ctx", axis=0, tiled=True)
    pre_act = mlp_pre(up_rows)
    activated = jax.nn.gelu(pre_act, approximate=False).astype(jnp.bfloat16)
    act_grad = jnp.einsum("td,nd->tn", grad_b, down_rows, preferred_element_type=jnp.float32)
    pre_grad = (act_grad * gelu_slope(pre_act)).astype(jnp.bfloat16)
    input_grad = jnp.dot(pre_grad, up_rows, preferred_element_type=jnp.float32)
    act_all = activated
    pre_grad_all = pre_grad
    act_all, pre_grad_all, mlp_in_grad = (act_all, pre_grad_all, input_grad)
    attended_grad = jnp.dot(
        grad_b, lax.all_gather(w_out, "ctx", axis=0, tiled=True), preferred_element_type=jnp.float32
    ).astype(jnp.bfloat16)
    attended_grad_heads = attended_grad.reshape(head_shape)
    row_delta = jnp.sum(attended_grad_heads.astype(jnp.float32) * attended_f, axis=-1)
    all_log_total, all_delta = (
        lax.all_gather(log_total, "ctx", axis=0, tiled=True),
        lax.all_gather(row_delta, "ctx", axis=0, tiled=True),
    )

    def back_block(fold_state, block_items):
        key_block, value_block, query_block, grad_block, block_start = block_items
        block_rows = key_block.shape[0]
        other_ids = block_start + jnp.arange(block_rows, dtype=jnp.int32)
        other_hot, other_reach = row_lookup(other_ids, seg_ends, ancestor_f)
        allowed_in = permitted(my_ids, my_reach, other_ids, other_hot)
        allowed_out = permitted(other_ids, other_reach, my_ids, my_hot)
        other_log = lax.dynamic_slice_in_dim(all_log_total, block_start, block_rows, 0)
        other_delta = lax.dynamic_slice_in_dim(all_delta, block_start, block_rows, 0)
        query_grad, key_grad, value_grad = fold_state
        scores = (
            jnp.einsum("qhd,khd->qhk", queries, key_block, preferred_element_type=jnp.float32)
            * scale_factor
        )
        scores = jnp.where(allowed_in[:, None, :], scores, masked_score)
        prob_mass = jnp.exp(scores - log_total[:, :, None])
        prob_grad = jnp.einsum(
            "qhd,khd->qhk", attended_grad_heads, value_block, preferred_element_type=jnp.float32
        )
        score_grad = (prob_mass * (prob_grad - row_delta[:, :, None])).astype(jnp.bfloat16)
        query_grad = (
            query_grad
            + jnp.einsum("qhk,khd->qhd", score_grad, key_block, preferred_element_type=jnp.float32)
            * scale_factor
        )
        outgoing_key_grad = key_grad
        outgoing_value_grad = value_grad
        scores = (
            jnp.einsum("qhd,khd->qhk", query_block, keys_heads, preferred_element_type=jnp.float32)
            * scale_factor
        )
        scores = jnp.where(allowed_out[:, None, :], scores, masked_score)
        prob_mass = jnp.exp(scores - other_log[:, :, None])
        outgoing_value_grad = outgoing_value_grad + jnp.einsum(
            "qhk,qhd->khd",
            prob_mass.astype(jnp.bfloat16),
            grad_block,
            preferred_element_type=jnp.float32,
        )
        prob_grad = jnp.einsum(
            "qhd,khd->qhk", grad_block, values_heads, preferred_element_type=jnp.float32
        )
        score_grad = (prob_mass * (prob_grad - other_delta[:, :, None])).astype(jnp.bfloat16)
        outgoing_key_grad = (
            outgoing_key_grad
            + jnp.einsum(
                "qhk,qhd->khd", score_grad, query_block, preferred_element_type=jnp.float32
            )
            * scale_factor
        )
        fold_state = (query_grad, outgoing_key_grad, outgoing_value_grad)
        return (fold_state, None)

    zero_heads = jnp.zeros(head_shape, jnp.float32)
    query_grad, key_grad, value_grad = lax.scan(
        back_block,
        (zero_heads, zero_heads, zero_heads),
        split_blocks(
            (
                lax.all_gather(keys_flat, "ctx", axis=0, tiled=True),
                lax.all_gather(values_flat, "ctx", axis=0, tiled=True),
                lax.all_gather(queries_flat, "ctx", axis=0, tiled=True),
                lax.all_gather(attended_grad, "ctx", axis=0, tiled=True),
            )
        ),
    )[0]

    def turn(head_values):
        return rotate(head_values, cosine, sine)

    unturn = jax.vjp(turn, zero_heads)[1]
    qkv_grad = jnp.concatenate(
        [
            unturn(query_grad)[0].reshape(local_rows, D),
            unturn(key_grad)[0].reshape(local_rows, D),
            value_grad.reshape(local_rows, D),
        ],
        axis=1,
    ).astype(jnp.bfloat16)
    attn_in_grad = jnp.dot(
        qkv_grad,
        lax.all_gather(w_qkv, "ctx", axis=0, tiled=True),
        preferred_element_type=jnp.float32,
    )
    pull_attn = jax.vjp(layer_norm, inputs_f, gain_a, shift_a)[1]
    input_part_a, gain_grad_a, shift_grad_a = pull_attn(attn_in_grad)
    pull_mlp = jax.vjp(layer_norm, inputs_f, gain_m, shift_m)[1]
    input_part_m, gain_grad_m, shift_grad_m = pull_mlp(mlp_in_grad)
    grad_in = (grad_f + input_part_a + input_part_m)[None]
    vector_sums = lax.psum(
        (
            gain_grad_a,
            shift_grad_a,
            gain_grad_m,
            shift_grad_m,
            jnp.sum(qkv_grad, axis=0, dtype=jnp.float32),
            jnp.sum(grad_f, axis=0),
            jnp.sum(pre_grad_all, axis=0, dtype=jnp.float32),
        ),
        ("dp", "ctx"),
    )
    group_count = lax.axis_size("ctx")
    section_rows = (3 * D // group_count, D // group_count, FF // group_count, FF // group_count)
    term_sources = (
        (qkv_grad, x_attn),
        (grad_b, attended),
        (pre_grad_all, x_mlp),
        (act_all, grad_b),
    )
    owner_rows = sum(section_rows)
    blocks = jnp.arange(owner_rows * lax.axis_size("ctx") // owner_rows, dtype=jnp.int32)
    parts_list = []
    for (column_source, other_side), full_rows in zip(term_sources, section_rows):
        sub_rows = full_rows // 1
        column_ids = (
            blocks[:, None] * sub_rows + jnp.arange(sub_rows, dtype=jnp.int32)[None, :]
        ).reshape(-1)
        columns = jnp.take(column_source, column_ids, axis=1)
        block_term = jnp.einsum(
            "tr,td->rd", columns, other_side, preferred_element_type=jnp.float32
        )
        parts_list.append(block_term.reshape(blocks.shape[0], sub_rows, D))
    owned_term = lax.psum_scatter(
        jnp.concatenate(parts_list, axis=1).reshape(-1, D).astype(jnp.bfloat16),
        "ctx",
        scatter_dimension=0,
        tiled=True,
    ).astype(jnp.float32)
    cut_a = section_rows[0]
    cut_b = cut_a + section_rows[1]
    cut_c = cut_b + section_rows[2]
    weight_grads = (
        lax.psum(owned_term[:cut_a].astype(jnp.bfloat16), "dp").astype(jnp.float32),
        lax.psum(owned_term[cut_a:cut_b].astype(jnp.bfloat16), "dp").astype(jnp.float32),
        lax.psum(owned_term[cut_b:cut_c].astype(jnp.bfloat16), "dp").astype(jnp.float32),
        lax.psum(owned_term[cut_c:].astype(jnp.bfloat16), "dp").astype(jnp.float32),
    )
    return (
        hidden_out[None],
        grad_in,
        vector_sums[0],
        vector_sums[1],
        weight_grads[0],
        vector_sums[4],
        weight_grads[1],
        vector_sums[5],
        vector_sums[2],
        vector_sums[3],
        weight_grads[2],
        vector_sums[6],
        weight_grads[3],
        vector_sums[5],
    )


def solution(mesh):
    token = P("dp", "ctx", None)
    rows = P("ctx", None)
    return jax.shard_map(
        body if HEADS % mesh.shape["ctx"] == 0 else gather_body,
        mesh=mesh,
        in_specs=(
            token,
            token,
            P("dp", None),
            P("dp", None),
            P(),
            P(),
            rows,
            P(),
            rows,
            P(),
            P(),
            P(),
            rows,
            P(),
            rows,
            P(),
        ),
        out_specs=(
            token,
            token,
            P(),
            P(),
            rows,
            P(),
            rows,
            P(),
            P(),
            P(),
            rows,
            P(),
            rows,
            P(),
        ),
        check_vma=False,
    )
```

```python
import functools
import math

import jax
import jax.numpy as jnp
from jax import lax
from jax.experimental import pallas as pl
from jax.experimental.pallas import tpu as pltpu
from jax.sharding import PartitionSpec as P

D = 2048
HEADS = 16
HEAD_DIM = 128
ROT_DIM = 32
FF = 8192

norm_eps = 1e-05
masked_score = -1e30
f32 = jnp.float32
bf16 = jnp.bfloat16


def tree_tables(seg_len, seg_parent):
    seg_count = seg_len.shape[0]
    labels = jnp.arange(seg_count, dtype=jnp.int32)
    earlier = labels[:, None] > labels[None, :]
    seg_starts = jnp.sum(jnp.where(earlier, seg_len[None, :], 0), axis=1)
    seg_ends = seg_starts + seg_len
    parent_hit = seg_parent[:, None] == labels[None, :]
    grand_parent = jnp.sum(jnp.where(parent_hit, seg_parent[None, :], 0), axis=1)
    itself = labels[:, None] == labels[None, :]
    ancestor = itself | parent_hit | (grand_parent[:, None] == labels[None, :])
    path_start = jnp.sum(jnp.where(ancestor & jnp.logical_not(itself), seg_len[None, :], 0), axis=1)
    return (seg_ends, seg_starts, ancestor, path_start)


def rotate(head_values, cosine, sine):
    half_dim = ROT_DIM // 2
    turned = head_values[..., :ROT_DIM]
    swapped = jnp.concatenate([-turned[..., half_dim:], turned[..., :half_dim]], axis=-1)
    mixed = turned * cosine[:, None, :] + swapped * sine[:, None, :]
    return jnp.concatenate([mixed, head_values[..., ROT_DIM:]], axis=-1)


def gelu_slope(pre_act):
    normal_cdf = 0.5 * (1.0 + lax.erf(pre_act / math.sqrt(2.0)))
    return normal_cdf + pre_act * jnp.exp(-0.5 * pre_act * pre_act) / math.sqrt(2.0 * math.pi)


def dot_nt(a, b):
    return lax.dot_general(a, b, (((1,), (1,)), ((), ())), preferred_element_type=f32)


def dot_nn(a, b):
    return lax.dot_general(a, b, (((1,), (0,)), ((), ())), preferred_element_type=f32)


def dot_tn(a, b):
    return lax.dot_general(a, b, (((0,), (0,)), ((), ())), preferred_element_type=f32)


MESH = pl.DeviceIdType.MESH
RAILS = 2


def place(group):
    dp = lax.axis_index("dp")
    ctx = lax.axis_index("ctx")
    return dp, ctx, ctx // RAILS, ctx % RAILS, group // RAILS


def copy_to(src, dst, send, recv, device):
    return pltpu.make_async_remote_copy(
        src_ref=src,
        dst_ref=dst,
        send_sem=send,
        recv_sem=recv,
        device_id=device,
        device_id_type=MESH,
    )


def signal(device):
    barrier = pltpu.get_barrier_semaphore()
    pl.semaphore_signal(barrier, inc=1, device_id=device, device_id_type=MESH)


def arrive(count):
    pl.semaphore_wait(pltpu.get_barrier_semaphore(), count)


def pair_order(z, depth):
    return [
        z,
        jnp.where(z > 0, z - 1, 1),
        jnp.where(z == depth - 1, 1, jnp.where(z == depth - 2, depth - 1, 2)),
        jnp.where(z < depth // 2, depth - 1, 0),
    ]


def layer_kernel(group, *refs):
    hidden, grad, w_up_in, w_down_in, w_qkv_in, norms, bias_up, bias_qkv, inverse = refs[:9]
    seg_len, seg_parent = refs[9:11]
    h_out, g_out, x_out, heads_out, part_out, back_out, down_out, up_out = refs[11:19]
    tables, sums, bias_sum = refs[19:22]
    h_buf, g_buf, w_up, w_down, w_qkv, x_mlp, x_attn, act, slope, pre_grad = refs[22:32]
    heads, part, back, down_grad, up_grad, mean, rstd = refs[32:39]
    own_sem, y_send, y_recv, up_send, up_recv, down_send, down_recv = refs[39:46]
    weight_sem, pair_sem, grad_sem, head_send, head_recv = refs[46:51]
    dp, ctx, z, y, depth = place(group)
    bufs, sources, outs = (h_buf, g_buf), (hidden, grad), (h_out, g_out)
    rows = hidden.shape[0]
    pair_rows = RAILS * rows
    tokens, columns = h_buf.shape
    units = act.shape[1]
    head_cols = heads.shape[2]
    other = (dp, z * RAILS + 1 - y)
    above = (dp, jnp.minimum(z + 1, depth - 1) * RAILS + y)
    below = (dp, jnp.maximum(z - 1, 0) * RAILS + y)
    has_above, has_below = z < depth - 1, z > 0
    order = pair_order(z, depth)

    for n in range(1, group):
        signal((dp, lax.rem(ctx + n, group)))
    arrive(group - 1)

    def chunk(i, at_z, at_y):
        start = pl.multiple_of((at_z * RAILS + at_y) * rows, rows)
        return bufs[i].at[pl.ds(start, rows)]

    def to_other(i, at_z, source=None):
        here = chunk(i, at_z, y)
        return copy_to(
            here if source is None else source, here, y_send.at[i, at_z], y_recv.at[i, at_z], other
        )

    def upward(i, at_z, source=None):
        here = chunk(i, at_z, y)
        return copy_to(
            here if source is None else source,
            here,
            up_send.at[i, at_z],
            up_recv.at[i, at_z],
            above,
        )

    def downward(i, at_z, source=None):
        here = chunk(i, at_z, y)
        return copy_to(
            here if source is None else source,
            here,
            down_send.at[i, at_z],
            down_recv.at[i, at_z],
            below,
        )

    def relay(i, k):
        @pl.when(z >= k)
        def _():
            at_z = jnp.maximum(z - k, 0)
            upward(i, at_z).wait_recv()
            pl.when(has_above)(lambda: upward(i, at_z).start())

        @pl.when(z + k < depth)
        def _():
            at_z = jnp.minimum(z + k, depth - 1)
            downward(i, at_z).wait_recv()
            pl.when(has_below)(lambda: downward(i, at_z).start())

    def turn(n):
        if n < depth:
            relay(0, n)
            pl.when((z == n - 1) & has_above)(lambda: upward(1, z, sources[1]).start())
            pl.when((z == depth - n) & has_below)(lambda: downward(1, z, sources[1]).start())
            to_other(0, order[n]).start()
        else:
            if n < 2 * depth - 1:
                relay(1, n - depth + 1)
            if n == depth:
                to_other(1, z, sources[1]).start()
            else:
                to_other(1, order[n - depth]).start()

    def y_arrive(i, s):
        here = chunk(i, order[s], 1 - y)
        copy_to(
            here, here, y_send.at[i, order[s]], y_recv.at[i, order[s]], other
        ).wait_recv()

    def pair_at(s):
        return pl.ds(pl.multiple_of(order[s] * pair_rows, pair_rows), pair_rows)

    def keep(n, s, buf, out):
        at = pair_at(s)
        return pltpu.make_async_copy(buf.at[at], out.at[at], pair_sem.at[n, s])

    own = [pltpu.make_async_copy(sources[i], chunk(i, z, y), own_sem.at[i]) for i in range(2)]
    weights = [
        pltpu.make_async_copy(source, held, weight_sem.at[n])
        for n, (source, held) in enumerate(
            ((w_up_in, w_up), (w_qkv_in, w_qkv), (w_down_in, w_down))
        )
    ]
    own[0].start()
    to_other(0, z, sources[0]).start()
    pl.when(has_above)(lambda: upward(0, z, sources[0]).start())
    pl.when(has_below)(lambda: downward(0, z, sources[0]).start())
    for copy in weights:
        copy.start()
    own[1].start()

    starts, shifts = [], []
    at = jnp.int32(0)
    for n in range(seg_len.shape[1]):
        parent = seg_parent[0, n]
        grand = seg_parent[0, parent]
        before = jnp.where(parent != n, seg_len[0, parent], 0) + jnp.where(
            (grand != n) & (grand != parent), seg_len[0, grand], 0
        )
        starts.append(at)
        shifts.append(before - at)
        at = at + seg_len[0, n]

    half = ROT_DIM // 2

    @pl.loop(0, tokens // rows)
    def _(n):
        at = pl.ds(pl.multiple_of(n * rows, rows), rows)
        token = n * rows + lax.broadcasted_iota(jnp.int32, (half, rows), 1)
        position = token + shifts[0]
        for m in range(1, len(starts)):
            position = position + jnp.where(token >= starts[m], shifts[m] - shifts[m - 1], 0)
        angle = position.astype(f32) * inverse[...]
        cosine, sine = jnp.cos(angle), jnp.sin(angle)
        still = jnp.zeros((HEAD_DIM - ROT_DIM, rows), f32)
        none = jnp.zeros((half, rows), f32)
        tables[0, at, :] = jnp.concatenate([cosine, cosine, still + 1.0], axis=0).T
        tables[1, at, :] = jnp.concatenate([-sine, none, still], axis=0).T
        tables[2, at, :] = jnp.concatenate([none, sine, still], axis=0).T

    sums[...] = jnp.zeros_like(sums)
    bias_sum[...] = jnp.zeros_like(bias_sum)

    def normalize(s):
        step = 32

        @pl.loop(0, pair_rows // step)
        def _(n):
            at = pl.ds(pl.multiple_of(order[s] * pair_rows + n * step, step), step)
            values = h_buf[at, :].astype(f32)
            average = jnp.mean(values, axis=1, keepdims=True)
            centred = values - average
            spread = lax.rsqrt(jnp.mean(centred * centred, axis=1, keepdims=True) + norm_eps)
            normed = centred * spread
            x_attn[at, :] = (normed * norms[0:1, :] + norms[1:2, :]).astype(bf16)
            x_mlp[at, :] = (normed * norms[2:3, :] + norms[3:4, :]).astype(bf16)
            mean[at, :] = average
            rstd[at, :] = spread
            lane = lax.broadcasted_iota(jnp.int32, (step, HEAD_DIM), 1)
            tables[3, at, :] = jnp.where(lane == 0, average, spread)

    wide = 512

    def feed(s):
        at = pair_at(s)

        @pl.loop(0, units // wide)
        def _(n):
            cols = pl.ds(pl.multiple_of(n * wide, wide), wide)
            pre = dot_nt(x_mlp[at, :], w_up[cols, :]) + bias_up[:, cols]
            normal_cdf = 0.5 * (1.0 + lax.erf(pre * math.sqrt(0.5)))
            act[at, cols] = (pre * normal_cdf).astype(bf16)
            slope[at, cols] = (
                normal_cdf + pre * jnp.exp(-0.5 * pre * pre) * (1.0 / math.sqrt(2.0 * math.pi))
            ).astype(slope.dtype)

    def project(s):
        at = pair_at(s)
        for j in range(3):
            block = pl.ds(j * head_cols, head_cols)
            raw = dot_nt(x_attn[at, :], w_qkv[block, :]) + bias_qkv[:, block]
            turns = lax.div(3 * ctx + j, group) < 2
            for m in range(head_cols // HEAD_DIM):
                one = raw[:, m * HEAD_DIM : (m + 1) * HEAD_DIM]
                turned = (
                    one * tables[0, at, :]
                    + pltpu.roll(one, HEAD_DIM - ROT_DIM // 2, 1) * tables[1, at, :]
                    + pltpu.roll(one, ROT_DIM // 2, 1) * tables[2, at, :]
                )
                heads[j, at, m * HEAD_DIM : (m + 1) * HEAD_DIM] = jnp.where(
                    turns, turned, one
                ).astype(bf16)

    def mix(s):
        at = pair_at(s)

        @pl.loop(0, columns // wide)
        def _(n):
            cols = pl.ds(pl.multiple_of(n * wide, wide), wide)
            part[at, cols] = dot_nn(act[at, :], w_down[:, cols]).astype(bf16)

    def back_feed(s):
        at = pair_at(s)

        @pl.loop(0, units // wide)
        def _(n):
            cols = pl.ds(pl.multiple_of(n * wide, wide), wide)
            rounded = (
                dot_nt(g_buf[at, :], w_down[cols, :]) * slope[at, cols].astype(f32)
            ).astype(bf16)
            pre_grad[at, cols] = rounded
            bias_sum[:, cols] += jnp.sum(rounded.astype(f32), axis=0, keepdims=True)

        @pl.loop(0, columns // wide)
        def _(n):
            cols = pl.ds(pl.multiple_of(n * wide, wide), wide)
            entry = dot_nn(pre_grad[at, :], w_up[:, cols])
            normed = (h_buf[at, cols].astype(f32) - mean[at, :]) * rstd[at, :]
            sums[0:1, cols] += jnp.sum(entry * normed, axis=0, keepdims=True)
            sums[1:2, cols] += jnp.sum(entry, axis=0, keepdims=True)
            back[at, cols] = (entry * norms[2:3, cols]).astype(bf16)

    def forward(s):
        keep(0, s, h_buf, h_out).start()
        normalize(s)
        keep(1, s, x_attn, x_out).start()
        if s == 0:
            weights[0].wait()
        feed(s)
        if s == 0:
            weights[1].wait()
        project(s)

    def backward(s):
        keep(2, s, g_buf, g_out).start()
        if s == 0:
            weights[2].wait()
        mix(s)
        keep(3, s, part, part_out).start()
        back_feed(s)
        keep(4, s, back, back_out).start()

    def outer(n, left, right, held, out):
        tall = 256
        for m in range(units // tall):
            mine = pl.ds(m * tall, tall)

            @pl.loop(0, columns // (2 * wide))
            def _(k):
                cols = pl.ds(pl.multiple_of(k * 2 * wide, 2 * wide), 2 * wide)
                held[mine, cols] = dot_tn(left[:, mine], right[:, cols]).astype(bf16)

            pltpu.make_async_copy(held.at[mine], out.at[mine], grad_sem.at[n, m]).start()

    def outer_wait(n, held, out):
        tall = 256
        for m in range(units // tall):
            mine = pl.ds(m * tall, tall)
            pltpu.make_async_copy(held.at[mine], out.at[mine], grad_sem.at[n, m]).wait()

    def to_head(j):
        target = lax.rem(3 * ctx + j, group)
        remote = copy_to(
            heads.at[j], heads_out.at[j], head_send.at[j], head_recv.at[j], (dp, target)
        )
        local = pltpu.make_async_copy(heads.at[j], heads_out.at[j], head_recv.at[j])
        return target == ctx, remote, local

    turn(1)
    own[0].wait()
    y_arrive(0, 0)
    forward(0)
    turn(2)
    y_arrive(0, 1)
    forward(1)
    turn(3)
    y_arrive(0, 2)
    forward(2)
    turn(4)
    y_arrive(0, 3)
    forward(3)
    turn(5)
    own[1].wait()
    y_arrive(1, 0)
    backward(0)
    turn(6)
    y_arrive(1, 1)
    backward(1)
    turn(7)
    for j in range(3):
        here, remote, local = to_head(j)
        pl.when(here)(lambda local=local: local.start())
        pl.when(jnp.logical_not(here))(lambda remote=remote: remote.start())
    y_arrive(1, 2)
    backward(2)
    y_arrive(1, 3)
    backward(3)
    outer(0, act, g_buf, down_grad, down_out)
    outer(1, pre_grad, x_mlp, up_grad, up_out)

    for at_z in range(depth):
        to_other(0, at_z).wait_send()
        to_other(1, at_z).wait_send()
        for i in range(2):
            pl.when(has_above & (at_z <= z))(lambda i=i: upward(i, at_z).wait_send())
            pl.when(has_below & (at_z >= z))(lambda i=i: downward(i, at_z).wait_send())
    for j in range(3):
        here, remote, local = to_head(j)
        pl.when(here)(lambda local=local: local.wait())
        pl.when(jnp.logical_not(here))(lambda remote=remote: remote.wait_send())
        source = lax.rem(3 * (ctx + group - j), group)
        pl.when(source != ctx)(lambda remote=remote: remote.wait_recv())
    for s in range(4):
        keep(0, s, h_buf, h_out).wait()
        keep(1, s, x_attn, x_out).wait()
        keep(2, s, g_buf, g_out).wait()
        keep(3, s, part, part_out).wait()
        keep(4, s, back, back_out).wait()
    outer_wait(0, down_grad, down_out)
    outer_wait(1, up_grad, up_out)


def layer_pass(group, hidden, grad, w_up, w_down, w_qkv, norms, bias_up, bias_qkv, seg_len, seg_parent):
    rows, columns = hidden.shape
    tokens, units, head_cols = group * rows, w_up.shape[0], w_qkv.shape[0] // 3
    depth = group // RAILS
    inverse = jnp.power(10000.0, -2.0 * jnp.arange(ROT_DIM // 2, dtype=f32) / ROT_DIM)
    inverse = jnp.broadcast_to(inverse[:, None], (ROT_DIM // 2, rows))
    sems = pltpu.SemaphoreType.DMA
    shape = jax.ShapeDtypeStruct
    anywhere = pl.BlockSpec(memory_space=pl.ANY)
    vmem = pl.BlockSpec(memory_space=pltpu.VMEM)
    smem = pl.BlockSpec(memory_space=pltpu.SMEM)
    whole = shape((tokens, columns), bf16)
    weight = shape((units, columns), bf16)
    return pl.pallas_call(
        functools.partial(layer_kernel, group),
        out_shape=(
            whole,
            whole,
            whole,
            shape((3, tokens, head_cols), bf16),
            whole,
            whole,
            weight,
            weight,
            shape((4, tokens, HEAD_DIM), f32),
            shape((2, columns), f32),
            shape((1, units), f32),
        ),
        in_specs=[anywhere] * 5 + [vmem] * 4 + [smem] * 2,
        out_specs=[anywhere] * 8 + [vmem] * 3,
        scratch_shapes=[pltpu.VMEM((tokens, columns), bf16)] * 2
        + [pltpu.VMEM((units, columns), bf16)] * 2
        + [pltpu.VMEM((3 * head_cols, columns), bf16)]
        + [pltpu.VMEM((tokens, columns), bf16)] * 2
        + [pltpu.VMEM((tokens, units), bf16)] * 3
        + [pltpu.VMEM((3, tokens, head_cols), bf16)]
        + [pltpu.VMEM((tokens, columns), bf16)] * 2
        + [pltpu.VMEM((units, columns), bf16)] * 2
        + [pltpu.VMEM((tokens, 1), f32)] * 2
        + [sems((2,))]
        + [sems((2, depth))] * 6
        + [sems((3,)), sems((5, 4)), sems((2, units // 256)), sems((3,)), sems((3,))],
        compiler_params=pltpu.CompilerParams(
            collective_id=0, has_side_effects=True, vmem_limit_bytes=60 * 2**20
        ),
        name="layer_pass",
    )(hidden, grad, w_up, w_down, w_qkv, norms, bias_up, bias_qkv, inverse, seg_len, seg_parent)


def reduce_kernel(group, tiles, *refs):
    count = len(tiles)
    parts, grads, vectors = refs[:2], refs[2 : 2 + count], refs[2 + count]
    refs = refs[3 + count :]
    outs, grads_out, vectors_out = refs[:2], refs[2 : 2 + count], refs[2 + count]
    refs = refs[3 + count :]
    own, y_buf, up_buf, down_buf, mine, from_core, from_x, vec_buf = refs[:8]
    (
        own_sem,
        y_send,
        y_recv,
        up_send,
        up_recv,
        down_send,
        down_recv,
        out_sem,
        mine_sem,
        core_send,
        core_recv,
        x_send,
        x_recv,
        keep_sem,
        done_send,
        done_recv,
        vec_send,
        vec_recv,
    ) = refs[8:]
    dp, ctx, z, y, depth = place(group)
    rows = outs[0].shape[0]
    x, core = dp // 2, dp % 2
    other = (dp, z * RAILS + 1 - y)
    above = (dp, jnp.minimum(z + 1, depth - 1) * RAILS + y)
    below = (dp, jnp.maximum(z - 1, 0) * RAILS + y)
    sibling = (x * 2 + 1 - core, ctx)
    across = ((1 - x) * 2 + core, ctx)
    pair = (dp, (z + 1 - 2 * (z % 2)) * RAILS + y)
    pair_far = (dp, lax.rem(z + 2, depth) * RAILS + y)
    has_above, has_below = z < depth - 1, z > 0

    for device in (other, sibling, across, pair, pair_far):
        signal(device)
    inner = (z > 0) & (z < depth - 1)
    pl.when(inner)(lambda: signal((dp, jnp.clip(z - 1 + 2 * (z % 2), 0, depth - 1) * RAILS + y)))
    arrive(5 + inner.astype(jnp.int32))

    def part_chunk(i, at_z, at_y):
        start = pl.multiple_of((at_z * RAILS + at_y) * rows, rows)
        return parts[i].at[pl.ds(start, rows)]

    half = mine.shape[1]

    spots = [(n, m) for n, amount in enumerate(tiles) for m in range(amount)]
    tiles = len(spots)

    def tile_half(arrays, t, which):
        n, m = spots[t]
        start = pl.multiple_of((2 * m + which) * half, half)
        return arrays[n].at[pl.ds(start, half)]

    def fetch(t):
        return pltpu.make_async_copy(tile_half(grads, t, core), mine.at[t], mine_sem.at[t])

    def to_core(t):
        return copy_to(
            tile_half(grads, t, 1 - core),
            from_core.at[t],
            core_send.at[t],
            core_recv.at[t],
            sibling,
        )

    def to_x(t):
        return copy_to(mine.at[t], from_x.at[t], x_send.at[t], x_recv.at[t], across)

    def keep(t):
        return pltpu.make_async_copy(
            from_core.at[t], tile_half(grads_out, t, core), keep_sem.at[t]
        )

    def finish(t):
        return copy_to(
            from_core.at[t],
            tile_half(grads_out, t, core),
            done_send.at[t],
            done_recv.at[t],
            sibling,
        )

    def add(target, left, right):
        step = 32

        @pl.loop(0, target.shape[0] // step)
        def _(n):
            at = pl.ds(pl.multiple_of(n * step, step), step)
            target[at, :] = (left[at, :].astype(f32) + right[at, :].astype(f32)).astype(
                target.dtype
            )

    def core_sum(t):
        fetch(t).wait()
        to_core(t).wait_recv()
        add(mine.at[t], mine.at[t], from_core.at[t])
        to_x(t).start()

    def x_sum(t):
        to_x(t).wait_recv()
        add(from_core.at[t], mine.at[t], from_x.at[t])
        keep(t).start()
        finish(t).start()

    low = z < depth // 2
    order = [
        jnp.where(low, depth - 1, 0),
        jnp.where(low, depth - 2, 1),
        jnp.where(low, 1 - z, 2 * depth - 3 - z),
        z,
    ]

    def hold(i, s):
        return pltpu.make_async_copy(
            part_chunk(i, order[s], y), own.at[i, order[s]], own_sem.at[i, s]
        )

    def swap(i, s):
        return copy_to(
            part_chunk(i, order[s], 1 - y),
            y_buf.at[i, order[s]],
            y_send.at[i, s],
            y_recv.at[i, s],
            other,
        )

    def upward(i, at):
        return copy_to(own.at[i, at], up_buf.at[i, at], up_send.at[i, at], up_recv.at[i, at], above)

    def downward(i, at):
        return copy_to(
            own.at[i, at], down_buf.at[i, at], down_send.at[i, at], down_recv.at[i, at], below
        )

    def scatter_step(i, s):
        at = order[s]
        hold(i, s).wait()
        swap(i, s).wait_recv()
        add(own.at[i, at], own.at[i, at], y_buf.at[i, at])

        @pl.when((at >= z) & has_below)
        def _():
            upward(i, at).wait_recv()
            add(own.at[i, at], own.at[i, at], up_buf.at[i, at])

        @pl.when((at <= z) & has_above)
        def _():
            downward(i, at).wait_recv()
            add(own.at[i, at], own.at[i, at], down_buf.at[i, at])

        pl.when(at > z)(lambda: upward(i, at).start())
        pl.when(at < z)(lambda: downward(i, at).start())

    def scatter_out(i):
        return pltpu.make_async_copy(own.at[i, z], outs[i], out_sem.at[i])

    stages = (sibling, across, other, pair, pair_far)

    def exchange(n):
        return copy_to(
            vec_buf.at[2 * n], vec_buf.at[2 * n + 1], vec_send.at[n], vec_recv.at[n], stages[n]
        )

    for t in range(tiles):
        fetch(t).start()
        to_core(t).start()
    vec_buf[0] = vectors[...]
    exchange(0).start()
    for i in range(2):
        for s in range(depth):
            hold(i, s).start()
            swap(i, s).start()
    core_sum(0)
    core_sum(1)
    steps = [(i, s) for i in range(2) for s in range(depth)]
    for t in range(tiles):
        if t + 2 < tiles:
            core_sum(t + 2)
        if t < len(stages):
            exchange(t).wait_recv()
            total = vec_buf[2 * t] + vec_buf[2 * t + 1]
            if t + 1 < len(stages):
                vec_buf[2 * t + 2] = total
                exchange(t + 1).start()
            else:
                vectors_out[...] = total
        if t < len(steps):
            scatter_step(*steps[t])
            if steps[t][1] == depth - 1:
                scatter_out(steps[t][0]).start()
        x_sum(t)
    for t in range(tiles):
        to_core(t).wait_send()
        to_x(t).wait_send()
        keep(t).wait()
        finish(t).wait_send()
        copy_to(
            from_core.at[t],
            tile_half(grads_out, t, 1 - core),
            done_send.at[t],
            done_recv.at[t],
            sibling,
        ).wait_recv()
    for n in range(len(stages)):
        exchange(n).wait_send()
    for i in range(2):
        scatter_out(i).wait()
        for s in range(depth):
            swap(i, s).wait_send()
            at = order[s]
            pl.when(at > z)(lambda: upward(i, at).wait_send())
            pl.when(at < z)(lambda: downward(i, at).wait_send())


def reduce_all(group, first, second, grads, vectors):
    tokens, columns = first.shape
    depth = group // RAILS
    rows = tokens // group
    half = 128
    tiles = [grad.shape[0] // (2 * half) for grad in grads]
    sems = pltpu.SemaphoreType.DMA
    part = jax.ShapeDtypeStruct((rows, columns), first.dtype)
    anywhere = pl.BlockSpec(memory_space=pl.ANY)
    vmem = pl.BlockSpec(memory_space=pltpu.VMEM)
    chunks = pltpu.VMEM((2, depth, rows, columns), first.dtype)
    halves = pltpu.VMEM((sum(tiles), half, columns), first.dtype)
    results = pl.pallas_call(
        functools.partial(reduce_kernel, group, tiles),
        out_shape=(
            part,
            part,
            *[jax.ShapeDtypeStruct(grad.shape, grad.dtype) for grad in grads],
            jax.ShapeDtypeStruct(vectors.shape, vectors.dtype),
        ),
        in_specs=[anywhere] * (2 + len(grads)) + [vmem],
        out_specs=[anywhere] * (2 + len(grads)) + [vmem],
        scratch_shapes=[chunks] * 4
        + [halves] * 3
        + [pltpu.VMEM((10,) + vectors.shape, vectors.dtype)]
        + [sems((2, depth))] * 7
        + [sems((2,))]
        + [sems((sum(tiles),))] * 8
        + [sems((5,))] * 2,
        compiler_params=pltpu.CompilerParams(
            collective_id=1, has_side_effects=True, vmem_limit_bytes=56 * 2**20
        ),
        name="reduce_all",
    )(first, second, *grads, vectors)
    return results[0], results[1], results[2:-1], results[-1]


def body(
    hidden_in,
    grad_out,
    seg_len,
    seg_parent,
    gain_attn,
    shift_attn,
    w_qkv,
    bias_qkv,
    w_out,
    bias_out,
    gain_mlp,
    shift_mlp,
    w_up,
    bias_up,
    w_down,
    bias_down,
):
    group = lax.axis_size("ctx")
    me = lax.axis_index("ctx")
    local_rows = hidden_in.shape[1]
    tokens = local_rows * group
    head_count = HEADS // group
    head_cols = head_count * HEAD_DIM
    head_shape = (tokens, head_count, HEAD_DIM)
    scale = 1.0 / math.sqrt(HEAD_DIM)

    seg_ends, seg_starts, ancestor, path_start = tree_tables(seg_len[0], seg_parent[0])
    ids = jnp.arange(tokens, dtype=jnp.int32)
    seg_index = jnp.sum((ids[:, None] >= seg_ends[None, :]).astype(jnp.int32), axis=1)
    labels = jnp.arange(seg_ends.shape[0], dtype=jnp.int32)
    hot = (seg_index[:, None] == labels[None, :]).astype(f32)
    reach = jnp.dot(hot, ancestor.astype(f32))
    allowed = (jnp.dot(reach, hot.T) > 0.5) & (ids[None, :] <= ids[:, None])

    norms = jnp.stack([gain_attn, shift_attn, gain_mlp, shift_mlp]).astype(f32)
    up_bias = lax.dynamic_slice_in_dim(bias_up, me * w_up.shape[0], w_up.shape[0])
    qkv_bias = lax.dynamic_slice_in_dim(bias_qkv, me * 3 * head_cols, 3 * head_cols)
    (
        hidden_all,
        grad_all,
        x_attn,
        arrived,
        mlp_part,
        mlp_back,
        grad_w_down,
        grad_w_up,
        tables,
        mlp_sums,
        up_sums,
    ) = layer_pass(
        group,
        hidden_in[0],
        grad_out[0],
        w_up,
        w_down,
        w_qkv,
        norms,
        up_bias.astype(f32)[None],
        qkv_bias.astype(f32)[None],
        seg_len,
        seg_parent,
    )
    w_out, arrived = lax.optimization_barrier((w_out, arrived))
    w_out_cols = lax.all_to_all(
        w_out, "ctx", split_axis=1, concat_axis=0, tiled=True
    )
    mean, rstd = tables[3, :, :1], tables[3, :, 1:2]
    cosine = tables[0, :, :ROT_DIM]
    sine = tables[2, :, ROT_DIM // 2 : ROT_DIM]
    sine = jnp.concatenate([sine, sine], axis=1)
    gain_a = norms[0]

    q, k, v = [
        lax.dynamic_index_in_dim(arrived, (kind * group + me) % 3, 0, keepdims=False).reshape(
            head_shape
        )
        for kind in range(3)
    ]
    scores = jnp.einsum("qhd,khd->hqk", q, k, preferred_element_type=f32) * scale
    scores = jnp.where(allowed[None], scores, masked_score)
    top = jnp.max(scores, axis=-1, keepdims=True)
    expo = jnp.exp(scores - top)
    probs = expo / jnp.sum(expo, axis=-1, keepdims=True)
    weights = probs.astype(bf16)
    attended = jnp.einsum("hqk,khd->qhd", weights, v, preferred_element_type=f32).astype(bf16)
    attended = attended.reshape(tokens, head_cols)

    partial = (dot_nt(attended, w_out_cols) + mlp_part.astype(f32)).astype(bf16)

    grad_w_out_cols = dot_tn(grad_all, attended).astype(bf16)
    att_grad = dot_nn(grad_all, w_out_cols).astype(bf16).reshape(head_shape)
    prob_grad = jnp.einsum("qhd,khd->hqk", att_grad, v, preferred_element_type=f32)
    delta = jnp.sum(probs * prob_grad, axis=-1, keepdims=True)
    score_grad = (probs * (prob_grad - delta)).astype(bf16)
    q_grad = jnp.einsum("hqk,khd->qhd", score_grad, k, preferred_element_type=f32) * scale
    k_grad = jnp.einsum("hqk,qhd->khd", score_grad, q, preferred_element_type=f32) * scale
    v_grad = jnp.einsum("hqk,qhd->khd", weights, att_grad, preferred_element_type=f32)
    qkv_grad = [
        rotate(q_grad, cosine, -sine).astype(bf16).reshape(tokens, head_cols),
        rotate(k_grad, cosine, -sine).astype(bf16).reshape(tokens, head_cols),
        v_grad.astype(bf16).reshape(tokens, head_cols),
    ]
    qkv_grad = jnp.stack(qkv_grad)
    returned = []
    for j in range(3):
        kind_of_slot = sum(
            kind * ((kind * group + me) % 3 == j).astype(jnp.int32) for kind in range(3)
        )
        block = lax.dynamic_index_in_dim(qkv_grad, kind_of_slot, 0, keepdims=False)
        returned.append(
            lax.ppermute(block, "ctx", [((3 * c + j) % group, c) for c in range(group)])
        )
    qkv_grad = jnp.concatenate(returned, axis=1)
    attn_in_grad = dot_nn(qkv_grad, w_qkv)
    grad_w_qkv = dot_tn(qkv_grad, x_attn).astype(bf16)
    grad_w_out = lax.all_to_all(
        grad_w_out_cols, "ctx", split_axis=0, concat_axis=1, tiled=True
    )
    back = (attn_in_grad * gain_a + mlp_back.astype(f32)).astype(bf16)
    normed = (hidden_all.astype(f32) - mean) * rstd

    def widen(part, length):
        at = me * part.shape[0]
        return lax.dynamic_update_slice(jnp.zeros((length,), f32), part, (at,))

    grad_f = grad_out[0].astype(f32)
    vectors = jnp.concatenate(
        [
            jnp.sum(attn_in_grad * normed, axis=0),
            jnp.sum(attn_in_grad, axis=0),
            mlp_sums[0],
            mlp_sums[1],
            widen(jnp.sum(qkv_grad, axis=0, dtype=f32), 3 * D),
            jnp.sum(grad_f, axis=0),
            widen(up_sums[0], FF),
        ]
    )
    summed, w_sum, sums, vectors = reduce_all(
        group,
        partial,
        back,
        (grad_w_down, grad_w_up, grad_w_out, grad_w_qkv),
        vectors.reshape(-1, 1024),
    )
    vectors = vectors.reshape(-1)
    w_sum = w_sum.astype(f32)
    hidden_out = (
        hidden_in[0].astype(f32) + summed.astype(f32) + bias_out.astype(f32) + bias_down.astype(f32)
    ).astype(bf16)
    start = me * local_rows
    my_rstd = lax.dynamic_slice_in_dim(rstd, start, local_rows)
    my_normed = (
        hidden_in[0].astype(f32) - lax.dynamic_slice_in_dim(mean, start, local_rows)
    ) * my_rstd
    grad_in = (
        grad_f
        + (
            w_sum
            - jnp.mean(w_sum, axis=-1, keepdims=True)
            - my_normed * jnp.mean(w_sum * my_normed, axis=-1, keepdims=True)
        )
        * my_rstd
    )

    cuts = [D, D, D, D, 3 * D, D, FF]
    ends = [sum(cuts[: i + 1]) for i in range(len(cuts))]
    gain_grad_a, shift_grad_a, gain_grad_m, shift_grad_m, qkv_bias_grad, out_bias_grad, up_bias_grad = [
        vectors[end - cut : end] for cut, end in zip(cuts, ends)
    ]

    return (
        hidden_out[None],
        grad_in[None],
        gain_grad_a,
        shift_grad_a,
        sums[3].astype(f32),
        qkv_bias_grad,
        sums[2].astype(f32),
        out_bias_grad,
        gain_grad_m,
        shift_grad_m,
        sums[1].astype(f32),
        up_bias_grad,
        sums[0].astype(f32),
        out_bias_grad,
    )


block_limit = 512


def rotary_tables(path_pos):
    half_dim = ROT_DIM // 2
    inverse = jnp.power(10000.0, -2.0 * jnp.arange(half_dim, dtype=jnp.float32) / ROT_DIM)
    angles = path_pos.astype(jnp.float32)[:, None] * inverse[None, :]
    angles = jnp.concatenate([angles, angles], axis=1)
    return (jnp.cos(angles), jnp.sin(angles))


def layer_norm(values, gain_vec, shift_vec):
    average = jnp.mean(values, axis=-1, keepdims=True)
    centred = values - average
    spread = jnp.mean(centred * centred, axis=-1, keepdims=True)
    return centred * lax.rsqrt(spread + norm_eps) * gain_vec + shift_vec


def segment_hot(row_ids, seg_ends):
    seg_index = jnp.sum((row_ids[:, None] >= seg_ends[None, :]).astype(jnp.int32), axis=1)
    labels = jnp.arange(seg_ends.shape[0], dtype=jnp.int32)
    return (seg_index[:, None] == labels[None, :]).astype(jnp.float32)


def row_lookup(row_ids, seg_ends, ancestor_f):
    row_hot = segment_hot(row_ids, seg_ends)
    return (row_hot, jnp.dot(row_hot, ancestor_f))


def permitted(query_ids, query_reach, key_ids, key_hot):
    linked = jnp.dot(query_reach, key_hot.T) > 0.5
    return linked & (key_ids[None, :] <= query_ids[:, None])


def inner_block(row_count):
    block_rows = row_count
    while block_rows > block_limit and block_rows % 2 == 0:
        block_rows = block_rows // 2
    return block_rows


def gather_body(
    hidden_in,
    grad_out,
    seg_len,
    seg_parent,
    gain_attn,
    shift_attn,
    w_qkv,
    bias_qkv,
    w_out,
    bias_out,
    gain_mlp,
    shift_mlp,
    w_up,
    bias_up,
    w_down,
    bias_down,
):
    local_rows = hidden_in.shape[1]
    scale_factor = 1.0 / math.sqrt(HEAD_DIM)
    head_shape = (local_rows, HEADS, HEAD_DIM)
    seg_ends, seg_starts, ancestor, path_start = tree_tables(seg_len[0], seg_parent[0])
    ancestor_f = ancestor.astype(jnp.float32)
    my_ids = lax.axis_index("ctx") * local_rows + jnp.arange(local_rows, dtype=jnp.int32)
    my_hot, my_reach = row_lookup(my_ids, seg_ends, ancestor_f)
    shift_table = path_start - seg_starts
    path_pos = my_ids + jnp.sum(my_hot.astype(jnp.int32) * shift_table[None, :], axis=1)
    cosine, sine = rotary_tables(path_pos)
    inputs_f = hidden_in[0].astype(jnp.float32)
    gain_a = gain_attn.astype(jnp.float32)
    shift_a = shift_attn.astype(jnp.float32)
    gain_m = gain_mlp.astype(jnp.float32)
    shift_m = shift_mlp.astype(jnp.float32)
    bias_up_f = bias_up.astype(jnp.float32)
    x_attn = layer_norm(inputs_f, gain_a, shift_a).astype(jnp.bfloat16)
    x_mlp = layer_norm(inputs_f, gain_m, shift_m).astype(jnp.bfloat16)
    qkv = jnp.einsum(
        "td,nd->tn",
        x_attn,
        lax.all_gather(w_qkv, "ctx", axis=0, tiled=True),
        preferred_element_type=jnp.float32,
    ) + bias_qkv.astype(jnp.float32)
    queries = rotate(qkv[:, :D].reshape(head_shape), cosine, sine).astype(jnp.bfloat16)
    keys_heads = rotate(qkv[:, D : 2 * D].reshape(head_shape), cosine, sine).astype(jnp.bfloat16)
    values_flat = qkv[:, 2 * D :].astype(jnp.bfloat16)
    values_heads = values_flat.reshape(head_shape)
    keys_flat = keys_heads.reshape(local_rows, D)
    queries_flat = queries.reshape(local_rows, D)

    def split_blocks(shard_pieces):
        row_count = shard_pieces[0].shape[0]
        block_rows = inner_block(row_count)
        block_count = row_count // block_rows
        shaped = tuple(
            (member.reshape(block_count, block_rows, HEADS, HEAD_DIM) for member in shard_pieces)
        )
        starts = block_rows * jnp.arange(block_count, dtype=jnp.int32)
        return shaped + (starts,)

    def attend_block(fold_state, block_items):
        key_block, value_block, block_start = block_items
        block_rows = key_block.shape[0]
        key_ids = block_start + jnp.arange(block_rows, dtype=jnp.int32)
        allowed = permitted(my_ids, my_reach, key_ids, segment_hot(key_ids, seg_ends))
        row_top, row_total, partial_value = fold_state
        scores = (
            jnp.einsum("qhd,khd->qhk", queries, key_block, preferred_element_type=jnp.float32)
            * scale_factor
        )
        scores = jnp.where(allowed[:, None, :], scores, masked_score)
        new_top = jnp.maximum(row_top, jnp.max(scores, axis=-1))
        factor = jnp.exp(row_top - new_top)
        weights = jnp.exp(scores - new_top[:, :, None])
        row_total = row_total * factor + jnp.sum(weights, axis=-1)
        partial_value = partial_value * factor[:, :, None] + jnp.einsum(
            "qhk,khd->qhd",
            weights.astype(jnp.bfloat16),
            value_block,
            preferred_element_type=jnp.float32,
        )
        fold_state = (new_top, row_total, partial_value)
        return (fold_state, None)

    start_state = (
        jnp.full((local_rows, HEADS), masked_score, jnp.float32),
        jnp.zeros((local_rows, HEADS), jnp.float32),
        jnp.zeros(head_shape, jnp.float32),
    )
    row_top, row_total, partial_value = lax.scan(
        attend_block,
        start_state,
        split_blocks(
            (
                lax.all_gather(keys_flat, "ctx", axis=0, tiled=True),
                lax.all_gather(values_flat, "ctx", axis=0, tiled=True),
            )
        ),
    )[0]
    log_total = row_top + jnp.log(row_total)
    attended_f = partial_value / row_total[:, :, None]
    attended = attended_f.reshape(local_rows, D).astype(jnp.bfloat16)
    attn_proj = jnp.einsum(
        "td,nd->tn",
        attended,
        lax.all_gather(w_out, "ctx", axis=0, tiled=True),
        preferred_element_type=jnp.float32,
    )

    def mlp_pre(up_rows):
        return (
            jnp.einsum("td,nd->tn", x_mlp, up_rows, preferred_element_type=jnp.float32) + bias_up_f
        )

    up_rows = lax.all_gather(w_up, "ctx", axis=0, tiled=True)
    down_rows = lax.all_gather(w_down, "ctx", axis=0, tiled=True)
    activated = jax.nn.gelu(mlp_pre(up_rows), approximate=False).astype(jnp.bfloat16)
    mlp_sum = jnp.dot(activated, down_rows, preferred_element_type=jnp.float32)
    bias_out_f = bias_out.astype(jnp.float32)
    bias_down_f = bias_down.astype(jnp.float32)
    hidden_out = (inputs_f + attn_proj + bias_out_f + mlp_sum + bias_down_f).astype(jnp.bfloat16)
    grad_b = grad_out[0]
    grad_f = grad_b.astype(jnp.float32)
    up_rows = lax.all_gather(w_up, "ctx", axis=0, tiled=True)
    down_rows = lax.all_gather(w_down, "ctx", axis=0, tiled=True)
    pre_act = mlp_pre(up_rows)
    activated = jax.nn.gelu(pre_act, approximate=False).astype(jnp.bfloat16)
    act_grad = jnp.einsum("td,nd->tn", grad_b, down_rows, preferred_element_type=jnp.float32)
    pre_grad = (act_grad * gelu_slope(pre_act)).astype(jnp.bfloat16)
    input_grad = jnp.dot(pre_grad, up_rows, preferred_element_type=jnp.float32)
    act_all = activated
    pre_grad_all = pre_grad
    act_all, pre_grad_all, mlp_in_grad = (act_all, pre_grad_all, input_grad)
    attended_grad = jnp.dot(
        grad_b, lax.all_gather(w_out, "ctx", axis=0, tiled=True), preferred_element_type=jnp.float32
    ).astype(jnp.bfloat16)
    attended_grad_heads = attended_grad.reshape(head_shape)
    row_delta = jnp.sum(attended_grad_heads.astype(jnp.float32) * attended_f, axis=-1)
    all_log_total, all_delta = (
        lax.all_gather(log_total, "ctx", axis=0, tiled=True),
        lax.all_gather(row_delta, "ctx", axis=0, tiled=True),
    )

    def back_block(fold_state, block_items):
        key_block, value_block, query_block, grad_block, block_start = block_items
        block_rows = key_block.shape[0]
        other_ids = block_start + jnp.arange(block_rows, dtype=jnp.int32)
        other_hot, other_reach = row_lookup(other_ids, seg_ends, ancestor_f)
        allowed_in = permitted(my_ids, my_reach, other_ids, other_hot)
        allowed_out = permitted(other_ids, other_reach, my_ids, my_hot)
        other_log = lax.dynamic_slice_in_dim(all_log_total, block_start, block_rows, 0)
        other_delta = lax.dynamic_slice_in_dim(all_delta, block_start, block_rows, 0)
        query_grad, key_grad, value_grad = fold_state
        scores = (
            jnp.einsum("qhd,khd->qhk", queries, key_block, preferred_element_type=jnp.float32)
            * scale_factor
        )
        scores = jnp.where(allowed_in[:, None, :], scores, masked_score)
        prob_mass = jnp.exp(scores - log_total[:, :, None])
        prob_grad = jnp.einsum(
            "qhd,khd->qhk", attended_grad_heads, value_block, preferred_element_type=jnp.float32
        )
        score_grad = (prob_mass * (prob_grad - row_delta[:, :, None])).astype(jnp.bfloat16)
        query_grad = (
            query_grad
            + jnp.einsum("qhk,khd->qhd", score_grad, key_block, preferred_element_type=jnp.float32)
            * scale_factor
        )
        outgoing_key_grad = key_grad
        outgoing_value_grad = value_grad
        scores = (
            jnp.einsum("qhd,khd->qhk", query_block, keys_heads, preferred_element_type=jnp.float32)
            * scale_factor
        )
        scores = jnp.where(allowed_out[:, None, :], scores, masked_score)
        prob_mass = jnp.exp(scores - other_log[:, :, None])
        outgoing_value_grad = outgoing_value_grad + jnp.einsum(
            "qhk,qhd->khd",
            prob_mass.astype(jnp.bfloat16),
            grad_block,
            preferred_element_type=jnp.float32,
        )
        prob_grad = jnp.einsum(
            "qhd,khd->qhk", grad_block, values_heads, preferred_element_type=jnp.float32
        )
        score_grad = (prob_mass * (prob_grad - other_delta[:, :, None])).astype(jnp.bfloat16)
        outgoing_key_grad = (
            outgoing_key_grad
            + jnp.einsum(
                "qhk,qhd->khd", score_grad, query_block, preferred_element_type=jnp.float32
            )
            * scale_factor
        )
        fold_state = (query_grad, outgoing_key_grad, outgoing_value_grad)
        return (fold_state, None)

    zero_heads = jnp.zeros(head_shape, jnp.float32)
    query_grad, key_grad, value_grad = lax.scan(
        back_block,
        (zero_heads, zero_heads, zero_heads),
        split_blocks(
            (
                lax.all_gather(keys_flat, "ctx", axis=0, tiled=True),
                lax.all_gather(values_flat, "ctx", axis=0, tiled=True),
                lax.all_gather(queries_flat, "ctx", axis=0, tiled=True),
                lax.all_gather(attended_grad, "ctx", axis=0, tiled=True),
            )
        ),
    )[0]

    def turn(head_values):
        return rotate(head_values, cosine, sine)

    unturn = jax.vjp(turn, zero_heads)[1]
    qkv_grad = jnp.concatenate(
        [
            unturn(query_grad)[0].reshape(local_rows, D),
            unturn(key_grad)[0].reshape(local_rows, D),
            value_grad.reshape(local_rows, D),
        ],
        axis=1,
    ).astype(jnp.bfloat16)
    attn_in_grad = jnp.dot(
        qkv_grad,
        lax.all_gather(w_qkv, "ctx", axis=0, tiled=True),
        preferred_element_type=jnp.float32,
    )
    pull_attn = jax.vjp(layer_norm, inputs_f, gain_a, shift_a)[1]
    input_part_a, gain_grad_a, shift_grad_a = pull_attn(attn_in_grad)
    pull_mlp = jax.vjp(layer_norm, inputs_f, gain_m, shift_m)[1]
    input_part_m, gain_grad_m, shift_grad_m = pull_mlp(mlp_in_grad)
    grad_in = (grad_f + input_part_a + input_part_m)[None]
    vector_sums = lax.psum(
        (
            gain_grad_a,
            shift_grad_a,
            gain_grad_m,
            shift_grad_m,
            jnp.sum(qkv_grad, axis=0, dtype=jnp.float32),
            jnp.sum(grad_f, axis=0),
            jnp.sum(pre_grad_all, axis=0, dtype=jnp.float32),
        ),
        ("dp", "ctx"),
    )
    group_count = lax.axis_size("ctx")
    section_rows = (3 * D // group_count, D // group_count, FF // group_count, FF // group_count)
    term_sources = (
        (qkv_grad, x_attn),
        (grad_b, attended),
        (pre_grad_all, x_mlp),
        (act_all, grad_b),
    )
    owner_rows = sum(section_rows)
    blocks = jnp.arange(owner_rows * lax.axis_size("ctx") // owner_rows, dtype=jnp.int32)
    parts_list = []
    for (column_source, other_side), full_rows in zip(term_sources, section_rows):
        sub_rows = full_rows // 1
        column_ids = (
            blocks[:, None] * sub_rows + jnp.arange(sub_rows, dtype=jnp.int32)[None, :]
        ).reshape(-1)
        columns = jnp.take(column_source, column_ids, axis=1)
        block_term = jnp.einsum(
            "tr,td->rd", columns, other_side, preferred_element_type=jnp.float32
        )
        parts_list.append(block_term.reshape(blocks.shape[0], sub_rows, D))
    owned_term = lax.psum_scatter(
        jnp.concatenate(parts_list, axis=1).reshape(-1, D).astype(jnp.bfloat16),
        "ctx",
        scatter_dimension=0,
        tiled=True,
    ).astype(jnp.float32)
    cut_a = section_rows[0]
    cut_b = cut_a + section_rows[1]
    cut_c = cut_b + section_rows[2]
    weight_grads = (
        lax.psum(owned_term[:cut_a].astype(jnp.bfloat16), "dp").astype(jnp.float32),
        lax.psum(owned_term[cut_a:cut_b].astype(jnp.bfloat16), "dp").astype(jnp.float32),
        lax.psum(owned_term[cut_b:cut_c].astype(jnp.bfloat16), "dp").astype(jnp.float32),
        lax.psum(owned_term[cut_c:].astype(jnp.bfloat16), "dp").astype(jnp.float32),
    )
    return (
        hidden_out[None],
        grad_in,
        vector_sums[0],
        vector_sums[1],
        weight_grads[0],
        vector_sums[4],
        weight_grads[1],
        vector_sums[5],
        vector_sums[2],
        vector_sums[3],
        weight_grads[2],
        vector_sums[6],
        weight_grads[3],
        vector_sums[5],
    )


def solution(mesh):
    token = P("dp", "ctx", None)
    rows = P("ctx", None)
    return jax.shard_map(
        body if HEADS % mesh.shape["ctx"] == 0 else gather_body,
        mesh=mesh,
        in_specs=(
            token,
            token,
            P("dp", None),
            P("dp", None),
            P(),
            P(),
            rows,
            P(),
            rows,
            P(),
            P(),
            P(),
            rows,
            P(),
            rows,
            P(),
        ),
        out_specs=(
            token,
            token,
            P(),
            P(),
            rows,
            P(),
            rows,
            P(),
            P(),
            P(),
            rows,
            P(),
            rows,
            P(),
        ),
        check_vma=False,
    )
```

```python
import functools
import math

import jax
import jax.numpy as jnp
from jax import lax
from jax.experimental import pallas as pl
from jax.experimental.pallas import tpu as pltpu
from jax.sharding import PartitionSpec as P

D = 2048
HEADS = 16
HEAD_DIM = 128
ROT_DIM = 32
FF = 8192

norm_eps = 1e-05
masked_score = -1e30
f32 = jnp.float32
bf16 = jnp.bfloat16


def dot_nt(a, b):
    return lax.dot_general(a, b, (((1,), (1,)), ((), ())), preferred_element_type=f32)


def dot_nn(a, b):
    return lax.dot_general(a, b, (((1,), (0,)), ((), ())), preferred_element_type=f32)


def dot_tn(a, b):
    return lax.dot_general(a, b, (((0,), (0,)), ((), ())), preferred_element_type=f32)


MESH = pl.DeviceIdType.MESH
RAILS = 2


def place(group):
    dp = lax.axis_index("dp")
    ctx = lax.axis_index("ctx")
    return dp, ctx, ctx // RAILS, ctx % RAILS, group // RAILS


def copy_to(src, dst, send, recv, device):
    return pltpu.make_async_remote_copy(
        src_ref=src,
        dst_ref=dst,
        send_sem=send,
        recv_sem=recv,
        device_id=device,
        device_id_type=MESH,
    )


def signal(device):
    barrier = pltpu.get_barrier_semaphore()
    pl.semaphore_signal(barrier, inc=1, device_id=device, device_id_type=MESH)


def arrive(count):
    pl.semaphore_wait(pltpu.get_barrier_semaphore(), count)


def pair_order(z, depth):
    return [
        z,
        jnp.where(z > 0, z - 1, 1),
        jnp.where(z == depth - 1, 1, jnp.where(z == depth - 2, depth - 1, 2)),
        jnp.where(z < depth // 2, depth - 1, 0),
    ]


def layer_kernel(group, *refs):
    hidden, grad, w_up_in, w_down_in, w_qkv_in, w_out = refs[:6]
    norms, bias_up, bias_qkv, inverse, seg_len, seg_parent = refs[6:12]
    h_out, g_out, x_out, heads_out, part_out, back_out, pairs_out, cols_out = refs[12:20]
    tables, sums, bias_sum = refs[20:23]
    h_buf, g_buf, w_up, w_down, w_qkv, x_mlp, x_attn, act, slope, pre_grad = refs[23:33]
    heads, part, back, down_grad, up_grad, core_buf, mean, rstd = refs[33:41]
    own_sem, y_send, y_recv, up_send, up_recv, down_send, down_recv = refs[41:48]
    weight_sem, pair_sem, grad_sem, head_send, head_recv = refs[48:53]
    core_send, core_recv, cols_send, cols_recv = refs[53:57]
    dp, ctx, z, y, depth = place(group)
    bufs, sources, outs = (h_buf, g_buf), (hidden, grad), (h_out, g_out)
    rows = hidden.shape[0]
    pair_rows = RAILS * rows
    tokens, columns = h_buf.shape
    units = act.shape[1]
    head_cols = heads.shape[2]
    other = (dp, z * RAILS + 1 - y)
    above = (dp, jnp.minimum(z + 1, depth - 1) * RAILS + y)
    below = (dp, jnp.maximum(z - 1, 0) * RAILS + y)
    has_above, has_below = z < depth - 1, z > 0
    order = pair_order(z, depth)

    x, core = dp // 2, dp % 2
    sibling = (x * 2 + 1 - core, ctx)
    across = ((1 - x) * 2 + core, ctx)

    for n in range(1, group):
        signal((dp, lax.rem(ctx + n, group)))
    signal(sibling)
    signal(across)
    arrive(group + 1)

    def chunk(i, at_z, at_y):
        start = pl.multiple_of((at_z * RAILS + at_y) * rows, rows)
        return bufs[i].at[pl.ds(start, rows)]

    def to_other(i, at_z, source=None):
        here = chunk(i, at_z, y)
        return copy_to(
            here if source is None else source, here, y_send.at[i, at_z], y_recv.at[i, at_z], other
        )

    def upward(i, at_z, source=None):
        here = chunk(i, at_z, y)
        return copy_to(
            here if source is None else source,
            here,
            up_send.at[i, at_z],
            up_recv.at[i, at_z],
            above,
        )

    def downward(i, at_z, source=None):
        here = chunk(i, at_z, y)
        return copy_to(
            here if source is None else source,
            here,
            down_send.at[i, at_z],
            down_recv.at[i, at_z],
            below,
        )

    def relay(i, k):
        @pl.when(z >= k)
        def _():
            at_z = jnp.maximum(z - k, 0)
            upward(i, at_z).wait_recv()
            pl.when(has_above)(lambda: upward(i, at_z).start())

        @pl.when(z + k < depth)
        def _():
            at_z = jnp.minimum(z + k, depth - 1)
            downward(i, at_z).wait_recv()
            pl.when(has_below)(lambda: downward(i, at_z).start())

    def turn(n):
        if n < depth:
            relay(0, n)
            pl.when((z == n - 1) & has_above)(lambda: upward(1, z, sources[1]).start())
            pl.when((z == depth - n) & has_below)(lambda: downward(1, z, sources[1]).start())
            to_other(0, order[n]).start()
        else:
            if n < 2 * depth - 1:
                relay(1, n - depth + 1)
            if n == depth:
                to_other(1, z, sources[1]).start()
            else:
                to_other(1, order[n - depth]).start()

    def y_arrive(i, s):
        here = chunk(i, order[s], 1 - y)
        copy_to(
            here, here, y_send.at[i, order[s]], y_recv.at[i, order[s]], other
        ).wait_recv()

    def pair_at(s):
        return pl.ds(pl.multiple_of(order[s] * pair_rows, pair_rows), pair_rows)

    def keep(n, s, buf, out):
        at = pair_at(s)
        return pltpu.make_async_copy(buf.at[at], out.at[at], pair_sem.at[n, s])

    own = [pltpu.make_async_copy(sources[i], chunk(i, z, y), own_sem.at[i]) for i in range(2)]
    weights = [
        pltpu.make_async_copy(source, held, weight_sem.at[n])
        for n, (source, held) in enumerate(
            ((w_up_in, w_up), (w_qkv_in, w_qkv), (w_down_in, w_down))
        )
    ]
    own[0].start()
    to_other(0, z, sources[0]).start()
    pl.when(has_above)(lambda: upward(0, z, sources[0]).start())
    pl.when(has_below)(lambda: downward(0, z, sources[0]).start())
    for copy in weights:
        copy.start()
    own[1].start()

    starts, shifts = [], []
    at = jnp.int32(0)
    for n in range(seg_len.shape[1]):
        parent = seg_parent[0, n]
        grand = seg_parent[0, parent]
        before = jnp.where(parent != n, seg_len[0, parent], 0) + jnp.where(
            (grand != n) & (grand != parent), seg_len[0, grand], 0
        )
        starts.append(at)
        shifts.append(before - at)
        at = at + seg_len[0, n]

    turned_half = ROT_DIM // 2

    @pl.loop(0, tokens // rows)
    def _(n):
        at = pl.ds(pl.multiple_of(n * rows, rows), rows)
        token = n * rows + lax.broadcasted_iota(jnp.int32, (turned_half, rows), 1)
        position = token + shifts[0]
        for m in range(1, len(starts)):
            position = position + jnp.where(token >= starts[m], shifts[m] - shifts[m - 1], 0)
        angle = position.astype(f32) * inverse[...]
        cosine, sine = jnp.cos(angle), jnp.sin(angle)
        still = jnp.zeros((HEAD_DIM - ROT_DIM, rows), f32)
        none = jnp.zeros((turned_half, rows), f32)
        tables[0, at, :] = jnp.concatenate([cosine, cosine, still + 1.0], axis=0).T
        tables[1, at, :] = jnp.concatenate([-sine, none, still], axis=0).T
        tables[2, at, :] = jnp.concatenate([none, sine, still], axis=0).T

    sums[...] = jnp.zeros_like(sums)
    bias_sum[...] = jnp.zeros_like(bias_sum)

    def normalize(s):
        step = 32

        @pl.loop(0, pair_rows // step)
        def _(n):
            at = pl.ds(pl.multiple_of(order[s] * pair_rows + n * step, step), step)
            values = h_buf[at, :].astype(f32)
            average = jnp.mean(values, axis=1, keepdims=True)
            centred = values - average
            spread = lax.rsqrt(jnp.mean(centred * centred, axis=1, keepdims=True) + norm_eps)
            normed = centred * spread
            x_attn[at, :] = (normed * norms[0:1, :] + norms[1:2, :]).astype(bf16)
            x_mlp[at, :] = (normed * norms[2:3, :] + norms[3:4, :]).astype(bf16)
            mean[at, :] = average
            rstd[at, :] = spread
            lane = lax.broadcasted_iota(jnp.int32, (step, HEAD_DIM), 1)
            tables[3, at, :] = jnp.where(lane == 0, average, spread)

    wide = 512

    def feed(s):
        at = pair_at(s)

        @pl.loop(0, units // wide)
        def _(n):
            cols = pl.ds(pl.multiple_of(n * wide, wide), wide)
            pre = dot_nt(x_mlp[at, :], w_up[cols, :]) + bias_up[:, cols]
            normal_cdf = 0.5 * (1.0 + lax.erf(pre * math.sqrt(0.5)))
            act[at, cols] = (pre * normal_cdf).astype(bf16)
            slope[at, cols] = (
                normal_cdf + pre * jnp.exp(-0.5 * pre * pre) * (1.0 / math.sqrt(2.0 * math.pi))
            ).astype(slope.dtype)

    def project(s):
        at = pair_at(s)
        for j in range(3):
            block = pl.ds(j * head_cols, head_cols)
            raw = dot_nt(x_attn[at, :], w_qkv[block, :]) + bias_qkv[:, block]
            turns = lax.div(3 * ctx + j, group) < 2
            for m in range(head_cols // HEAD_DIM):
                one = raw[:, m * HEAD_DIM : (m + 1) * HEAD_DIM]
                turned = (
                    one * tables[0, at, :]
                    + pltpu.roll(one, HEAD_DIM - ROT_DIM // 2, 1) * tables[1, at, :]
                    + pltpu.roll(one, ROT_DIM // 2, 1) * tables[2, at, :]
                )
                heads[j, at, m * HEAD_DIM : (m + 1) * HEAD_DIM] = jnp.where(
                    turns, turned, one
                ).astype(bf16)

    def mix(s):
        at = pair_at(s)

        @pl.loop(0, columns // wide)
        def _(n):
            cols = pl.ds(pl.multiple_of(n * wide, wide), wide)
            part[at, cols] = dot_nn(act[at, :], w_down[:, cols]).astype(bf16)

    def back_feed(s):
        at = pair_at(s)

        @pl.loop(0, units // wide)
        def _(n):
            cols = pl.ds(pl.multiple_of(n * wide, wide), wide)
            rounded = (
                dot_nt(g_buf[at, :], w_down[cols, :]) * slope[at, cols].astype(f32)
            ).astype(bf16)
            pre_grad[at, cols] = rounded
            bias_sum[:, cols] += jnp.sum(rounded.astype(f32), axis=0, keepdims=True)

        @pl.loop(0, columns // wide)
        def _(n):
            cols = pl.ds(pl.multiple_of(n * wide, wide), wide)
            entry = dot_nn(pre_grad[at, :], w_up[:, cols])
            normed = (h_buf[at, cols].astype(f32) - mean[at, :]) * rstd[at, :]
            sums[0:1, cols] += jnp.sum(entry * normed, axis=0, keepdims=True)
            sums[1:2, cols] += jnp.sum(entry, axis=0, keepdims=True)
            back[at, cols] = (entry * norms[2:3, cols]).astype(bf16)

    def forward(s):
        keep(0, s, h_buf, h_out).start()
        normalize(s)
        keep(1, s, x_attn, x_out).start()
        if s == 0:
            weights[0].wait()
        feed(s)
        if s == 0:
            weights[1].wait()
        project(s)

    def backward(s):
        keep(2, s, g_buf, g_out).start()
        if s == 0:
            weights[2].wait()
        mix(s)
        keep(3, s, part, part_out).start()
        back_feed(s)
        keep(4, s, back, back_out).start()

    tall = 256
    half = core_buf.shape[1]
    tiles = units // tall
    held = (down_grad, up_grad)

    def grad_half(t, which):
        start = pl.multiple_of((t % tiles) * tall + which * half, half)
        return held[t // tiles].at[pl.ds(start, half)]

    def to_core(t):
        return copy_to(
            grad_half(t, 1 - core), core_buf.at[t], core_send.at[t], core_recv.at[t], sibling
        )

    def grad_keep(t):
        return pltpu.make_async_copy(
            grad_half(t, core), pairs_out.at[pl.ds(t * half, half)], grad_sem.at[t]
        )

    def outer(n, left, right):
        for m in range(tiles):
            mine = pl.ds(m * tall, tall)

            @pl.loop(0, columns // (2 * wide))
            def _(k):
                cols = pl.ds(pl.multiple_of(k * 2 * wide, 2 * wide), 2 * wide)
                held[n][mine, cols] = dot_tn(left[:, mine], right[:, cols]).astype(bf16)

            to_core(n * tiles + m).start()

    def outer_sum(n):
        for t in range(n * tiles, (n + 1) * tiles):
            to_core(t).wait_recv()
            mine = grad_half(t, core)

            @pl.loop(0, half // 32)
            def _(k):
                at = pl.ds(pl.multiple_of(k * 32, 32), 32)
                mine[at, :] = (mine[at, :].astype(f32) + core_buf[t, at, :].astype(f32)).astype(
                    bf16
                )

            grad_keep(t).start()

    share = cols_out.shape[2]

    def to_columns(n):
        owner = lax.rem(ctx + n, group)
        block = w_out.at[
            pl.ds(pl.multiple_of(dp * share, share), share),
            pl.ds(pl.multiple_of(owner * head_cols, head_cols), head_cols),
        ]
        if n == 0:
            return pltpu.make_async_copy(block, cols_out.at[ctx, dp], cols_send.at[0])
        return copy_to(
            block, cols_out.at[ctx, dp], cols_send.at[n], cols_recv.at[n], (dp, owner)
        )

    def columns_arrive():
        to_columns(0).wait()
        for n in range(1, group):
            source = lax.rem(ctx + group - n, group)
            here = cols_out.at[source, dp]
            copy_to(here, here, cols_send.at[n], cols_recv.at[n], other).wait_recv()

    def columns_core(which):
        here = cols_out.at[:, pl.ds(2 * x + which, 1)]
        return copy_to(here, here, cols_send.at[group], cols_recv.at[group], sibling)

    def columns_x(which):
        here = cols_out.at[:, pl.ds(2 * which, 2)]
        return copy_to(here, here, cols_send.at[group + 1], cols_recv.at[group + 1], across)

    def to_head(j):
        target = lax.rem(3 * ctx + j, group)
        remote = copy_to(
            heads.at[j], heads_out.at[j], head_send.at[j], head_recv.at[j], (dp, target)
        )
        local = pltpu.make_async_copy(heads.at[j], heads_out.at[j], head_recv.at[j])
        return target == ctx, remote, local

    for n in range(group):
        to_columns(n).start()
    turn(1)
    own[0].wait()
    y_arrive(0, 0)
    forward(0)
    turn(2)
    y_arrive(0, 1)
    forward(1)
    turn(3)
    y_arrive(0, 2)
    forward(2)
    turn(4)
    y_arrive(0, 3)
    forward(3)
    turn(5)
    own[1].wait()
    y_arrive(1, 0)
    backward(0)
    turn(6)
    y_arrive(1, 1)
    backward(1)
    turn(7)
    for j in range(3):
        here, remote, local = to_head(j)
        pl.when(here)(lambda local=local: local.start())
        pl.when(jnp.logical_not(here))(lambda remote=remote: remote.start())
    columns_arrive()
    columns_core(core).start()
    y_arrive(1, 2)
    backward(2)
    columns_core(1 - core).wait_recv()
    columns_x(x).start()
    y_arrive(1, 3)
    backward(3)
    outer(0, act, g_buf)
    outer(1, pre_grad, x_mlp)
    outer_sum(0)
    outer_sum(1)

    for at_z in range(depth):
        to_other(0, at_z).wait_send()
        to_other(1, at_z).wait_send()
        for i in range(2):
            pl.when(has_above & (at_z <= z))(lambda i=i: upward(i, at_z).wait_send())
            pl.when(has_below & (at_z >= z))(lambda i=i: downward(i, at_z).wait_send())
    for j in range(3):
        here, remote, local = to_head(j)
        pl.when(here)(lambda local=local: local.wait())
        pl.when(jnp.logical_not(here))(lambda remote=remote: remote.wait_send())
        source = lax.rem(pow(3, -1, group) * (ctx + group - j), group)
        pl.when(source != ctx)(lambda remote=remote: remote.wait_recv())
    for s in range(4):
        keep(0, s, h_buf, h_out).wait()
        keep(1, s, x_attn, x_out).wait()
        keep(2, s, g_buf, g_out).wait()
        keep(3, s, part, part_out).wait()
        keep(4, s, back, back_out).wait()
    for t in range(2 * tiles):
        to_core(t).wait_send()
        grad_keep(t).wait()
    for n in range(1, group):
        to_columns(n).wait_send()
    columns_core(core).wait_send()
    columns_x(x).wait_send()
    columns_x(1 - x).wait_recv()


def layer_pass(
    group, hidden, grad, w_up, w_down, w_qkv, w_out, norms, bias_up, bias_qkv, seg_len, seg_parent
):
    rows, columns = hidden.shape
    tokens, units, head_cols = group * rows, w_up.shape[0], w_qkv.shape[0] // 3
    depth = group // RAILS
    inverse = jnp.power(10000.0, -2.0 * jnp.arange(ROT_DIM // 2, dtype=f32) / ROT_DIM)
    inverse = jnp.broadcast_to(inverse[:, None], (ROT_DIM // 2, rows))
    sems = pltpu.SemaphoreType.DMA
    shape = jax.ShapeDtypeStruct
    anywhere = pl.BlockSpec(memory_space=pl.ANY)
    vmem = pl.BlockSpec(memory_space=pltpu.VMEM)
    smem = pl.BlockSpec(memory_space=pltpu.SMEM)
    whole = shape((tokens, columns), bf16)
    half = 128
    copies = lax.axis_size("dp")
    return pl.pallas_call(
        functools.partial(layer_kernel, group),
        out_shape=(
            whole,
            whole,
            whole,
            shape((3, tokens, head_cols), bf16),
            whole,
            whole,
            shape((units, columns), bf16),
            shape((group, copies, columns // group // copies, head_cols), bf16),
            shape((4, tokens, HEAD_DIM), f32),
            shape((2, columns), f32),
            shape((1, units), f32),
        ),
        in_specs=[anywhere] * 6 + [vmem] * 4 + [smem] * 2,
        out_specs=[anywhere] * 8 + [vmem] * 3,
        scratch_shapes=[pltpu.VMEM((tokens, columns), bf16)] * 2
        + [pltpu.VMEM((units, columns), bf16)] * 2
        + [pltpu.VMEM((3 * head_cols, columns), bf16)]
        + [pltpu.VMEM((tokens, columns), bf16)] * 2
        + [pltpu.VMEM((tokens, units), bf16)] * 3
        + [pltpu.VMEM((3, tokens, head_cols), bf16)]
        + [pltpu.VMEM((tokens, columns), bf16)] * 2
        + [pltpu.VMEM((units, columns), bf16)] * 2
        + [pltpu.VMEM((units // half, half, columns), bf16)]
        + [pltpu.VMEM((tokens, 1), f32)] * 2
        + [sems((2,))]
        + [sems((2, depth))] * 6
        + [sems((3,)), sems((5, 4)), sems((units // half,)), sems((3,)), sems((3,))]
        + [sems((units // half,))] * 2
        + [sems((group + 2,))] * 2,
        compiler_params=pltpu.CompilerParams(
            collective_id=0, has_side_effects=True, vmem_limit_bytes=61 * 2**20
        ),
        name="layer_pass",
    )(hidden, grad, w_up, w_down, w_qkv, w_out, norms, bias_up, bias_qkv, inverse, seg_len, seg_parent)


def tail_kernel(group, *refs):
    pairs, arrived_in, grad_in, w_cols_in, part_in, back_in, x_in, w_qkv_in, hidden_in = refs[:9]
    tables_in, norms, mlp_sums, up_sums, local_sums, seg_len, seg_parent = refs[9:16]
    part_out, back_out, down_out, up_out, out_out, qkv_out, vectors_out = refs[16:23]
    refs = refs[23:]
    arrived, g_buf, w_cols, part, back, x_buf, w_qkv, h_buf, tables = refs[:9]
    att_grad, attended, returns, returned, y_buf, z_buf = refs[9:15]
    out_grad, qkv_grad, qkv_core, out_core, out_rows, from_x, pairs_x, key_acc, value_acc = refs[15:24]
    sums, vec_buf = refs[24:26]
    (
        load_sem,
        y_send,
        y_recv,
        up_send,
        up_recv,
        down_send,
        down_recv,
        result_sem,
        head_send,
        head_recv,
        pair_send,
        pair_recv,
        core_send,
        core_recv,
        block_send,
        block_recv,
        x_send,
        x_recv,
        keep_sem,
        done_send,
        done_recv,
        vec_send,
        vec_recv,
        sum_sem,
    ) = refs[26:]
    dp, ctx, z, y, depth = place(group)
    tokens, columns = g_buf.shape
    rows = tokens // group
    head_cols = attended.shape[1]
    heads = head_cols // HEAD_DIM
    half = qkv_core.shape[1]
    pair_tiles = pairs_x.shape[0]
    x, core = dp // 2, dp % 2
    other = (dp, z * RAILS + 1 - y)
    above = (dp, jnp.minimum(z + 1, depth - 1) * RAILS + y)
    below = (dp, jnp.maximum(z - 1, 0) * RAILS + y)
    sibling = (x * 2 + 1 - core, ctx)
    across = ((1 - x) * 2 + core, ctx)
    near = (dp, (z + 1 - 2 * (z % 2)) * RAILS + y)
    far = (dp, lax.rem(z + 2, depth) * RAILS + y)
    has_above, has_below = z < depth - 1, z > 0

    for n in range(1, group):
        signal((dp, lax.rem(ctx + n, group)))
    signal(sibling)
    signal(across)
    arrive(group + 1)

    def add(target, left, right):
        step = 32

        @pl.loop(0, target.shape[0] // step)
        def _(n):
            at = pl.ds(pl.multiple_of(n * step, step), step)
            target[at, :] = (left[at, :].astype(f32) + right[at, :].astype(f32)).astype(
                target.dtype
            )

    def pair_x(t):
        return copy_to(
            pairs.at[pl.ds(t * half, half)],
            pairs_x.at[t],
            pair_send.at[t],
            pair_recv.at[t],
            across,
        )

    for t in range(pair_tiles):
        pair_x(t).start()
    loads = [
        pltpu.make_async_copy(source, held, load_sem.at[n])
        for n, (source, held) in enumerate(
            (
                (w_cols_in, w_cols),
                (grad_in, g_buf),
                (arrived_in, arrived),
                (tables_in, tables),
                (part_in, part),
                (w_qkv_in, w_qkv),
                (back_in, back),
                (hidden_in, h_buf),
                (x_in, x_buf),
            )
        )
    ]
    for copy in loads:
        copy.start()

    wide = 512
    tall = 256
    scale = 1.0 / math.sqrt(HEAD_DIM)
    loads[0].wait()
    loads[1].wait()

    @pl.loop(0, tokens // tall)
    def _(n):
        at = pl.ds(pl.multiple_of(n * tall, tall), tall)
        att_grad[at, :] = dot_nn(g_buf[at, :], w_cols[...]).astype(bf16)

    starts, reaches = [], []
    at = jnp.int32(0)
    for n in range(seg_len.shape[1]):
        parent = seg_parent[0, n]
        grand = seg_parent[0, parent]
        starts.append(at)
        reaches.append(
            (jnp.int32(1) << n) | (jnp.int32(1) << parent) | (jnp.int32(1) << grand)
        )
        at = at + seg_len[0, n]
    loads[2].wait()
    loads[3].wait()
    slots = [lax.rem(kind * group + ctx, 3) for kind in range(3)]

    def unturn(values, at):
        return (
            values * tables[0, at, :]
            - pltpu.roll(values, HEAD_DIM - ROT_DIM // 2, 1) * tables[1, at, :]
            - pltpu.roll(values, ROT_DIM // 2, 1) * tables[2, at, :]
        )

    for m in range(heads):
        lanes = slice(m * HEAD_DIM, (m + 1) * HEAD_DIM)
        key_acc[...] = jnp.zeros_like(key_acc)
        value_acc[...] = jnp.zeros_like(value_acc)
        for n in range(tokens // tall):
            mine = pl.ds(n * tall, tall)
            seen = (n + 1) * tall
            upto = pl.ds(0, seen)
            token = n * tall + lax.broadcasted_iota(jnp.int32, (tall, 1), 0)
            key = lax.broadcasted_iota(jnp.int32, (1, seen), 1)
            reach = jnp.zeros((tall, 1), jnp.int32) + reaches[0]
            label = jnp.ones((1, seen), jnp.int32)
            for k in range(1, len(starts)):
                reach = jnp.where(token >= starts[k], reaches[k], reach)
                label = jnp.where(key >= starts[k], 1 << k, label)
            allowed = ((reach & label) != 0) & (key <= token)
            query = arrived[slots[0], mine, lanes]
            keys = arrived[slots[1], upto, lanes]
            values = arrived[slots[2], upto, lanes]
            out_grad_rows = att_grad[mine, lanes]
            scores = jnp.where(allowed, dot_nt(query, keys) * scale, masked_score)
            expo = jnp.exp(scores - jnp.max(scores, axis=1, keepdims=True))
            probs = expo * (1.0 / jnp.sum(expo, axis=1, keepdims=True))
            weights = probs.astype(bf16)
            attended[mine, lanes] = dot_nn(weights, values).astype(bf16)
            prob_grad = dot_nt(out_grad_rows, values)
            delta = jnp.sum(probs * prob_grad, axis=1, keepdims=True)
            score_grad = (probs * (prob_grad - delta)).astype(bf16)
            query_grad = dot_nn(score_grad, keys) * scale
            returns[slots[0], mine, lanes] = unturn(query_grad, mine).astype(bf16)
            key_acc[upto, :] += dot_tn(score_grad, query)
            value_acc[upto, :] += dot_tn(weights, out_grad_rows)

        for n in range(tokens // tall):
            mine = pl.ds(n * tall, tall)
            returns[slots[1], mine, lanes] = unturn(key_acc[mine, :] * scale, mine).astype(bf16)
            returns[slots[2], mine, lanes] = value_acc[mine, :].astype(bf16)

    back_step = pow(3, -1, group)

    def to_owner(j):
        owner = lax.rem(back_step * (ctx + group - j), group)
        remote = copy_to(
            returns.at[j], returned.at[j], head_send.at[j], head_recv.at[j], (dp, owner)
        )
        local = pltpu.make_async_copy(returns.at[j], returned.at[j], head_recv.at[j])
        return owner == ctx, remote, local

    for j in range(3):
        here, remote, local = to_owner(j)
        pl.when(here)(lambda local=local: local.start())
        pl.when(jnp.logical_not(here))(lambda remote=remote: remote.start())

    @pl.loop(0, group)
    def _(n):
        at = pl.ds(pl.multiple_of(n * head_cols, head_cols), head_cols)
        out_grad[n] = dot_tn(g_buf[:, at], attended[...]).astype(bf16)

    core_tiles = qkv_core.shape[0]
    out_to_core = copy_to(
        out_grad.at[:, pl.ds((1 - core) * half, half)],
        out_core,
        core_send.at[core_tiles],
        core_recv.at[core_tiles],
        sibling,
    )
    out_to_core.start()

    loads[4].wait()

    @pl.loop(0, tokens // tall)
    def _(n):
        at = pl.ds(pl.multiple_of(n * tall, tall), tall)

        @pl.loop(0, columns // wide)
        def _(m):
            cols = pl.ds(pl.multiple_of(m * wide, wide), wide)
            part[at, cols] = (
                part[at, cols].astype(f32) + dot_nt(attended[at, :], w_cols[cols, :])
            ).astype(bf16)

    out_to_core.wait_recv()

    @pl.loop(0, group)
    def _(n):
        out_core[n] = (
            out_core[n].astype(f32)
            + out_grad[n, pl.ds(pl.multiple_of(core * half, half), half), :].astype(f32)
        ).astype(bf16)

    my_cols = pl.ds(pl.multiple_of(ctx * head_cols, head_cols), head_cols)

    def out_block(n):
        owner = lax.rem(ctx + n, group)
        return copy_to(
            out_core.at[owner],
            out_rows.at[:, my_cols],
            block_send.at[n],
            block_recv.at[n],
            (dp, owner),
        )

    for n in range(1, group):
        out_block(n).start()
    own_block = pltpu.make_async_copy(out_core.at[ctx], out_rows.at[:, my_cols], block_send.at[0])
    own_block.start()

    low = z < depth // 2
    order = [
        jnp.where(low, depth - 1, 0),
        jnp.where(low, depth - 2, 1),
        jnp.where(low, 1 - z, 2 * depth - 3 - z),
        z,
    ]
    parts = (part, back)

    def chunk(i, at_z, at_y):
        return parts[i].at[pl.ds(pl.multiple_of((at_z * RAILS + at_y) * rows, rows), rows)]

    def swap(i, s):
        return copy_to(
            chunk(i, order[s], 1 - y),
            y_buf.at[i, order[s]],
            y_send.at[i, s],
            y_recv.at[i, s],
            other,
        )

    def upward(i, at):
        return copy_to(
            chunk(i, at, y), z_buf.at[i, at], up_send.at[i, at], up_recv.at[i, at], above
        )

    def downward(i, at, slot):
        return copy_to(
            chunk(i, at, y), z_buf.at[i, slot], down_send.at[i, at], down_recv.at[i, at], below
        )

    def down_slot(at, owner_z):
        return jnp.where(at == owner_z, depth, at)

    def scatter_step(i, s):
        at = order[s]
        swap(i, s).wait_recv()
        mine = chunk(i, at, y)
        add(mine, mine, y_buf.at[i, at])

        @pl.when((at >= z) & has_below)
        def _():
            upward(i, at).wait_recv()
            add(mine, mine, z_buf.at[i, at])

        @pl.when((at <= z) & has_above)
        def _():
            slot = down_slot(at, z)
            downward(i, at, slot).wait_recv()
            add(mine, mine, z_buf.at[i, slot])

        pl.when(at > z)(lambda: upward(i, at).start())
        pl.when(at < z)(lambda: downward(i, at, down_slot(at, z - 1)).start())

    results = (part_out, back_out)

    def scatter_out(i):
        return pltpu.make_async_copy(chunk(i, z, y), results[i], result_sem.at[i])

    for s in range(depth):
        swap(0, s).start()

    for j in range(3):
        here, remote, local = to_owner(j)
        pl.when(here)(lambda local=local: local.wait())
        target = lax.rem(3 * ctx + j, group)
        pl.when(target != ctx)(lambda remote=remote: remote.wait_recv())
    for n in (5, 6, 7):
        loads[n].wait()
    sums[...] = jnp.zeros_like(sums)

    @pl.loop(0, tokens // tall)
    def _(n):
        at = pl.ds(pl.multiple_of(n * tall, tall), tall)

        @pl.loop(0, columns // wide)
        def _(m):
            cols = pl.ds(pl.multiple_of(m * wide, wide), wide)
            entry = dot_nn(returned[0, at, :], w_qkv[0:head_cols, cols])
            for j in range(1, 3):
                entry += dot_nn(
                    returned[j, at, :], w_qkv[j * head_cols : (j + 1) * head_cols, cols]
                )
            normed = (h_buf[at, cols].astype(f32) - tables[3, at, 0:1]) * tables[3, at, 1:2]
            sums[0:1, cols] += jnp.sum(entry * normed, axis=0, keepdims=True)
            sums[1:2, cols] += jnp.sum(entry, axis=0, keepdims=True)
            back[at, cols] = (back[at, cols].astype(f32) + entry * norms[0:1, cols]).astype(bf16)

    stages = (sibling, other, near, far, across)

    def exchange(n):
        return copy_to(
            vec_buf.at[2 * n], vec_buf.at[2 * n + 1], vec_send.at[n], vec_recv.at[n], stages[n]
        )

    lane_cols = vec_buf.shape[2]

    def place_vector(at, values):
        for n in range(values.shape[1] // lane_cols):
            vec_buf[0, pl.ds(at + n, 1), :] = values[:, n * lane_cols : (n + 1) * lane_cols]

    vec_buf[0] = jnp.zeros(vec_buf.shape[1:], f32)
    long = columns // lane_cols
    place_vector(0, sums[0:1, :])
    place_vector(long, sums[1:2, :])
    place_vector(2 * long, mlp_sums[0:1, :])
    place_vector(3 * long, mlp_sums[1:2, :])
    place_vector(4 * long, local_sums[...])
    each = head_cols // lane_cols
    for j in range(3):
        place_vector(
            5 * long + (3 * ctx + j) * each,
            jnp.sum(returned[j].astype(f32), axis=0, keepdims=True),
        )
    place_vector(
        5 * long + 3 * group * each + ctx * (up_sums.shape[1] // lane_cols), up_sums[...]
    )
    exchange(0).start()

    def vector_step(n):
        exchange(n).wait_recv()
        total = vec_buf[2 * n] + vec_buf[2 * n + 1]
        if n + 1 < len(stages):
            vec_buf[2 * n + 2] = total
            exchange(n + 1).start()
        else:
            vectors_out[...] = total

    vector_step(0)
    for s in range(depth):
        swap(1, s).start()

    loads[8].wait()

    def qkv_half(t, which):
        start = pl.multiple_of(t * 2 * half + which * half, half)
        return qkv_grad.at[pl.ds(start, half)]

    def to_core(t):
        return copy_to(
            qkv_half(t, 1 - core), qkv_core.at[t], core_send.at[t], core_recv.at[t], sibling
        )

    for t in range(core_tiles):

        @pl.loop(0, columns // (2 * wide))
        def _(m):
            cols = pl.ds(pl.multiple_of(m * 2 * wide, 2 * wide), 2 * wide)
            qkv_grad[pl.ds(t * 2 * half, 2 * half), cols] = dot_tn(
                returned[t], x_buf[:, cols]
            ).astype(bf16)

        to_core(t).start()

    def across_x(t):
        source = qkv_half(t, core) if t < core_tiles else out_rows
        return copy_to(source, from_x.at[t], x_send.at[t], x_recv.at[t], across)

    spots = (
        [(down_out, 2 * half * t) for t in range(pair_tiles // 2)]
        + [(up_out, 2 * half * t) for t in range(pair_tiles // 2)]
        + [(qkv_out, 2 * half * t) for t in range(core_tiles)]
        + [(out_out, 0)]
    )
    again = pltpu.make_async_copy(pairs, g_buf, sum_sem.at[0])
    again.start()

    def total_of(t):
        return pairs_x.at[t] if t < pair_tiles else from_x.at[t - pair_tiles]

    def spot(t, which):
        array, first = spots[t]
        return array.at[pl.ds(pl.multiple_of(first + which * half, half), half)]

    def keep(t):
        return pltpu.make_async_copy(total_of(t), spot(t, core), keep_sem.at[t])

    def finish(t, which):
        return copy_to(total_of(t), spot(t, which), done_send.at[t], done_recv.at[t], sibling)

    def x_sum(t):
        total = total_of(t)
        if t < pair_tiles:
            pair_x(t).wait_recv()
            add(total, total, g_buf.at[pl.ds(t * half, half)])
        else:
            n = t - pair_tiles
            across_x(n).wait_recv()
            add(total, total, qkv_half(n, core) if n < core_tiles else out_rows)
        keep(t).start()
        finish(t, core).start()

    for t in range(core_tiles):
        to_core(t).wait_recv()
        mine = qkv_half(t, core)
        add(mine, mine, qkv_core.at[t])
        across_x(t).start()
    own_block.wait()
    for n in range(1, group):
        source = lax.rem(ctx + group - n, group)
        theirs = pl.ds(pl.multiple_of(source * head_cols, head_cols), head_cols)
        copy_to(
            out_core.at[ctx], out_rows.at[:, theirs], block_send.at[n], block_recv.at[n], other
        ).wait_recv()
    again.wait()
    for s in range(depth):
        scatter_step(0, s)
        x_sum(2 * s)
        x_sum(2 * s + 1)
    scatter_out(0).start()
    vector_step(1)
    for s in range(depth):
        scatter_step(1, s)
        if s < 2:
            vector_step(s + 2)
        if s == 1:
            across_x(core_tiles).start()
        x_sum(pair_tiles + s)
    vector_step(4)
    scatter_out(1).start()

    for j in range(3):
        here, remote, local = to_owner(j)
        pl.when(jnp.logical_not(here))(lambda remote=remote: remote.wait_send())
    for n in range(1, group):
        out_block(n).wait_send()
    out_to_core.wait_send()
    for t in range(core_tiles):
        to_core(t).wait_send()
    for t in range(core_tiles + 1):
        across_x(t).wait_send()
    for t in range(pair_tiles):
        pair_x(t).wait_send()
    for t in range(len(spots)):
        keep(t).wait()
        finish(t, core).wait_send()
        finish(t, 1 - core).wait_recv()
    for n in range(len(stages)):
        exchange(n).wait_send()
    for i in range(2):
        scatter_out(i).wait()
        for s in range(depth):
            swap(i, s).wait_send()
            at = order[s]
            pl.when(at > z)(lambda i=i, at=at: upward(i, at).wait_send())
            pl.when(at < z)(
                lambda i=i, at=at: downward(i, at, down_slot(at, z - 1)).wait_send()
            )


def tail_pass(
    group,
    pairs,
    arrived,
    grad_all,
    w_cols,
    part,
    back,
    x_attn,
    w_qkv,
    hidden_all,
    tables,
    norms,
    mlp_sums,
    up_sums,
    local_sums,
    seg_len,
    seg_parent,
):
    tokens, columns = hidden_all.shape
    depth = group // RAILS
    rows = tokens // group
    head_cols = arrived.shape[2]
    units = up_sums.shape[1]
    half = 128
    pair_tiles = pairs.shape[0] // half
    core_tiles = w_qkv.shape[0] // (2 * half)
    lane_cols = 256
    vectors = (5 * columns + 3 * columns + group * units) // lane_cols
    sems = pltpu.SemaphoreType.DMA
    shape = jax.ShapeDtypeStruct
    vmem = pltpu.VMEM
    anywhere = pl.BlockSpec(memory_space=pl.ANY)
    small = pl.BlockSpec(memory_space=pltpu.VMEM)
    smem = pl.BlockSpec(memory_space=pltpu.SMEM)
    whole = vmem((tokens, columns), bf16)
    every = pair_tiles + core_tiles + 1
    return pl.pallas_call(
        functools.partial(tail_kernel, group),
        out_shape=(
            shape((rows, columns), bf16),
            shape((rows, columns), bf16),
            shape((units, columns), bf16),
            shape((units, columns), bf16),
            shape((2 * half, columns), bf16),
            shape(w_qkv.shape, bf16),
            shape((vectors, lane_cols), f32),
        ),
        in_specs=[anywhere] * 10 + [small] * 4 + [smem] * 2,
        out_specs=[anywhere] * 6 + [small],
        scratch_shapes=[
            vmem(arrived.shape, bf16),
            whole,
            vmem(w_cols.shape, bf16),
            whole,
            whole,
            whole,
            vmem(w_qkv.shape, bf16),
            whole,
            vmem(tables.shape, f32),
            vmem((tokens, head_cols), bf16),
            vmem((tokens, head_cols), bf16),
            vmem(arrived.shape, bf16),
            vmem(arrived.shape, bf16),
            vmem((2, depth, rows, columns), bf16),
            vmem((2, depth + 1, rows, columns), bf16),
            vmem((group, 2 * half, head_cols), bf16),
            vmem(w_qkv.shape, bf16),
            vmem((core_tiles, half, columns), bf16),
            vmem((group, half, head_cols), bf16),
            vmem((half, columns), bf16),
            vmem((core_tiles + 1, half, columns), bf16),
            vmem((pair_tiles, half, columns), bf16),
            vmem((tokens, HEAD_DIM), f32),
            vmem((tokens, HEAD_DIM), f32),
            vmem((2, columns), f32),
            vmem((10, vectors, lane_cols), f32),
            sems((9,)),
        ]
        + [sems((2, depth))] * 6
        + [sems((2,)), sems((3,)), sems((3,)), sems((pair_tiles,)), sems((pair_tiles,))]
        + [sems((core_tiles + 1,))] * 2
        + [sems((group,))] * 2
        + [sems((core_tiles + 1,))] * 2
        + [sems((every,))] * 3
        + [sems((5,))] * 2
        + [sems((1,))],
        compiler_params=pltpu.CompilerParams(
            collective_id=1, has_side_effects=True, vmem_limit_bytes=61 * 2**20
        ),
        name="tail_pass",
    )(
        pairs,
        arrived,
        grad_all,
        w_cols,
        part,
        back,
        x_attn,
        w_qkv,
        hidden_all,
        tables,
        norms,
        mlp_sums,
        up_sums,
        local_sums,
        seg_len,
        seg_parent,
    )


def body(
    hidden_in,
    grad_out,
    seg_len,
    seg_parent,
    gain_attn,
    shift_attn,
    w_qkv,
    bias_qkv,
    w_out,
    bias_out,
    gain_mlp,
    shift_mlp,
    w_up,
    bias_up,
    w_down,
    bias_down,
):
    group = lax.axis_size("ctx")
    me = lax.axis_index("ctx")
    local_rows = hidden_in.shape[1]
    tokens = local_rows * group
    head_count = HEADS // group
    head_cols = head_count * HEAD_DIM
    norms = jnp.stack([gain_attn, shift_attn, gain_mlp, shift_mlp]).astype(f32)
    up_bias = lax.dynamic_slice_in_dim(bias_up, me * w_up.shape[0], w_up.shape[0])
    qkv_bias = lax.dynamic_slice_in_dim(bias_qkv, me * 3 * head_cols, 3 * head_cols)
    (
        hidden_all,
        grad_all,
        x_attn,
        arrived,
        mlp_part,
        mlp_back,
        pairs,
        w_cols,
        tables,
        mlp_sums,
        up_sums,
    ) = layer_pass(
        group,
        hidden_in[0],
        grad_out[0],
        w_up,
        w_down,
        w_qkv,
        w_out,
        norms,
        up_bias.astype(f32)[None],
        qkv_bias.astype(f32)[None],
        seg_len,
        seg_parent,
    )
    grad_f = grad_out[0].astype(f32)
    summed, w_sum, down_grad, up_grad, out_grad, qkv_grad, vectors = tail_pass(
        group,
        pairs,
        arrived,
        grad_all,
        w_cols.reshape(D, head_cols),
        mlp_part,
        mlp_back,
        x_attn,
        w_qkv,
        hidden_all,
        tables,
        norms,
        mlp_sums,
        up_sums,
        jnp.sum(grad_f, axis=0)[None],
        seg_len,
        seg_parent,
    )
    vectors = vectors.reshape(-1)
    w_sum = w_sum.astype(f32)
    hidden_out = (
        hidden_in[0].astype(f32) + summed.astype(f32) + bias_out.astype(f32) + bias_down.astype(f32)
    ).astype(bf16)
    mine = lax.dynamic_slice_in_dim(tables[3], me * local_rows, local_rows)
    my_rstd = mine[:, 1:2]
    my_normed = (hidden_in[0].astype(f32) - mine[:, :1]) * my_rstd
    grad_in = (
        grad_f
        + (
            w_sum
            - jnp.mean(w_sum, axis=-1, keepdims=True)
            - my_normed * jnp.mean(w_sum * my_normed, axis=-1, keepdims=True)
        )
        * my_rstd
    )

    cuts = [D, D, D, D, D, 3 * D, FF]
    ends = [sum(cuts[: i + 1]) for i in range(len(cuts))]
    (
        gain_grad_a,
        shift_grad_a,
        gain_grad_m,
        shift_grad_m,
        out_bias_grad,
        qkv_bias_grad,
        up_bias_grad,
    ) = [vectors[end - cut : end] for cut, end in zip(cuts, ends)]
    return (
        hidden_out[None],
        grad_in[None],
        gain_grad_a,
        shift_grad_a,
        qkv_grad.astype(f32),
        qkv_bias_grad,
        out_grad.astype(f32),
        out_bias_grad,
        gain_grad_m,
        shift_grad_m,
        up_grad.astype(f32),
        up_bias_grad,
        down_grad.astype(f32),
        out_bias_grad,
    )


block_limit = 512


def tree_tables(seg_len, seg_parent):
    seg_count = seg_len.shape[0]
    labels = jnp.arange(seg_count, dtype=jnp.int32)
    earlier = labels[:, None] > labels[None, :]
    seg_starts = jnp.sum(jnp.where(earlier, seg_len[None, :], 0), axis=1)
    seg_ends = seg_starts + seg_len
    parent_hit = seg_parent[:, None] == labels[None, :]
    grand_parent = jnp.sum(jnp.where(parent_hit, seg_parent[None, :], 0), axis=1)
    itself = labels[:, None] == labels[None, :]
    ancestor = itself | parent_hit | (grand_parent[:, None] == labels[None, :])
    path_start = jnp.sum(jnp.where(ancestor & jnp.logical_not(itself), seg_len[None, :], 0), axis=1)
    return (seg_ends, seg_starts, ancestor, path_start)


def rotary_tables(path_pos):
    half_dim = ROT_DIM // 2
    inverse = jnp.power(10000.0, -2.0 * jnp.arange(half_dim, dtype=jnp.float32) / ROT_DIM)
    angles = path_pos.astype(jnp.float32)[:, None] * inverse[None, :]
    angles = jnp.concatenate([angles, angles], axis=1)
    return (jnp.cos(angles), jnp.sin(angles))


def rotate(head_values, cosine, sine):
    half_dim = ROT_DIM // 2
    turned = head_values[..., :ROT_DIM]
    swapped = jnp.concatenate([-turned[..., half_dim:], turned[..., :half_dim]], axis=-1)
    mixed = turned * cosine[:, None, :] + swapped * sine[:, None, :]
    return jnp.concatenate([mixed, head_values[..., ROT_DIM:]], axis=-1)


def gelu_slope(pre_act):
    normal_cdf = 0.5 * (1.0 + lax.erf(pre_act / math.sqrt(2.0)))
    return normal_cdf + pre_act * jnp.exp(-0.5 * pre_act * pre_act) / math.sqrt(2.0 * math.pi)


def layer_norm(values, gain_vec, shift_vec):
    average = jnp.mean(values, axis=-1, keepdims=True)
    centred = values - average
    spread = jnp.mean(centred * centred, axis=-1, keepdims=True)
    return centred * lax.rsqrt(spread + norm_eps) * gain_vec + shift_vec


def segment_hot(row_ids, seg_ends):
    seg_index = jnp.sum((row_ids[:, None] >= seg_ends[None, :]).astype(jnp.int32), axis=1)
    labels = jnp.arange(seg_ends.shape[0], dtype=jnp.int32)
    return (seg_index[:, None] == labels[None, :]).astype(jnp.float32)


def row_lookup(row_ids, seg_ends, ancestor_f):
    row_hot = segment_hot(row_ids, seg_ends)
    return (row_hot, jnp.dot(row_hot, ancestor_f))


def permitted(query_ids, query_reach, key_ids, key_hot):
    linked = jnp.dot(query_reach, key_hot.T) > 0.5
    return linked & (key_ids[None, :] <= query_ids[:, None])


def inner_block(row_count):
    block_rows = row_count
    while block_rows > block_limit and block_rows % 2 == 0:
        block_rows = block_rows // 2
    return block_rows


def gather_body(
    hidden_in,
    grad_out,
    seg_len,
    seg_parent,
    gain_attn,
    shift_attn,
    w_qkv,
    bias_qkv,
    w_out,
    bias_out,
    gain_mlp,
    shift_mlp,
    w_up,
    bias_up,
    w_down,
    bias_down,
):
    local_rows = hidden_in.shape[1]
    scale_factor = 1.0 / math.sqrt(HEAD_DIM)
    head_shape = (local_rows, HEADS, HEAD_DIM)
    seg_ends, seg_starts, ancestor, path_start = tree_tables(seg_len[0], seg_parent[0])
    ancestor_f = ancestor.astype(jnp.float32)
    my_ids = lax.axis_index("ctx") * local_rows + jnp.arange(local_rows, dtype=jnp.int32)
    my_hot, my_reach = row_lookup(my_ids, seg_ends, ancestor_f)
    shift_table = path_start - seg_starts
    path_pos = my_ids + jnp.sum(my_hot.astype(jnp.int32) * shift_table[None, :], axis=1)
    cosine, sine = rotary_tables(path_pos)
    inputs_f = hidden_in[0].astype(jnp.float32)
    gain_a = gain_attn.astype(jnp.float32)
    shift_a = shift_attn.astype(jnp.float32)
    gain_m = gain_mlp.astype(jnp.float32)
    shift_m = shift_mlp.astype(jnp.float32)
    bias_up_f = bias_up.astype(jnp.float32)
    x_attn = layer_norm(inputs_f, gain_a, shift_a).astype(jnp.bfloat16)
    x_mlp = layer_norm(inputs_f, gain_m, shift_m).astype(jnp.bfloat16)
    qkv = jnp.einsum(
        "td,nd->tn",
        x_attn,
        lax.all_gather(w_qkv, "ctx", axis=0, tiled=True),
        preferred_element_type=jnp.float32,
    ) + bias_qkv.astype(jnp.float32)
    queries = rotate(qkv[:, :D].reshape(head_shape), cosine, sine).astype(jnp.bfloat16)
    keys_heads = rotate(qkv[:, D : 2 * D].reshape(head_shape), cosine, sine).astype(jnp.bfloat16)
    values_flat = qkv[:, 2 * D :].astype(jnp.bfloat16)
    values_heads = values_flat.reshape(head_shape)
    keys_flat = keys_heads.reshape(local_rows, D)
    queries_flat = queries.reshape(local_rows, D)

    def split_blocks(shard_pieces):
        row_count = shard_pieces[0].shape[0]
        block_rows = inner_block(row_count)
        block_count = row_count // block_rows
        shaped = tuple(
            (member.reshape(block_count, block_rows, HEADS, HEAD_DIM) for member in shard_pieces)
        )
        starts = block_rows * jnp.arange(block_count, dtype=jnp.int32)
        return shaped + (starts,)

    def attend_block(fold_state, block_items):
        key_block, value_block, block_start = block_items
        block_rows = key_block.shape[0]
        key_ids = block_start + jnp.arange(block_rows, dtype=jnp.int32)
        allowed = permitted(my_ids, my_reach, key_ids, segment_hot(key_ids, seg_ends))
        row_top, row_total, partial_value = fold_state
        scores = (
            jnp.einsum("qhd,khd->qhk", queries, key_block, preferred_element_type=jnp.float32)
            * scale_factor
        )
        scores = jnp.where(allowed[:, None, :], scores, masked_score)
        new_top = jnp.maximum(row_top, jnp.max(scores, axis=-1))
        factor = jnp.exp(row_top - new_top)
        weights = jnp.exp(scores - new_top[:, :, None])
        row_total = row_total * factor + jnp.sum(weights, axis=-1)
        partial_value = partial_value * factor[:, :, None] + jnp.einsum(
            "qhk,khd->qhd",
            weights.astype(jnp.bfloat16),
            value_block,
            preferred_element_type=jnp.float32,
        )
        fold_state = (new_top, row_total, partial_value)
        return (fold_state, None)

    start_state = (
        jnp.full((local_rows, HEADS), masked_score, jnp.float32),
        jnp.zeros((local_rows, HEADS), jnp.float32),
        jnp.zeros(head_shape, jnp.float32),
    )
    row_top, row_total, partial_value = lax.scan(
        attend_block,
        start_state,
        split_blocks(
            (
                lax.all_gather(keys_flat, "ctx", axis=0, tiled=True),
                lax.all_gather(values_flat, "ctx", axis=0, tiled=True),
            )
        ),
    )[0]
    log_total = row_top + jnp.log(row_total)
    attended_f = partial_value / row_total[:, :, None]
    attended = attended_f.reshape(local_rows, D).astype(jnp.bfloat16)
    attn_proj = jnp.einsum(
        "td,nd->tn",
        attended,
        lax.all_gather(w_out, "ctx", axis=0, tiled=True),
        preferred_element_type=jnp.float32,
    )

    def mlp_pre(up_rows):
        return (
            jnp.einsum("td,nd->tn", x_mlp, up_rows, preferred_element_type=jnp.float32) + bias_up_f
        )

    up_rows = lax.all_gather(w_up, "ctx", axis=0, tiled=True)
    down_rows = lax.all_gather(w_down, "ctx", axis=0, tiled=True)
    activated = jax.nn.gelu(mlp_pre(up_rows), approximate=False).astype(jnp.bfloat16)
    mlp_sum = jnp.dot(activated, down_rows, preferred_element_type=jnp.float32)
    bias_out_f = bias_out.astype(jnp.float32)
    bias_down_f = bias_down.astype(jnp.float32)
    hidden_out = (inputs_f + attn_proj + bias_out_f + mlp_sum + bias_down_f).astype(jnp.bfloat16)
    grad_b = grad_out[0]
    grad_f = grad_b.astype(jnp.float32)
    up_rows = lax.all_gather(w_up, "ctx", axis=0, tiled=True)
    down_rows = lax.all_gather(w_down, "ctx", axis=0, tiled=True)
    pre_act = mlp_pre(up_rows)
    activated = jax.nn.gelu(pre_act, approximate=False).astype(jnp.bfloat16)
    act_grad = jnp.einsum("td,nd->tn", grad_b, down_rows, preferred_element_type=jnp.float32)
    pre_grad = (act_grad * gelu_slope(pre_act)).astype(jnp.bfloat16)
    input_grad = jnp.dot(pre_grad, up_rows, preferred_element_type=jnp.float32)
    act_all = activated
    pre_grad_all = pre_grad
    act_all, pre_grad_all, mlp_in_grad = (act_all, pre_grad_all, input_grad)
    attended_grad = jnp.dot(
        grad_b, lax.all_gather(w_out, "ctx", axis=0, tiled=True), preferred_element_type=jnp.float32
    ).astype(jnp.bfloat16)
    attended_grad_heads = attended_grad.reshape(head_shape)
    row_delta = jnp.sum(attended_grad_heads.astype(jnp.float32) * attended_f, axis=-1)
    all_log_total, all_delta = (
        lax.all_gather(log_total, "ctx", axis=0, tiled=True),
        lax.all_gather(row_delta, "ctx", axis=0, tiled=True),
    )

    def back_block(fold_state, block_items):
        key_block, value_block, query_block, grad_block, block_start = block_items
        block_rows = key_block.shape[0]
        other_ids = block_start + jnp.arange(block_rows, dtype=jnp.int32)
        other_hot, other_reach = row_lookup(other_ids, seg_ends, ancestor_f)
        allowed_in = permitted(my_ids, my_reach, other_ids, other_hot)
        allowed_out = permitted(other_ids, other_reach, my_ids, my_hot)
        other_log = lax.dynamic_slice_in_dim(all_log_total, block_start, block_rows, 0)
        other_delta = lax.dynamic_slice_in_dim(all_delta, block_start, block_rows, 0)
        query_grad, key_grad, value_grad = fold_state
        scores = (
            jnp.einsum("qhd,khd->qhk", queries, key_block, preferred_element_type=jnp.float32)
            * scale_factor
        )
        scores = jnp.where(allowed_in[:, None, :], scores, masked_score)
        prob_mass = jnp.exp(scores - log_total[:, :, None])
        prob_grad = jnp.einsum(
            "qhd,khd->qhk", attended_grad_heads, value_block, preferred_element_type=jnp.float32
        )
        score_grad = (prob_mass * (prob_grad - row_delta[:, :, None])).astype(jnp.bfloat16)
        query_grad = (
            query_grad
            + jnp.einsum("qhk,khd->qhd", score_grad, key_block, preferred_element_type=jnp.float32)
            * scale_factor
        )
        outgoing_key_grad = key_grad
        outgoing_value_grad = value_grad
        scores = (
            jnp.einsum("qhd,khd->qhk", query_block, keys_heads, preferred_element_type=jnp.float32)
            * scale_factor
        )
        scores = jnp.where(allowed_out[:, None, :], scores, masked_score)
        prob_mass = jnp.exp(scores - other_log[:, :, None])
        outgoing_value_grad = outgoing_value_grad + jnp.einsum(
            "qhk,qhd->khd",
            prob_mass.astype(jnp.bfloat16),
            grad_block,
            preferred_element_type=jnp.float32,
        )
        prob_grad = jnp.einsum(
            "qhd,khd->qhk", grad_block, values_heads, preferred_element_type=jnp.float32
        )
        score_grad = (prob_mass * (prob_grad - other_delta[:, :, None])).astype(jnp.bfloat16)
        outgoing_key_grad = (
            outgoing_key_grad
            + jnp.einsum(
                "qhk,qhd->khd", score_grad, query_block, preferred_element_type=jnp.float32
            )
            * scale_factor
        )
        fold_state = (query_grad, outgoing_key_grad, outgoing_value_grad)
        return (fold_state, None)

    zero_heads = jnp.zeros(head_shape, jnp.float32)
    query_grad, key_grad, value_grad = lax.scan(
        back_block,
        (zero_heads, zero_heads, zero_heads),
        split_blocks(
            (
                lax.all_gather(keys_flat, "ctx", axis=0, tiled=True),
                lax.all_gather(values_flat, "ctx", axis=0, tiled=True),
                lax.all_gather(queries_flat, "ctx", axis=0, tiled=True),
                lax.all_gather(attended_grad, "ctx", axis=0, tiled=True),
            )
        ),
    )[0]

    def turn(head_values):
        return rotate(head_values, cosine, sine)

    unturn = jax.vjp(turn, zero_heads)[1]
    qkv_grad = jnp.concatenate(
        [
            unturn(query_grad)[0].reshape(local_rows, D),
            unturn(key_grad)[0].reshape(local_rows, D),
            value_grad.reshape(local_rows, D),
        ],
        axis=1,
    ).astype(jnp.bfloat16)
    attn_in_grad = jnp.dot(
        qkv_grad,
        lax.all_gather(w_qkv, "ctx", axis=0, tiled=True),
        preferred_element_type=jnp.float32,
    )
    pull_attn = jax.vjp(layer_norm, inputs_f, gain_a, shift_a)[1]
    input_part_a, gain_grad_a, shift_grad_a = pull_attn(attn_in_grad)
    pull_mlp = jax.vjp(layer_norm, inputs_f, gain_m, shift_m)[1]
    input_part_m, gain_grad_m, shift_grad_m = pull_mlp(mlp_in_grad)
    grad_in = (grad_f + input_part_a + input_part_m)[None]
    vector_sums = lax.psum(
        (
            gain_grad_a,
            shift_grad_a,
            gain_grad_m,
            shift_grad_m,
            jnp.sum(qkv_grad, axis=0, dtype=jnp.float32),
            jnp.sum(grad_f, axis=0),
            jnp.sum(pre_grad_all, axis=0, dtype=jnp.float32),
        ),
        ("dp", "ctx"),
    )
    group_count = lax.axis_size("ctx")
    section_rows = (3 * D // group_count, D // group_count, FF // group_count, FF // group_count)
    term_sources = (
        (qkv_grad, x_attn),
        (grad_b, attended),
        (pre_grad_all, x_mlp),
        (act_all, grad_b),
    )
    owner_rows = sum(section_rows)
    blocks = jnp.arange(owner_rows * lax.axis_size("ctx") // owner_rows, dtype=jnp.int32)
    parts_list = []
    for (column_source, other_side), full_rows in zip(term_sources, section_rows):
        sub_rows = full_rows // 1
        column_ids = (
            blocks[:, None] * sub_rows + jnp.arange(sub_rows, dtype=jnp.int32)[None, :]
        ).reshape(-1)
        columns = jnp.take(column_source, column_ids, axis=1)
        block_term = jnp.einsum(
            "tr,td->rd", columns, other_side, preferred_element_type=jnp.float32
        )
        parts_list.append(block_term.reshape(blocks.shape[0], sub_rows, D))
    owned_term = lax.psum_scatter(
        jnp.concatenate(parts_list, axis=1).reshape(-1, D).astype(jnp.bfloat16),
        "ctx",
        scatter_dimension=0,
        tiled=True,
    ).astype(jnp.float32)
    cut_a = section_rows[0]
    cut_b = cut_a + section_rows[1]
    cut_c = cut_b + section_rows[2]
    weight_grads = (
        lax.psum(owned_term[:cut_a].astype(jnp.bfloat16), "dp").astype(jnp.float32),
        lax.psum(owned_term[cut_a:cut_b].astype(jnp.bfloat16), "dp").astype(jnp.float32),
        lax.psum(owned_term[cut_b:cut_c].astype(jnp.bfloat16), "dp").astype(jnp.float32),
        lax.psum(owned_term[cut_c:].astype(jnp.bfloat16), "dp").astype(jnp.float32),
    )
    return (
        hidden_out[None],
        grad_in,
        vector_sums[0],
        vector_sums[1],
        weight_grads[0],
        vector_sums[4],
        weight_grads[1],
        vector_sums[5],
        vector_sums[2],
        vector_sums[3],
        weight_grads[2],
        vector_sums[6],
        weight_grads[3],
        vector_sums[5],
    )


def solution(mesh):
    token = P("dp", "ctx", None)
    rows = P("ctx", None)
    return jax.shard_map(
        body if HEADS % mesh.shape["ctx"] == 0 else gather_body,
        mesh=mesh,
        in_specs=(
            token,
            token,
            P("dp", None),
            P("dp", None),
            P(),
            P(),
            rows,
            P(),
            rows,
            P(),
            P(),
            P(),
            rows,
            P(),
            rows,
            P(),
        ),
        out_specs=(
            token,
            token,
            P(),
            P(),
            rows,
            P(),
            rows,
            P(),
            P(),
            P(),
            rows,
            P(),
            rows,
            P(),
        ),
        check_vma=False,
    )
```

```python
import functools
import math

import jax
import jax.numpy as jnp
import numpy as np
from jax import lax
from jax.experimental import pallas as pl
from jax.experimental.pallas import tpu as pltpu
from jax.sharding import PartitionSpec as P

D = 2048
HEADS = 16
HEAD_DIM = 128
ROT_DIM = 32
FF = 8192

norm_eps = 1e-05
masked_score = -1e30
f32 = jnp.float32
bf16 = jnp.bfloat16


def dot_nt(a, b):
    return lax.dot_general(a, b, (((1,), (1,)), ((), ())), preferred_element_type=f32)


def dot_nn(a, b):
    return lax.dot_general(a, b, (((1,), (0,)), ((), ())), preferred_element_type=f32)


def dot_tn(a, b):
    return lax.dot_general(a, b, (((0,), (0,)), ((), ())), preferred_element_type=f32)


MESH = pl.DeviceIdType.MESH
RAILS = 2


def place(group):
    dp = lax.axis_index("dp")
    ctx = lax.axis_index("ctx")
    return dp, ctx, ctx // RAILS, ctx % RAILS, group // RAILS


def copy_to(src, dst, send, recv, device):
    return pltpu.make_async_remote_copy(
        src_ref=src,
        dst_ref=dst,
        send_sem=send,
        recv_sem=recv,
        device_id=device,
        device_id_type=MESH,
    )


def signal(device):
    barrier = pltpu.get_barrier_semaphore()
    pl.semaphore_signal(barrier, inc=1, device_id=device, device_id_type=MESH)


def arrive(count):
    pl.semaphore_wait(pltpu.get_barrier_semaphore(), count)


def pair_of(ctx, group):
    if group != 8:
        return ctx
    return ctx + jnp.where(
        (ctx == 1) | (ctx == 4), 2, jnp.where((ctx == 3) | (ctx == 6), -2, 0)
    )


def pair_order(z, depth):
    return [
        z,
        jnp.where(z > 0, z - 1, 1),
        jnp.where(z == depth - 1, 1, jnp.where(z == depth - 2, depth - 1, 2)),
        jnp.where(z < depth // 2, depth - 1, 0),
    ]


def layer_kernel(group, *refs):
    hidden, grad, w_up_in, w_down_in, w_qkv_in, w_out = refs[:6]
    vectors, (inverse, seg_len, seg_parent), refs = refs[6:14], refs[14:17], refs[7:]
    h_out, g_out, x_out, heads_out, part_out, back_out, pairs_out, early_out, cols_out = refs[10:19]
    tables, sums, bias_sum, local_sum, norms = refs[19:24]
    h_buf, g_buf, w_up, w_down, w_qkv, x_mlp, x_attn, act, slope, pre_grad = refs[24:34]
    heads, part, back, down_grad, up_grad, core_buf, mean, rstd, bias_up, bias_qkv = refs[34:44]
    all_qkv, all_up = refs[44:46]
    refs = refs[2:]
    own_sem, y_send, y_recv, up_send, up_recv, down_send, down_recv = refs[44:51]
    weight_sem, pair_sem, grad_sem, head_send, head_recv = refs[51:56]
    core_send, core_recv, cols_send, cols_recv, early_send, early_recv = refs[56:62]
    dp, ctx, z, y, depth = place(group)
    bufs, sources, outs = (h_buf, g_buf), (hidden, grad), (h_out, g_out)
    rows = hidden.shape[0]
    pair_rows = RAILS * rows
    tokens, columns = h_buf.shape
    units = act.shape[1]
    head_cols = heads.shape[2]
    other = (dp, z * RAILS + 1 - y)
    above = (dp, jnp.minimum(z + 1, depth - 1) * RAILS + y)
    below = (dp, jnp.maximum(z - 1, 0) * RAILS + y)
    has_above, has_below = z < depth - 1, z > 0
    order = pair_order(z, depth)

    x, core = dp // 2, dp % 2
    sibling = (x * 2 + 1 - core, ctx)
    across = ((1 - x) * 2 + core, ctx)

    for n in range(1, group):
        signal((dp, lax.rem(ctx + n, group)))
    signal(sibling)
    signal(across)
    arrive(group + 1)

    def chunk(i, at_z, at_y):
        start = pl.multiple_of((at_z * RAILS + at_y) * rows, rows)
        return bufs[i].at[pl.ds(start, rows)]

    def to_other(i, at_z, source=None):
        here = chunk(i, at_z, y)
        return copy_to(
            here if source is None else source, here, y_send.at[i, at_z], y_recv.at[i, at_z], other
        )

    def upward(i, at_z, source=None):
        here = chunk(i, at_z, y)
        return copy_to(
            here if source is None else source,
            here,
            up_send.at[i, at_z],
            up_recv.at[i, at_z],
            above,
        )

    def downward(i, at_z, source=None):
        here = chunk(i, at_z, y)
        return copy_to(
            here if source is None else source,
            here,
            down_send.at[i, at_z],
            down_recv.at[i, at_z],
            below,
        )

    def relay_up(i, k):
        at_z = jnp.maximum(z - k, 0)
        upward(i, at_z).wait_recv()
        pl.when(has_above)(lambda: upward(i, at_z).start())

    def relay_down(i, k):
        at_z = jnp.minimum(z + k, depth - 1)
        downward(i, at_z).wait_recv()
        pl.when(has_below)(lambda: downward(i, at_z).start())

    def turn(n):
        if n < depth:
            pl.when(z >= n)(lambda: relay_up(0, n))
            pl.when(z + n < depth)(lambda: relay_down(0, n))
            to_other(0, order[n]).start()
            pl.when((z == n - 1) & has_above)(lambda: upward(1, z, sources[1]).start())
            pl.when((z == depth - n) & has_below)(lambda: downward(1, z, sources[1]).start())
        for k in range(1, depth):
            pl.when((z == n - k) & (z >= k))(lambda k=k: relay_up(1, k))
            pl.when((depth - 1 - z == n - k) & (z + k < depth))(lambda k=k: relay_down(1, k))
        if n == depth:
            to_other(1, z, sources[1]).start()
        if n > depth:
            to_other(1, order[n - depth]).start()

    def y_arrive(i, s):
        here = chunk(i, order[s], 1 - y)
        copy_to(
            here, here, y_send.at[i, order[s]], y_recv.at[i, order[s]], other
        ).wait_recv()

    def pair_at(s):
        return pl.ds(pl.multiple_of(order[s] * pair_rows, pair_rows), pair_rows)

    def keep(n, s, buf, out):
        at = pair_at(s)
        return pltpu.make_async_copy(buf.at[at], out.at[at], pair_sem.at[n, s])

    own = [pltpu.make_async_copy(sources[i], chunk(i, z, y), own_sem.at[i]) for i in range(2)]
    weights = [
        pltpu.make_async_copy(source, held, weight_sem.at[n])
        for n, (source, held) in enumerate(
            ((w_up_in, w_up), (w_qkv_in, w_qkv), (w_down_in, w_down))
        )
    ]
    own[0].start()
    to_other(0, z, sources[0]).start()
    pl.when(has_above)(lambda: upward(0, z, sources[0]).start())
    pl.when(has_below)(lambda: downward(0, z, sources[0]).start())
    for copy in weights:
        copy.start()
    own[1].start()

    starts, shifts = [], []
    at = jnp.int32(0)
    for n in range(seg_len.shape[1]):
        parent = seg_parent[0, n]
        grand = seg_parent[0, parent]
        before = jnp.where(parent != n, seg_len[0, parent], 0) + jnp.where(
            (grand != n) & (grand != parent), seg_len[0, grand], 0
        )
        starts.append(at)
        shifts.append(before - at)
        at = at + seg_len[0, n]

    turned_half = ROT_DIM // 2

    @pl.loop(0, tokens // rows)
    def _(n):
        at = pl.ds(pl.multiple_of(n * rows, rows), rows)
        token = n * rows + lax.broadcasted_iota(jnp.int32, (turned_half, rows), 1)
        position = token + shifts[0]
        for m in range(1, len(starts)):
            position = position + jnp.where(token >= starts[m], shifts[m] - shifts[m - 1], 0)
        angle = position.astype(f32) * inverse[...]
        cosine, sine = jnp.cos(angle), jnp.sin(angle)
        still = jnp.zeros((HEAD_DIM - ROT_DIM, rows), f32)
        none = jnp.zeros((turned_half, rows), f32)
        tables[0, at, :] = jnp.concatenate([cosine, cosine, still + 1.0], axis=0).T
        tables[1, at, :] = jnp.concatenate([-sine, none, still], axis=0).T
        tables[2, at, :] = jnp.concatenate([none, sine, still], axis=0).T

    sums[...] = jnp.zeros_like(sums)
    bias_sum[...] = jnp.zeros_like(bias_sum)
    for n in range(6):
        norms[n : n + 1, :] = vectors[n][...].astype(f32).reshape(1, columns)
    norms[6:8, :] = jnp.zeros((2, columns), f32)

    def take_mine(target, vector, wide_row):
        wide_row[...] = vector[...].astype(f32).reshape(wide_row.shape)
        size = target.shape[1]
        target[...] = wide_row[:, pl.ds(pl.multiple_of(ctx * size, HEAD_DIM), size)]

    take_mine(bias_qkv, vectors[6], all_qkv)
    take_mine(bias_up, vectors[7], all_up)

    def normalize(s):
        step = 32

        @pl.loop(0, pair_rows // step)
        def _(n):
            at = pl.ds(pl.multiple_of(order[s] * pair_rows + n * step, step), step)
            values = h_buf[at, :].astype(f32)
            average = jnp.mean(values, axis=1, keepdims=True)
            centred = values - average
            spread = lax.rsqrt(jnp.mean(centred * centred, axis=1, keepdims=True) + norm_eps)
            normed = centred * spread
            x_attn[at, :] = (normed * norms[0:1, :] + norms[1:2, :]).astype(bf16)
            x_mlp[at, :] = (normed * norms[2:3, :] + norms[3:4, :]).astype(bf16)
            mean[at, :] = average
            rstd[at, :] = spread
            lane = lax.broadcasted_iota(jnp.int32, (step, HEAD_DIM), 1)
            tables[3, at, :] = jnp.where(lane == 0, average, spread)

    wide = 512

    def feed(s):
        at = pair_at(s)

        @pl.loop(0, units // wide)
        def _(n):
            cols = pl.ds(pl.multiple_of(n * wide, wide), wide)
            pre = dot_nt(x_mlp[at, :], w_up[cols, :]) + bias_up[:, cols]
            normal_cdf = 0.5 * (1.0 + lax.erf(pre * math.sqrt(0.5)))
            act[at, cols] = (pre * normal_cdf).astype(bf16)
            slope[at, cols] = (
                normal_cdf + pre * jnp.exp(-0.5 * pre * pre) * (1.0 / math.sqrt(2.0 * math.pi))
            ).astype(slope.dtype)

    def project(s):
        at = pair_at(s)
        for j in range(3):
            block = pl.ds(j * head_cols, head_cols)
            raw = dot_nt(x_attn[at, :], w_qkv[block, :]) + bias_qkv[:, block]
            turns = lax.div(3 * ctx + j, group) < 2
            for m in range(head_cols // HEAD_DIM):
                one = raw[:, m * HEAD_DIM : (m + 1) * HEAD_DIM]
                turned = (
                    one * tables[0, at, :]
                    + pltpu.roll(one, HEAD_DIM - ROT_DIM // 2, 1) * tables[1, at, :]
                    + pltpu.roll(one, ROT_DIM // 2, 1) * tables[2, at, :]
                )
                heads[j, at, m * HEAD_DIM : (m + 1) * HEAD_DIM] = jnp.where(
                    turns, turned, one
                ).astype(bf16)

    def mix(s):
        at = pair_at(s)

        @pl.loop(0, columns // wide)
        def _(n):
            cols = pl.ds(pl.multiple_of(n * wide, wide), wide)
            part[at, cols] = dot_nn(act[at, :], w_down[:, cols]).astype(bf16)

    def back_feed(s):
        at = pair_at(s)

        @pl.loop(0, units // wide)
        def _(n):
            cols = pl.ds(pl.multiple_of(n * wide, wide), wide)
            rounded = (
                dot_nt(g_buf[at, :], w_down[cols, :]) * slope[at, cols].astype(f32)
            ).astype(bf16)
            pre_grad[at, cols] = rounded
            bias_sum[:, cols] += jnp.sum(rounded.astype(f32), axis=0, keepdims=True)

        @pl.loop(0, columns // wide)
        def _(n):
            cols = pl.ds(pl.multiple_of(n * wide, wide), wide)
            entry = dot_nn(pre_grad[at, :], w_up[:, cols])
            normed = (h_buf[at, cols].astype(f32) - mean[at, :]) * rstd[at, :]
            sums[0:1, cols] += jnp.sum(entry * normed, axis=0, keepdims=True)
            sums[1:2, cols] += jnp.sum(entry, axis=0, keepdims=True)
            back[at, cols] = (entry * norms[2:3, cols]).astype(bf16)

    def forward(s):
        keep(0, s, h_buf, h_out).start()
        normalize(s)
        keep(1, s, x_attn, x_out).start()
        if s == 0:
            weights[0].wait()
        feed(s)
        if s == 0:
            weights[1].wait()
        project(s)

    def backward(s):
        keep(2, s, g_buf, g_out).start()
        if s == 0:
            weights[2].wait()
        mix(s)
        keep(3, s, part, part_out).start()
        back_feed(s)
        keep(4, s, back, back_out).start()

    tall = 256
    half = core_buf.shape[1]
    tiles = units // tall
    held = (down_grad, up_grad)

    def grad_half(t, which):
        start = pl.multiple_of((t % tiles) * tall + which * half, half)
        return held[t // tiles].at[pl.ds(start, half)]

    def to_core(t):
        return copy_to(
            grad_half(t, 1 - core), core_buf.at[t], core_send.at[t], core_recv.at[t], sibling
        )

    def grad_keep(t):
        return pltpu.make_async_copy(
            grad_half(t, core), pairs_out.at[pl.ds(t * half, half)], grad_sem.at[t]
        )

    def outer(n, left, right, last, ms=range(units // tall)):
        first, second = (pair_at(2), pair_at(3)) if last else (pair_at(0), pair_at(1))
        for m in ms:
            mine = pl.ds(m * tall, tall)

            @pl.loop(0, columns // (2 * wide))
            def _(k):
                cols = pl.ds(pl.multiple_of(k * 2 * wide, 2 * wide), 2 * wide)
                term = dot_tn(left[first, mine], right[first, cols])
                term += dot_tn(left[second, mine], right[second, cols])
                if last:
                    term += held[n][mine, cols].astype(f32)
                held[n][mine, cols] = term.astype(bf16)

            if last:
                to_core(n * tiles + m).start()

    def early_x(t):
        return copy_to(
            grad_half(t, core), early_out.at[t], early_send.at[t], early_recv.at[t], across
        )

    def outer_sum(ts):
        for t in ts:
            to_core(t).wait_recv()
            mine = grad_half(t, core)

            @pl.loop(0, half // 32)
            def _(k):
                at = pl.ds(pl.multiple_of(k * 32, 32), 32)
                mine[at, :] = (mine[at, :].astype(f32) + core_buf[t, at, :].astype(f32)).astype(
                    bf16
                )

            grad_keep(t).start()
            if t < early_out.shape[0]:
                early_x(t).start()

    share = cols_out.shape[2]

    def to_columns(n):
        owner = lax.rem(ctx + n, group)
        block = w_out.at[
            pl.ds(pl.multiple_of(dp * share, share), share),
            pl.ds(pl.multiple_of(pair_of(owner, group) * head_cols, head_cols), head_cols),
        ]
        if n == 0:
            return pltpu.make_async_copy(block, cols_out.at[ctx, dp], cols_send.at[0])
        return copy_to(
            block, cols_out.at[ctx, dp], cols_send.at[n], cols_recv.at[n], (dp, owner)
        )

    def columns_arrive():
        to_columns(0).wait()
        for n in range(1, group):
            source = lax.rem(ctx + group - n, group)
            here = cols_out.at[source, dp]
            copy_to(here, here, cols_send.at[n], cols_recv.at[n], other).wait_recv()

    def columns_core(which):
        here = cols_out.at[:, pl.ds(2 * x + which, 1)]
        return copy_to(here, here, cols_send.at[group], cols_recv.at[group], sibling)

    def columns_x(which):
        here = cols_out.at[:, pl.ds(2 * which, 2)]
        return copy_to(here, here, cols_send.at[group + 1], cols_recv.at[group + 1], across)

    def to_head(j):
        block = 3 * ctx + j
        kind, target = lax.div(block, group), pair_of(lax.rem(block, group), group)
        remote = copy_to(
            heads.at[j], heads_out.at[kind], head_send.at[j], head_recv.at[kind], (dp, target)
        )
        local = pltpu.make_async_copy(heads.at[j], heads_out.at[kind], head_send.at[j])
        return target == ctx, remote, local

    def send_heads(crossing):
        for j in range(3):
            here, remote, local = to_head(j)
            target = pair_of(lax.rem(3 * ctx + j, group), group)
            crosses = target % RAILS != ctx % RAILS
            if crossing:
                pl.when(crosses)(lambda remote=remote: remote.start())
            else:
                pl.when(here)(lambda local=local: local.start())
                pl.when(jnp.logical_not(here | crosses))(lambda remote=remote: remote.start())

    def head_source(kind):
        return lax.div(kind * group + pair_of(ctx, group), 3)

    turn(1)
    own[0].wait()
    y_arrive(0, 0)
    forward(0)
    turn(2)
    y_arrive(0, 1)
    forward(1)
    turn(3)
    y_arrive(0, 2)
    forward(2)
    turn(4)
    for n in range(group):
        to_columns(n).start()
    y_arrive(0, 3)
    forward(3)
    turn(5)
    send_heads(False)
    own[1].wait()
    y_arrive(1, 0)
    backward(0)
    at = pl.ds(pl.multiple_of(ctx * rows, rows), rows)
    local_sum[...] = jnp.sum(g_buf[at, :].astype(f32), axis=0, keepdims=True)
    turn(6)
    y_arrive(1, 1)
    backward(1)
    turn(7)
    columns_arrive()
    columns_core(core).start()
    outer(0, act, g_buf, False)
    outer(1, pre_grad, x_mlp, False)
    columns_core(1 - core).wait_recv()
    columns_x(x).start()
    y_arrive(1, 2)
    backward(2)
    send_heads(True)
    y_arrive(1, 3)
    backward(3)
    early = early_out.shape[0]
    outer(0, act, g_buf, True, range(early + 1))
    outer_sum(range(early))
    outer(0, act, g_buf, True, range(early + 1, tiles))
    outer(1, pre_grad, x_mlp, True)
    outer_sum(range(early, 2 * tiles))

    for at_z in range(depth):
        to_other(0, at_z).wait_send()
        to_other(1, at_z).wait_send()
        for i in range(2):
            pl.when(has_above & (at_z <= z))(lambda i=i: upward(i, at_z).wait_send())
            pl.when(has_below & (at_z >= z))(lambda i=i: downward(i, at_z).wait_send())
    for j in range(3):
        here, remote, local = to_head(j)
        pl.when(here)(lambda local=local: local.wait())
        pl.when(jnp.logical_not(here))(lambda remote=remote: remote.wait_send())
    for kind in range(3):
        arriving = copy_to(
            heads.at[0], heads_out.at[kind], head_send.at[0], head_recv.at[kind], other
        )
        pl.when(head_source(kind) != ctx)(lambda arriving=arriving: arriving.wait_recv())
    for s in range(4):
        keep(0, s, h_buf, h_out).wait()
        keep(1, s, x_attn, x_out).wait()
        keep(2, s, g_buf, g_out).wait()
        keep(3, s, part, part_out).wait()
        keep(4, s, back, back_out).wait()
    for t in range(2 * tiles):
        to_core(t).wait_send()
        grad_keep(t).wait()
    for n in range(1, group):
        to_columns(n).wait_send()
    for t in range(early):
        early_x(t).wait_send()
        early_x(t).wait_recv()
    columns_core(core).wait_send()
    columns_x(x).wait_send()
    columns_x(1 - x).wait_recv()


def layer_pass(
    group, hidden, grad, w_up, w_down, w_qkv, w_out, vectors, seg_len, seg_parent
):
    rows, columns = hidden.shape
    tokens, units, head_cols = group * rows, w_up.shape[0], w_qkv.shape[0] // 3
    depth = group // RAILS
    inverse = 10000.0 ** (-2.0 * np.arange(ROT_DIM // 2) / ROT_DIM)
    inverse = jnp.asarray(np.broadcast_to(inverse[:, None], (ROT_DIM // 2, rows)), f32)
    early = 1
    sems = pltpu.SemaphoreType.DMA
    shape = jax.ShapeDtypeStruct
    anywhere = pl.BlockSpec(memory_space=pl.ANY)
    vmem = pl.BlockSpec(memory_space=pltpu.VMEM)
    smem = pl.BlockSpec(memory_space=pltpu.SMEM)
    whole = shape((tokens, columns), bf16)
    half = 128
    copies = lax.axis_size("dp")
    return pl.pallas_call(
        functools.partial(layer_kernel, group),
        out_shape=(
            whole,
            whole,
            whole,
            shape((3, tokens, head_cols), bf16),
            whole,
            whole,
            shape((units, columns), bf16),
            shape((early, half, columns), bf16),
            shape((group, copies, columns // group // copies, head_cols), bf16),
            shape((4, tokens, HEAD_DIM), f32),
            shape((2, columns), f32),
            shape((1, units), f32),
            shape((1, columns), f32),
            shape((8, columns), f32),
        ),
        in_specs=[anywhere] * 6 + [vmem] * 9 + [smem] * 2,
        out_specs=[anywhere] * 9 + [vmem] * 5,
        scratch_shapes=[pltpu.VMEM((tokens, columns), bf16)] * 2
        + [pltpu.VMEM((units, columns), bf16)] * 2
        + [pltpu.VMEM((3 * head_cols, columns), bf16)]
        + [pltpu.VMEM((tokens, columns), bf16)] * 2
        + [pltpu.VMEM((tokens, units), bf16)] * 3
        + [pltpu.VMEM((3, tokens, head_cols), bf16)]
        + [pltpu.VMEM((tokens, columns), bf16)] * 2
        + [pltpu.VMEM((units, columns), bf16)] * 2
        + [pltpu.VMEM((units // half, half, columns), bf16)]
        + [pltpu.VMEM((tokens, 1), f32)] * 2
        + [pltpu.VMEM((1, units), f32), pltpu.VMEM((1, 3 * head_cols), f32)]
        + [pltpu.VMEM((1, vector.shape[0]), f32) for vector in vectors[6:]]
        + [sems((2,))]
        + [sems((2, depth))] * 6
        + [sems((3,)), sems((5, 4)), sems((units // half,)), sems((3,)), sems((3,))]
        + [sems((units // half,))] * 2
        + [sems((group + 2,))] * 2
        + [sems((early,))] * 2,
        compiler_params=pltpu.CompilerParams(
            collective_id=0, has_side_effects=True, vmem_limit_bytes=62 * 2**20
        ),
        name="layer_pass",
    )(hidden, grad, w_up, w_down, w_qkv, w_out, *vectors, inverse, seg_len, seg_parent)


def tail_kernel(group, *refs):
    pairs, arrived_in, grad_in, w_cols_in, part_in, back_in, x_in, w_qkv_in, hidden_in = refs[:9]
    tables_in, early_in, norms, mlp_sums, up_sums, local_sums, seg_len, seg_parent = refs[9:17]
    part_out, back_out, down_out, up_out, out_out, qkv_out, vectors_out, stats_out = refs[17:25]
    refs = refs[25:]
    arrived, g_buf, w_cols, part, back, x_buf, w_qkv, h_buf, tables = refs[:9]
    att_grad, attended, returns, returned, y_buf, z_buf = refs[9:15]
    out_grad, qkv_grad, qkv_core, out_core, out_rows, from_x, pairs_x, key_acc, value_acc = refs[15:24]
    sums, vec_buf = refs[24:26]
    (
        load_sem,
        y_send,
        y_recv,
        up_send,
        up_recv,
        down_send,
        down_recv,
        result_sem,
        head_send,
        head_recv,
        pair_send,
        pair_recv,
        core_send,
        core_recv,
        block_send,
        block_recv,
        x_send,
        x_recv,
        keep_sem,
        done_send,
        done_recv,
        vec_send,
        vec_recv,
        sum_sem,
    ) = refs[26:]
    dp, ctx, z, y, depth = place(group)
    tokens, columns = g_buf.shape
    rows = tokens // group
    head_cols = attended.shape[1]
    heads = head_cols // HEAD_DIM
    half = qkv_core.shape[1]
    pair_tiles = pairs_x.shape[0]
    x, core = dp // 2, dp % 2
    other = (dp, z * RAILS + 1 - y)
    above = (dp, jnp.minimum(z + 1, depth - 1) * RAILS + y)
    below = (dp, jnp.maximum(z - 1, 0) * RAILS + y)
    sibling = (x * 2 + 1 - core, ctx)
    across = ((1 - x) * 2 + core, ctx)
    near = (dp, (z + 1 - 2 * (z % 2)) * RAILS + y)
    far = (dp, lax.rem(z + 2, depth) * RAILS + y)
    has_above, has_below = z < depth - 1, z > 0

    for n in range(1, group):
        signal((dp, lax.rem(ctx + n, group)))
    signal(sibling)
    signal(across)
    arrive(group + 1)

    def add(target, left, right):
        step = 32

        @pl.loop(0, target.shape[0] // step)
        def _(n):
            at = pl.ds(pl.multiple_of(n * step, step), step)
            target[at, :] = (left[at, :].astype(f32) + right[at, :].astype(f32)).astype(
                target.dtype
            )

    def pair_x(t):
        return copy_to(
            pairs.at[pl.ds(t * half, half)],
            pairs_x.at[t],
            pair_send.at[t],
            pair_recv.at[t],
            across,
        )

    early = early_in.shape[0]
    for t in range(early, pair_tiles):
        pair_x(t).start()
    loads = [
        pltpu.make_async_copy(source, target, load_sem.at[n])
        for n, (source, target) in enumerate(
            (
                (w_cols_in, w_cols),
                (grad_in, g_buf),
                (arrived_in, arrived),
                (tables_in, tables),
                (part_in, part),
                (w_qkv_in, w_qkv),
                (back_in, back),
                (hidden_in, h_buf),
                (x_in, x_buf),
                (early_in, pairs_x.at[pl.ds(0, early)]),
            )
        )
    ]
    for copy in loads:
        copy.start()

    wide = 512
    tall = 256
    scale = 1.0 / math.sqrt(HEAD_DIM)
    loads[0].wait()
    loads[1].wait()

    @pl.loop(0, tokens // tall)
    def _(n):
        at = pl.ds(pl.multiple_of(n * tall, tall), tall)
        att_grad[at, :] = dot_nn(g_buf[at, :], w_cols[...]).astype(bf16)

    starts, reaches = [], []
    at = jnp.int32(0)
    for n in range(seg_len.shape[1]):
        parent = seg_parent[0, n]
        grand = seg_parent[0, parent]
        starts.append(at)
        reaches.append(
            (jnp.int32(1) << n) | (jnp.int32(1) << parent) | (jnp.int32(1) << grand)
        )
        at = at + seg_len[0, n]
    loads[2].wait()
    loads[3].wait()

    def unturn(values, at):
        return (
            values * tables[0, at, :]
            - pltpu.roll(values, HEAD_DIM - ROT_DIM // 2, 1) * tables[1, at, :]
            - pltpu.roll(values, ROT_DIM // 2, 1) * tables[2, at, :]
        )

    for m in range(heads):
        lanes = slice(m * HEAD_DIM, (m + 1) * HEAD_DIM)
        key_acc[...] = jnp.zeros_like(key_acc)
        value_acc[...] = jnp.zeros_like(value_acc)
        for n in range(tokens // tall):
            mine = pl.ds(n * tall, tall)
            seen = (n + 1) * tall
            upto = pl.ds(0, seen)
            token = n * tall + lax.broadcasted_iota(jnp.int32, (tall, 1), 0)
            key = lax.broadcasted_iota(jnp.int32, (1, seen), 1)
            reach = jnp.zeros((tall, 1), jnp.int32) + reaches[0]
            label = jnp.ones((1, seen), jnp.int32)
            for k in range(1, len(starts)):
                reach = jnp.where(token >= starts[k], reaches[k], reach)
                label = jnp.where(key >= starts[k], 1 << k, label)
            allowed = ((reach & label) != 0) & (key <= token)
            query = arrived[0, mine, lanes]
            keys = arrived[1, upto, lanes]
            values = arrived[2, upto, lanes]
            out_grad_rows = att_grad[mine, lanes]
            scores = jnp.where(allowed, dot_nt(query, keys) * scale, masked_score)
            expo = jnp.exp(scores - jnp.max(scores, axis=1, keepdims=True))
            probs = expo * (1.0 / jnp.sum(expo, axis=1, keepdims=True))
            weights = probs.astype(bf16)
            attended[mine, lanes] = dot_nn(weights, values).astype(bf16)
            prob_grad = dot_nt(out_grad_rows, values)
            delta = jnp.sum(probs * prob_grad, axis=1, keepdims=True)
            score_grad = (probs * (prob_grad - delta)).astype(bf16)
            query_grad = dot_nn(score_grad, keys) * scale
            returns[0, mine, lanes] = unturn(query_grad, mine).astype(bf16)
            key_acc[upto, :] += dot_tn(score_grad, query)
            value_acc[upto, :] += dot_tn(weights, out_grad_rows)

        for n in range(tokens // tall):
            mine = pl.ds(n * tall, tall)
            returns[1, mine, lanes] = unturn(key_acc[mine, :] * scale, mine).astype(bf16)
            returns[2, mine, lanes] = value_acc[mine, :].astype(bf16)

    def to_owner(kind):
        block = kind * group + pair_of(ctx, group)
        owner, slot = lax.div(block, 3), lax.rem(block, 3)
        remote = copy_to(
            returns.at[kind], returned.at[slot], head_send.at[kind], head_recv.at[slot], (dp, owner)
        )
        local = pltpu.make_async_copy(returns.at[kind], returned.at[slot], head_send.at[kind])
        return owner == ctx, remote, local

    for kind in range(3):
        here, remote, local = to_owner(kind)
        pl.when(here)(lambda local=local: local.start())
        pl.when(jnp.logical_not(here))(lambda remote=remote: remote.start())

    @pl.loop(0, group)
    def _(n):
        at = pl.ds(pl.multiple_of(n * head_cols, head_cols), head_cols)
        out_grad[n] = dot_tn(g_buf[:, at], attended[...]).astype(bf16)

    core_tiles = qkv_core.shape[0]
    out_to_core = copy_to(
        out_grad.at[:, pl.ds((1 - core) * half, half)],
        out_core,
        core_send.at[core_tiles],
        core_recv.at[core_tiles],
        sibling,
    )
    out_to_core.start()

    loads[4].wait()

    @pl.loop(0, tokens // tall)
    def _(n):
        at = pl.ds(pl.multiple_of(n * tall, tall), tall)

        @pl.loop(0, columns // wide)
        def _(m):
            cols = pl.ds(pl.multiple_of(m * wide, wide), wide)
            part[at, cols] = (
                part[at, cols].astype(f32) + dot_nt(attended[at, :], w_cols[cols, :])
            ).astype(bf16)

    low = z < depth // 2
    order = [
        jnp.where(low, depth - 1, 0),
        jnp.where(low, depth - 2, 1),
        jnp.where(low, 1 - z, 2 * depth - 3 - z),
        z,
    ]
    parts = (part, back)

    def chunk(i, at_z, at_y):
        return parts[i].at[pl.ds(pl.multiple_of((at_z * RAILS + at_y) * rows, rows), rows)]

    def swap(i, s):
        return copy_to(
            chunk(i, order[s], 1 - y),
            y_buf.at[i, order[s]],
            y_send.at[i, s],
            y_recv.at[i, s],
            other,
        )

    def upward(i, at):
        return copy_to(
            chunk(i, at, y), z_buf.at[i, at], up_send.at[i, at], up_recv.at[i, at], above
        )

    def downward(i, at, slot):
        return copy_to(
            chunk(i, at, y), z_buf.at[i, slot], down_send.at[i, at], down_recv.at[i, at], below
        )

    def down_slot(at, owner_z):
        return jnp.where(at == owner_z, depth, at)

    def scatter_step(i, s):
        at = order[s]
        swap(i, s).wait_recv()
        mine = chunk(i, at, y)
        add(mine, mine, y_buf.at[i, at])

        @pl.when((at >= z) & has_below)
        def _():
            upward(i, at).wait_recv()
            add(mine, mine, z_buf.at[i, at])

        @pl.when((at <= z) & has_above)
        def _():
            slot = down_slot(at, z)
            downward(i, at, slot).wait_recv()
            add(mine, mine, z_buf.at[i, slot])

        pl.when(at > z)(lambda: upward(i, at).start())
        pl.when(at < z)(lambda: downward(i, at, down_slot(at, z - 1)).start())

    results = (part_out, back_out)

    def scatter_out(i):
        return pltpu.make_async_copy(chunk(i, z, y), results[i], result_sem.at[i])

    for s in range(depth):
        swap(0, s).start()

    out_to_core.wait_recv()

    @pl.loop(0, group)
    def _(n):
        out_core[n] = (
            out_core[n].astype(f32)
            + out_grad[n, pl.ds(pl.multiple_of(core * half, half), half), :].astype(f32)
        ).astype(bf16)

    my_cols = pl.ds(pl.multiple_of(pair_of(ctx, group) * head_cols, head_cols), head_cols)

    def out_block(n):
        owner = lax.rem(ctx + n, group)
        return copy_to(
            out_core.at[owner],
            out_rows.at[:, my_cols],
            block_send.at[n],
            block_recv.at[n],
            (dp, owner),
        )

    for n in range(1, group):
        out_block(n).start()
    own_block = pltpu.make_async_copy(out_core.at[ctx], out_rows.at[:, my_cols], block_send.at[0])
    own_block.start()

    again = pltpu.make_async_copy(pairs, g_buf, sum_sem.at[0])
    again.start()

    def qkv_half(t, which):
        start = pl.multiple_of(t * 2 * half + which * half, half)
        return qkv_grad.at[pl.ds(start, half)]

    def to_core(t):
        return copy_to(
            qkv_half(t, 1 - core), qkv_core.at[t], core_send.at[t], core_recv.at[t], sibling
        )

    def across_x(t):
        source = qkv_half(t, core) if t < core_tiles else out_rows
        return copy_to(source, from_x.at[t], x_send.at[t], x_recv.at[t], across)

    spots = (
        [(down_out, 2 * half * t) for t in range(pair_tiles // 2)]
        + [(up_out, 2 * half * t) for t in range(pair_tiles // 2)]
        + [(qkv_out, 2 * half * t) for t in range(core_tiles)]
        + [(out_out, 0)]
    )
    def total_of(t):
        return pairs_x.at[t] if t < pair_tiles else from_x.at[t - pair_tiles]

    def spot(t, which):
        array, first = spots[t]
        return array.at[pl.ds(pl.multiple_of(first + which * half, half), half)]

    def keep(t):
        return pltpu.make_async_copy(total_of(t), spot(t, core), keep_sem.at[t])

    def finish(t, which):
        return copy_to(total_of(t), spot(t, which), done_send.at[t], done_recv.at[t], sibling)

    def x_sum(t):
        total = total_of(t)
        if t < pair_tiles:
            if t >= early:
                pair_x(t).wait_recv()
            add(total, total, g_buf.at[pl.ds(t * half, half)])
        else:
            n = t - pair_tiles
            across_x(n).wait_recv()
            add(total, total, qkv_half(n, core) if n < core_tiles else out_rows)
        keep(t).start()
        finish(t, core).start()

    loads[9].wait()
    again.wait()
    x_sum(0)
    for j in range(3):
        here, remote, local = to_owner(j)
        pl.when(here)(lambda local=local: local.wait())
        source = pair_of(lax.rem(3 * ctx + j, group), group)
        arriving = copy_to(
            returns.at[0], returned.at[j], head_send.at[0], head_recv.at[j], other
        )
        pl.when(source != ctx)(lambda arriving=arriving: arriving.wait_recv())
    for n in (5, 6, 7):
        loads[n].wait()
    sums[...] = jnp.zeros_like(sums)

    @pl.loop(0, tokens // tall)
    def _(n):
        at = pl.ds(pl.multiple_of(n * tall, tall), tall)

        @pl.loop(0, columns // wide)
        def _(m):
            cols = pl.ds(pl.multiple_of(m * wide, wide), wide)
            entry = dot_nn(returned[0, at, :], w_qkv[0:head_cols, cols])
            for j in range(1, 3):
                entry += dot_nn(
                    returned[j, at, :], w_qkv[j * head_cols : (j + 1) * head_cols, cols]
                )
            normed = (h_buf[at, cols].astype(f32) - tables[3, at, 0:1]) * tables[3, at, 1:2]
            sums[0:1, cols] += jnp.sum(entry * normed, axis=0, keepdims=True)
            sums[1:2, cols] += jnp.sum(entry, axis=0, keepdims=True)
            back[at, cols] = (back[at, cols].astype(f32) + entry * norms[0:1, cols]).astype(bf16)

    stages = (sibling, other, near, far, across)

    def exchange(n):
        return copy_to(
            vec_buf.at[2 * n], vec_buf.at[2 * n + 1], vec_send.at[n], vec_recv.at[n], stages[n]
        )

    lane_cols = vec_buf.shape[2]

    def place_vector(at, values):
        for n in range(values.shape[1] // lane_cols):
            vec_buf[0, pl.ds(at + n, 1), :] = values[:, n * lane_cols : (n + 1) * lane_cols]

    vec_buf[0] = jnp.zeros(vec_buf.shape[1:], f32)
    long = columns // lane_cols
    place_vector(0, sums[0:1, :])
    place_vector(long, sums[1:2, :])
    place_vector(2 * long, mlp_sums[0:1, :])
    place_vector(3 * long, mlp_sums[1:2, :])
    place_vector(4 * long, local_sums[...])
    each = head_cols // lane_cols
    for j in range(3):
        place_vector(
            5 * long + (3 * ctx + j) * each,
            jnp.sum(returned[j].astype(f32), axis=0, keepdims=True),
        )
    place_vector(
        5 * long + 3 * group * each + ctx * (up_sums.shape[1] // lane_cols), up_sums[...]
    )
    exchange(0).start()

    def vector_step(n):
        exchange(n).wait_recv()
        total = vec_buf[2 * n] + vec_buf[2 * n + 1]
        if n + 1 < len(stages):
            vec_buf[2 * n + 2] = total
            exchange(n + 1).start()
        else:
            vectors_out[...] = total

    vector_step(0)
    for s in range(depth):
        swap(1, s).start()

    loads[8].wait()
    for t in range(core_tiles):

        @pl.loop(0, columns // (2 * wide))
        def _(m):
            cols = pl.ds(pl.multiple_of(m * 2 * wide, 2 * wide), 2 * wide)
            qkv_grad[pl.ds(t * 2 * half, 2 * half), cols] = dot_tn(
                returned[t], x_buf[:, cols]
            ).astype(bf16)

        to_core(t).start()

    for t in range(core_tiles):
        to_core(t).wait_recv()
        mine = qkv_half(t, core)
        add(mine, mine, qkv_core.at[t])
        across_x(t).start()
    stats_out[...] = tables[3, pl.ds(pl.multiple_of(ctx * rows, rows), rows), :]
    for s in range(depth):
        scatter_step(0, s)
        if s == 0:
            x_sum(1)
            x_sum(2)
        x_sum(3 + s)
    scatter_out(0).start()
    own_block.wait()
    for n in range(1, group):
        source = lax.rem(ctx + group - n, group)
        theirs = pl.ds(
            pl.multiple_of(pair_of(source, group) * head_cols, head_cols), head_cols
        )
        copy_to(
            out_core.at[ctx], out_rows.at[:, theirs], block_send.at[n], block_recv.at[n], other
        ).wait_recv()
    across_x(core_tiles).start()
    vector_step(1)
    x_sum(7)
    scatter_step(1, 0)
    vector_step(2)
    x_sum(pair_tiles)
    scatter_step(1, 1)
    vector_step(3)
    x_sum(pair_tiles + 1)
    scatter_step(1, 2)
    x_sum(pair_tiles + 2)
    scatter_step(1, 3)
    scatter_out(1).start()
    x_sum(pair_tiles + 3)
    vector_step(4)

    for j in range(3):
        here, remote, local = to_owner(j)
        pl.when(jnp.logical_not(here))(lambda remote=remote: remote.wait_send())
    for n in range(1, group):
        out_block(n).wait_send()
    out_to_core.wait_send()
    for t in range(core_tiles):
        to_core(t).wait_send()
    for t in range(core_tiles + 1):
        across_x(t).wait_send()
    for t in range(early, pair_tiles):
        pair_x(t).wait_send()
    for t in range(len(spots)):
        keep(t).wait()
        finish(t, core).wait_send()
        finish(t, 1 - core).wait_recv()
    for n in range(len(stages)):
        exchange(n).wait_send()
    for i in range(2):
        scatter_out(i).wait()
        for s in range(depth):
            swap(i, s).wait_send()
            at = order[s]
            pl.when(at > z)(lambda i=i, at=at: upward(i, at).wait_send())
            pl.when(at < z)(
                lambda i=i, at=at: downward(i, at, down_slot(at, z - 1)).wait_send()
            )


def tail_pass(
    group,
    pairs,
    arrived,
    grad_all,
    w_cols,
    part,
    back,
    x_attn,
    w_qkv,
    hidden_all,
    tables,
    early,
    norms,
    mlp_sums,
    up_sums,
    local_sums,
    seg_len,
    seg_parent,
):
    tokens, columns = hidden_all.shape
    depth = group // RAILS
    rows = tokens // group
    head_cols = arrived.shape[2]
    units = up_sums.shape[1]
    half = 128
    pair_tiles = pairs.shape[0] // half
    core_tiles = w_qkv.shape[0] // (2 * half)
    lane_cols = 256
    vectors = (5 * columns + 3 * columns + group * units) // lane_cols
    sems = pltpu.SemaphoreType.DMA
    shape = jax.ShapeDtypeStruct
    vmem = pltpu.VMEM
    anywhere = pl.BlockSpec(memory_space=pl.ANY)
    small = pl.BlockSpec(memory_space=pltpu.VMEM)
    smem = pl.BlockSpec(memory_space=pltpu.SMEM)
    whole = vmem((tokens, columns), bf16)
    every = pair_tiles + core_tiles + 1
    return pl.pallas_call(
        functools.partial(tail_kernel, group),
        out_shape=(
            shape((rows, columns), bf16),
            shape((rows, columns), bf16),
            shape((units, columns), bf16),
            shape((units, columns), bf16),
            shape((2 * half, columns), bf16),
            shape(w_qkv.shape, bf16),
            shape((vectors, lane_cols), f32),
            shape((rows, HEAD_DIM), f32),
        ),
        in_specs=[anywhere] * 11 + [small] * 4 + [smem] * 2,
        out_specs=[anywhere] * 6 + [small] * 2,
        scratch_shapes=[
            vmem(arrived.shape, bf16),
            whole,
            vmem(w_cols.shape, bf16),
            whole,
            whole,
            whole,
            vmem(w_qkv.shape, bf16),
            whole,
            vmem(tables.shape, f32),
            vmem((tokens, head_cols), bf16),
            vmem((tokens, head_cols), bf16),
            vmem(arrived.shape, bf16),
            vmem(arrived.shape, bf16),
            vmem((2, depth, rows, columns), bf16),
            vmem((2, depth + 1, rows, columns), bf16),
            vmem((group, 2 * half, head_cols), bf16),
            vmem(w_qkv.shape, bf16),
            vmem((core_tiles, half, columns), bf16),
            vmem((group, half, head_cols), bf16),
            vmem((half, columns), bf16),
            vmem((core_tiles + 1, half, columns), bf16),
            vmem((pair_tiles, half, columns), bf16),
            vmem((tokens, HEAD_DIM), f32),
            vmem((tokens, HEAD_DIM), f32),
            vmem((2, columns), f32),
            vmem((10, vectors, lane_cols), f32),
            sems((10,)),
        ]
        + [sems((2, depth))] * 6
        + [sems((2,)), sems((3,)), sems((3,)), sems((pair_tiles,)), sems((pair_tiles,))]
        + [sems((core_tiles + 1,))] * 2
        + [sems((group,))] * 2
        + [sems((core_tiles + 1,))] * 2
        + [sems((every,))] * 3
        + [sems((5,))] * 2
        + [sems((1,))],
        compiler_params=pltpu.CompilerParams(
            collective_id=1, has_side_effects=True, vmem_limit_bytes=62 * 2**20
        ),
        name="tail_pass",
    )(
        pairs,
        arrived,
        grad_all,
        w_cols,
        part,
        back,
        x_attn,
        w_qkv,
        hidden_all,
        tables,
        early,
        norms,
        mlp_sums,
        up_sums,
        local_sums,
        seg_len,
        seg_parent,
    )


def finish_kernel(*refs):
    grads, (hidden, grad, summed, w_sum, stats, norms, vectors) = refs[:4], refs[4:11]
    outs, (hidden_out, grad_in), vector_outs = refs[11:15], refs[15:17], refs[17:25]
    narrow, wide, in_sem, out_sem = refs[25:]
    tall = narrow.shape[1]
    tiles = [(n, m) for n in range(4) for m in range(grads[n].shape[0] // tall)]

    def fetch(t):
        n, m = tiles[t]
        return pltpu.make_async_copy(
            grads[n].at[pl.ds(m * tall, tall)], narrow.at[t], in_sem.at[t]
        )

    def store(t):
        n, m = tiles[t]
        return pltpu.make_async_copy(wide.at[t], outs[n].at[pl.ds(m * tall, tall)], out_sem.at[t])

    for t in range(len(tiles)):
        fetch(t).start()
    rows = 32
    for t in range(len(tiles)):
        fetch(t).wait()

        @pl.loop(0, tall // rows)
        def _(n):
            at = pl.ds(pl.multiple_of(n * rows, rows), rows)
            wide[t, at, :] = narrow[t, at, :].astype(f32)

        store(t).start()

    @pl.loop(0, hidden.shape[0] // rows)
    def _(n):
        at = pl.ds(pl.multiple_of(n * rows, rows), rows)
        values = hidden[at, :].astype(f32)
        hidden_out[at, :] = (
            values + summed[at, :].astype(f32) + norms[4:5, :] + norms[5:6, :]
        ).astype(bf16)
        rstd = stats[at, 1:2]
        normed = (values - stats[at, 0:1]) * rstd
        back = w_sum[at, :].astype(f32)
        along = jnp.mean(back * normed, axis=1, keepdims=True)
        grad_in[at, :] = (
            grad[at, :].astype(f32)
            + (back - jnp.mean(back, axis=1, keepdims=True) - normed * along) * rstd
        )

    lane_cols = vectors.shape[1]
    places = [0, 1, 2, 3, 4, 4, 5, 8]
    each = hidden.shape[1] // lane_cols
    for out, place_of in zip(vector_outs, places):
        for n in range(out.shape[0] // lane_cols):
            out[pl.ds(n * lane_cols, lane_cols)] = vectors[place_of * each + n, :]
    for t in range(len(tiles)):
        store(t).wait()


def finish_pass(down, up, qkv, out, hidden, grad, summed, w_sum, stats, norms, vectors):
    tall = 256
    columns = hidden.shape[1]
    grads = (down, up, qkv, out)
    tiles = sum(array.shape[0] for array in grads) // tall
    shape = jax.ShapeDtypeStruct
    anywhere = pl.BlockSpec(memory_space=pl.ANY)
    vmem = pl.BlockSpec(memory_space=pltpu.VMEM)
    lengths = [columns] * 6 + [3 * columns, vectors.size - 8 * columns]
    return pl.pallas_call(
        finish_kernel,
        out_shape=[shape(array.shape, f32) for array in grads]
        + [shape(hidden.shape, bf16), shape(hidden.shape, f32)]
        + [shape((length,), f32) for length in lengths],
        in_specs=[anywhere] * 4 + [vmem] * 7,
        out_specs=[anywhere] * 4 + [vmem] * 10,
        scratch_shapes=[
            pltpu.VMEM((tiles, tall, columns), bf16),
            pltpu.VMEM((tiles, tall, columns), f32),
            pltpu.SemaphoreType.DMA((tiles,)),
            pltpu.SemaphoreType.DMA((tiles,)),
        ],
        compiler_params=pltpu.CompilerParams(vmem_limit_bytes=56 * 2**20),
        name="finish_pass",
    )(*grads, hidden, grad, summed, w_sum, stats, norms, vectors)


def body(
    hidden_in,
    grad_out,
    seg_len,
    seg_parent,
    gain_attn,
    shift_attn,
    w_qkv,
    bias_qkv,
    w_out,
    bias_out,
    gain_mlp,
    shift_mlp,
    w_up,
    bias_up,
    w_down,
    bias_down,
):
    group = lax.axis_size("ctx")
    head_cols = HEADS // group * HEAD_DIM
    vectors = (
        gain_attn,
        shift_attn,
        gain_mlp,
        shift_mlp,
        bias_out,
        bias_down,
        bias_qkv,
        bias_up,
    )
    (
        hidden_all,
        grad_all,
        x_attn,
        arrived,
        mlp_part,
        mlp_back,
        pairs,
        early,
        w_cols,
        tables,
        mlp_sums,
        up_sums,
        local_sums,
        norms,
    ) = layer_pass(
        group,
        hidden_in[0],
        grad_out[0],
        w_up,
        w_down,
        w_qkv,
        w_out,
        vectors,
        seg_len,
        seg_parent,
    )
    summed, w_sum, down_grad, up_grad, out_grad, qkv_grad, vectors, stats = tail_pass(
        group,
        pairs,
        arrived,
        grad_all,
        w_cols.reshape(D, head_cols),
        mlp_part,
        mlp_back,
        x_attn,
        w_qkv,
        hidden_all,
        tables,
        early,
        norms,
        mlp_sums,
        up_sums,
        local_sums,
        seg_len,
        seg_parent,
    )
    (
        down_grad,
        up_grad,
        qkv_grad,
        out_grad,
        hidden_out,
        grad_in,
        gain_grad_a,
        shift_grad_a,
        gain_grad_m,
        shift_grad_m,
        out_bias_grad,
        down_bias_grad,
        qkv_bias_grad,
        up_bias_grad,
    ) = finish_pass(
        down_grad,
        up_grad,
        qkv_grad,
        out_grad,
        hidden_in[0],
        grad_out[0],
        summed,
        w_sum,
        stats,
        norms,
        vectors,
    )
    return (
        hidden_out[None],
        grad_in[None],
        gain_grad_a,
        shift_grad_a,
        qkv_grad,
        qkv_bias_grad,
        out_grad,
        out_bias_grad,
        gain_grad_m,
        shift_grad_m,
        up_grad,
        up_bias_grad,
        down_grad,
        down_bias_grad,
    )


block_limit = 512


def tree_tables(seg_len, seg_parent):
    seg_count = seg_len.shape[0]
    labels = jnp.arange(seg_count, dtype=jnp.int32)
    earlier = labels[:, None] > labels[None, :]
    seg_starts = jnp.sum(jnp.where(earlier, seg_len[None, :], 0), axis=1)
    seg_ends = seg_starts + seg_len
    parent_hit = seg_parent[:, None] == labels[None, :]
    grand_parent = jnp.sum(jnp.where(parent_hit, seg_parent[None, :], 0), axis=1)
    itself = labels[:, None] == labels[None, :]
    ancestor = itself | parent_hit | (grand_parent[:, None] == labels[None, :])
    path_start = jnp.sum(jnp.where(ancestor & jnp.logical_not(itself), seg_len[None, :], 0), axis=1)
    return (seg_ends, seg_starts, ancestor, path_start)


def rotary_tables(path_pos):
    half_dim = ROT_DIM // 2
    inverse = jnp.power(10000.0, -2.0 * jnp.arange(half_dim, dtype=jnp.float32) / ROT_DIM)
    angles = path_pos.astype(jnp.float32)[:, None] * inverse[None, :]
    angles = jnp.concatenate([angles, angles], axis=1)
    return (jnp.cos(angles), jnp.sin(angles))


def rotate(head_values, cosine, sine):
    half_dim = ROT_DIM // 2
    turned = head_values[..., :ROT_DIM]
    swapped = jnp.concatenate([-turned[..., half_dim:], turned[..., :half_dim]], axis=-1)
    mixed = turned * cosine[:, None, :] + swapped * sine[:, None, :]
    return jnp.concatenate([mixed, head_values[..., ROT_DIM:]], axis=-1)


def gelu_slope(pre_act):
    normal_cdf = 0.5 * (1.0 + lax.erf(pre_act / math.sqrt(2.0)))
    return normal_cdf + pre_act * jnp.exp(-0.5 * pre_act * pre_act) / math.sqrt(2.0 * math.pi)


def layer_norm(values, gain_vec, shift_vec):
    average = jnp.mean(values, axis=-1, keepdims=True)
    centred = values - average
    spread = jnp.mean(centred * centred, axis=-1, keepdims=True)
    return centred * lax.rsqrt(spread + norm_eps) * gain_vec + shift_vec


def segment_hot(row_ids, seg_ends):
    seg_index = jnp.sum((row_ids[:, None] >= seg_ends[None, :]).astype(jnp.int32), axis=1)
    labels = jnp.arange(seg_ends.shape[0], dtype=jnp.int32)
    return (seg_index[:, None] == labels[None, :]).astype(jnp.float32)


def row_lookup(row_ids, seg_ends, ancestor_f):
    row_hot = segment_hot(row_ids, seg_ends)
    return (row_hot, jnp.dot(row_hot, ancestor_f))


def permitted(query_ids, query_reach, key_ids, key_hot):
    linked = jnp.dot(query_reach, key_hot.T) > 0.5
    return linked & (key_ids[None, :] <= query_ids[:, None])


def inner_block(row_count):
    block_rows = row_count
    while block_rows > block_limit and block_rows % 2 == 0:
        block_rows = block_rows // 2
    return block_rows


def gather_body(
    hidden_in,
    grad_out,
    seg_len,
    seg_parent,
    gain_attn,
    shift_attn,
    w_qkv,
    bias_qkv,
    w_out,
    bias_out,
    gain_mlp,
    shift_mlp,
    w_up,
    bias_up,
    w_down,
    bias_down,
):
    local_rows = hidden_in.shape[1]
    scale_factor = 1.0 / math.sqrt(HEAD_DIM)
    head_shape = (local_rows, HEADS, HEAD_DIM)
    seg_ends, seg_starts, ancestor, path_start = tree_tables(seg_len[0], seg_parent[0])
    ancestor_f = ancestor.astype(jnp.float32)
    my_ids = lax.axis_index("ctx") * local_rows + jnp.arange(local_rows, dtype=jnp.int32)
    my_hot, my_reach = row_lookup(my_ids, seg_ends, ancestor_f)
    shift_table = path_start - seg_starts
    path_pos = my_ids + jnp.sum(my_hot.astype(jnp.int32) * shift_table[None, :], axis=1)
    cosine, sine = rotary_tables(path_pos)
    inputs_f = hidden_in[0].astype(jnp.float32)
    gain_a = gain_attn.astype(jnp.float32)
    shift_a = shift_attn.astype(jnp.float32)
    gain_m = gain_mlp.astype(jnp.float32)
    shift_m = shift_mlp.astype(jnp.float32)
    bias_up_f = bias_up.astype(jnp.float32)
    x_attn = layer_norm(inputs_f, gain_a, shift_a).astype(jnp.bfloat16)
    x_mlp = layer_norm(inputs_f, gain_m, shift_m).astype(jnp.bfloat16)
    qkv = jnp.einsum(
        "td,nd->tn",
        x_attn,
        lax.all_gather(w_qkv, "ctx", axis=0, tiled=True),
        preferred_element_type=jnp.float32,
    ) + bias_qkv.astype(jnp.float32)
    queries = rotate(qkv[:, :D].reshape(head_shape), cosine, sine).astype(jnp.bfloat16)
    keys_heads = rotate(qkv[:, D : 2 * D].reshape(head_shape), cosine, sine).astype(jnp.bfloat16)
    values_flat = qkv[:, 2 * D :].astype(jnp.bfloat16)
    values_heads = values_flat.reshape(head_shape)
    keys_flat = keys_heads.reshape(local_rows, D)
    queries_flat = queries.reshape(local_rows, D)

    def split_blocks(shard_pieces):
        row_count = shard_pieces[0].shape[0]
        block_rows = inner_block(row_count)
        block_count = row_count // block_rows
        shaped = tuple(
            (member.reshape(block_count, block_rows, HEADS, HEAD_DIM) for member in shard_pieces)
        )
        starts = block_rows * jnp.arange(block_count, dtype=jnp.int32)
        return shaped + (starts,)

    def attend_block(fold_state, block_items):
        key_block, value_block, block_start = block_items
        block_rows = key_block.shape[0]
        key_ids = block_start + jnp.arange(block_rows, dtype=jnp.int32)
        allowed = permitted(my_ids, my_reach, key_ids, segment_hot(key_ids, seg_ends))
        row_top, row_total, partial_value = fold_state
        scores = (
            jnp.einsum("qhd,khd->qhk", queries, key_block, preferred_element_type=jnp.float32)
            * scale_factor
        )
        scores = jnp.where(allowed[:, None, :], scores, masked_score)
        new_top = jnp.maximum(row_top, jnp.max(scores, axis=-1))
        factor = jnp.exp(row_top - new_top)
        weights = jnp.exp(scores - new_top[:, :, None])
        row_total = row_total * factor + jnp.sum(weights, axis=-1)
        partial_value = partial_value * factor[:, :, None] + jnp.einsum(
            "qhk,khd->qhd",
            weights.astype(jnp.bfloat16),
            value_block,
            preferred_element_type=jnp.float32,
        )
        fold_state = (new_top, row_total, partial_value)
        return (fold_state, None)

    start_state = (
        jnp.full((local_rows, HEADS), masked_score, jnp.float32),
        jnp.zeros((local_rows, HEADS), jnp.float32),
        jnp.zeros(head_shape, jnp.float32),
    )
    row_top, row_total, partial_value = lax.scan(
        attend_block,
        start_state,
        split_blocks(
            (
                lax.all_gather(keys_flat, "ctx", axis=0, tiled=True),
                lax.all_gather(values_flat, "ctx", axis=0, tiled=True),
            )
        ),
    )[0]
    log_total = row_top + jnp.log(row_total)
    attended_f = partial_value / row_total[:, :, None]
    attended = attended_f.reshape(local_rows, D).astype(jnp.bfloat16)
    attn_proj = jnp.einsum(
        "td,nd->tn",
        attended,
        lax.all_gather(w_out, "ctx", axis=0, tiled=True),
        preferred_element_type=jnp.float32,
    )

    def mlp_pre(up_rows):
        return (
            jnp.einsum("td,nd->tn", x_mlp, up_rows, preferred_element_type=jnp.float32) + bias_up_f
        )

    up_rows = lax.all_gather(w_up, "ctx", axis=0, tiled=True)
    down_rows = lax.all_gather(w_down, "ctx", axis=0, tiled=True)
    activated = jax.nn.gelu(mlp_pre(up_rows), approximate=False).astype(jnp.bfloat16)
    mlp_sum = jnp.dot(activated, down_rows, preferred_element_type=jnp.float32)
    bias_out_f = bias_out.astype(jnp.float32)
    bias_down_f = bias_down.astype(jnp.float32)
    hidden_out = (inputs_f + attn_proj + bias_out_f + mlp_sum + bias_down_f).astype(jnp.bfloat16)
    grad_b = grad_out[0]
    grad_f = grad_b.astype(jnp.float32)
    up_rows = lax.all_gather(w_up, "ctx", axis=0, tiled=True)
    down_rows = lax.all_gather(w_down, "ctx", axis=0, tiled=True)
    pre_act = mlp_pre(up_rows)
    activated = jax.nn.gelu(pre_act, approximate=False).astype(jnp.bfloat16)
    act_grad = jnp.einsum("td,nd->tn", grad_b, down_rows, preferred_element_type=jnp.float32)
    pre_grad = (act_grad * gelu_slope(pre_act)).astype(jnp.bfloat16)
    input_grad = jnp.dot(pre_grad, up_rows, preferred_element_type=jnp.float32)
    act_all = activated
    pre_grad_all = pre_grad
    act_all, pre_grad_all, mlp_in_grad = (act_all, pre_grad_all, input_grad)
    attended_grad = jnp.dot(
        grad_b, lax.all_gather(w_out, "ctx", axis=0, tiled=True), preferred_element_type=jnp.float32
    ).astype(jnp.bfloat16)
    attended_grad_heads = attended_grad.reshape(head_shape)
    row_delta = jnp.sum(attended_grad_heads.astype(jnp.float32) * attended_f, axis=-1)
    all_log_total, all_delta = (
        lax.all_gather(log_total, "ctx", axis=0, tiled=True),
        lax.all_gather(row_delta, "ctx", axis=0, tiled=True),
    )

    def back_block(fold_state, block_items):
        key_block, value_block, query_block, grad_block, block_start = block_items
        block_rows = key_block.shape[0]
        other_ids = block_start + jnp.arange(block_rows, dtype=jnp.int32)
        other_hot, other_reach = row_lookup(other_ids, seg_ends, ancestor_f)
        allowed_in = permitted(my_ids, my_reach, other_ids, other_hot)
        allowed_out = permitted(other_ids, other_reach, my_ids, my_hot)
        other_log = lax.dynamic_slice_in_dim(all_log_total, block_start, block_rows, 0)
        other_delta = lax.dynamic_slice_in_dim(all_delta, block_start, block_rows, 0)
        query_grad, key_grad, value_grad = fold_state
        scores = (
            jnp.einsum("qhd,khd->qhk", queries, key_block, preferred_element_type=jnp.float32)
            * scale_factor
        )
        scores = jnp.where(allowed_in[:, None, :], scores, masked_score)
        prob_mass = jnp.exp(scores - log_total[:, :, None])
        prob_grad = jnp.einsum(
            "qhd,khd->qhk", attended_grad_heads, value_block, preferred_element_type=jnp.float32
        )
        score_grad = (prob_mass * (prob_grad - row_delta[:, :, None])).astype(jnp.bfloat16)
        query_grad = (
            query_grad
            + jnp.einsum("qhk,khd->qhd", score_grad, key_block, preferred_element_type=jnp.float32)
            * scale_factor
        )
        outgoing_key_grad = key_grad
        outgoing_value_grad = value_grad
        scores = (
            jnp.einsum("qhd,khd->qhk", query_block, keys_heads, preferred_element_type=jnp.float32)
            * scale_factor
        )
        scores = jnp.where(allowed_out[:, None, :], scores, masked_score)
        prob_mass = jnp.exp(scores - other_log[:, :, None])
        outgoing_value_grad = outgoing_value_grad + jnp.einsum(
            "qhk,qhd->khd",
            prob_mass.astype(jnp.bfloat16),
            grad_block,
            preferred_element_type=jnp.float32,
        )
        prob_grad = jnp.einsum(
            "qhd,khd->qhk", grad_block, values_heads, preferred_element_type=jnp.float32
        )
        score_grad = (prob_mass * (prob_grad - other_delta[:, :, None])).astype(jnp.bfloat16)
        outgoing_key_grad = (
            outgoing_key_grad
            + jnp.einsum(
                "qhk,qhd->khd", score_grad, query_block, preferred_element_type=jnp.float32
            )
            * scale_factor
        )
        fold_state = (query_grad, outgoing_key_grad, outgoing_value_grad)
        return (fold_state, None)

    zero_heads = jnp.zeros(head_shape, jnp.float32)
    query_grad, key_grad, value_grad = lax.scan(
        back_block,
        (zero_heads, zero_heads, zero_heads),
        split_blocks(
            (
                lax.all_gather(keys_flat, "ctx", axis=0, tiled=True),
                lax.all_gather(values_flat, "ctx", axis=0, tiled=True),
                lax.all_gather(queries_flat, "ctx", axis=0, tiled=True),
                lax.all_gather(attended_grad, "ctx", axis=0, tiled=True),
            )
        ),
    )[0]

    def turn(head_values):
        return rotate(head_values, cosine, sine)

    unturn = jax.vjp(turn, zero_heads)[1]
    qkv_grad = jnp.concatenate(
        [
            unturn(query_grad)[0].reshape(local_rows, D),
            unturn(key_grad)[0].reshape(local_rows, D),
            value_grad.reshape(local_rows, D),
        ],
        axis=1,
    ).astype(jnp.bfloat16)
    attn_in_grad = jnp.dot(
        qkv_grad,
        lax.all_gather(w_qkv, "ctx", axis=0, tiled=True),
        preferred_element_type=jnp.float32,
    )
    pull_attn = jax.vjp(layer_norm, inputs_f, gain_a, shift_a)[1]
    input_part_a, gain_grad_a, shift_grad_a = pull_attn(attn_in_grad)
    pull_mlp = jax.vjp(layer_norm, inputs_f, gain_m, shift_m)[1]
    input_part_m, gain_grad_m, shift_grad_m = pull_mlp(mlp_in_grad)
    grad_in = (grad_f + input_part_a + input_part_m)[None]
    vector_sums = lax.psum(
        (
            gain_grad_a,
            shift_grad_a,
            gain_grad_m,
            shift_grad_m,
            jnp.sum(qkv_grad, axis=0, dtype=jnp.float32),
            jnp.sum(grad_f, axis=0),
            jnp.sum(pre_grad_all, axis=0, dtype=jnp.float32),
        ),
        ("dp", "ctx"),
    )
    group_count = lax.axis_size("ctx")
    section_rows = (3 * D // group_count, D // group_count, FF // group_count, FF // group_count)
    term_sources = (
        (qkv_grad, x_attn),
        (grad_b, attended),
        (pre_grad_all, x_mlp),
        (act_all, grad_b),
    )
    owner_rows = sum(section_rows)
    blocks = jnp.arange(owner_rows * lax.axis_size("ctx") // owner_rows, dtype=jnp.int32)
    parts_list = []
    for (column_source, other_side), full_rows in zip(term_sources, section_rows):
        sub_rows = full_rows // 1
        column_ids = (
            blocks[:, None] * sub_rows + jnp.arange(sub_rows, dtype=jnp.int32)[None, :]
        ).reshape(-1)
        columns = jnp.take(column_source, column_ids, axis=1)
        block_term = jnp.einsum(
            "tr,td->rd", columns, other_side, preferred_element_type=jnp.float32
        )
        parts_list.append(block_term.reshape(blocks.shape[0], sub_rows, D))
    owned_term = lax.psum_scatter(
        jnp.concatenate(parts_list, axis=1).reshape(-1, D).astype(jnp.bfloat16),
        "ctx",
        scatter_dimension=0,
        tiled=True,
    ).astype(jnp.float32)
    cut_a = section_rows[0]
    cut_b = cut_a + section_rows[1]
    cut_c = cut_b + section_rows[2]
    weight_grads = (
        lax.psum(owned_term[:cut_a].astype(jnp.bfloat16), "dp").astype(jnp.float32),
        lax.psum(owned_term[cut_a:cut_b].astype(jnp.bfloat16), "dp").astype(jnp.float32),
        lax.psum(owned_term[cut_b:cut_c].astype(jnp.bfloat16), "dp").astype(jnp.float32),
        lax.psum(owned_term[cut_c:].astype(jnp.bfloat16), "dp").astype(jnp.float32),
    )
    return (
        hidden_out[None],
        grad_in,
        vector_sums[0],
        vector_sums[1],
        weight_grads[0],
        vector_sums[4],
        weight_grads[1],
        vector_sums[5],
        vector_sums[2],
        vector_sums[3],
        weight_grads[2],
        vector_sums[6],
        weight_grads[3],
        vector_sums[5],
    )


def solution(mesh):
    token = P("dp", "ctx", None)
    rows = P("ctx", None)
    return jax.shard_map(
        body if HEADS % mesh.shape["ctx"] == 0 else gather_body,
        mesh=mesh,
        in_specs=(
            token,
            token,
            P("dp", None),
            P("dp", None),
            P(),
            P(),
            rows,
            P(),
            rows,
            P(),
            P(),
            P(),
            rows,
            P(),
            rows,
            P(),
        ),
        out_specs=(
            token,
            token,
            P(),
            P(),
            rows,
            P(),
            rows,
            P(),
            P(),
            P(),
            rows,
            P(),
            rows,
            P(),
        ),
        check_vma=False,
    )
```

```python
import functools
import math

import jax
import jax.numpy as jnp
import numpy as np
from jax import lax
from jax.experimental import pallas as pl
from jax.experimental.pallas import tpu as pltpu
from jax.sharding import PartitionSpec as P

D = 2048
HEADS = 16
HEAD_DIM = 128
ROT_DIM = 32
FF = 8192

norm_eps = 1e-05
masked_score = -1e30
f32 = jnp.float32
bf16 = jnp.bfloat16


def dot_nt(a, b):
    return lax.dot_general(a, b, (((1,), (1,)), ((), ())), preferred_element_type=f32)


def dot_nn(a, b):
    return lax.dot_general(a, b, (((1,), (0,)), ((), ())), preferred_element_type=f32)


def dot_tn(a, b):
    return lax.dot_general(a, b, (((0,), (0,)), ((), ())), preferred_element_type=f32)


MESH = pl.DeviceIdType.MESH
RAILS = 2


def place(group):
    dp = lax.axis_index("dp")
    ctx = lax.axis_index("ctx")
    return dp, ctx, ctx // RAILS, ctx % RAILS, group // RAILS


def copy_to(src, dst, send, recv, device):
    return pltpu.make_async_remote_copy(
        src_ref=src,
        dst_ref=dst,
        send_sem=send,
        recv_sem=recv,
        device_id=device,
        device_id_type=MESH,
    )


def signal(device):
    barrier = pltpu.get_barrier_semaphore()
    pl.semaphore_signal(barrier, inc=1, device_id=device, device_id_type=MESH)


def arrive(count):
    pl.semaphore_wait(pltpu.get_barrier_semaphore(), count)


def pair_of(ctx, group):
    if group != 8:
        return ctx
    return ctx + jnp.where(
        (ctx == 1) | (ctx == 4), 2, jnp.where((ctx == 3) | (ctx == 6), -2, 0)
    )


def pair_order(z, depth):
    return [
        z,
        jnp.where(z > 0, z - 1, 1),
        jnp.where(z == depth - 1, 1, jnp.where(z == depth - 2, depth - 1, 2)),
        jnp.where(z < depth // 2, depth - 1, 0),
    ]


def layer_kernel(group, *refs):
    hidden, grad, w_up_in, w_down_in, w_qkv_in, w_out = refs[:6]
    vectors, (inverse, seg_len, seg_parent), refs = refs[6:14], refs[14:17], refs[7:]
    h_out, g_out, x_out, heads_out, part_out, back_out, pairs_out, early_out, cols_out = refs[10:19]
    passing, refs = refs[19], refs[1:]
    tables, sums, bias_sum, local_sum, norms = refs[19:24]
    h_buf, g_buf, w_up, w_down, w_qkv, x_mlp, x_attn, act, slope, pre_grad = refs[24:34]
    heads, part, back, down_grad, up_grad, core_buf, mean, rstd, bias_up, bias_qkv = refs[34:44]
    all_qkv, all_up = refs[44:46]
    refs = refs[2:]
    own_sem, y_send, y_recv, up_send, up_recv, down_send, down_recv = refs[44:51]
    weight_sem, pair_sem, grad_sem, head_send, head_recv = refs[51:56]
    core_send, core_recv, cols_send, cols_recv, early_send, early_recv = refs[56:62]
    pass_send, pass_recv = refs[62:64]
    dp, ctx, z, y, depth = place(group)
    bufs, sources, outs = (h_buf, g_buf), (hidden, grad), (h_out, g_out)
    rows = hidden.shape[0]
    pair_rows = RAILS * rows
    tokens, columns = h_buf.shape
    units = act.shape[1]
    head_cols = heads.shape[2]
    other = (dp, z * RAILS + 1 - y)
    above = (dp, jnp.minimum(z + 1, depth - 1) * RAILS + y)
    below = (dp, jnp.maximum(z - 1, 0) * RAILS + y)
    has_above, has_below = z < depth - 1, z > 0
    order = pair_order(z, depth)

    x, core = dp // 2, dp % 2
    sibling = (x * 2 + 1 - core, ctx)
    across = ((1 - x) * 2 + core, ctx)

    for n in range(1, group):
        signal((dp, lax.rem(ctx + n, group)))
    signal(sibling)
    signal(across)
    arrive(group + 1)

    def chunk(i, at_z, at_y):
        start = pl.multiple_of((at_z * RAILS + at_y) * rows, rows)
        return bufs[i].at[pl.ds(start, rows)]

    def to_other(i, at_z, source=None):
        here = chunk(i, at_z, y)
        return copy_to(
            here if source is None else source, here, y_send.at[i, at_z], y_recv.at[i, at_z], other
        )

    def upward(i, at_z, source=None):
        here = chunk(i, at_z, y)
        return copy_to(
            here if source is None else source,
            here,
            up_send.at[i, at_z],
            up_recv.at[i, at_z],
            above,
        )

    def downward(i, at_z, source=None):
        here = chunk(i, at_z, y)
        return copy_to(
            here if source is None else source,
            here,
            down_send.at[i, at_z],
            down_recv.at[i, at_z],
            below,
        )

    def relay_up(i, k):
        at_z = jnp.maximum(z - k, 0)
        upward(i, at_z).wait_recv()
        pl.when(has_above)(lambda: upward(i, at_z).start())

    def relay_down(i, k):
        at_z = jnp.minimum(z + k, depth - 1)
        downward(i, at_z).wait_recv()
        pl.when(has_below)(lambda: downward(i, at_z).start())

    def turn(n):
        if n < depth:
            pl.when(z >= n)(lambda: relay_up(0, n))
            pl.when(z + n < depth)(lambda: relay_down(0, n))
            to_other(0, order[n]).start()
            pl.when((z == n - 1) & has_above)(lambda: upward(1, z, sources[1]).start())
            pl.when((z == depth - n) & has_below)(lambda: downward(1, z, sources[1]).start())
        for k in range(1, depth):
            pl.when((z == n - k) & (z >= k))(lambda k=k: relay_up(1, k))
            pl.when((depth - 1 - z == n - k) & (z + k < depth))(lambda k=k: relay_down(1, k))
        if n == depth:
            to_other(1, z, sources[1]).start()
        if n > depth:
            to_other(1, order[n - depth]).start()

    def y_arrive(i, s):
        here = chunk(i, order[s], 1 - y)
        copy_to(
            here, here, y_send.at[i, order[s]], y_recv.at[i, order[s]], other
        ).wait_recv()

    def pair_at(s):
        return pl.ds(pl.multiple_of(order[s] * pair_rows, pair_rows), pair_rows)

    def keep(n, s, buf, out):
        at = pair_at(s)
        return pltpu.make_async_copy(buf.at[at], out.at[at], pair_sem.at[n, s])

    own = [pltpu.make_async_copy(sources[i], chunk(i, z, y), own_sem.at[i]) for i in range(2)]
    weights = [
        pltpu.make_async_copy(source, held, weight_sem.at[n])
        for n, (source, held) in enumerate(
            ((w_up_in, w_up), (w_qkv_in, w_qkv), (w_down_in, w_down))
        )
    ]
    own[0].start()
    to_other(0, z, sources[0]).start()
    pl.when(has_above)(lambda: upward(0, z, sources[0]).start())
    pl.when(has_below)(lambda: downward(0, z, sources[0]).start())
    for copy in weights:
        copy.start()
    own[1].start()

    starts, shifts = [], []
    at = jnp.int32(0)
    for n in range(seg_len.shape[1]):
        parent = seg_parent[0, n]
        grand = seg_parent[0, parent]
        before = jnp.where(parent != n, seg_len[0, parent], 0) + jnp.where(
            (grand != n) & (grand != parent), seg_len[0, grand], 0
        )
        starts.append(at)
        shifts.append(before - at)
        at = at + seg_len[0, n]

    turned_half = ROT_DIM // 2

    @pl.loop(0, tokens // rows)
    def _(n):
        at = pl.ds(pl.multiple_of(n * rows, rows), rows)
        token = n * rows + lax.broadcasted_iota(jnp.int32, (turned_half, rows), 1)
        position = token + shifts[0]
        for m in range(1, len(starts)):
            position = position + jnp.where(token >= starts[m], shifts[m] - shifts[m - 1], 0)
        angle = position.astype(f32) * inverse[...]
        cosine, sine = jnp.cos(angle), jnp.sin(angle)
        still = jnp.zeros((HEAD_DIM - ROT_DIM, rows), f32)
        none = jnp.zeros((turned_half, rows), f32)
        tables[0, at, :] = jnp.concatenate([cosine, cosine, still + 1.0], axis=0).T
        tables[1, at, :] = jnp.concatenate([-sine, none, still], axis=0).T
        tables[2, at, :] = jnp.concatenate([none, sine, still], axis=0).T

    sums[...] = jnp.zeros_like(sums)
    bias_sum[...] = jnp.zeros_like(bias_sum)
    for n in range(6):
        norms[n : n + 1, :] = vectors[n][...].astype(f32).reshape(1, columns)
    norms[6:8, :] = jnp.zeros((2, columns), f32)

    def take_mine(target, vector, wide_row):
        wide_row[...] = vector[...].astype(f32).reshape(wide_row.shape)
        size = target.shape[1]
        target[...] = wide_row[:, pl.ds(pl.multiple_of(ctx * size, HEAD_DIM), size)]

    take_mine(bias_qkv, vectors[6], all_qkv)
    take_mine(bias_up, vectors[7], all_up)

    def normalize(s):
        step = 32

        @pl.loop(0, pair_rows // step)
        def _(n):
            at = pl.ds(pl.multiple_of(order[s] * pair_rows + n * step, step), step)
            values = h_buf[at, :].astype(f32)
            average = jnp.mean(values, axis=1, keepdims=True)
            centred = values - average
            spread = lax.rsqrt(jnp.mean(centred * centred, axis=1, keepdims=True) + norm_eps)
            normed = centred * spread
            x_attn[at, :] = (normed * norms[0:1, :] + norms[1:2, :]).astype(bf16)
            x_mlp[at, :] = (normed * norms[2:3, :] + norms[3:4, :]).astype(bf16)
            mean[at, :] = average
            rstd[at, :] = spread
            lane = lax.broadcasted_iota(jnp.int32, (step, HEAD_DIM), 1)
            tables[3, at, :] = jnp.where(lane == 0, average, spread)

    wide = 512

    def feed(s):
        at = pair_at(s)

        @pl.loop(0, units // wide)
        def _(n):
            cols = pl.ds(pl.multiple_of(n * wide, wide), wide)
            pre = dot_nt(x_mlp[at, :], w_up[cols, :]) + bias_up[:, cols]
            normal_cdf = 0.5 * (1.0 + lax.erf(pre * math.sqrt(0.5)))
            act[at, cols] = (pre * normal_cdf).astype(bf16)
            slope[at, cols] = (
                normal_cdf + pre * jnp.exp(-0.5 * pre * pre) * (1.0 / math.sqrt(2.0 * math.pi))
            ).astype(slope.dtype)

    def project(s):
        at = pair_at(s)
        for j in range(3):
            block = pl.ds(j * head_cols, head_cols)
            raw = dot_nt(x_attn[at, :], w_qkv[block, :]) + bias_qkv[:, block]
            turns = lax.div(3 * ctx + j, group) < 2
            for m in range(head_cols // HEAD_DIM):
                one = raw[:, m * HEAD_DIM : (m + 1) * HEAD_DIM]
                turned = (
                    one * tables[0, at, :]
                    + pltpu.roll(one, HEAD_DIM - ROT_DIM // 2, 1) * tables[1, at, :]
                    + pltpu.roll(one, ROT_DIM // 2, 1) * tables[2, at, :]
                )
                heads[j, at, m * HEAD_DIM : (m + 1) * HEAD_DIM] = jnp.where(
                    turns, turned, one
                ).astype(bf16)

    def mix(s):
        at = pair_at(s)

        @pl.loop(0, columns // wide)
        def _(n):
            cols = pl.ds(pl.multiple_of(n * wide, wide), wide)
            part[at, cols] = dot_nn(act[at, :], w_down[:, cols]).astype(bf16)

    def back_feed(s):
        at = pair_at(s)

        @pl.loop(0, units // wide)
        def _(n):
            cols = pl.ds(pl.multiple_of(n * wide, wide), wide)
            rounded = (
                dot_nt(g_buf[at, :], w_down[cols, :]) * slope[at, cols].astype(f32)
            ).astype(bf16)
            pre_grad[at, cols] = rounded
            bias_sum[:, cols] += jnp.sum(rounded.astype(f32), axis=0, keepdims=True)

        @pl.loop(0, columns // wide)
        def _(n):
            cols = pl.ds(pl.multiple_of(n * wide, wide), wide)
            entry = dot_nn(pre_grad[at, :], w_up[:, cols])
            normed = (h_buf[at, cols].astype(f32) - mean[at, :]) * rstd[at, :]
            sums[0:1, cols] += jnp.sum(entry * normed, axis=0, keepdims=True)
            sums[1:2, cols] += jnp.sum(entry, axis=0, keepdims=True)
            back[at, cols] = (entry * norms[2:3, cols]).astype(bf16)

    def forward(s):
        keep(0, s, h_buf, h_out).start()
        normalize(s)
        keep(1, s, x_attn, x_out).start()
        if s == 0:
            weights[0].wait()
        feed(s)
        if s == 0:
            weights[1].wait()
        project(s)

    def backward(s):
        keep(2, s, g_buf, g_out).start()
        if s == 0:
            weights[2].wait()
        mix(s)
        keep(3, s, part, part_out).start()
        back_feed(s)
        keep(4, s, back, back_out).start()

    tall = 256
    half = core_buf.shape[1]
    tiles = units // tall
    held = (down_grad, up_grad)

    def grad_half(t, which):
        start = pl.multiple_of((t % tiles) * tall + which * half, half)
        return held[t // tiles].at[pl.ds(start, half)]

    def to_core(t):
        return copy_to(
            grad_half(t, 1 - core), core_buf.at[t], core_send.at[t], core_recv.at[t], sibling
        )

    def grad_keep(t):
        return pltpu.make_async_copy(
            grad_half(t, core), pairs_out.at[pl.ds(t * half, half)], grad_sem.at[t]
        )

    def outer(n, left, right, last, ms=range(units // tall)):
        first, second = (pair_at(2), pair_at(3)) if last else (pair_at(0), pair_at(1))
        for m in ms:
            mine = pl.ds(m * tall, tall)

            @pl.loop(0, columns // (2 * wide))
            def _(k):
                cols = pl.ds(pl.multiple_of(k * 2 * wide, 2 * wide), 2 * wide)
                term = dot_tn(left[first, mine], right[first, cols])
                term += dot_tn(left[second, mine], right[second, cols])
                if last:
                    term += held[n][mine, cols].astype(f32)
                held[n][mine, cols] = term.astype(bf16)

            if last:
                to_core(n * tiles + m).start()

    def early_x(t):
        return copy_to(
            grad_half(t, core), early_out.at[t], early_send.at[t], early_recv.at[t], across
        )

    def outer_sum(ts):
        for t in ts:
            to_core(t).wait_recv()
            mine = grad_half(t, core)

            @pl.loop(0, half // 32)
            def _(k):
                at = pl.ds(pl.multiple_of(k * 32, 32), 32)
                mine[at, :] = (mine[at, :].astype(f32) + core_buf[t, at, :].astype(f32)).astype(
                    bf16
                )

            grad_keep(t).start()
            if t < early_out.shape[0]:
                early_x(t).start()

    share = cols_out.shape[2]

    def to_columns(n):
        owner = lax.rem(ctx + n, group)
        block = w_out.at[
            pl.ds(pl.multiple_of(dp * share, share), share),
            pl.ds(pl.multiple_of(pair_of(owner, group) * head_cols, head_cols), head_cols),
        ]
        if n == 0:
            return pltpu.make_async_copy(block, cols_out.at[ctx, dp], cols_send.at[0])
        return copy_to(
            block, cols_out.at[ctx, dp], cols_send.at[n], cols_recv.at[n], (dp, owner)
        )

    def columns_arrive():
        to_columns(0).wait()
        for n in range(1, group):
            source = lax.rem(ctx + group - n, group)
            here = cols_out.at[source, dp]
            copy_to(here, here, cols_send.at[n], cols_recv.at[n], other).wait_recv()

    def columns_core(which):
        here = cols_out.at[:, pl.ds(2 * x + which, 1)]
        return copy_to(here, here, cols_send.at[group], cols_recv.at[group], sibling)

    def columns_x(which):
        here = cols_out.at[:, pl.ds(2 * which, 2)]
        return copy_to(here, here, cols_send.at[group + 1], cols_recv.at[group + 1], across)

    def to_head(j):
        block = 3 * ctx + j
        kind, target = lax.div(block, group), pair_of(lax.rem(block, group), group)
        remote = copy_to(
            heads.at[j], heads_out.at[kind], head_send.at[j], head_recv.at[kind], (dp, target)
        )
        local = pltpu.make_async_copy(heads.at[j], heads_out.at[kind], head_send.at[j])
        return target == ctx, remote, local

    def turns_corner(device, target):
        return (device % RAILS != target % RAILS) & (
            lax.div(device, RAILS) == lax.div(target, RAILS) + 99
        )

    def to_corner(j):
        target = pair_of(lax.rem(3 * ctx + j, group), group)
        middle = (dp, lax.div(target, RAILS) * RAILS + y)
        return copy_to(heads.at[j], passing, head_send.at[j], pass_recv.at[0], middle)

    def send_heads(crossing):
        for j in range(3):
            here, remote, local = to_head(j)
            target = pair_of(lax.rem(3 * ctx + j, group), group)
            corner = turns_corner(ctx, target)
            crosses = (target % RAILS != y) & jnp.logical_not(corner)
            if crossing:
                pl.when(crosses)(lambda remote=remote: remote.start())
            else:
                first = to_corner(j)
                pl.when(here)(lambda local=local: local.start())
                pl.when(corner)(lambda first=first: first.start())
                pl.when(jnp.logical_not(here | crosses | corner))(
                    lambda remote=remote: remote.start()
                )

    def hand_on(act_on):
        partner = ctx + 1 - 2 * y
        for kind in range(3):
            source = lax.div(kind * group + pair_of(partner, group), 3)
            arriving = copy_to(passing, passing, pass_send.at[0], pass_recv.at[0], other)
            onward = copy_to(
                passing, heads_out.at[kind], pass_send.at[0], head_recv.at[kind], other
            )
            pl.when(turns_corner(source, partner))(
                lambda arriving=arriving, onward=onward: act_on(arriving, onward)
            )

    def pass_on(arriving, onward):
        arriving.wait_recv()
        onward.start()

    def head_source(kind):
        return lax.div(kind * group + pair_of(ctx, group), 3)

    turn(1)
    own[0].wait()
    y_arrive(0, 0)
    forward(0)
    turn(2)
    y_arrive(0, 1)
    forward(1)
    turn(3)
    y_arrive(0, 2)
    forward(2)
    turn(4)
    for n in range(group):
        to_columns(n).start()
    y_arrive(0, 3)
    forward(3)
    turn(5)
    send_heads(False)
    own[1].wait()
    y_arrive(1, 0)
    backward(0)
    at = pl.ds(pl.multiple_of(ctx * rows, rows), rows)
    local_sum[...] = jnp.sum(g_buf[at, :].astype(f32), axis=0, keepdims=True)
    turn(6)
    y_arrive(1, 1)
    backward(1)
    turn(7)
    columns_arrive()
    columns_core(core).start()
    outer(0, act, g_buf, False)
    outer(1, pre_grad, x_mlp, False)
    columns_core(1 - core).wait_recv()
    columns_x(x).start()
    y_arrive(1, 2)
    backward(2)
    send_heads(True)
    y_arrive(1, 3)
    early = early_out.shape[0]
    outer(0, act, g_buf, True, range(early + 1))
    outer_sum(range(early))
    outer(0, act, g_buf, True, range(early + 1, tiles))
    backward(3)
    outer_sum(range(early, tiles))
    outer(1, pre_grad, x_mlp, True)
    outer_sum(range(tiles, 2 * tiles))

    for at_z in range(depth):
        to_other(0, at_z).wait_send()
        to_other(1, at_z).wait_send()
        for i in range(2):
            pl.when(has_above & (at_z <= z))(lambda i=i: upward(i, at_z).wait_send())
            pl.when(has_below & (at_z >= z))(lambda i=i: downward(i, at_z).wait_send())
    for j in range(3):
        here, remote, local = to_head(j)
        first = to_corner(j)
        corner = turns_corner(ctx, pair_of(lax.rem(3 * ctx + j, group), group))
        pl.when(here)(lambda local=local: local.wait())
        pl.when(corner)(lambda first=first: first.wait_send())
        pl.when(jnp.logical_not(here | corner))(lambda remote=remote: remote.wait_send())
    for kind in range(3):
        arriving = copy_to(
            heads.at[0], heads_out.at[kind], head_send.at[0], head_recv.at[kind], other
        )
        pl.when(head_source(kind) != ctx)(lambda arriving=arriving: arriving.wait_recv())
    for s in range(4):
        keep(0, s, h_buf, h_out).wait()
        keep(1, s, x_attn, x_out).wait()
        keep(2, s, g_buf, g_out).wait()
        keep(3, s, part, part_out).wait()
        keep(4, s, back, back_out).wait()
    for t in range(2 * tiles):
        to_core(t).wait_send()
        grad_keep(t).wait()
    for n in range(1, group):
        to_columns(n).wait_send()
    for t in range(early):
        early_x(t).wait_send()
        early_x(t).wait_recv()
    columns_core(core).wait_send()
    columns_x(x).wait_send()
    columns_x(1 - x).wait_recv()


def layer_pass(
    group, hidden, grad, w_up, w_down, w_qkv, w_out, vectors, seg_len, seg_parent
):
    rows, columns = hidden.shape
    tokens, units, head_cols = group * rows, w_up.shape[0], w_qkv.shape[0] // 3
    depth = group // RAILS
    inverse = 10000.0 ** (-2.0 * np.arange(ROT_DIM // 2) / ROT_DIM)
    inverse = jnp.asarray(np.broadcast_to(inverse[:, None], (ROT_DIM // 2, rows)), f32)
    early = 1
    sems = pltpu.SemaphoreType.DMA
    shape = jax.ShapeDtypeStruct
    anywhere = pl.BlockSpec(memory_space=pl.ANY)
    vmem = pl.BlockSpec(memory_space=pltpu.VMEM)
    smem = pl.BlockSpec(memory_space=pltpu.SMEM)
    whole = shape((tokens, columns), bf16)
    half = 128
    copies = lax.axis_size("dp")
    return pl.pallas_call(
        functools.partial(layer_kernel, group),
        out_shape=(
            whole,
            whole,
            whole,
            shape((3, tokens, head_cols), bf16),
            whole,
            whole,
            shape((units, columns), bf16),
            shape((early, half, columns), bf16),
            shape((group, copies, columns // group // copies, head_cols), bf16),
            shape((tokens, head_cols), bf16),
            shape((4, tokens, HEAD_DIM), f32),
            shape((2, columns), f32),
            shape((1, units), f32),
            shape((1, columns), f32),
            shape((8, columns), f32),
        ),
        in_specs=[anywhere] * 6 + [vmem] * 9 + [smem] * 2,
        out_specs=[anywhere] * 10 + [vmem] * 5,
        scratch_shapes=[pltpu.VMEM((tokens, columns), bf16)] * 2
        + [pltpu.VMEM((units, columns), bf16)] * 2
        + [pltpu.VMEM((3 * head_cols, columns), bf16)]
        + [pltpu.VMEM((tokens, columns), bf16)] * 2
        + [pltpu.VMEM((tokens, units), bf16)] * 3
        + [pltpu.VMEM((3, tokens, head_cols), bf16)]
        + [pltpu.VMEM((tokens, columns), bf16)] * 2
        + [pltpu.VMEM((units, columns), bf16)] * 2
        + [pltpu.VMEM((units // half, half, columns), bf16)]
        + [pltpu.VMEM((tokens, 1), f32)] * 2
        + [pltpu.VMEM((1, units), f32), pltpu.VMEM((1, 3 * head_cols), f32)]
        + [pltpu.VMEM((1, vector.shape[0]), f32) for vector in vectors[6:]]
        + [sems((2,))]
        + [sems((2, depth))] * 6
        + [sems((3,)), sems((5, 4)), sems((units // half,)), sems((3,)), sems((3,))]
        + [sems((units // half,))] * 2
        + [sems((group + 2,))] * 2
        + [sems((early,))] * 2
        + [sems((1,))] * 2,
        compiler_params=pltpu.CompilerParams(
            collective_id=0, has_side_effects=True, vmem_limit_bytes=62 * 2**20
        ),
        name="layer_pass",
    )(hidden, grad, w_up, w_down, w_qkv, w_out, *vectors, inverse, seg_len, seg_parent)


def tail_kernel(group, *refs):
    pairs, arrived_in, grad_in, w_cols_in, part_in, back_in, x_in, w_qkv_in, hidden_in = refs[:9]
    tables_in, early_in, norms, mlp_sums, up_sums, local_sums, seg_len, seg_parent = refs[9:17]
    part_out, back_out, down_out, up_out, out_out, qkv_out, passing = refs[17:24]
    vectors_out, stats_out = refs[24:26]
    refs = refs[26:]
    arrived, g_buf, w_cols, part, back, x_buf, w_qkv, h_buf, tables = refs[:9]
    att_grad, attended, returns, returned, y_buf, z_buf = refs[9:15]
    out_grad, qkv_grad, qkv_core, out_core, out_rows, from_x, pairs_x, key_acc, value_acc = refs[15:24]
    sums, vec_buf = refs[24:26]
    (
        load_sem,
        y_send,
        y_recv,
        up_send,
        up_recv,
        down_send,
        down_recv,
        result_sem,
        head_send,
        head_recv,
        pair_send,
        pair_recv,
        core_send,
        core_recv,
        block_send,
        block_recv,
        x_send,
        x_recv,
        keep_sem,
        done_send,
        done_recv,
        vec_send,
        vec_recv,
        sum_sem,
        pass_send,
        pass_recv,
    ) = refs[26:]
    dp, ctx, z, y, depth = place(group)
    tokens, columns = g_buf.shape
    rows = tokens // group
    head_cols = attended.shape[1]
    heads = head_cols // HEAD_DIM
    half = qkv_core.shape[1]
    pair_tiles = pairs_x.shape[0]
    x, core = dp // 2, dp % 2
    other = (dp, z * RAILS + 1 - y)
    above = (dp, jnp.minimum(z + 1, depth - 1) * RAILS + y)
    below = (dp, jnp.maximum(z - 1, 0) * RAILS + y)
    sibling = (x * 2 + 1 - core, ctx)
    across = ((1 - x) * 2 + core, ctx)
    near = (dp, (z + 1 - 2 * (z % 2)) * RAILS + y)
    far = (dp, lax.rem(z + 2, depth) * RAILS + y)
    has_above, has_below = z < depth - 1, z > 0

    for n in range(1, group):
        signal((dp, lax.rem(ctx + n, group)))
    signal(sibling)
    signal(across)
    arrive(group + 1)

    def add(target, left, right):
        step = 32

        @pl.loop(0, target.shape[0] // step)
        def _(n):
            at = pl.ds(pl.multiple_of(n * step, step), step)
            target[at, :] = (left[at, :].astype(f32) + right[at, :].astype(f32)).astype(
                target.dtype
            )

    def pair_x(t):
        return copy_to(
            pairs.at[pl.ds(t * half, half)],
            pairs_x.at[t],
            pair_send.at[t],
            pair_recv.at[t],
            across,
        )

    early = early_in.shape[0]
    for t in range(early, pair_tiles):
        pair_x(t).start()
    loads = [
        pltpu.make_async_copy(source, target, load_sem.at[n])
        for n, (source, target) in enumerate(
            (
                (w_cols_in, w_cols),
                (grad_in, g_buf),
                (arrived_in, arrived),
                (tables_in, tables),
                (part_in, part),
                (w_qkv_in, w_qkv),
                (back_in, back),
                (hidden_in, h_buf),
                (x_in, x_buf),
                (early_in, pairs_x.at[pl.ds(0, early)]),
            )
        )
    ]
    for copy in loads:
        copy.start()

    wide = 512
    tall = 256
    scale = 1.0 / math.sqrt(HEAD_DIM)
    loads[0].wait()
    loads[1].wait()

    @pl.loop(0, tokens // tall)
    def _(n):
        at = pl.ds(pl.multiple_of(n * tall, tall), tall)
        att_grad[at, :] = dot_nn(g_buf[at, :], w_cols[...]).astype(bf16)

    starts, reaches = [], []
    at = jnp.int32(0)
    for n in range(seg_len.shape[1]):
        parent = seg_parent[0, n]
        grand = seg_parent[0, parent]
        starts.append(at)
        reaches.append(
            (jnp.int32(1) << n) | (jnp.int32(1) << parent) | (jnp.int32(1) << grand)
        )
        at = at + seg_len[0, n]
    loads[2].wait()
    loads[3].wait()

    def unturn(values, at):
        return (
            values * tables[0, at, :]
            - pltpu.roll(values, HEAD_DIM - ROT_DIM // 2, 1) * tables[1, at, :]
            - pltpu.roll(values, ROT_DIM // 2, 1) * tables[2, at, :]
        )

    for m in range(heads):
        lanes = slice(m * HEAD_DIM, (m + 1) * HEAD_DIM)
        key_acc[...] = jnp.zeros_like(key_acc)
        value_acc[...] = jnp.zeros_like(value_acc)
        for n in range(tokens // tall):
            mine = pl.ds(n * tall, tall)
            seen = (n + 1) * tall
            upto = pl.ds(0, seen)
            token = n * tall + lax.broadcasted_iota(jnp.int32, (tall, 1), 0)
            key = lax.broadcasted_iota(jnp.int32, (1, seen), 1)
            reach = jnp.zeros((tall, 1), jnp.int32) + reaches[0]
            label = jnp.ones((1, seen), jnp.int32)
            for k in range(1, len(starts)):
                reach = jnp.where(token >= starts[k], reaches[k], reach)
                label = jnp.where(key >= starts[k], 1 << k, label)
            allowed = ((reach & label) != 0) & (key <= token)
            query = arrived[0, mine, lanes]
            keys = arrived[1, upto, lanes]
            values = arrived[2, upto, lanes]
            out_grad_rows = att_grad[mine, lanes]
            scores = jnp.where(allowed, dot_nt(query, keys) * scale, masked_score)
            expo = jnp.exp(scores - jnp.max(scores, axis=1, keepdims=True))
            probs = expo * (1.0 / jnp.sum(expo, axis=1, keepdims=True))
            weights = probs.astype(bf16)
            attended[mine, lanes] = dot_nn(weights, values).astype(bf16)
            prob_grad = dot_nt(out_grad_rows, values)
            delta = jnp.sum(probs * prob_grad, axis=1, keepdims=True)
            score_grad = (probs * (prob_grad - delta)).astype(bf16)
            query_grad = dot_nn(score_grad, keys) * scale
            returns[0, mine, lanes] = unturn(query_grad, mine).astype(bf16)
            key_acc[upto, :] += dot_tn(score_grad, query)
            value_acc[upto, :] += dot_tn(weights, out_grad_rows)

        for n in range(tokens // tall):
            mine = pl.ds(n * tall, tall)
            returns[1, mine, lanes] = unturn(key_acc[mine, :] * scale, mine).astype(bf16)
            returns[2, mine, lanes] = value_acc[mine, :].astype(bf16)

    def to_owner(kind):
        block = kind * group + pair_of(ctx, group)
        owner, slot = lax.div(block, 3), lax.rem(block, 3)
        remote = copy_to(
            returns.at[kind], returned.at[slot], head_send.at[kind], head_recv.at[slot], (dp, owner)
        )
        local = pltpu.make_async_copy(returns.at[kind], returned.at[slot], head_send.at[kind])
        return owner == ctx, remote, local

    def turns_corner(device, target):
        return (device % RAILS != target % RAILS) & (
            lax.div(device, RAILS) != lax.div(target, RAILS)
        )

    def owner_of(device, kind):
        block = kind * group + pair_of(device, group)
        return lax.div(block, 3), lax.rem(block, 3)

    def to_corner(kind):
        return copy_to(returns.at[kind], passing, head_send.at[kind], pass_recv.at[0], other)

    def hand_on(act_on):
        partner = ctx + 1 - 2 * y
        for kind in range(3):
            owner, slot = owner_of(partner, kind)
            arriving = copy_to(passing, passing, pass_send.at[0], pass_recv.at[0], other)
            onward = copy_to(
                passing, returned.at[slot], pass_send.at[0], head_recv.at[slot], (dp, owner)
            )
            pl.when(turns_corner(partner, owner))(
                lambda arriving=arriving, onward=onward: act_on(arriving, onward)
            )

    def pass_on(arriving, onward):
        arriving.wait_recv()
        onward.start()

    for kind in range(3):
        here, remote, local = to_owner(kind)
        first = to_corner(kind)
        corner = turns_corner(ctx, owner_of(ctx, kind)[0])
        pl.when(here)(lambda local=local: local.start())
        pl.when(corner)(lambda first=first: first.start())
        pl.when(jnp.logical_not(here | corner))(lambda remote=remote: remote.start())

    @pl.loop(0, group)
    def _(n):
        at = pl.ds(pl.multiple_of(n * head_cols, head_cols), head_cols)
        out_grad[n] = dot_tn(g_buf[:, at], attended[...]).astype(bf16)

    core_tiles = qkv_core.shape[0]
    out_to_core = copy_to(
        out_grad.at[:, pl.ds((1 - core) * half, half)],
        out_core,
        core_send.at[core_tiles],
        core_recv.at[core_tiles],
        sibling,
    )
    out_to_core.start()

    loads[4].wait()

    @pl.loop(0, tokens // tall)
    def _(n):
        at = pl.ds(pl.multiple_of(n * tall, tall), tall)

        @pl.loop(0, columns // wide)
        def _(m):
            cols = pl.ds(pl.multiple_of(m * wide, wide), wide)
            part[at, cols] = (
                part[at, cols].astype(f32) + dot_nt(attended[at, :], w_cols[cols, :])
            ).astype(bf16)

    low = z < depth // 2
    order = [
        jnp.where(low, depth - 1, 0),
        jnp.where(low, depth - 2, 1),
        jnp.where(low, 1 - z, 2 * depth - 3 - z),
        z,
    ]
    parts = (part, back)

    def chunk(i, at_z, at_y):
        return parts[i].at[pl.ds(pl.multiple_of((at_z * RAILS + at_y) * rows, rows), rows)]

    def swap(i, s):
        return copy_to(
            chunk(i, order[s], 1 - y),
            y_buf.at[i, order[s]],
            y_send.at[i, s],
            y_recv.at[i, s],
            other,
        )

    def upward(i, at):
        return copy_to(
            chunk(i, at, y), z_buf.at[i, at], up_send.at[i, at], up_recv.at[i, at], above
        )

    def downward(i, at, slot):
        return copy_to(
            chunk(i, at, y), z_buf.at[i, slot], down_send.at[i, at], down_recv.at[i, at], below
        )

    def down_slot(at, owner_z):
        return jnp.where(at == owner_z, depth, at)

    def scatter_step(i, s):
        at = order[s]
        swap(i, s).wait_recv()
        mine = chunk(i, at, y)
        add(mine, mine, y_buf.at[i, at])

        @pl.when((at >= z) & has_below)
        def _():
            upward(i, at).wait_recv()
            add(mine, mine, z_buf.at[i, at])

        @pl.when((at <= z) & has_above)
        def _():
            slot = down_slot(at, z)
            downward(i, at, slot).wait_recv()
            add(mine, mine, z_buf.at[i, slot])

        pl.when(at > z)(lambda: upward(i, at).start())
        pl.when(at < z)(lambda: downward(i, at, down_slot(at, z - 1)).start())

    results = (part_out, back_out)

    def scatter_out(i):
        return pltpu.make_async_copy(chunk(i, z, y), results[i], result_sem.at[i])

    for s in range(depth):
        swap(0, s).start()

    hand_on(pass_on)
    out_to_core.wait_recv()

    @pl.loop(0, group)
    def _(n):
        out_core[n] = (
            out_core[n].astype(f32)
            + out_grad[n, pl.ds(pl.multiple_of(core * half, half), half), :].astype(f32)
        ).astype(bf16)

    my_cols = pl.ds(pl.multiple_of(pair_of(ctx, group) * head_cols, head_cols), head_cols)

    def out_block(n):
        owner = lax.rem(ctx + n, group)
        return copy_to(
            out_core.at[owner],
            out_rows.at[:, my_cols],
            block_send.at[n],
            block_recv.at[n],
            (dp, owner),
        )

    for n in range(1, group):
        out_block(n).start()
    own_block = pltpu.make_async_copy(out_core.at[ctx], out_rows.at[:, my_cols], block_send.at[0])
    own_block.start()

    again = pltpu.make_async_copy(pairs, g_buf, sum_sem.at[0])
    again.start()

    def qkv_half(t, which):
        start = pl.multiple_of(t * 2 * half + which * half, half)
        return qkv_grad.at[pl.ds(start, half)]

    def to_core(t):
        return copy_to(
            qkv_half(t, 1 - core), qkv_core.at[t], core_send.at[t], core_recv.at[t], sibling
        )

    def across_x(t):
        source = qkv_half(t, core) if t < core_tiles else out_rows
        return copy_to(source, from_x.at[t], x_send.at[t], x_recv.at[t], across)

    spots = (
        [(down_out, 2 * half * t) for t in range(pair_tiles // 2)]
        + [(up_out, 2 * half * t) for t in range(pair_tiles // 2)]
        + [(qkv_out, 2 * half * t) for t in range(core_tiles)]
        + [(out_out, 0)]
    )
    def total_of(t):
        return pairs_x.at[t] if t < pair_tiles else from_x.at[t - pair_tiles]

    def spot(t, which):
        array, first = spots[t]
        return array.at[pl.ds(pl.multiple_of(first + which * half, half), half)]

    def keep(t):
        return pltpu.make_async_copy(total_of(t), spot(t, core), keep_sem.at[t])

    def finish(t, which):
        return copy_to(total_of(t), spot(t, which), done_send.at[t], done_recv.at[t], sibling)

    def x_sum(t):
        total = total_of(t)
        if t < pair_tiles:
            if t >= early:
                pair_x(t).wait_recv()
            add(total, total, g_buf.at[pl.ds(t * half, half)])
        else:
            n = t - pair_tiles
            across_x(n).wait_recv()
            add(total, total, qkv_half(n, core) if n < core_tiles else out_rows)
        keep(t).start()
        finish(t, core).start()

    loads[9].wait()
    again.wait()
    x_sum(0)
    for j in range(3):
        here, remote, local = to_owner(j)
        pl.when(here)(lambda local=local: local.wait())
        source = pair_of(lax.rem(3 * ctx + j, group), group)
        arriving = copy_to(
            returns.at[0], returned.at[j], head_send.at[0], head_recv.at[j], other
        )
        pl.when(source != ctx)(lambda arriving=arriving: arriving.wait_recv())
    for n in (5, 6, 7):
        loads[n].wait()
    sums[...] = jnp.zeros_like(sums)

    @pl.loop(0, tokens // tall)
    def _(n):
        at = pl.ds(pl.multiple_of(n * tall, tall), tall)

        @pl.loop(0, columns // wide)
        def _(m):
            cols = pl.ds(pl.multiple_of(m * wide, wide), wide)
            entry = dot_nn(returned[0, at, :], w_qkv[0:head_cols, cols])
            for j in range(1, 3):
                entry += dot_nn(
                    returned[j, at, :], w_qkv[j * head_cols : (j + 1) * head_cols, cols]
                )
            normed = (h_buf[at, cols].astype(f32) - tables[3, at, 0:1]) * tables[3, at, 1:2]
            sums[0:1, cols] += jnp.sum(entry * normed, axis=0, keepdims=True)
            sums[1:2, cols] += jnp.sum(entry, axis=0, keepdims=True)
            back[at, cols] = (back[at, cols].astype(f32) + entry * norms[0:1, cols]).astype(bf16)

    stages = (sibling, other, near, far, across)

    def exchange(n):
        return copy_to(
            vec_buf.at[2 * n], vec_buf.at[2 * n + 1], vec_send.at[n], vec_recv.at[n], stages[n]
        )

    lane_cols = vec_buf.shape[2]

    def place_vector(at, values):
        for n in range(values.shape[1] // lane_cols):
            vec_buf[0, pl.ds(at + n, 1), :] = values[:, n * lane_cols : (n + 1) * lane_cols]

    vec_buf[0] = jnp.zeros(vec_buf.shape[1:], f32)
    long = columns // lane_cols
    place_vector(0, sums[0:1, :])
    place_vector(long, sums[1:2, :])
    place_vector(2 * long, mlp_sums[0:1, :])
    place_vector(3 * long, mlp_sums[1:2, :])
    place_vector(4 * long, local_sums[...])
    each = head_cols // lane_cols
    for j in range(3):
        place_vector(
            5 * long + (3 * ctx + j) * each,
            jnp.sum(returned[j].astype(f32), axis=0, keepdims=True),
        )
    place_vector(
        5 * long + 3 * group * each + ctx * (up_sums.shape[1] // lane_cols), up_sums[...]
    )
    exchange(0).start()

    def vector_step(n):
        exchange(n).wait_recv()
        total = vec_buf[2 * n] + vec_buf[2 * n + 1]
        if n + 1 < len(stages):
            vec_buf[2 * n + 2] = total
            exchange(n + 1).start()
        else:
            vectors_out[...] = total

    vector_step(0)
    for s in range(depth):
        swap(1, s).start()

    loads[8].wait()
    for t in range(core_tiles):

        @pl.loop(0, columns // (2 * wide))
        def _(m):
            cols = pl.ds(pl.multiple_of(m * 2 * wide, 2 * wide), 2 * wide)
            qkv_grad[pl.ds(t * 2 * half, 2 * half), cols] = dot_tn(
                returned[t], x_buf[:, cols]
            ).astype(bf16)

        to_core(t).start()

    for t in range(core_tiles):
        to_core(t).wait_recv()
        mine = qkv_half(t, core)
        add(mine, mine, qkv_core.at[t])
        across_x(t).start()
    stats_out[...] = tables[3, pl.ds(pl.multiple_of(ctx * rows, rows), rows), :]
    for s in range(depth):
        scatter_step(0, s)
        if s == 0:
            x_sum(1)
            x_sum(2)
        x_sum(3 + s)
    scatter_out(0).start()
    own_block.wait()
    for n in range(1, group):
        source = lax.rem(ctx + group - n, group)
        theirs = pl.ds(
            pl.multiple_of(pair_of(source, group) * head_cols, head_cols), head_cols
        )
        copy_to(
            out_core.at[ctx], out_rows.at[:, theirs], block_send.at[n], block_recv.at[n], other
        ).wait_recv()
    across_x(core_tiles).start()
    vector_step(1)
    x_sum(7)
    scatter_step(1, 0)
    vector_step(2)
    x_sum(pair_tiles)
    scatter_step(1, 1)
    vector_step(3)
    x_sum(pair_tiles + 1)
    scatter_step(1, 2)
    x_sum(pair_tiles + 2)
    scatter_step(1, 3)
    scatter_out(1).start()
    x_sum(pair_tiles + 3)
    vector_step(4)

    hand_on(lambda arriving, onward: onward.wait_send())
    for kind in range(3):
        here, remote, _ = to_owner(kind)
        first = to_corner(kind)
        corner = turns_corner(ctx, owner_of(ctx, kind)[0])
        pl.when(corner)(lambda first=first: first.wait_send())
        pl.when(jnp.logical_not(here | corner))(lambda remote=remote: remote.wait_send())
    for n in range(1, group):
        out_block(n).wait_send()
    out_to_core.wait_send()
    for t in range(core_tiles):
        to_core(t).wait_send()
    for t in range(core_tiles + 1):
        across_x(t).wait_send()
    for t in range(early, pair_tiles):
        pair_x(t).wait_send()
    for t in range(len(spots)):
        keep(t).wait()
        finish(t, core).wait_send()
        finish(t, 1 - core).wait_recv()
    for n in range(len(stages)):
        exchange(n).wait_send()
    for i in range(2):
        scatter_out(i).wait()
        for s in range(depth):
            swap(i, s).wait_send()
            at = order[s]
            pl.when(at > z)(lambda i=i, at=at: upward(i, at).wait_send())
            pl.when(at < z)(
                lambda i=i, at=at: downward(i, at, down_slot(at, z - 1)).wait_send()
            )


def tail_pass(
    group,
    pairs,
    arrived,
    grad_all,
    w_cols,
    part,
    back,
    x_attn,
    w_qkv,
    hidden_all,
    tables,
    early,
    norms,
    mlp_sums,
    up_sums,
    local_sums,
    seg_len,
    seg_parent,
):
    tokens, columns = hidden_all.shape
    depth = group // RAILS
    rows = tokens // group
    head_cols = arrived.shape[2]
    units = up_sums.shape[1]
    half = 128
    pair_tiles = pairs.shape[0] // half
    core_tiles = w_qkv.shape[0] // (2 * half)
    lane_cols = 256
    vectors = (5 * columns + 3 * columns + group * units) // lane_cols
    sems = pltpu.SemaphoreType.DMA
    shape = jax.ShapeDtypeStruct
    vmem = pltpu.VMEM
    anywhere = pl.BlockSpec(memory_space=pl.ANY)
    small = pl.BlockSpec(memory_space=pltpu.VMEM)
    smem = pl.BlockSpec(memory_space=pltpu.SMEM)
    whole = vmem((tokens, columns), bf16)
    every = pair_tiles + core_tiles + 1
    return pl.pallas_call(
        functools.partial(tail_kernel, group),
        out_shape=(
            shape((rows, columns), bf16),
            shape((rows, columns), bf16),
            shape((units, columns), bf16),
            shape((units, columns), bf16),
            shape((2 * half, columns), bf16),
            shape(w_qkv.shape, bf16),
            shape((tokens, head_cols), bf16),
            shape((vectors, lane_cols), f32),
            shape((rows, HEAD_DIM), f32),
        ),
        in_specs=[anywhere] * 11 + [small] * 4 + [smem] * 2,
        out_specs=[anywhere] * 7 + [small] * 2,
        scratch_shapes=[
            vmem(arrived.shape, bf16),
            whole,
            vmem(w_cols.shape, bf16),
            whole,
            whole,
            whole,
            vmem(w_qkv.shape, bf16),
            whole,
            vmem(tables.shape, f32),
            vmem((tokens, head_cols), bf16),
            vmem((tokens, head_cols), bf16),
            vmem(arrived.shape, bf16),
            vmem(arrived.shape, bf16),
            vmem((2, depth, rows, columns), bf16),
            vmem((2, depth + 1, rows, columns), bf16),
            vmem((group, 2 * half, head_cols), bf16),
            vmem(w_qkv.shape, bf16),
            vmem((core_tiles, half, columns), bf16),
            vmem((group, half, head_cols), bf16),
            vmem((half, columns), bf16),
            vmem((core_tiles + 1, half, columns), bf16),
            vmem((pair_tiles, half, columns), bf16),
            vmem((tokens, HEAD_DIM), f32),
            vmem((tokens, HEAD_DIM), f32),
            vmem((2, columns), f32),
            vmem((10, vectors, lane_cols), f32),
            sems((10,)),
        ]
        + [sems((2, depth))] * 6
        + [sems((2,)), sems((3,)), sems((3,)), sems((pair_tiles,)), sems((pair_tiles,))]
        + [sems((core_tiles + 1,))] * 2
        + [sems((group,))] * 2
        + [sems((core_tiles + 1,))] * 2
        + [sems((every,))] * 3
        + [sems((5,))] * 2
        + [sems((1,))] * 3,
        compiler_params=pltpu.CompilerParams(
            collective_id=1, has_side_effects=True, vmem_limit_bytes=62 * 2**20
        ),
        name="tail_pass",
    )(
        pairs,
        arrived,
        grad_all,
        w_cols,
        part,
        back,
        x_attn,
        w_qkv,
        hidden_all,
        tables,
        early,
        norms,
        mlp_sums,
        up_sums,
        local_sums,
        seg_len,
        seg_parent,
    )


def finish_kernel(*refs):
    grads, (hidden, grad, summed, w_sum, stats, norms, vectors) = refs[:4], refs[4:11]
    outs, (hidden_out, grad_in), vector_outs = refs[11:15], refs[15:17], refs[17:25]
    narrow, wide, in_sem, out_sem = refs[25:]
    tall = narrow.shape[1]
    tiles = [(n, m) for n in range(4) for m in range(grads[n].shape[0] // tall)]

    def fetch(t):
        n, m = tiles[t]
        return pltpu.make_async_copy(
            grads[n].at[pl.ds(m * tall, tall)], narrow.at[t], in_sem.at[t]
        )

    def store(t):
        n, m = tiles[t]
        return pltpu.make_async_copy(wide.at[t], outs[n].at[pl.ds(m * tall, tall)], out_sem.at[t])

    for t in range(len(tiles)):
        fetch(t).start()
    rows = 32
    for t in range(len(tiles)):
        fetch(t).wait()

        @pl.loop(0, tall // rows)
        def _(n):
            at = pl.ds(pl.multiple_of(n * rows, rows), rows)
            wide[t, at, :] = narrow[t, at, :].astype(f32)

        store(t).start()

    @pl.loop(0, hidden.shape[0] // rows)
    def _(n):
        at = pl.ds(pl.multiple_of(n * rows, rows), rows)
        values = hidden[at, :].astype(f32)
        hidden_out[at, :] = (
            values + summed[at, :].astype(f32) + norms[4:5, :] + norms[5:6, :]
        ).astype(bf16)
        rstd = stats[at, 1:2]
        normed = (values - stats[at, 0:1]) * rstd
        back = w_sum[at, :].astype(f32)
        along = jnp.mean(back * normed, axis=1, keepdims=True)
        grad_in[at, :] = (
            grad[at, :].astype(f32)
            + (back - jnp.mean(back, axis=1, keepdims=True) - normed * along) * rstd
        )

    lane_cols = vectors.shape[1]
    places = [0, 1, 2, 3, 4, 4, 5, 8]
    each = hidden.shape[1] // lane_cols
    for out, place_of in zip(vector_outs, places):
        for n in range(out.shape[0] // lane_cols):
            out[pl.ds(n * lane_cols, lane_cols)] = vectors[place_of * each + n, :]
    for t in range(len(tiles)):
        store(t).wait()


def finish_pass(down, up, qkv, out, hidden, grad, summed, w_sum, stats, norms, vectors):
    tall = 256
    columns = hidden.shape[1]
    grads = (down, up, qkv, out)
    tiles = sum(array.shape[0] for array in grads) // tall
    shape = jax.ShapeDtypeStruct
    anywhere = pl.BlockSpec(memory_space=pl.ANY)
    vmem = pl.BlockSpec(memory_space=pltpu.VMEM)
    lengths = [columns] * 6 + [3 * columns, vectors.size - 8 * columns]
    return pl.pallas_call(
        finish_kernel,
        out_shape=[shape(array.shape, f32) for array in grads]
        + [shape(hidden.shape, bf16), shape(hidden.shape, f32)]
        + [shape((length,), f32) for length in lengths],
        in_specs=[anywhere] * 4 + [vmem] * 7,
        out_specs=[anywhere] * 4 + [vmem] * 10,
        scratch_shapes=[
            pltpu.VMEM((tiles, tall, columns), bf16),
            pltpu.VMEM((tiles, tall, columns), f32),
            pltpu.SemaphoreType.DMA((tiles,)),
            pltpu.SemaphoreType.DMA((tiles,)),
        ],
        compiler_params=pltpu.CompilerParams(vmem_limit_bytes=56 * 2**20),
        name="finish_pass",
    )(*grads, hidden, grad, summed, w_sum, stats, norms, vectors)


def body(
    hidden_in,
    grad_out,
    seg_len,
    seg_parent,
    gain_attn,
    shift_attn,
    w_qkv,
    bias_qkv,
    w_out,
    bias_out,
    gain_mlp,
    shift_mlp,
    w_up,
    bias_up,
    w_down,
    bias_down,
):
    group = lax.axis_size("ctx")
    head_cols = HEADS // group * HEAD_DIM
    vectors = (
        gain_attn,
        shift_attn,
        gain_mlp,
        shift_mlp,
        bias_out,
        bias_down,
        bias_qkv,
        bias_up,
    )
    (
        hidden_all,
        grad_all,
        x_attn,
        arrived,
        mlp_part,
        mlp_back,
        pairs,
        early,
        w_cols,
        _,
        tables,
        mlp_sums,
        up_sums,
        local_sums,
        norms,
    ) = layer_pass(
        group,
        hidden_in[0],
        grad_out[0],
        w_up,
        w_down,
        w_qkv,
        w_out,
        vectors,
        seg_len,
        seg_parent,
    )
    summed, w_sum, down_grad, up_grad, out_grad, qkv_grad, _, vectors, stats = tail_pass(
        group,
        pairs,
        arrived,
        grad_all,
        w_cols.reshape(D, head_cols),
        mlp_part,
        mlp_back,
        x_attn,
        w_qkv,
        hidden_all,
        tables,
        early,
        norms,
        mlp_sums,
        up_sums,
        local_sums,
        seg_len,
        seg_parent,
    )
    (
        down_grad,
        up_grad,
        qkv_grad,
        out_grad,
        hidden_out,
        grad_in,
        gain_grad_a,
        shift_grad_a,
        gain_grad_m,
        shift_grad_m,
        out_bias_grad,
        down_bias_grad,
        qkv_bias_grad,
        up_bias_grad,
    ) = finish_pass(
        down_grad,
        up_grad,
        qkv_grad,
        out_grad,
        hidden_in[0],
        grad_out[0],
        summed,
        w_sum,
        stats,
        norms,
        vectors,
    )
    return (
        hidden_out[None],
        grad_in[None],
        gain_grad_a,
        shift_grad_a,
        qkv_grad,
        qkv_bias_grad,
        out_grad,
        out_bias_grad,
        gain_grad_m,
        shift_grad_m,
        up_grad,
        up_bias_grad,
        down_grad,
        down_bias_grad,
    )


block_limit = 512


def tree_tables(seg_len, seg_parent):
    seg_count = seg_len.shape[0]
    labels = jnp.arange(seg_count, dtype=jnp.int32)
    earlier = labels[:, None] > labels[None, :]
    seg_starts = jnp.sum(jnp.where(earlier, seg_len[None, :], 0), axis=1)
    seg_ends = seg_starts + seg_len
    parent_hit = seg_parent[:, None] == labels[None, :]
    grand_parent = jnp.sum(jnp.where(parent_hit, seg_parent[None, :], 0), axis=1)
    itself = labels[:, None] == labels[None, :]
    ancestor = itself | parent_hit | (grand_parent[:, None] == labels[None, :])
    path_start = jnp.sum(jnp.where(ancestor & jnp.logical_not(itself), seg_len[None, :], 0), axis=1)
    return (seg_ends, seg_starts, ancestor, path_start)


def rotary_tables(path_pos):
    half_dim = ROT_DIM // 2
    inverse = jnp.power(10000.0, -2.0 * jnp.arange(half_dim, dtype=jnp.float32) / ROT_DIM)
    angles = path_pos.astype(jnp.float32)[:, None] * inverse[None, :]
    angles = jnp.concatenate([angles, angles], axis=1)
    return (jnp.cos(angles), jnp.sin(angles))


def rotate(head_values, cosine, sine):
    half_dim = ROT_DIM // 2
    turned = head_values[..., :ROT_DIM]
    swapped = jnp.concatenate([-turned[..., half_dim:], turned[..., :half_dim]], axis=-1)
    mixed = turned * cosine[:, None, :] + swapped * sine[:, None, :]
    return jnp.concatenate([mixed, head_values[..., ROT_DIM:]], axis=-1)


def gelu_slope(pre_act):
    normal_cdf = 0.5 * (1.0 + lax.erf(pre_act / math.sqrt(2.0)))
    return normal_cdf + pre_act * jnp.exp(-0.5 * pre_act * pre_act) / math.sqrt(2.0 * math.pi)


def layer_norm(values, gain_vec, shift_vec):
    average = jnp.mean(values, axis=-1, keepdims=True)
    centred = values - average
    spread = jnp.mean(centred * centred, axis=-1, keepdims=True)
    return centred * lax.rsqrt(spread + norm_eps) * gain_vec + shift_vec


def segment_hot(row_ids, seg_ends):
    seg_index = jnp.sum((row_ids[:, None] >= seg_ends[None, :]).astype(jnp.int32), axis=1)
    labels = jnp.arange(seg_ends.shape[0], dtype=jnp.int32)
    return (seg_index[:, None] == labels[None, :]).astype(jnp.float32)


def row_lookup(row_ids, seg_ends, ancestor_f):
    row_hot = segment_hot(row_ids, seg_ends)
    return (row_hot, jnp.dot(row_hot, ancestor_f))


def permitted(query_ids, query_reach, key_ids, key_hot):
    linked = jnp.dot(query_reach, key_hot.T) > 0.5
    return linked & (key_ids[None, :] <= query_ids[:, None])


def inner_block(row_count):
    block_rows = row_count
    while block_rows > block_limit and block_rows % 2 == 0:
        block_rows = block_rows // 2
    return block_rows


def gather_body(
    hidden_in,
    grad_out,
    seg_len,
    seg_parent,
    gain_attn,
    shift_attn,
    w_qkv,
    bias_qkv,
    w_out,
    bias_out,
    gain_mlp,
    shift_mlp,
    w_up,
    bias_up,
    w_down,
    bias_down,
):
    local_rows = hidden_in.shape[1]
    scale_factor = 1.0 / math.sqrt(HEAD_DIM)
    head_shape = (local_rows, HEADS, HEAD_DIM)
    seg_ends, seg_starts, ancestor, path_start = tree_tables(seg_len[0], seg_parent[0])
    ancestor_f = ancestor.astype(jnp.float32)
    my_ids = lax.axis_index("ctx") * local_rows + jnp.arange(local_rows, dtype=jnp.int32)
    my_hot, my_reach = row_lookup(my_ids, seg_ends, ancestor_f)
    shift_table = path_start - seg_starts
    path_pos = my_ids + jnp.sum(my_hot.astype(jnp.int32) * shift_table[None, :], axis=1)
    cosine, sine = rotary_tables(path_pos)
    inputs_f = hidden_in[0].astype(jnp.float32)
    gain_a = gain_attn.astype(jnp.float32)
    shift_a = shift_attn.astype(jnp.float32)
    gain_m = gain_mlp.astype(jnp.float32)
    shift_m = shift_mlp.astype(jnp.float32)
    bias_up_f = bias_up.astype(jnp.float32)
    x_attn = layer_norm(inputs_f, gain_a, shift_a).astype(jnp.bfloat16)
    x_mlp = layer_norm(inputs_f, gain_m, shift_m).astype(jnp.bfloat16)
    qkv = jnp.einsum(
        "td,nd->tn",
        x_attn,
        lax.all_gather(w_qkv, "ctx", axis=0, tiled=True),
        preferred_element_type=jnp.float32,
    ) + bias_qkv.astype(jnp.float32)
    queries = rotate(qkv[:, :D].reshape(head_shape), cosine, sine).astype(jnp.bfloat16)
    keys_heads = rotate(qkv[:, D : 2 * D].reshape(head_shape), cosine, sine).astype(jnp.bfloat16)
    values_flat = qkv[:, 2 * D :].astype(jnp.bfloat16)
    values_heads = values_flat.reshape(head_shape)
    keys_flat = keys_heads.reshape(local_rows, D)
    queries_flat = queries.reshape(local_rows, D)

    def split_blocks(shard_pieces):
        row_count = shard_pieces[0].shape[0]
        block_rows = inner_block(row_count)
        block_count = row_count // block_rows
        shaped = tuple(
            (member.reshape(block_count, block_rows, HEADS, HEAD_DIM) for member in shard_pieces)
        )
        starts = block_rows * jnp.arange(block_count, dtype=jnp.int32)
        return shaped + (starts,)

    def attend_block(fold_state, block_items):
        key_block, value_block, block_start = block_items
        block_rows = key_block.shape[0]
        key_ids = block_start + jnp.arange(block_rows, dtype=jnp.int32)
        allowed = permitted(my_ids, my_reach, key_ids, segment_hot(key_ids, seg_ends))
        row_top, row_total, partial_value = fold_state
        scores = (
            jnp.einsum("qhd,khd->qhk", queries, key_block, preferred_element_type=jnp.float32)
            * scale_factor
        )
        scores = jnp.where(allowed[:, None, :], scores, masked_score)
        new_top = jnp.maximum(row_top, jnp.max(scores, axis=-1))
        factor = jnp.exp(row_top - new_top)
        weights = jnp.exp(scores - new_top[:, :, None])
        row_total = row_total * factor + jnp.sum(weights, axis=-1)
        partial_value = partial_value * factor[:, :, None] + jnp.einsum(
            "qhk,khd->qhd",
            weights.astype(jnp.bfloat16),
            value_block,
            preferred_element_type=jnp.float32,
        )
        fold_state = (new_top, row_total, partial_value)
        return (fold_state, None)

    start_state = (
        jnp.full((local_rows, HEADS), masked_score, jnp.float32),
        jnp.zeros((local_rows, HEADS), jnp.float32),
        jnp.zeros(head_shape, jnp.float32),
    )
    row_top, row_total, partial_value = lax.scan(
        attend_block,
        start_state,
        split_blocks(
            (
                lax.all_gather(keys_flat, "ctx", axis=0, tiled=True),
                lax.all_gather(values_flat, "ctx", axis=0, tiled=True),
            )
        ),
    )[0]
    log_total = row_top + jnp.log(row_total)
    attended_f = partial_value / row_total[:, :, None]
    attended = attended_f.reshape(local_rows, D).astype(jnp.bfloat16)
    attn_proj = jnp.einsum(
        "td,nd->tn",
        attended,
        lax.all_gather(w_out, "ctx", axis=0, tiled=True),
        preferred_element_type=jnp.float32,
    )

    def mlp_pre(up_rows):
        return (
            jnp.einsum("td,nd->tn", x_mlp, up_rows, preferred_element_type=jnp.float32) + bias_up_f
        )

    up_rows = lax.all_gather(w_up, "ctx", axis=0, tiled=True)
    down_rows = lax.all_gather(w_down, "ctx", axis=0, tiled=True)
    activated = jax.nn.gelu(mlp_pre(up_rows), approximate=False).astype(jnp.bfloat16)
    mlp_sum = jnp.dot(activated, down_rows, preferred_element_type=jnp.float32)
    bias_out_f = bias_out.astype(jnp.float32)
    bias_down_f = bias_down.astype(jnp.float32)
    hidden_out = (inputs_f + attn_proj + bias_out_f + mlp_sum + bias_down_f).astype(jnp.bfloat16)
    grad_b = grad_out[0]
    grad_f = grad_b.astype(jnp.float32)
    up_rows = lax.all_gather(w_up, "ctx", axis=0, tiled=True)
    down_rows = lax.all_gather(w_down, "ctx", axis=0, tiled=True)
    pre_act = mlp_pre(up_rows)
    activated = jax.nn.gelu(pre_act, approximate=False).astype(jnp.bfloat16)
    act_grad = jnp.einsum("td,nd->tn", grad_b, down_rows, preferred_element_type=jnp.float32)
    pre_grad = (act_grad * gelu_slope(pre_act)).astype(jnp.bfloat16)
    input_grad = jnp.dot(pre_grad, up_rows, preferred_element_type=jnp.float32)
    act_all = activated
    pre_grad_all = pre_grad
    act_all, pre_grad_all, mlp_in_grad = (act_all, pre_grad_all, input_grad)
    attended_grad = jnp.dot(
        grad_b, lax.all_gather(w_out, "ctx", axis=0, tiled=True), preferred_element_type=jnp.float32
    ).astype(jnp.bfloat16)
    attended_grad_heads = attended_grad.reshape(head_shape)
    row_delta = jnp.sum(attended_grad_heads.astype(jnp.float32) * attended_f, axis=-1)
    all_log_total, all_delta = (
        lax.all_gather(log_total, "ctx", axis=0, tiled=True),
        lax.all_gather(row_delta, "ctx", axis=0, tiled=True),
    )

    def back_block(fold_state, block_items):
        key_block, value_block, query_block, grad_block, block_start = block_items
        block_rows = key_block.shape[0]
        other_ids = block_start + jnp.arange(block_rows, dtype=jnp.int32)
        other_hot, other_reach = row_lookup(other_ids, seg_ends, ancestor_f)
        allowed_in = permitted(my_ids, my_reach, other_ids, other_hot)
        allowed_out = permitted(other_ids, other_reach, my_ids, my_hot)
        other_log = lax.dynamic_slice_in_dim(all_log_total, block_start, block_rows, 0)
        other_delta = lax.dynamic_slice_in_dim(all_delta, block_start, block_rows, 0)
        query_grad, key_grad, value_grad = fold_state
        scores = (
            jnp.einsum("qhd,khd->qhk", queries, key_block, preferred_element_type=jnp.float32)
            * scale_factor
        )
        scores = jnp.where(allowed_in[:, None, :], scores, masked_score)
        prob_mass = jnp.exp(scores - log_total[:, :, None])
        prob_grad = jnp.einsum(
            "qhd,khd->qhk", attended_grad_heads, value_block, preferred_element_type=jnp.float32
        )
        score_grad = (prob_mass * (prob_grad - row_delta[:, :, None])).astype(jnp.bfloat16)
        query_grad = (
            query_grad
            + jnp.einsum("qhk,khd->qhd", score_grad, key_block, preferred_element_type=jnp.float32)
            * scale_factor
        )
        outgoing_key_grad = key_grad
        outgoing_value_grad = value_grad
        scores = (
            jnp.einsum("qhd,khd->qhk", query_block, keys_heads, preferred_element_type=jnp.float32)
            * scale_factor
        )
        scores = jnp.where(allowed_out[:, None, :], scores, masked_score)
        prob_mass = jnp.exp(scores - other_log[:, :, None])
        outgoing_value_grad = outgoing_value_grad + jnp.einsum(
            "qhk,qhd->khd",
            prob_mass.astype(jnp.bfloat16),
            grad_block,
            preferred_element_type=jnp.float32,
        )
        prob_grad = jnp.einsum(
            "qhd,khd->qhk", grad_block, values_heads, preferred_element_type=jnp.float32
        )
        score_grad = (prob_mass * (prob_grad - other_delta[:, :, None])).astype(jnp.bfloat16)
        outgoing_key_grad = (
            outgoing_key_grad
            + jnp.einsum(
                "qhk,qhd->khd", score_grad, query_block, preferred_element_type=jnp.float32
            )
            * scale_factor
        )
        fold_state = (query_grad, outgoing_key_grad, outgoing_value_grad)
        return (fold_state, None)

    zero_heads = jnp.zeros(head_shape, jnp.float32)
    query_grad, key_grad, value_grad = lax.scan(
        back_block,
        (zero_heads, zero_heads, zero_heads),
        split_blocks(
            (
                lax.all_gather(keys_flat, "ctx", axis=0, tiled=True),
                lax.all_gather(values_flat, "ctx", axis=0, tiled=True),
                lax.all_gather(queries_flat, "ctx", axis=0, tiled=True),
                lax.all_gather(attended_grad, "ctx", axis=0, tiled=True),
            )
        ),
    )[0]

    def turn(head_values):
        return rotate(head_values, cosine, sine)

    unturn = jax.vjp(turn, zero_heads)[1]
    qkv_grad = jnp.concatenate(
        [
            unturn(query_grad)[0].reshape(local_rows, D),
            unturn(key_grad)[0].reshape(local_rows, D),
            value_grad.reshape(local_rows, D),
        ],
        axis=1,
    ).astype(jnp.bfloat16)
    attn_in_grad = jnp.dot(
        qkv_grad,
        lax.all_gather(w_qkv, "ctx", axis=0, tiled=True),
        preferred_element_type=jnp.float32,
    )
    pull_attn = jax.vjp(layer_norm, inputs_f, gain_a, shift_a)[1]
    input_part_a, gain_grad_a, shift_grad_a = pull_attn(attn_in_grad)
    pull_mlp = jax.vjp(layer_norm, inputs_f, gain_m, shift_m)[1]
    input_part_m, gain_grad_m, shift_grad_m = pull_mlp(mlp_in_grad)
    grad_in = (grad_f + input_part_a + input_part_m)[None]
    vector_sums = lax.psum(
        (
            gain_grad_a,
            shift_grad_a,
            gain_grad_m,
            shift_grad_m,
            jnp.sum(qkv_grad, axis=0, dtype=jnp.float32),
            jnp.sum(grad_f, axis=0),
            jnp.sum(pre_grad_all, axis=0, dtype=jnp.float32),
        ),
        ("dp", "ctx"),
    )
    group_count = lax.axis_size("ctx")
    section_rows = (3 * D // group_count, D // group_count, FF // group_count, FF // group_count)
    term_sources = (
        (qkv_grad, x_attn),
        (grad_b, attended),
        (pre_grad_all, x_mlp),
        (act_all, grad_b),
    )
    owner_rows = sum(section_rows)
    blocks = jnp.arange(owner_rows * lax.axis_size("ctx") // owner_rows, dtype=jnp.int32)
    parts_list = []
    for (column_source, other_side), full_rows in zip(term_sources, section_rows):
        sub_rows = full_rows // 1
        column_ids = (
            blocks[:, None] * sub_rows + jnp.arange(sub_rows, dtype=jnp.int32)[None, :]
        ).reshape(-1)
        columns = jnp.take(column_source, column_ids, axis=1)
        block_term = jnp.einsum(
            "tr,td->rd", columns, other_side, preferred_element_type=jnp.float32
        )
        parts_list.append(block_term.reshape(blocks.shape[0], sub_rows, D))
    owned_term = lax.psum_scatter(
        jnp.concatenate(parts_list, axis=1).reshape(-1, D).astype(jnp.bfloat16),
        "ctx",
        scatter_dimension=0,
        tiled=True,
    ).astype(jnp.float32)
    cut_a = section_rows[0]
    cut_b = cut_a + section_rows[1]
    cut_c = cut_b + section_rows[2]
    weight_grads = (
        lax.psum(owned_term[:cut_a].astype(jnp.bfloat16), "dp").astype(jnp.float32),
        lax.psum(owned_term[cut_a:cut_b].astype(jnp.bfloat16), "dp").astype(jnp.float32),
        lax.psum(owned_term[cut_b:cut_c].astype(jnp.bfloat16), "dp").astype(jnp.float32),
        lax.psum(owned_term[cut_c:].astype(jnp.bfloat16), "dp").astype(jnp.float32),
    )
    return (
        hidden_out[None],
        grad_in,
        vector_sums[0],
        vector_sums[1],
        weight_grads[0],
        vector_sums[4],
        weight_grads[1],
        vector_sums[5],
        vector_sums[2],
        vector_sums[3],
        weight_grads[2],
        vector_sums[6],
        weight_grads[3],
        vector_sums[5],
    )


def solution(mesh):
    token = P("dp", "ctx", None)
    rows = P("ctx", None)
    return jax.shard_map(
        body if mesh.shape["ctx"] == 8 and mesh.shape["dp"] == 4 else gather_body,
        mesh=mesh,
        in_specs=(
            token,
            token,
            P("dp", None),
            P("dp", None),
            P(),
            P(),
            rows,
            P(),
            rows,
            P(),
            P(),
            P(),
            rows,
            P(),
            rows,
            P(),
        ),
        out_specs=(
            token,
            token,
            P(),
            P(),
            rows,
            P(),
            rows,
            P(),
            P(),
            P(),
            rows,
            P(),
            rows,
            P(),
        ),
        check_vma=False,
    )
```

```python
import functools
import math

import jax
import jax.numpy as jnp
import numpy as np
from jax import lax
from jax.experimental import pallas as pl
from jax.experimental.pallas import tpu as pltpu
from jax.sharding import PartitionSpec as P

D = 2048
HEADS = 16
HEAD_DIM = 128
ROT_DIM = 32
FF = 8192

norm_eps = 1e-05
masked_score = -1e30
f32 = jnp.float32
bf16 = jnp.bfloat16


def dot_nt(a, b):
    return lax.dot_general(a, b, (((1,), (1,)), ((), ())), preferred_element_type=f32)


def dot_nn(a, b):
    return lax.dot_general(a, b, (((1,), (0,)), ((), ())), preferred_element_type=f32)


def dot_tn(a, b):
    return lax.dot_general(a, b, (((0,), (0,)), ((), ())), preferred_element_type=f32)


MESH = pl.DeviceIdType.MESH
RAILS = 2


def place(group):
    dp = lax.axis_index("dp")
    ctx = lax.axis_index("ctx")
    return dp, ctx, ctx // RAILS, ctx % RAILS, group // RAILS


def copy_to(src, dst, send, recv, device):
    return pltpu.make_async_remote_copy(
        src_ref=src,
        dst_ref=dst,
        send_sem=send,
        recv_sem=recv,
        device_id=device,
        device_id_type=MESH,
    )


def signal(device):
    barrier = pltpu.get_barrier_semaphore()
    pl.semaphore_signal(barrier, inc=1, device_id=device, device_id_type=MESH)


def arrive(count):
    pl.semaphore_wait(pltpu.get_barrier_semaphore(), count)


def pair_of(ctx, group):
    if group != 8:
        return ctx
    return ctx + jnp.where(
        (ctx == 1) | (ctx == 4), 2, jnp.where((ctx == 3) | (ctx == 6), -2, 0)
    )


def pair_order(z, depth):
    return [
        z,
        jnp.where(z > 0, z - 1, 1),
        jnp.where(z == depth - 1, 1, jnp.where(z == depth - 2, depth - 1, 2)),
        jnp.where(z < depth // 2, depth - 1, 0),
    ]


def layer_kernel(group, *refs):
    hidden, grad, w_up_in, w_down_in, w_qkv_in, w_out = refs[:6]
    vectors, (inverse, seg_len, seg_parent), refs = refs[6:14], refs[14:17], refs[7:]
    h_out, g_out, x_out, heads_out, part_out, back_out, pairs_out, early_out, cols_out = refs[10:19]
    passing, refs = refs[19], refs[1:]
    tables, sums, bias_sum, local_sum, norms = refs[19:24]
    h_buf, g_buf, w_up, w_down, w_qkv, x_mlp, x_attn, act, slope, pre_grad = refs[24:34]
    heads, part, back, down_grad, up_grad, core_buf, mean, rstd, bias_up, bias_qkv = refs[34:44]
    all_qkv, all_up = refs[44:46]
    refs = refs[2:]
    own_sem, y_send, y_recv, up_send, up_recv, down_send, down_recv = refs[44:51]
    weight_sem, pair_sem, grad_sem, head_send, head_recv = refs[51:56]
    core_send, core_recv, cols_send, cols_recv, early_send, early_recv = refs[56:62]
    pass_send, pass_recv = refs[62:64]
    dp, ctx, z, y, depth = place(group)
    bufs, sources, outs = (h_buf, g_buf), (hidden, grad), (h_out, g_out)
    rows = hidden.shape[0]
    pair_rows = RAILS * rows
    tokens, columns = h_buf.shape
    units = act.shape[1]
    head_cols = heads.shape[2]
    other = (dp, z * RAILS + 1 - y)
    above = (dp, jnp.minimum(z + 1, depth - 1) * RAILS + y)
    below = (dp, jnp.maximum(z - 1, 0) * RAILS + y)
    has_above, has_below = z < depth - 1, z > 0
    order = pair_order(z, depth)

    x, core = dp // 2, dp % 2
    sibling = (x * 2 + 1 - core, ctx)
    across = ((1 - x) * 2 + core, ctx)

    for n in range(1, group):
        signal((dp, lax.rem(ctx + n, group)))
    signal(sibling)
    signal(across)
    arrive(group + 1)

    def chunk(i, at_z, at_y):
        start = pl.multiple_of((at_z * RAILS + at_y) * rows, rows)
        return bufs[i].at[pl.ds(start, rows)]

    def to_other(i, at_z, source=None):
        here = chunk(i, at_z, y)
        return copy_to(
            here if source is None else source, here, y_send.at[i, at_z], y_recv.at[i, at_z], other
        )

    def upward(i, at_z, source=None):
        here = chunk(i, at_z, y)
        return copy_to(
            here if source is None else source,
            here,
            up_send.at[i, at_z],
            up_recv.at[i, at_z],
            above,
        )

    def downward(i, at_z, source=None):
        here = chunk(i, at_z, y)
        return copy_to(
            here if source is None else source,
            here,
            down_send.at[i, at_z],
            down_recv.at[i, at_z],
            below,
        )

    def relay_up(i, k):
        at_z = jnp.maximum(z - k, 0)
        upward(i, at_z).wait_recv()
        pl.when(has_above)(lambda: upward(i, at_z).start())

    def relay_down(i, k):
        at_z = jnp.minimum(z + k, depth - 1)
        downward(i, at_z).wait_recv()
        pl.when(has_below)(lambda: downward(i, at_z).start())

    def turn(n):
        if n < depth:
            pl.when(z >= n)(lambda: relay_up(0, n))
            pl.when(z + n < depth)(lambda: relay_down(0, n))
            to_other(0, order[n]).start()
            pl.when((z == n - 1) & has_above)(lambda: upward(1, z, sources[1]).start())
            pl.when((z == depth - n) & has_below)(lambda: downward(1, z, sources[1]).start())
        for k in range(1, depth):
            pl.when((z == n - k) & (z >= k))(lambda k=k: relay_up(1, k))
            pl.when((depth - 1 - z == n - k) & (z + k < depth))(lambda k=k: relay_down(1, k))
        if n == depth:
            to_other(1, z, sources[1]).start()
        if n > depth:
            to_other(1, order[n - depth]).start()

    def y_arrive(i, s):
        here = chunk(i, order[s], 1 - y)
        copy_to(
            here, here, y_send.at[i, order[s]], y_recv.at[i, order[s]], other
        ).wait_recv()

    def pair_at(s):
        return pl.ds(pl.multiple_of(order[s] * pair_rows, pair_rows), pair_rows)

    def keep(n, s, buf, out):
        at = pair_at(s)
        return pltpu.make_async_copy(buf.at[at], out.at[at], pair_sem.at[n, s])

    own = [pltpu.make_async_copy(sources[i], chunk(i, z, y), own_sem.at[i]) for i in range(2)]
    weights = [
        pltpu.make_async_copy(source, held, weight_sem.at[n])
        for n, (source, held) in enumerate(
            ((w_up_in, w_up), (w_qkv_in, w_qkv), (w_down_in, w_down))
        )
    ]
    own[0].start()
    to_other(0, z, sources[0]).start()
    pl.when(has_above)(lambda: upward(0, z, sources[0]).start())
    pl.when(has_below)(lambda: downward(0, z, sources[0]).start())
    for copy in weights:
        copy.start()
    own[1].start()

    starts, shifts = [], []
    at = jnp.int32(0)
    for n in range(seg_len.shape[1]):
        parent = seg_parent[0, n]
        grand = seg_parent[0, parent]
        before = jnp.where(parent != n, seg_len[0, parent], 0) + jnp.where(
            (grand != n) & (grand != parent), seg_len[0, grand], 0
        )
        starts.append(at)
        shifts.append(before - at)
        at = at + seg_len[0, n]

    turned_half = ROT_DIM // 2

    @pl.loop(0, tokens // rows)
    def _(n):
        at = pl.ds(pl.multiple_of(n * rows, rows), rows)
        token = n * rows + lax.broadcasted_iota(jnp.int32, (turned_half, rows), 1)
        position = token + shifts[0]
        for m in range(1, len(starts)):
            position = position + jnp.where(token >= starts[m], shifts[m] - shifts[m - 1], 0)
        angle = position.astype(f32) * inverse[...]
        cosine, sine = jnp.cos(angle), jnp.sin(angle)
        still = jnp.zeros((HEAD_DIM - ROT_DIM, rows), f32)
        none = jnp.zeros((turned_half, rows), f32)
        tables[0, at, :] = jnp.concatenate([cosine, cosine, still + 1.0], axis=0).T
        tables[1, at, :] = jnp.concatenate([-sine, none, still], axis=0).T
        tables[2, at, :] = jnp.concatenate([none, sine, still], axis=0).T

    sums[...] = jnp.zeros_like(sums)
    bias_sum[...] = jnp.zeros_like(bias_sum)
    for n in range(6):
        norms[n : n + 1, :] = vectors[n][...].astype(f32).reshape(1, columns)
    norms[6:8, :] = jnp.zeros((2, columns), f32)

    def take_mine(target, vector, wide_row):
        wide_row[...] = vector[...].astype(f32).reshape(wide_row.shape)
        size = target.shape[1]
        target[...] = wide_row[:, pl.ds(pl.multiple_of(ctx * size, HEAD_DIM), size)]

    take_mine(bias_qkv, vectors[6], all_qkv)
    take_mine(bias_up, vectors[7], all_up)

    def normalize(s):
        step = 32

        @pl.loop(0, pair_rows // step)
        def _(n):
            at = pl.ds(pl.multiple_of(order[s] * pair_rows + n * step, step), step)
            values = h_buf[at, :].astype(f32)
            average = jnp.mean(values, axis=1, keepdims=True)
            centred = values - average
            spread = lax.rsqrt(jnp.mean(centred * centred, axis=1, keepdims=True) + norm_eps)
            normed = centred * spread
            x_attn[at, :] = (normed * norms[0:1, :] + norms[1:2, :]).astype(bf16)
            x_mlp[at, :] = (normed * norms[2:3, :] + norms[3:4, :]).astype(bf16)
            mean[at, :] = average
            rstd[at, :] = spread
            lane = lax.broadcasted_iota(jnp.int32, (step, HEAD_DIM), 1)
            tables[3, at, :] = jnp.where(lane == 0, average, spread)

    wide = 512

    def feed(s):
        at = pair_at(s)

        @pl.loop(0, units // wide)
        def _(n):
            cols = pl.ds(pl.multiple_of(n * wide, wide), wide)
            pre = dot_nt(x_mlp[at, :], w_up[cols, :]) + bias_up[:, cols]
            normal_cdf = 0.5 * (1.0 + lax.erf(pre * math.sqrt(0.5)))
            act[at, cols] = (pre * normal_cdf).astype(bf16)
            slope[at, cols] = (
                normal_cdf + pre * jnp.exp(-0.5 * pre * pre) * (1.0 / math.sqrt(2.0 * math.pi))
            ).astype(slope.dtype)

    def project(s):
        at = pair_at(s)
        for j in range(3):
            block = pl.ds(j * head_cols, head_cols)
            raw = dot_nt(x_attn[at, :], w_qkv[block, :]) + bias_qkv[:, block]
            turns = lax.div(3 * ctx + j, group) < 2
            for m in range(head_cols // HEAD_DIM):
                one = raw[:, m * HEAD_DIM : (m + 1) * HEAD_DIM]
                turned = (
                    one * tables[0, at, :]
                    + pltpu.roll(one, HEAD_DIM - ROT_DIM // 2, 1) * tables[1, at, :]
                    + pltpu.roll(one, ROT_DIM // 2, 1) * tables[2, at, :]
                )
                heads[j, at, m * HEAD_DIM : (m + 1) * HEAD_DIM] = jnp.where(
                    turns, turned, one
                ).astype(bf16)

    def mix(s):
        at = pair_at(s)

        @pl.loop(0, columns // wide)
        def _(n):
            cols = pl.ds(pl.multiple_of(n * wide, wide), wide)
            part[at, cols] = dot_nn(act[at, :], w_down[:, cols]).astype(bf16)

    def back_feed(s):
        at = pair_at(s)

        @pl.loop(0, units // wide)
        def _(n):
            cols = pl.ds(pl.multiple_of(n * wide, wide), wide)
            rounded = (
                dot_nt(g_buf[at, :], w_down[cols, :]) * slope[at, cols].astype(f32)
            ).astype(bf16)
            pre_grad[at, cols] = rounded
            bias_sum[:, cols] += jnp.sum(rounded.astype(f32), axis=0, keepdims=True)

        @pl.loop(0, columns // wide)
        def _(n):
            cols = pl.ds(pl.multiple_of(n * wide, wide), wide)
            entry = dot_nn(pre_grad[at, :], w_up[:, cols])
            normed = (h_buf[at, cols].astype(f32) - mean[at, :]) * rstd[at, :]
            sums[0:1, cols] += jnp.sum(entry * normed, axis=0, keepdims=True)
            sums[1:2, cols] += jnp.sum(entry, axis=0, keepdims=True)
            back[at, cols] = (entry * norms[2:3, cols]).astype(bf16)

    def forward(s):
        keep(0, s, h_buf, h_out).start()
        normalize(s)
        keep(1, s, x_attn, x_out).start()
        if s == 0:
            weights[0].wait()
        feed(s)
        if s == 0:
            weights[1].wait()
        project(s)

    def backward(s):
        keep(2, s, g_buf, g_out).start()
        if s == 0:
            weights[2].wait()
        mix(s)
        keep(3, s, part, part_out).start()
        back_feed(s)
        keep(4, s, back, back_out).start()

    tall = 256
    half = core_buf.shape[1]
    tiles = units // tall
    held = (down_grad, up_grad)

    def grad_half(t, which):
        start = pl.multiple_of((t % tiles) * tall + which * half, half)
        return held[t // tiles].at[pl.ds(start, half)]

    def to_core(t):
        return copy_to(
            grad_half(t, 1 - core), core_buf.at[t], core_send.at[t], core_recv.at[t], sibling
        )

    def grad_keep(t):
        return pltpu.make_async_copy(
            grad_half(t, core), pairs_out.at[pl.ds(t * half, half)], grad_sem.at[t]
        )

    def outer(n, left, right, steps, ms=range(units // tall)):
        for m in ms:
            mine = pl.ds(m * tall, tall)

            @pl.loop(0, columns // (2 * wide))
            def _(k):
                cols = pl.ds(pl.multiple_of(k * 2 * wide, 2 * wide), 2 * wide)
                terms = [dot_tn(left[pair_at(s), mine], right[pair_at(s), cols]) for s in steps]
                if steps[0] > 0:
                    terms.append(held[n][mine, cols].astype(f32))
                held[n][mine, cols] = sum(terms[1:], terms[0]).astype(bf16)

            if steps[-1] == depth - 1:
                to_core(n * tiles + m).start()

    def early_x(t):
        return copy_to(
            held[0].at[pl.ds(pl.multiple_of(t * tall + core * half, half), half // 2)],
            early_out.at[t],
            early_send.at[t],
            early_recv.at[t],
            across,
        )

    def outer_sum(ts):
        for t in ts:
            to_core(t).wait_recv()
            mine = grad_half(t, core)

            @pl.loop(0, half // 32)
            def _(k):
                at = pl.ds(pl.multiple_of(k * 32, 32), 32)
                mine[at, :] = (mine[at, :].astype(f32) + core_buf[t, at, :].astype(f32)).astype(
                    bf16
                )

            grad_keep(t).start()
            if t < early_out.shape[0]:
                early_x(t).start()

    share = cols_out.shape[2]

    def to_columns(n):
        owner = lax.rem(ctx + n, group)
        block = w_out.at[
            pl.ds(pl.multiple_of(dp * share, share), share),
            pl.ds(pl.multiple_of(pair_of(owner, group) * head_cols, head_cols), head_cols),
        ]
        if n == 0:
            return pltpu.make_async_copy(block, cols_out.at[ctx, dp], cols_send.at[0])
        return copy_to(
            block, cols_out.at[ctx, dp], cols_send.at[n], cols_recv.at[n], (dp, owner)
        )

    def columns_arrive():
        to_columns(0).wait()
        for n in range(1, group):
            source = lax.rem(ctx + group - n, group)
            here = cols_out.at[source, dp]
            copy_to(here, here, cols_send.at[n], cols_recv.at[n], other).wait_recv()

    def columns_core(which):
        here = cols_out.at[:, pl.ds(2 * x + which, 1)]
        return copy_to(here, here, cols_send.at[group], cols_recv.at[group], sibling)

    def columns_x(which):
        here = cols_out.at[:, pl.ds(2 * which, 2)]
        return copy_to(here, here, cols_send.at[group + 1], cols_recv.at[group + 1], across)

    def to_head(j):
        block = 3 * ctx + j
        kind, target = lax.div(block, group), pair_of(lax.rem(block, group), group)
        remote = copy_to(
            heads.at[j], heads_out.at[kind], head_send.at[j], head_recv.at[kind], (dp, target)
        )
        local = pltpu.make_async_copy(heads.at[j], heads_out.at[kind], head_send.at[j])
        return target == ctx, remote, local

    def turns_corner(device, target):
        return (device % RAILS != target % RAILS) & (
            lax.div(device, RAILS) == lax.div(target, RAILS) + 99
        )

    def to_corner(j):
        target = pair_of(lax.rem(3 * ctx + j, group), group)
        middle = (dp, lax.div(target, RAILS) * RAILS + y)
        return copy_to(heads.at[j], passing, head_send.at[j], pass_recv.at[0], middle)

    def send_heads(crossing):
        for j in range(3):
            here, remote, local = to_head(j)
            target = pair_of(lax.rem(3 * ctx + j, group), group)
            corner = turns_corner(ctx, target)
            crosses = (target % RAILS != y) & jnp.logical_not(corner)
            if crossing:
                pl.when(crosses)(lambda remote=remote: remote.start())
            else:
                first = to_corner(j)
                pl.when(here)(lambda local=local: local.start())
                pl.when(corner)(lambda first=first: first.start())
                pl.when(jnp.logical_not(here | crosses | corner))(
                    lambda remote=remote: remote.start()
                )

    def hand_on(act_on):
        partner = ctx + 1 - 2 * y
        for kind in range(3):
            source = lax.div(kind * group + pair_of(partner, group), 3)
            arriving = copy_to(passing, passing, pass_send.at[0], pass_recv.at[0], other)
            onward = copy_to(
                passing, heads_out.at[kind], pass_send.at[0], head_recv.at[kind], other
            )
            pl.when(turns_corner(source, partner))(
                lambda arriving=arriving, onward=onward: act_on(arriving, onward)
            )

    def pass_on(arriving, onward):
        arriving.wait_recv()
        onward.start()

    def head_source(kind):
        return lax.div(kind * group + pair_of(ctx, group), 3)

    turn(1)
    own[0].wait()
    y_arrive(0, 0)
    forward(0)
    turn(2)
    y_arrive(0, 1)
    forward(1)
    turn(3)
    y_arrive(0, 2)
    forward(2)
    turn(4)
    for n in range(group):
        to_columns(n).start()
    y_arrive(0, 3)
    forward(3)
    turn(5)
    send_heads(False)
    own[1].wait()
    y_arrive(1, 0)
    backward(0)
    at = pl.ds(pl.multiple_of(ctx * rows, rows), rows)
    local_sum[...] = jnp.sum(g_buf[at, :].astype(f32), axis=0, keepdims=True)
    turn(6)
    y_arrive(1, 1)
    backward(1)
    turn(7)
    columns_arrive()
    columns_core(core).start()
    outer(0, act, g_buf, (0, 1))
    outer(1, pre_grad, x_mlp, (0, 1))
    columns_core(1 - core).wait_recv()
    columns_x(x).start()
    y_arrive(1, 2)
    backward(2)
    outer(0, act, g_buf, (2,))
    outer(1, pre_grad, x_mlp, (2,))
    y_arrive(1, 3)
    send_heads(True)
    early = early_out.shape[0]
    outer(0, act, g_buf, (3,), range(early + 1))
    outer_sum(range(early))
    outer(0, act, g_buf, (3,), range(early + 1, tiles))
    backward(3)
    outer_sum(range(early, tiles))
    outer(1, pre_grad, x_mlp, (3,))
    outer_sum(range(tiles, 2 * tiles))

    for at_z in range(depth):
        to_other(0, at_z).wait_send()
        to_other(1, at_z).wait_send()
        for i in range(2):
            pl.when(has_above & (at_z <= z))(lambda i=i: upward(i, at_z).wait_send())
            pl.when(has_below & (at_z >= z))(lambda i=i: downward(i, at_z).wait_send())
    for j in range(3):
        here, remote, local = to_head(j)
        first = to_corner(j)
        corner = turns_corner(ctx, pair_of(lax.rem(3 * ctx + j, group), group))
        pl.when(here)(lambda local=local: local.wait())
        pl.when(corner)(lambda first=first: first.wait_send())
        pl.when(jnp.logical_not(here | corner))(lambda remote=remote: remote.wait_send())
    for kind in range(3):
        arriving = copy_to(
            heads.at[0], heads_out.at[kind], head_send.at[0], head_recv.at[kind], other
        )
        pl.when(head_source(kind) != ctx)(lambda arriving=arriving: arriving.wait_recv())
    for s in range(4):
        keep(0, s, h_buf, h_out).wait()
        keep(1, s, x_attn, x_out).wait()
        keep(2, s, g_buf, g_out).wait()
        keep(3, s, part, part_out).wait()
        keep(4, s, back, back_out).wait()
    for t in range(2 * tiles):
        to_core(t).wait_send()
        grad_keep(t).wait()
    for n in range(1, group):
        to_columns(n).wait_send()
    for t in range(early):
        early_x(t).wait_send()
        early_x(t).wait_recv()
    columns_core(core).wait_send()
    columns_x(x).wait_send()
    columns_x(1 - x).wait_recv()


def layer_pass(
    group, hidden, grad, w_up, w_down, w_qkv, w_out, vectors, seg_len, seg_parent
):
    rows, columns = hidden.shape
    tokens, units, head_cols = group * rows, w_up.shape[0], w_qkv.shape[0] // 3
    depth = group // RAILS
    inverse = 10000.0 ** (-2.0 * np.arange(ROT_DIM // 2) / ROT_DIM)
    inverse = jnp.asarray(np.broadcast_to(inverse[:, None], (ROT_DIM // 2, rows)), f32)
    early = 1
    sems = pltpu.SemaphoreType.DMA
    shape = jax.ShapeDtypeStruct
    anywhere = pl.BlockSpec(memory_space=pl.ANY)
    vmem = pl.BlockSpec(memory_space=pltpu.VMEM)
    smem = pl.BlockSpec(memory_space=pltpu.SMEM)
    whole = shape((tokens, columns), bf16)
    half = 128
    copies = lax.axis_size("dp")
    return pl.pallas_call(
        functools.partial(layer_kernel, group),
        out_shape=(
            whole,
            whole,
            whole,
            shape((3, tokens, head_cols), bf16),
            whole,
            whole,
            shape((units, columns), bf16),
            shape((early, half // 2, columns), bf16),
            shape((group, copies, columns // group // copies, head_cols), bf16),
            shape((tokens, head_cols), bf16),
            shape((4, tokens, HEAD_DIM), f32),
            shape((2, columns), f32),
            shape((1, units), f32),
            shape((1, columns), f32),
            shape((8, columns), f32),
        ),
        in_specs=[anywhere] * 6 + [vmem] * 9 + [smem] * 2,
        out_specs=[anywhere] * 10 + [vmem] * 5,
        scratch_shapes=[pltpu.VMEM((tokens, columns), bf16)] * 2
        + [pltpu.VMEM((units, columns), bf16)] * 2
        + [pltpu.VMEM((3 * head_cols, columns), bf16)]
        + [pltpu.VMEM((tokens, columns), bf16)] * 2
        + [pltpu.VMEM((tokens, units), bf16)] * 3
        + [pltpu.VMEM((3, tokens, head_cols), bf16)]
        + [pltpu.VMEM((tokens, columns), bf16)] * 2
        + [pltpu.VMEM((units, columns), bf16)] * 2
        + [pltpu.VMEM((units // half, half, columns), bf16)]
        + [pltpu.VMEM((tokens, 1), f32)] * 2
        + [pltpu.VMEM((1, units), f32), pltpu.VMEM((1, 3 * head_cols), f32)]
        + [pltpu.VMEM((1, vector.shape[0]), f32) for vector in vectors[6:]]
        + [sems((2,))]
        + [sems((2, depth))] * 6
        + [sems((3,)), sems((5, 4)), sems((units // half,)), sems((3,)), sems((3,))]
        + [sems((units // half,))] * 2
        + [sems((group + 2,))] * 2
        + [sems((early,))] * 2
        + [sems((1,))] * 2,
        compiler_params=pltpu.CompilerParams(
            collective_id=0, has_side_effects=True, vmem_limit_bytes=62 * 2**20
        ),
        name="layer_pass",
    )(hidden, grad, w_up, w_down, w_qkv, w_out, *vectors, inverse, seg_len, seg_parent)


def tail_kernel(group, *refs):
    pairs, arrived_in, grad_in, w_cols_in, part_in, back_in, x_in, w_qkv_in, hidden_in = refs[:9]
    tables_in, early_in, norms, mlp_sums, up_sums, local_sums, seg_len, seg_parent = refs[9:17]
    part_out, back_out, down_out, up_out, out_out, qkv_out, passing = refs[17:24]
    vectors_out, stats_out = refs[24:26]
    refs = refs[26:]
    arrived, g_buf, w_cols, part, back, x_buf, w_qkv, h_buf, tables = refs[:9]
    att_grad, attended, returns, returned, y_buf, z_buf = refs[9:15]
    out_grad, qkv_grad, qkv_core, out_core, out_rows, from_x, pairs_x, key_acc, value_acc = refs[15:24]
    sums, vec_buf = refs[24:26]
    (
        load_sem,
        y_send,
        y_recv,
        up_send,
        up_recv,
        down_send,
        down_recv,
        result_sem,
        head_send,
        head_recv,
        pair_send,
        pair_recv,
        core_send,
        core_recv,
        block_send,
        block_recv,
        x_send,
        x_recv,
        keep_sem,
        done_send,
        done_recv,
        vec_send,
        vec_recv,
        sum_sem,
        pass_send,
        pass_recv,
    ) = refs[26:]
    dp, ctx, z, y, depth = place(group)
    tokens, columns = g_buf.shape
    rows = tokens // group
    head_cols = attended.shape[1]
    heads = head_cols // HEAD_DIM
    half = qkv_core.shape[1]
    pair_tiles = pairs_x.shape[0]
    x, core = dp // 2, dp % 2
    other = (dp, z * RAILS + 1 - y)
    above = (dp, jnp.minimum(z + 1, depth - 1) * RAILS + y)
    below = (dp, jnp.maximum(z - 1, 0) * RAILS + y)
    sibling = (x * 2 + 1 - core, ctx)
    across = ((1 - x) * 2 + core, ctx)
    near = (dp, (z + 1 - 2 * (z % 2)) * RAILS + y)
    far = (dp, lax.rem(z + 2, depth) * RAILS + y)
    has_above, has_below = z < depth - 1, z > 0

    for n in range(1, group):
        signal((dp, lax.rem(ctx + n, group)))
    signal(sibling)
    signal(across)
    arrive(group + 1)

    def add(target, left, right):
        step = 32

        @pl.loop(0, target.shape[0] // step)
        def _(n):
            at = pl.ds(pl.multiple_of(n * step, step), step)
            target[at, :] = (left[at, :].astype(f32) + right[at, :].astype(f32)).astype(
                target.dtype
            )

    early = early_in.shape[0]

    def pair_x(t):
        first = half // 2 if t < early else 0
        return copy_to(
            pairs.at[pl.ds(t * half + first, half - first)],
            pairs_x.at[t, pl.ds(first, half - first)],
            pair_send.at[t],
            pair_recv.at[t],
            across,
        )

    for t in range(pair_tiles):
        pair_x(t).start()
    loads = [
        pltpu.make_async_copy(source, target, load_sem.at[n])
        for n, (source, target) in enumerate(
            (
                (w_cols_in, w_cols),
                (grad_in, g_buf),
                (arrived_in, arrived),
                (tables_in, tables),
                (part_in, part),
                (w_qkv_in, w_qkv),
                (back_in, back),
                (hidden_in, h_buf),
                (x_in, x_buf),
                (early_in, pairs_x.at[pl.ds(0, early), pl.ds(0, half // 2)]),
            )
        )
    ]
    for copy in loads:
        copy.start()

    wide = 512
    tall = 256
    scale = 1.0 / math.sqrt(HEAD_DIM)
    loads[0].wait()
    loads[1].wait()

    @pl.loop(0, tokens // tall)
    def _(n):
        at = pl.ds(pl.multiple_of(n * tall, tall), tall)
        att_grad[at, :] = dot_nn(g_buf[at, :], w_cols[...]).astype(bf16)

    starts, reaches = [], []
    at = jnp.int32(0)
    for n in range(seg_len.shape[1]):
        parent = seg_parent[0, n]
        grand = seg_parent[0, parent]
        starts.append(at)
        reaches.append(
            (jnp.int32(1) << n) | (jnp.int32(1) << parent) | (jnp.int32(1) << grand)
        )
        at = at + seg_len[0, n]
    loads[2].wait()
    loads[3].wait()

    def unturn(values, at):
        return (
            values * tables[0, at, :]
            - pltpu.roll(values, HEAD_DIM - ROT_DIM // 2, 1) * tables[1, at, :]
            - pltpu.roll(values, ROT_DIM // 2, 1) * tables[2, at, :]
        )

    for m in range(heads):
        lanes = slice(m * HEAD_DIM, (m + 1) * HEAD_DIM)
        key_acc[...] = jnp.zeros_like(key_acc)
        value_acc[...] = jnp.zeros_like(value_acc)
        for n in range(tokens // tall):
            mine = pl.ds(n * tall, tall)
            seen = (n + 1) * tall
            upto = pl.ds(0, seen)
            token = n * tall + lax.broadcasted_iota(jnp.int32, (tall, 1), 0)
            key = lax.broadcasted_iota(jnp.int32, (1, seen), 1)
            reach = jnp.zeros((tall, 1), jnp.int32) + reaches[0]
            label = jnp.ones((1, seen), jnp.int32)
            for k in range(1, len(starts)):
                reach = jnp.where(token >= starts[k], reaches[k], reach)
                label = jnp.where(key >= starts[k], 1 << k, label)
            allowed = ((reach & label) != 0) & (key <= token)
            query = arrived[0, mine, lanes]
            keys = arrived[1, upto, lanes]
            values = arrived[2, upto, lanes]
            out_grad_rows = att_grad[mine, lanes]
            scores = jnp.where(allowed, dot_nt(query, keys) * scale, masked_score)
            expo = jnp.exp(scores - jnp.max(scores, axis=1, keepdims=True))
            probs = expo * (1.0 / jnp.sum(expo, axis=1, keepdims=True))
            weights = probs.astype(bf16)
            attended[mine, lanes] = dot_nn(weights, values).astype(bf16)
            prob_grad = dot_nt(out_grad_rows, values)
            delta = jnp.sum(probs * prob_grad, axis=1, keepdims=True)
            score_grad = (probs * (prob_grad - delta)).astype(bf16)
            query_grad = dot_nn(score_grad, keys) * scale
            returns[0, mine, lanes] = unturn(query_grad, mine).astype(bf16)
            key_acc[upto, :] += dot_tn(score_grad, query)
            value_acc[upto, :] += dot_tn(weights, out_grad_rows)

        for n in range(tokens // tall):
            mine = pl.ds(n * tall, tall)
            returns[1, mine, lanes] = unturn(key_acc[mine, :] * scale, mine).astype(bf16)
            returns[2, mine, lanes] = value_acc[mine, :].astype(bf16)

    def to_owner(kind):
        block = kind * group + pair_of(ctx, group)
        owner, slot = lax.div(block, 3), lax.rem(block, 3)
        remote = copy_to(
            returns.at[kind], returned.at[slot], head_send.at[kind], head_recv.at[slot], (dp, owner)
        )
        local = pltpu.make_async_copy(returns.at[kind], returned.at[slot], head_send.at[kind])
        return owner == ctx, remote, local

    def turns_corner(device, target):
        return (device % RAILS != target % RAILS) & (
            lax.div(device, RAILS) != lax.div(target, RAILS)
        )

    def owner_of(device, kind):
        block = kind * group + pair_of(device, group)
        return lax.div(block, 3), lax.rem(block, 3)

    def to_corner(kind):
        return copy_to(returns.at[kind], passing, head_send.at[kind], pass_recv.at[0], other)

    def hand_on(act_on):
        partner = ctx + 1 - 2 * y
        for kind in range(3):
            owner, slot = owner_of(partner, kind)
            arriving = copy_to(passing, passing, pass_send.at[0], pass_recv.at[0], other)
            onward = copy_to(
                passing, returned.at[slot], pass_send.at[0], head_recv.at[slot], (dp, owner)
            )
            pl.when(turns_corner(partner, owner))(
                lambda arriving=arriving, onward=onward: act_on(arriving, onward)
            )

    def pass_on(arriving, onward):
        arriving.wait_recv()
        onward.start()

    for kind in range(3):
        here, remote, local = to_owner(kind)
        first = to_corner(kind)
        corner = turns_corner(ctx, owner_of(ctx, kind)[0])
        pl.when(here)(lambda local=local: local.start())
        pl.when(corner)(lambda first=first: first.start())
        pl.when(jnp.logical_not(here | corner))(lambda remote=remote: remote.start())

    @pl.loop(0, group)
    def _(n):
        at = pl.ds(pl.multiple_of(n * head_cols, head_cols), head_cols)
        out_grad[n] = dot_tn(g_buf[:, at], attended[...]).astype(bf16)

    core_tiles = qkv_core.shape[0]
    out_to_core = copy_to(
        out_grad.at[:, pl.ds((1 - core) * half, half)],
        out_core,
        core_send.at[core_tiles],
        core_recv.at[core_tiles],
        sibling,
    )
    out_to_core.start()

    loads[4].wait()

    @pl.loop(0, tokens // tall)
    def _(n):
        at = pl.ds(pl.multiple_of(n * tall, tall), tall)

        @pl.loop(0, columns // wide)
        def _(m):
            cols = pl.ds(pl.multiple_of(m * wide, wide), wide)
            part[at, cols] = (
                part[at, cols].astype(f32) + dot_nt(attended[at, :], w_cols[cols, :])
            ).astype(bf16)

    low = z < depth // 2
    order = [
        jnp.where(low, depth - 1, 0),
        jnp.where(low, depth - 2, 1),
        jnp.where(low, 1 - z, 2 * depth - 3 - z),
        z,
    ]
    parts = (part, back)

    def chunk(i, at_z, at_y):
        return parts[i].at[pl.ds(pl.multiple_of((at_z * RAILS + at_y) * rows, rows), rows)]

    def swap(i, s):
        return copy_to(
            chunk(i, order[s], 1 - y),
            y_buf.at[i, order[s]],
            y_send.at[i, s],
            y_recv.at[i, s],
            other,
        )

    def upward(i, at):
        return copy_to(
            chunk(i, at, y), z_buf.at[i, at], up_send.at[i, at], up_recv.at[i, at], above
        )

    def downward(i, at, slot):
        return copy_to(
            chunk(i, at, y), z_buf.at[i, slot], down_send.at[i, at], down_recv.at[i, at], below
        )

    def down_slot(at, owner_z):
        return jnp.where(at == owner_z, depth, at)

    def scatter_step(i, s):
        at = order[s]
        swap(i, s).wait_recv()
        mine = chunk(i, at, y)
        add(mine, mine, y_buf.at[i, at])

        @pl.when((at >= z) & has_below)
        def _():
            upward(i, at).wait_recv()
            add(mine, mine, z_buf.at[i, at])

        @pl.when((at <= z) & has_above)
        def _():
            slot = down_slot(at, z)
            downward(i, at, slot).wait_recv()
            add(mine, mine, z_buf.at[i, slot])

        pl.when(at > z)(lambda: upward(i, at).start())
        pl.when(at < z)(lambda: downward(i, at, down_slot(at, z - 1)).start())

    results = (part_out, back_out)

    def scatter_out(i):
        return pltpu.make_async_copy(chunk(i, z, y), results[i], result_sem.at[i])

    for s in range(depth):
        swap(0, s).start()

    hand_on(pass_on)
    out_to_core.wait_recv()

    @pl.loop(0, group)
    def _(n):
        out_core[n] = (
            out_core[n].astype(f32)
            + out_grad[n, pl.ds(pl.multiple_of(core * half, half), half), :].astype(f32)
        ).astype(bf16)

    my_cols = pl.ds(pl.multiple_of(pair_of(ctx, group) * head_cols, head_cols), head_cols)

    def out_block(n):
        owner = lax.rem(ctx + n, group)
        return copy_to(
            out_core.at[owner],
            out_rows.at[:, my_cols],
            block_send.at[n],
            block_recv.at[n],
            (dp, owner),
        )

    for n in range(1, group):
        out_block(n).start()
    own_block = pltpu.make_async_copy(out_core.at[ctx], out_rows.at[:, my_cols], block_send.at[0])
    own_block.start()

    again = pltpu.make_async_copy(pairs, g_buf, sum_sem.at[0])
    again.start()

    def qkv_half(t, which):
        start = pl.multiple_of(t * 2 * half + which * half, half)
        return qkv_grad.at[pl.ds(start, half)]

    def to_core(t):
        return copy_to(
            qkv_half(t, 1 - core), qkv_core.at[t], core_send.at[t], core_recv.at[t], sibling
        )

    def across_x(t):
        source = qkv_half(t, core) if t < core_tiles else out_rows
        return copy_to(source, from_x.at[t], x_send.at[t], x_recv.at[t], across)

    spots = (
        [(down_out, 2 * half * t) for t in range(pair_tiles // 2)]
        + [(up_out, 2 * half * t) for t in range(pair_tiles // 2)]
        + [(qkv_out, 2 * half * t) for t in range(core_tiles)]
        + [(out_out, 0)]
    )
    def total_of(t):
        return pairs_x.at[t] if t < pair_tiles else from_x.at[t - pair_tiles]

    def spot(t, which):
        array, first = spots[t]
        return array.at[pl.ds(pl.multiple_of(first + which * half, half), half)]

    def keep(t):
        return pltpu.make_async_copy(total_of(t), spot(t, core), keep_sem.at[t])

    def finish(t, which):
        return copy_to(total_of(t), spot(t, which), done_send.at[t], done_recv.at[t], sibling)

    def x_sum(t):
        total = total_of(t)
        if t < pair_tiles:
            pair_x(t).wait_recv()
            add(total, total, g_buf.at[pl.ds(t * half, half)])
        else:
            n = t - pair_tiles
            across_x(n).wait_recv()
            add(total, total, qkv_half(n, core) if n < core_tiles else out_rows)
        keep(t).start()
        finish(t, core).start()

    loads[9].wait()
    again.wait()
    for j in range(3):
        here, remote, local = to_owner(j)
        pl.when(here)(lambda local=local: local.wait())
        source = pair_of(lax.rem(3 * ctx + j, group), group)
        arriving = copy_to(
            returns.at[0], returned.at[j], head_send.at[0], head_recv.at[j], other
        )
        pl.when(source != ctx)(lambda arriving=arriving: arriving.wait_recv())
    for n in (5, 6, 7):
        loads[n].wait()
    sums[...] = jnp.zeros_like(sums)

    @pl.loop(0, tokens // tall)
    def _(n):
        at = pl.ds(pl.multiple_of(n * tall, tall), tall)

        @pl.loop(0, columns // wide)
        def _(m):
            cols = pl.ds(pl.multiple_of(m * wide, wide), wide)
            entry = dot_nn(returned[0, at, :], w_qkv[0:head_cols, cols])
            for j in range(1, 3):
                entry += dot_nn(
                    returned[j, at, :], w_qkv[j * head_cols : (j + 1) * head_cols, cols]
                )
            normed = (h_buf[at, cols].astype(f32) - tables[3, at, 0:1]) * tables[3, at, 1:2]
            sums[0:1, cols] += jnp.sum(entry * normed, axis=0, keepdims=True)
            sums[1:2, cols] += jnp.sum(entry, axis=0, keepdims=True)
            back[at, cols] = (back[at, cols].astype(f32) + entry * norms[0:1, cols]).astype(bf16)

    stages = (sibling, other, near, far, across)

    def exchange(n):
        return copy_to(
            vec_buf.at[2 * n], vec_buf.at[2 * n + 1], vec_send.at[n], vec_recv.at[n], stages[n]
        )

    lane_cols = vec_buf.shape[2]

    def place_vector(at, values):
        for n in range(values.shape[1] // lane_cols):
            vec_buf[0, pl.ds(at + n, 1), :] = values[:, n * lane_cols : (n + 1) * lane_cols]

    vec_buf[0] = jnp.zeros(vec_buf.shape[1:], f32)
    long = columns // lane_cols
    place_vector(0, sums[0:1, :])
    place_vector(long, sums[1:2, :])
    place_vector(2 * long, mlp_sums[0:1, :])
    place_vector(3 * long, mlp_sums[1:2, :])
    place_vector(4 * long, local_sums[...])
    each = head_cols // lane_cols
    for j in range(3):
        place_vector(
            5 * long + (3 * ctx + j) * each,
            jnp.sum(returned[j].astype(f32), axis=0, keepdims=True),
        )
    place_vector(
        5 * long + 3 * group * each + ctx * (up_sums.shape[1] // lane_cols), up_sums[...]
    )
    exchange(0).start()

    def vector_step(n):
        exchange(n).wait_recv()
        total = vec_buf[2 * n] + vec_buf[2 * n + 1]
        if n + 1 < len(stages):
            vec_buf[2 * n + 2] = total
            exchange(n + 1).start()
        else:
            vectors_out[...] = total

    vector_step(0)
    for s in range(depth):
        swap(1, s).start()

    loads[8].wait()
    for t in range(core_tiles):

        @pl.loop(0, columns // (2 * wide))
        def _(m):
            cols = pl.ds(pl.multiple_of(m * 2 * wide, 2 * wide), 2 * wide)
            qkv_grad[pl.ds(t * 2 * half, 2 * half), cols] = dot_tn(
                returned[t], x_buf[:, cols]
            ).astype(bf16)

        to_core(t).start()

    for t in range(core_tiles):
        to_core(t).wait_recv()
        mine = qkv_half(t, core)
        add(mine, mine, qkv_core.at[t])
        across_x(t).start()
    stats_out[...] = tables[3, pl.ds(pl.multiple_of(ctx * rows, rows), rows), :]
    for s in range(depth):
        scatter_step(0, s)
        if s == 0:
            x_sum(0)
            x_sum(1)
            x_sum(2)
        x_sum(3 + s)
    scatter_out(0).start()
    own_block.wait()
    for n in range(1, group):
        source = lax.rem(ctx + group - n, group)
        theirs = pl.ds(
            pl.multiple_of(pair_of(source, group) * head_cols, head_cols), head_cols
        )
        copy_to(
            out_core.at[ctx], out_rows.at[:, theirs], block_send.at[n], block_recv.at[n], other
        ).wait_recv()
    across_x(core_tiles).start()
    vector_step(1)
    x_sum(7)
    scatter_step(1, 0)
    vector_step(2)
    x_sum(pair_tiles)
    scatter_step(1, 1)
    vector_step(3)
    x_sum(pair_tiles + 1)
    scatter_step(1, 2)
    x_sum(pair_tiles + 2)
    scatter_step(1, 3)
    scatter_out(1).start()
    x_sum(pair_tiles + 3)
    vector_step(4)

    hand_on(lambda arriving, onward: onward.wait_send())
    for kind in range(3):
        here, remote, _ = to_owner(kind)
        first = to_corner(kind)
        corner = turns_corner(ctx, owner_of(ctx, kind)[0])
        pl.when(corner)(lambda first=first: first.wait_send())
        pl.when(jnp.logical_not(here | corner))(lambda remote=remote: remote.wait_send())
    for n in range(1, group):
        out_block(n).wait_send()
    out_to_core.wait_send()
    for t in range(core_tiles):
        to_core(t).wait_send()
    for t in range(core_tiles + 1):
        across_x(t).wait_send()
    for t in range(pair_tiles):
        pair_x(t).wait_send()
    for t in range(len(spots)):
        keep(t).wait()
        finish(t, core).wait_send()
        finish(t, 1 - core).wait_recv()
    for n in range(len(stages)):
        exchange(n).wait_send()
    for i in range(2):
        scatter_out(i).wait()
        for s in range(depth):
            swap(i, s).wait_send()
            at = order[s]
            pl.when(at > z)(lambda i=i, at=at: upward(i, at).wait_send())
            pl.when(at < z)(
                lambda i=i, at=at: downward(i, at, down_slot(at, z - 1)).wait_send()
            )


def tail_pass(
    group,
    pairs,
    arrived,
    grad_all,
    w_cols,
    part,
    back,
    x_attn,
    w_qkv,
    hidden_all,
    tables,
    early,
    norms,
    mlp_sums,
    up_sums,
    local_sums,
    seg_len,
    seg_parent,
):
    tokens, columns = hidden_all.shape
    depth = group // RAILS
    rows = tokens // group
    head_cols = arrived.shape[2]
    units = up_sums.shape[1]
    half = 128
    pair_tiles = pairs.shape[0] // half
    core_tiles = w_qkv.shape[0] // (2 * half)
    lane_cols = 256
    vectors = (5 * columns + 3 * columns + group * units) // lane_cols
    sems = pltpu.SemaphoreType.DMA
    shape = jax.ShapeDtypeStruct
    vmem = pltpu.VMEM
    anywhere = pl.BlockSpec(memory_space=pl.ANY)
    small = pl.BlockSpec(memory_space=pltpu.VMEM)
    smem = pl.BlockSpec(memory_space=pltpu.SMEM)
    whole = vmem((tokens, columns), bf16)
    every = pair_tiles + core_tiles + 1
    return pl.pallas_call(
        functools.partial(tail_kernel, group),
        out_shape=(
            shape((rows, columns), bf16),
            shape((rows, columns), bf16),
            shape((units, columns), bf16),
            shape((units, columns), bf16),
            shape((2 * half, columns), bf16),
            shape(w_qkv.shape, bf16),
            shape((tokens, head_cols), bf16),
            shape((vectors, lane_cols), f32),
            shape((rows, HEAD_DIM), f32),
        ),
        in_specs=[anywhere] * 11 + [small] * 4 + [smem] * 2,
        out_specs=[anywhere] * 7 + [small] * 2,
        scratch_shapes=[
            vmem(arrived.shape, bf16),
            whole,
            vmem(w_cols.shape, bf16),
            whole,
            whole,
            whole,
            vmem(w_qkv.shape, bf16),
            whole,
            vmem(tables.shape, f32),
            vmem((tokens, head_cols), bf16),
            vmem((tokens, head_cols), bf16),
            vmem(arrived.shape, bf16),
            vmem(arrived.shape, bf16),
            vmem((2, depth, rows, columns), bf16),
            vmem((2, depth + 1, rows, columns), bf16),
            vmem((group, 2 * half, head_cols), bf16),
            vmem(w_qkv.shape, bf16),
            vmem((core_tiles, half, columns), bf16),
            vmem((group, half, head_cols), bf16),
            vmem((half, columns), bf16),
            vmem((core_tiles + 1, half, columns), bf16),
            vmem((pair_tiles, half, columns), bf16),
            vmem((tokens, HEAD_DIM), f32),
            vmem((tokens, HEAD_DIM), f32),
            vmem((2, columns), f32),
            vmem((10, vectors, lane_cols), f32),
            sems((10,)),
        ]
        + [sems((2, depth))] * 6
        + [sems((2,)), sems((3,)), sems((3,)), sems((pair_tiles,)), sems((pair_tiles,))]
        + [sems((core_tiles + 1,))] * 2
        + [sems((group,))] * 2
        + [sems((core_tiles + 1,))] * 2
        + [sems((every,))] * 3
        + [sems((5,))] * 2
        + [sems((1,))] * 3,
        compiler_params=pltpu.CompilerParams(
            collective_id=1, has_side_effects=True, vmem_limit_bytes=62 * 2**20
        ),
        name="tail_pass",
    )(
        pairs,
        arrived,
        grad_all,
        w_cols,
        part,
        back,
        x_attn,
        w_qkv,
        hidden_all,
        tables,
        early,
        norms,
        mlp_sums,
        up_sums,
        local_sums,
        seg_len,
        seg_parent,
    )


def finish_kernel(*refs):
    grads, (hidden, grad, summed, w_sum, stats, norms, vectors) = refs[:4], refs[4:11]
    outs, (hidden_out, grad_in), vector_outs = refs[11:15], refs[15:17], refs[17:25]
    narrow, wide, in_sem, out_sem = refs[25:]
    tall = narrow.shape[1]
    tiles = [(n, m) for n in range(4) for m in range(grads[n].shape[0] // tall)]

    def fetch(t):
        n, m = tiles[t]
        return pltpu.make_async_copy(
            grads[n].at[pl.ds(m * tall, tall)], narrow.at[t], in_sem.at[t]
        )

    def store(t):
        n, m = tiles[t]
        return pltpu.make_async_copy(wide.at[t], outs[n].at[pl.ds(m * tall, tall)], out_sem.at[t])

    for t in range(len(tiles)):
        fetch(t).start()
    rows = 32
    for t in range(len(tiles)):
        fetch(t).wait()

        @pl.loop(0, tall // rows)
        def _(n):
            at = pl.ds(pl.multiple_of(n * rows, rows), rows)
            wide[t, at, :] = narrow[t, at, :].astype(f32)

        store(t).start()

    @pl.loop(0, hidden.shape[0] // rows)
    def _(n):
        at = pl.ds(pl.multiple_of(n * rows, rows), rows)
        values = hidden[at, :].astype(f32)
        hidden_out[at, :] = (
            values + summed[at, :].astype(f32) + norms[4:5, :] + norms[5:6, :]
        ).astype(bf16)
        rstd = stats[at, 1:2]
        normed = (values - stats[at, 0:1]) * rstd
        back = w_sum[at, :].astype(f32)
        along = jnp.mean(back * normed, axis=1, keepdims=True)
        grad_in[at, :] = (
            grad[at, :].astype(f32)
            + (back - jnp.mean(back, axis=1, keepdims=True) - normed * along) * rstd
        )

    lane_cols = vectors.shape[1]
    places = [0, 1, 2, 3, 4, 4, 5, 8]
    each = hidden.shape[1] // lane_cols
    for out, place_of in zip(vector_outs, places):
        for n in range(out.shape[0] // lane_cols):
            out[pl.ds(n * lane_cols, lane_cols)] = vectors[place_of * each + n, :]
    for t in range(len(tiles)):
        store(t).wait()


def finish_pass(down, up, qkv, out, hidden, grad, summed, w_sum, stats, norms, vectors):
    tall = 256
    columns = hidden.shape[1]
    grads = (down, up, qkv, out)
    tiles = sum(array.shape[0] for array in grads) // tall
    shape = jax.ShapeDtypeStruct
    anywhere = pl.BlockSpec(memory_space=pl.ANY)
    vmem = pl.BlockSpec(memory_space=pltpu.VMEM)
    lengths = [columns] * 6 + [3 * columns, vectors.size - 8 * columns]
    return pl.pallas_call(
        finish_kernel,
        out_shape=[shape(array.shape, f32) for array in grads]
        + [shape(hidden.shape, bf16), shape(hidden.shape, f32)]
        + [shape((length,), f32) for length in lengths],
        in_specs=[anywhere] * 4 + [vmem] * 7,
        out_specs=[anywhere] * 4 + [vmem] * 10,
        scratch_shapes=[
            pltpu.VMEM((tiles, tall, columns), bf16),
            pltpu.VMEM((tiles, tall, columns), f32),
            pltpu.SemaphoreType.DMA((tiles,)),
            pltpu.SemaphoreType.DMA((tiles,)),
        ],
        compiler_params=pltpu.CompilerParams(vmem_limit_bytes=56 * 2**20),
        name="finish_pass",
    )(*grads, hidden, grad, summed, w_sum, stats, norms, vectors)


def body(
    hidden_in,
    grad_out,
    seg_len,
    seg_parent,
    gain_attn,
    shift_attn,
    w_qkv,
    bias_qkv,
    w_out,
    bias_out,
    gain_mlp,
    shift_mlp,
    w_up,
    bias_up,
    w_down,
    bias_down,
):
    group = lax.axis_size("ctx")
    head_cols = HEADS // group * HEAD_DIM
    vectors = (
        gain_attn,
        shift_attn,
        gain_mlp,
        shift_mlp,
        bias_out,
        bias_down,
        bias_qkv,
        bias_up,
    )
    (
        hidden_all,
        grad_all,
        x_attn,
        arrived,
        mlp_part,
        mlp_back,
        pairs,
        early,
        w_cols,
        _,
        tables,
        mlp_sums,
        up_sums,
        local_sums,
        norms,
    ) = layer_pass(
        group,
        hidden_in[0],
        grad_out[0],
        w_up,
        w_down,
        w_qkv,
        w_out,
        vectors,
        seg_len,
        seg_parent,
    )
    summed, w_sum, down_grad, up_grad, out_grad, qkv_grad, _, vectors, stats = tail_pass(
        group,
        pairs,
        arrived,
        grad_all,
        w_cols.reshape(D, head_cols),
        mlp_part,
        mlp_back,
        x_attn,
        w_qkv,
        hidden_all,
        tables,
        early,
        norms,
        mlp_sums,
        up_sums,
        local_sums,
        seg_len,
        seg_parent,
    )
    (
        down_grad,
        up_grad,
        qkv_grad,
        out_grad,
        hidden_out,
        grad_in,
        gain_grad_a,
        shift_grad_a,
        gain_grad_m,
        shift_grad_m,
        out_bias_grad,
        down_bias_grad,
        qkv_bias_grad,
        up_bias_grad,
    ) = finish_pass(
        down_grad,
        up_grad,
        qkv_grad,
        out_grad,
        hidden_in[0],
        grad_out[0],
        summed,
        w_sum,
        stats,
        norms,
        vectors,
    )
    return (
        hidden_out[None],
        grad_in[None],
        gain_grad_a,
        shift_grad_a,
        qkv_grad,
        qkv_bias_grad,
        out_grad,
        out_bias_grad,
        gain_grad_m,
        shift_grad_m,
        up_grad,
        up_bias_grad,
        down_grad,
        down_bias_grad,
    )


block_limit = 512


def tree_tables(seg_len, seg_parent):
    seg_count = seg_len.shape[0]
    labels = jnp.arange(seg_count, dtype=jnp.int32)
    earlier = labels[:, None] > labels[None, :]
    seg_starts = jnp.sum(jnp.where(earlier, seg_len[None, :], 0), axis=1)
    seg_ends = seg_starts + seg_len
    parent_hit = seg_parent[:, None] == labels[None, :]
    grand_parent = jnp.sum(jnp.where(parent_hit, seg_parent[None, :], 0), axis=1)
    itself = labels[:, None] == labels[None, :]
    ancestor = itself | parent_hit | (grand_parent[:, None] == labels[None, :])
    path_start = jnp.sum(jnp.where(ancestor & jnp.logical_not(itself), seg_len[None, :], 0), axis=1)
    return (seg_ends, seg_starts, ancestor, path_start)


def rotary_tables(path_pos):
    half_dim = ROT_DIM // 2
    inverse = jnp.power(10000.0, -2.0 * jnp.arange(half_dim, dtype=jnp.float32) / ROT_DIM)
    angles = path_pos.astype(jnp.float32)[:, None] * inverse[None, :]
    angles = jnp.concatenate([angles, angles], axis=1)
    return (jnp.cos(angles), jnp.sin(angles))


def rotate(head_values, cosine, sine):
    half_dim = ROT_DIM // 2
    turned = head_values[..., :ROT_DIM]
    swapped = jnp.concatenate([-turned[..., half_dim:], turned[..., :half_dim]], axis=-1)
    mixed = turned * cosine[:, None, :] + swapped * sine[:, None, :]
    return jnp.concatenate([mixed, head_values[..., ROT_DIM:]], axis=-1)


def gelu_slope(pre_act):
    normal_cdf = 0.5 * (1.0 + lax.erf(pre_act / math.sqrt(2.0)))
    return normal_cdf + pre_act * jnp.exp(-0.5 * pre_act * pre_act) / math.sqrt(2.0 * math.pi)


def layer_norm(values, gain_vec, shift_vec):
    average = jnp.mean(values, axis=-1, keepdims=True)
    centred = values - average
    spread = jnp.mean(centred * centred, axis=-1, keepdims=True)
    return centred * lax.rsqrt(spread + norm_eps) * gain_vec + shift_vec


def segment_hot(row_ids, seg_ends):
    seg_index = jnp.sum((row_ids[:, None] >= seg_ends[None, :]).astype(jnp.int32), axis=1)
    labels = jnp.arange(seg_ends.shape[0], dtype=jnp.int32)
    return (seg_index[:, None] == labels[None, :]).astype(jnp.float32)


def row_lookup(row_ids, seg_ends, ancestor_f):
    row_hot = segment_hot(row_ids, seg_ends)
    return (row_hot, jnp.dot(row_hot, ancestor_f))


def permitted(query_ids, query_reach, key_ids, key_hot):
    linked = jnp.dot(query_reach, key_hot.T) > 0.5
    return linked & (key_ids[None, :] <= query_ids[:, None])


def inner_block(row_count):
    block_rows = row_count
    while block_rows > block_limit and block_rows % 2 == 0:
        block_rows = block_rows // 2
    return block_rows


def gather_body(
    hidden_in,
    grad_out,
    seg_len,
    seg_parent,
    gain_attn,
    shift_attn,
    w_qkv,
    bias_qkv,
    w_out,
    bias_out,
    gain_mlp,
    shift_mlp,
    w_up,
    bias_up,
    w_down,
    bias_down,
):
    local_rows = hidden_in.shape[1]
    scale_factor = 1.0 / math.sqrt(HEAD_DIM)
    head_shape = (local_rows, HEADS, HEAD_DIM)
    seg_ends, seg_starts, ancestor, path_start = tree_tables(seg_len[0], seg_parent[0])
    ancestor_f = ancestor.astype(jnp.float32)
    my_ids = lax.axis_index("ctx") * local_rows + jnp.arange(local_rows, dtype=jnp.int32)
    my_hot, my_reach = row_lookup(my_ids, seg_ends, ancestor_f)
    shift_table = path_start - seg_starts
    path_pos = my_ids + jnp.sum(my_hot.astype(jnp.int32) * shift_table[None, :], axis=1)
    cosine, sine = rotary_tables(path_pos)
    inputs_f = hidden_in[0].astype(jnp.float32)
    gain_a = gain_attn.astype(jnp.float32)
    shift_a = shift_attn.astype(jnp.float32)
    gain_m = gain_mlp.astype(jnp.float32)
    shift_m = shift_mlp.astype(jnp.float32)
    bias_up_f = bias_up.astype(jnp.float32)
    x_attn = layer_norm(inputs_f, gain_a, shift_a).astype(jnp.bfloat16)
    x_mlp = layer_norm(inputs_f, gain_m, shift_m).astype(jnp.bfloat16)
    qkv = jnp.einsum(
        "td,nd->tn",
        x_attn,
        lax.all_gather(w_qkv, "ctx", axis=0, tiled=True),
        preferred_element_type=jnp.float32,
    ) + bias_qkv.astype(jnp.float32)
    queries = rotate(qkv[:, :D].reshape(head_shape), cosine, sine).astype(jnp.bfloat16)
    keys_heads = rotate(qkv[:, D : 2 * D].reshape(head_shape), cosine, sine).astype(jnp.bfloat16)
    values_flat = qkv[:, 2 * D :].astype(jnp.bfloat16)
    values_heads = values_flat.reshape(head_shape)
    keys_flat = keys_heads.reshape(local_rows, D)
    queries_flat = queries.reshape(local_rows, D)

    def split_blocks(shard_pieces):
        row_count = shard_pieces[0].shape[0]
        block_rows = inner_block(row_count)
        block_count = row_count // block_rows
        shaped = tuple(
            (member.reshape(block_count, block_rows, HEADS, HEAD_DIM) for member in shard_pieces)
        )
        starts = block_rows * jnp.arange(block_count, dtype=jnp.int32)
        return shaped + (starts,)

    def attend_block(fold_state, block_items):
        key_block, value_block, block_start = block_items
        block_rows = key_block.shape[0]
        key_ids = block_start + jnp.arange(block_rows, dtype=jnp.int32)
        allowed = permitted(my_ids, my_reach, key_ids, segment_hot(key_ids, seg_ends))
        row_top, row_total, partial_value = fold_state
        scores = (
            jnp.einsum("qhd,khd->qhk", queries, key_block, preferred_element_type=jnp.float32)
            * scale_factor
        )
        scores = jnp.where(allowed[:, None, :], scores, masked_score)
        new_top = jnp.maximum(row_top, jnp.max(scores, axis=-1))
        factor = jnp.exp(row_top - new_top)
        weights = jnp.exp(scores - new_top[:, :, None])
        row_total = row_total * factor + jnp.sum(weights, axis=-1)
        partial_value = partial_value * factor[:, :, None] + jnp.einsum(
            "qhk,khd->qhd",
            weights.astype(jnp.bfloat16),
            value_block,
            preferred_element_type=jnp.float32,
        )
        fold_state = (new_top, row_total, partial_value)
        return (fold_state, None)

    start_state = (
        jnp.full((local_rows, HEADS), masked_score, jnp.float32),
        jnp.zeros((local_rows, HEADS), jnp.float32),
        jnp.zeros(head_shape, jnp.float32),
    )
    row_top, row_total, partial_value = lax.scan(
        attend_block,
        start_state,
        split_blocks(
            (
                lax.all_gather(keys_flat, "ctx", axis=0, tiled=True),
                lax.all_gather(values_flat, "ctx", axis=0, tiled=True),
            )
        ),
    )[0]
    log_total = row_top + jnp.log(row_total)
    attended_f = partial_value / row_total[:, :, None]
    attended = attended_f.reshape(local_rows, D).astype(jnp.bfloat16)
    attn_proj = jnp.einsum(
        "td,nd->tn",
        attended,
        lax.all_gather(w_out, "ctx", axis=0, tiled=True),
        preferred_element_type=jnp.float32,
    )

    def mlp_pre(up_rows):
        return (
            jnp.einsum("td,nd->tn", x_mlp, up_rows, preferred_element_type=jnp.float32) + bias_up_f
        )

    up_rows = lax.all_gather(w_up, "ctx", axis=0, tiled=True)
    down_rows = lax.all_gather(w_down, "ctx", axis=0, tiled=True)
    activated = jax.nn.gelu(mlp_pre(up_rows), approximate=False).astype(jnp.bfloat16)
    mlp_sum = jnp.dot(activated, down_rows, preferred_element_type=jnp.float32)
    bias_out_f = bias_out.astype(jnp.float32)
    bias_down_f = bias_down.astype(jnp.float32)
    hidden_out = (inputs_f + attn_proj + bias_out_f + mlp_sum + bias_down_f).astype(jnp.bfloat16)
    grad_b = grad_out[0]
    grad_f = grad_b.astype(jnp.float32)
    up_rows = lax.all_gather(w_up, "ctx", axis=0, tiled=True)
    down_rows = lax.all_gather(w_down, "ctx", axis=0, tiled=True)
    pre_act = mlp_pre(up_rows)
    activated = jax.nn.gelu(pre_act, approximate=False).astype(jnp.bfloat16)
    act_grad = jnp.einsum("td,nd->tn", grad_b, down_rows, preferred_element_type=jnp.float32)
    pre_grad = (act_grad * gelu_slope(pre_act)).astype(jnp.bfloat16)
    input_grad = jnp.dot(pre_grad, up_rows, preferred_element_type=jnp.float32)
    act_all = activated
    pre_grad_all = pre_grad
    act_all, pre_grad_all, mlp_in_grad = (act_all, pre_grad_all, input_grad)
    attended_grad = jnp.dot(
        grad_b, lax.all_gather(w_out, "ctx", axis=0, tiled=True), preferred_element_type=jnp.float32
    ).astype(jnp.bfloat16)
    attended_grad_heads = attended_grad.reshape(head_shape)
    row_delta = jnp.sum(attended_grad_heads.astype(jnp.float32) * attended_f, axis=-1)
    all_log_total, all_delta = (
        lax.all_gather(log_total, "ctx", axis=0, tiled=True),
        lax.all_gather(row_delta, "ctx", axis=0, tiled=True),
    )

    def back_block(fold_state, block_items):
        key_block, value_block, query_block, grad_block, block_start = block_items
        block_rows = key_block.shape[0]
        other_ids = block_start + jnp.arange(block_rows, dtype=jnp.int32)
        other_hot, other_reach = row_lookup(other_ids, seg_ends, ancestor_f)
        allowed_in = permitted(my_ids, my_reach, other_ids, other_hot)
        allowed_out = permitted(other_ids, other_reach, my_ids, my_hot)
        other_log = lax.dynamic_slice_in_dim(all_log_total, block_start, block_rows, 0)
        other_delta = lax.dynamic_slice_in_dim(all_delta, block_start, block_rows, 0)
        query_grad, key_grad, value_grad = fold_state
        scores = (
            jnp.einsum("qhd,khd->qhk", queries, key_block, preferred_element_type=jnp.float32)
            * scale_factor
        )
        scores = jnp.where(allowed_in[:, None, :], scores, masked_score)
        prob_mass = jnp.exp(scores - log_total[:, :, None])
        prob_grad = jnp.einsum(
            "qhd,khd->qhk", attended_grad_heads, value_block, preferred_element_type=jnp.float32
        )
        score_grad = (prob_mass * (prob_grad - row_delta[:, :, None])).astype(jnp.bfloat16)
        query_grad = (
            query_grad
            + jnp.einsum("qhk,khd->qhd", score_grad, key_block, preferred_element_type=jnp.float32)
            * scale_factor
        )
        outgoing_key_grad = key_grad
        outgoing_value_grad = value_grad
        scores = (
            jnp.einsum("qhd,khd->qhk", query_block, keys_heads, preferred_element_type=jnp.float32)
            * scale_factor
        )
        scores = jnp.where(allowed_out[:, None, :], scores, masked_score)
        prob_mass = jnp.exp(scores - other_log[:, :, None])
        outgoing_value_grad = outgoing_value_grad + jnp.einsum(
            "qhk,qhd->khd",
            prob_mass.astype(jnp.bfloat16),
            grad_block,
            preferred_element_type=jnp.float32,
        )
        prob_grad = jnp.einsum(
            "qhd,khd->qhk", grad_block, values_heads, preferred_element_type=jnp.float32
        )
        score_grad = (prob_mass * (prob_grad - other_delta[:, :, None])).astype(jnp.bfloat16)
        outgoing_key_grad = (
            outgoing_key_grad
            + jnp.einsum(
                "qhk,qhd->khd", score_grad, query_block, preferred_element_type=jnp.float32
            )
            * scale_factor
        )
        fold_state = (query_grad, outgoing_key_grad, outgoing_value_grad)
        return (fold_state, None)

    zero_heads = jnp.zeros(head_shape, jnp.float32)
    query_grad, key_grad, value_grad = lax.scan(
        back_block,
        (zero_heads, zero_heads, zero_heads),
        split_blocks(
            (
                lax.all_gather(keys_flat, "ctx", axis=0, tiled=True),
                lax.all_gather(values_flat, "ctx", axis=0, tiled=True),
                lax.all_gather(queries_flat, "ctx", axis=0, tiled=True),
                lax.all_gather(attended_grad, "ctx", axis=0, tiled=True),
            )
        ),
    )[0]

    def turn(head_values):
        return rotate(head_values, cosine, sine)

    unturn = jax.vjp(turn, zero_heads)[1]
    qkv_grad = jnp.concatenate(
        [
            unturn(query_grad)[0].reshape(local_rows, D),
            unturn(key_grad)[0].reshape(local_rows, D),
            value_grad.reshape(local_rows, D),
        ],
        axis=1,
    ).astype(jnp.bfloat16)
    attn_in_grad = jnp.dot(
        qkv_grad,
        lax.all_gather(w_qkv, "ctx", axis=0, tiled=True),
        preferred_element_type=jnp.float32,
    )
    pull_attn = jax.vjp(layer_norm, inputs_f, gain_a, shift_a)[1]
    input_part_a, gain_grad_a, shift_grad_a = pull_attn(attn_in_grad)
    pull_mlp = jax.vjp(layer_norm, inputs_f, gain_m, shift_m)[1]
    input_part_m, gain_grad_m, shift_grad_m = pull_mlp(mlp_in_grad)
    grad_in = (grad_f + input_part_a + input_part_m)[None]
    vector_sums = lax.psum(
        (
            gain_grad_a,
            shift_grad_a,
            gain_grad_m,
            shift_grad_m,
            jnp.sum(qkv_grad, axis=0, dtype=jnp.float32),
            jnp.sum(grad_f, axis=0),
            jnp.sum(pre_grad_all, axis=0, dtype=jnp.float32),
        ),
        ("dp", "ctx"),
    )
    group_count = lax.axis_size("ctx")
    section_rows = (3 * D // group_count, D // group_count, FF // group_count, FF // group_count)
    term_sources = (
        (qkv_grad, x_attn),
        (grad_b, attended),
        (pre_grad_all, x_mlp),
        (act_all, grad_b),
    )
    owner_rows = sum(section_rows)
    blocks = jnp.arange(owner_rows * lax.axis_size("ctx") // owner_rows, dtype=jnp.int32)
    parts_list = []
    for (column_source, other_side), full_rows in zip(term_sources, section_rows):
        sub_rows = full_rows // 1
        column_ids = (
            blocks[:, None] * sub_rows + jnp.arange(sub_rows, dtype=jnp.int32)[None, :]
        ).reshape(-1)
        columns = jnp.take(column_source, column_ids, axis=1)
        block_term = jnp.einsum(
            "tr,td->rd", columns, other_side, preferred_element_type=jnp.float32
        )
        parts_list.append(block_term.reshape(blocks.shape[0], sub_rows, D))
    owned_term = lax.psum_scatter(
        jnp.concatenate(parts_list, axis=1).reshape(-1, D).astype(jnp.bfloat16),
        "ctx",
        scatter_dimension=0,
        tiled=True,
    ).astype(jnp.float32)
    cut_a = section_rows[0]
    cut_b = cut_a + section_rows[1]
    cut_c = cut_b + section_rows[2]
    weight_grads = (
        lax.psum(owned_term[:cut_a].astype(jnp.bfloat16), "dp").astype(jnp.float32),
        lax.psum(owned_term[cut_a:cut_b].astype(jnp.bfloat16), "dp").astype(jnp.float32),
        lax.psum(owned_term[cut_b:cut_c].astype(jnp.bfloat16), "dp").astype(jnp.float32),
        lax.psum(owned_term[cut_c:].astype(jnp.bfloat16), "dp").astype(jnp.float32),
    )
    return (
        hidden_out[None],
        grad_in,
        vector_sums[0],
        vector_sums[1],
        weight_grads[0],
        vector_sums[4],
        weight_grads[1],
        vector_sums[5],
        vector_sums[2],
        vector_sums[3],
        weight_grads[2],
        vector_sums[6],
        weight_grads[3],
        vector_sums[5],
    )


def solution(mesh):
    token = P("dp", "ctx", None)
    rows = P("ctx", None)
    return jax.shard_map(
        body if mesh.shape["ctx"] == 8 and mesh.shape["dp"] == 4 else gather_body,
        mesh=mesh,
        in_specs=(
            token,
            token,
            P("dp", None),
            P("dp", None),
            P(),
            P(),
            rows,
            P(),
            rows,
            P(),
            P(),
            P(),
            rows,
            P(),
            rows,
            P(),
        ),
        out_specs=(
            token,
            token,
            P(),
            P(),
            rows,
            P(),
            rows,
            P(),
            P(),
            P(),
            rows,
            P(),
            rows,
            P(),
        ),
        check_vma=False,
    )
```
